32 devices in a mesh: dp: 4 (over y, x), fsdp: 8 (over z, core).
Axes of the slice: x: 2, y: 2, z: 4, core: 2. Of those that a mesh axis runs over, the one named last changes fastest.
Arguments:
- latents: bfloat16 [32, 256, 768], P(('dp', 'fsdp')), may hold values from -6 to 6
- conditioning: bfloat16 [32, 768], P(('dp', 'fsdp')), may hold values from -6 to 6
- cotangent: bfloat16 [32, 256, 768], P(('dp', 'fsdp')), may hold values from -6 to 6
- latent_count: int32 [32], P(('dp', 'fsdp')), may hold values from 0 to 1, as said below
- ada_weight: bfloat16 [768, 4608], P('dp', 'fsdp'), may hold values from -0.21875 to 0.21875
- ada_bias: bfloat16 [4608], P('fsdp'), may hold values from -3 to 3
- qkv_weight: bfloat16 [768, 2304], P('dp', 'fsdp'), may hold values from -0.21875 to 0.21875
- qv_bias: bfloat16 [1536], P('fsdp'), may hold values from -3 to 3
- proj_weight: bfloat16 [768, 768], P('dp', 'fsdp'), may hold values from -0.875 to 0.875
- proj_bias: bfloat16 [768], P('fsdp'), may hold values from -3 to 3
- fc1_weight: bfloat16 [768, 3072], P('dp', 'fsdp'), may hold values from -0.21875 to 0.21875
- fc1_bias: bfloat16 [3072], P('fsdp'), may hold values from -3 to 3
- fc2_weight: bfloat16 [3072, 768], P('dp', 'fsdp'), may hold values from -0.109375 to 0.109375
- fc2_bias: bfloat16 [768], P('fsdp'), may hold values from -3 to 3
Outputs:
- block_out: bfloat16 [32, 256, 768], P(('dp', 'fsdp'))
- latents_grad: bfloat16 [32, 256, 768], P(('dp', 'fsdp'))
- conditioning_grad: float32 [32, 768], P(('dp', 'fsdp'))
- ada_weight_grad: float32 [768, 4608], P('dp', 'fsdp')
- ada_bias_grad: float32 [4608], P('fsdp')
- qkv_weight_grad: float32 [768, 2304], P('dp', 'fsdp')
- qv_bias_grad: float32 [1536], P('fsdp')
- proj_weight_grad: float32 [768, 768], P('dp', 'fsdp')
- proj_bias_grad: float32 [768], P('fsdp')
- fc1_weight_grad: float32 [768, 3072], P('dp', 'fsdp')
- fc1_bias_grad: float32 [3072], P('fsdp')
- fc2_weight_grad: float32 [3072, 768], P('dp', 'fsdp')
- fc2_bias_grad: float32 [768], P('fsdp')
The draws below stay inside these ranges and needn't reach their ends.
Inputs may be any that keep to these rules, and one draw needn't show every extreme that they name: `latent_count`: exactly 8 slots hold no latent.
All inputs are finite; a program needn't handle non-finite values.
Results may differ from the reference program's by a relative error of at most 0.015.
The reference program's roundings to bfloat16 on the way count: a program that leaves them out, or rounds other values in their place, can miss the bound.
Values may be sent and summed in bfloat16 or wider, within the bound.
A program may use at most 128 MiB of HBM per device.

```python
import math
import jax
import jax.numpy as jnp
from jax import lax

D = 768
HEADS = 12
FF = 3072
SEQ = 256
LATENTS = 32


def draw_latent_count(key, part):
    shuffled = jax.random.permutation(jax.random.fold_in(key, 11), LATENTS)
    return (shuffled >= LATENTS // 4).astype(jnp.int32)


def block_scale(stream_key, dims, shards, least, top_value):
    def one(position, blocks):
        heights = jax.random.uniform(jax.random.fold_in(jax.random.fold_in(stream_key, 6), position), (blocks,), jnp.float32, least / len(shards), top_value / len(shards))
        return jnp.repeat(jnp.exp(heights), dims[position] // blocks).reshape((-1,) + (1,) * (len(dims) - position - 1))

    gain = one(*shards[0])
    for cut in shards[1:]:
        gain = gain * one(*cut)
    return gain


def bell_draw(rng, shape, scale, reach, cuts=(), held_as=jnp.bfloat16):
    array = scale * jax.random.normal(rng, shape, jnp.float32)
    if cuts:
        array = array * block_scale(rng, shape, cuts, -0.22, 0.18)
    return jnp.clip(array, -reach, reach).astype(held_as)


def setup_inputs(seed: int = 0) -> dict:
    splits = jax.random.split(jax.random.key(seed), 15)
    latents = bell_draw(splits[0], (LATENTS, SEQ, D), 1.0, 6.0, ((0, 32),))
    conditioning = bell_draw(splits[1], (LATENTS, D), 1.0, 6.0, ((0, 32),))
    cotangent = bell_draw(splits[2], (LATENTS, SEQ, D), 1.0, 6.0, ((0, 32),))
    latent_count = draw_latent_count(jax.random.fold_in(splits[14], 71), 0)
    ada_weight = bell_draw(splits[4], (D, 6 * D), D ** -0.5, 0.21875, ((0, 4), (1, 8)))
    ada_bias = bell_draw(splits[5], (6 * D,), 0.5, 3.0, ((0, 8),))
    qkv_weight = bell_draw(splits[6], (D, 3 * D), D ** -0.5, 0.21875, ((0, 4), (1, 8)))
    qv_bias = bell_draw(splits[7], (2 * D,), 0.5, 3.0, ((0, 8),))
    proj_weight = bell_draw(splits[8], (D, D), (D // 16) ** -0.5, 0.875, ((0, 4), (1, 8)))
    proj_bias = bell_draw(splits[9], (D,), 0.5, 3.0, ((0, 8),))
    fc1_weight = bell_draw(splits[10], (D, FF), D ** -0.5, 0.21875, ((0, 4), (1, 8)))
    fc1_bias = bell_draw(splits[11], (FF,), 0.5, 3.0, ((0, 8),))
    fc2_weight = bell_draw(splits[12], (FF, D), FF ** -0.5, 0.109375, ((0, 4), (1, 8)))
    fc2_bias = bell_draw(splits[13], (D,), 0.5, 3.0, ((0, 8),))
    return dict(latents=latents, conditioning=conditioning, cotangent=cotangent, latent_count=latent_count, ada_weight=ada_weight, ada_bias=ada_bias, qkv_weight=qkv_weight, qv_bias=qv_bias, proj_weight=proj_weight, proj_bias=proj_bias, fc1_weight=fc1_weight, fc1_bias=fc1_bias, fc2_weight=fc2_weight, fc2_bias=fc2_bias)


@jax.custom_vjp
def low(v):
    return lax.optimization_barrier(v.astype(jnp.bfloat16)).astype(jnp.float32)

@jax.custom_vjp
def low_back(v):
    return v

def low_keep(v):
    return (low(v), None)

def low_pass(kept, grad):
    return (grad,)

def back_keep(v):
    return (v, None)

def back_low(kept, grad):
    return (low(grad),)
low.defvjp(low_keep, low_pass)
low_back.defvjp(back_keep, back_low)
highest = lax.Precision.HIGHEST

def normalize(values):
    center = lax.optimization_barrier(jnp.mean(values, axis=-1, keepdims=True))
    spread = lax.optimization_barrier(jnp.mean(jnp.square(values - center), axis=-1, keepdims=True))
    return (values - center) * lax.rsqrt(spread + 1e-06)

def forward(latent_rows, cond_rows, live_rows, params):
    ada_weight, ada_bias, qkv_weight, qv_bias, proj_weight, proj_bias, fc1_weight, fc1_bias, fc2_weight, fc2_bias = params
    group_count, length, model_width = latent_rows.shape
    head_size = model_width // HEADS
    cond_act = low(jax.nn.silu(cond_rows))
    modulation = jnp.dot(cond_act, ada_weight, precision=highest) + ada_bias
    pieces = [segment[:, None, :] for segment in jnp.split(modulation, 6, axis=-1)]
    shift_one, scale_one, gate_one, shift_two, scale_two, gate_two = pieces
    hidden_one = low(normalize(latent_rows) * (1.0 + scale_one) + shift_one)
    qkv_bias = jnp.concatenate([qv_bias[:model_width], jnp.zeros((model_width,), jnp.float32), qv_bias[model_width:]])
    projected = low(low_back(jnp.einsum('gsd,de->gse', hidden_one, qkv_weight, precision=highest) + qkv_bias))
    queries, key_rows, values = [segment.reshape(group_count, length, HEADS, head_size) for segment in jnp.split(projected, 3, axis=-1)]
    scores = low_back(jnp.einsum('gqhe,gkhe->ghqk', queries, key_rows, precision=highest) * head_size ** (-0.5))
    row_max = lax.optimization_barrier(jnp.max(scores, axis=-1, keepdims=True))
    shifted = jnp.exp(scores - row_max)
    probability = low(shifted / lax.optimization_barrier(jnp.sum(shifted, axis=-1, keepdims=True)))
    attended = jnp.einsum('ghqk,gkhe->gqhe', probability, values, precision=highest).reshape(group_count, length, model_width)
    attended = low(low_back(attended))
    branch = low_back(jnp.einsum('gsd,de->gse', attended, proj_weight, precision=highest) + proj_bias)
    middle = latent_rows + gate_one * branch
    hidden_two = low(normalize(middle) * (1.0 + scale_two) + shift_two)
    pre_gelu = low_back(jnp.einsum('gsd,df->gsf', hidden_two, fc1_weight, precision=highest) + fc1_bias)
    activated = low(jax.nn.gelu(pre_gelu, approximate=True))
    mlp_out = low_back(jnp.einsum('gsf,fd->gsd', activated, fc2_weight, precision=highest) + fc2_bias)
    return (middle + gate_two * mlp_out) * live_rows[:, None, None]

def reference(latents, conditioning, cotangent, latent_count, ada_weight, ada_bias, qkv_weight, qv_bias, proj_weight, proj_bias, fc1_weight, fc1_bias, fc2_weight, fc2_bias):
    params = tuple((tensor.astype(jnp.float32) for tensor in (ada_weight, ada_bias, qkv_weight, qv_bias, proj_weight, proj_bias, fc1_weight, fc1_bias, fc2_weight, fc2_bias)))
    group_size = math.gcd(LATENTS, 16)
    rounds = LATENTS // group_size
    stacked = (latents.astype(jnp.float32).reshape(rounds, group_size, SEQ, D), conditioning.astype(jnp.float32).reshape(rounds, group_size, D), cotangent.astype(jnp.float32).reshape(rounds, group_size, SEQ, D), latent_count.astype(jnp.float32).reshape(rounds, group_size))

    def accumulate(totals, inputs):
        latent_rows, cond_rows, grad_rows, live_rows = inputs

        def run_layer(rows_in, cond_in, weights_in):
            return forward(rows_in, cond_in, live_rows, weights_in)
        result, pullback = jax.vjp(run_layer, latent_rows, cond_rows, params)
        latent_grad, cond_grad, param_grads = pullback(grad_rows)
        totals = jax.tree.map(lambda earlier, update: earlier + update, totals, param_grads)
        return (totals, (result.astype(jnp.bfloat16), latent_grad.astype(jnp.bfloat16), cond_grad))
    initial = jax.tree.map(jnp.zeros_like, params)
    totals, (outputs, latent_grads, cond_grads) = lax.scan(accumulate, initial, stacked)
    return (outputs.reshape(LATENTS, SEQ, D), latent_grads.reshape(LATENTS, SEQ, D), cond_grads.reshape(LATENTS, D), totals[0], totals[1], totals[2], totals[3], totals[4], totals[5], totals[6], totals[7], totals[8], totals[9])
```

```python
import functools
import jax
import jax.numpy as jnp
from jax import lax
from jax.sharding import PartitionSpec as P
from jax.experimental import pallas as pl
from jax.experimental.pallas import tpu as pltpu

MESH_IDS = pl.DeviceIdType.MESH
D = 768
HEADS = 12
HEAD = 64
FF = 3072

highest = lax.Precision.HIGHEST
bfloat = jnp.bfloat16


def place(dp_index, z_index, core):
    return (dp_index, z_index * 2 + core)


def z_order(size):
    steps = [0]
    for distance in range(1, size // 2 + 1):
        steps.append(distance)
        if size - distance != distance:
            steps.append(size - distance)
    return steps


def device_of(index, columns):
    return (index // columns, lax.rem(index, columns))


def enter_barrier(me, rows, columns):
    barrier = pltpu.get_barrier_semaphore()
    count = rows * columns

    @pl.loop(1, count)
    def _(step):
        target = device_of(lax.rem(me + step, count), columns)
        pl.semaphore_signal(barrier, inc=1, device_id=target, device_id_type=MESH_IDS)

    pl.semaphore_wait(barrier, count - 1)


class Exchange:
    def __init__(self, me, rows, columns, row_for, landing, send_sems, recv_sems):
        self.me, self.columns, self.count = me, columns, rows * columns
        self.row_for, self.landing = row_for, landing
        self.send_sems, self.recv_sems = send_sems, recv_sems

    def start(self):
        @pl.loop(1, self.count)
        def _(step):
            target = lax.rem(self.me + step, self.count)
            pltpu.make_async_remote_copy(
                src_ref=self.row_for(target),
                dst_ref=self.landing.at[self.me],
                send_sem=self.send_sems.at[target],
                recv_sem=self.recv_sems.at[self.me],
                device_id=device_of(target, self.columns),
                device_id_type=MESH_IDS,
            ).start()

        self.landing[self.me] = self.row_for(self.me)[...]

    def pair(self, other):
        return pltpu.make_async_remote_copy(
            src_ref=self.row_for(other),
            dst_ref=self.landing.at[other],
            send_sem=self.send_sems.at[other],
            recv_sem=self.recv_sems.at[other],
            device_id=device_of(other, self.columns),
            device_id_type=MESH_IDS,
        )

    def wait_arrivals(self):
        @pl.loop(1, self.count)
        def _(step):
            self.pair(lax.rem(self.me + step, self.count)).wait_recv()

    def wait_sends(self):
        @pl.loop(1, self.count)
        def _(step):
            self.pair(lax.rem(self.me + step, self.count)).wait_send()


def positions(rows, depth):
    dp = lax.axis_index("dp")
    column = lax.axis_index("fsdp")
    z, core = column // 2, column % 2
    others = [(dp ^ 1), (dp ^ 2)] if rows == 4 else [(dp + step) % rows for step in range(1, rows)]
    return dp, z, core, others


def block_of(array, line, row, shape, turned):
    if len(array.shape) == 4:
        return array.at[line, row]
    high, wide = (line, row) if turned else (row, line)
    height, width = shape
    return array.at[
        pl.ds(pl.multiple_of(high * height, height), height),
        pl.ds(pl.multiple_of(wide * width, width), width),
    ]


def whole_shape(shape, turned, rows, columns):
    height, width = shape
    if width % 128 == 0 and height % 32 == 0:
        return (columns * height, rows * width) if turned else (rows * height, columns * width)
    return (columns, rows, height, width)


def gather_kernel(rows, depth, *refs):
    shards = refs[:3]
    cond_rows, ada_ref, ada_bias, bias_row = refs[3:7]
    outs, mod_out, bias_out, cond_in = refs[7:10], refs[10], refs[11], refs[12]
    (
        own_sems, send_sems, recv_sems, bias_in, part_out, part_in,
        cond_send, cond_recv, part_send, part_recv, bias_send, bias_recv,
    ) = refs[13:]
    dp, z, core, others = positions(rows, depth)
    columns = 2 * depth
    column = lax.axis_index("fsdp")
    me = dp * columns + column
    sibling = place(dp, z, 1 - core)
    enter_barrier(me, rows, columns)
    sends = []

    cond_swap = Exchange(
        me, rows, columns, lambda target: cond_rows.at[target // columns], cond_in,
        cond_send, cond_recv)
    part_swap = Exchange(
        me, rows, columns, lambda target: part_out.at[target], part_in, part_send, part_recv)
    cond_swap.start()

    def bias_copy(target, slot):
        return pltpu.make_async_remote_copy(
            src_ref=bias_row, dst_ref=bias_in.at[slot], send_sem=bias_send.at[target],
            recv_sem=bias_recv.at[slot], device_id=(dp, target), device_id_type=MESH_IDS)

    @pl.loop(1, columns)
    def _(step):
        bias_copy(lax.rem(column + step, columns), column).start()

    bias_in[column] = bias_row[...]

    def slot_of(part, line, row):
        return block_of(outs[part], line, row, shards[part].shape, part == 2)

    def half_of(ref, part, which):
        half = shards[part].shape[0] // 2
        return ref.at[pl.ds(which * half, half)]

    def send(line, row, target, which=None, own=False):
        for part in range(3):
            destination = slot_of(part, line, row)
            source = shards[part] if own else destination
            if which is not None:
                source, destination = half_of(source, part, which), half_of(destination, part, which)
            copy = pltpu.make_async_remote_copy(
                src_ref=source,
                dst_ref=destination,
                send_sem=send_sems.at[len(sends)],
                recv_sem=recv_sems.at[which or 0, part, line, row],
                device_id=target,
                device_id_type=MESH_IDS,
            )
            copy.start()
            sends.append(copy)

    def arrive(line, row, which=None):
        for part in range(3):
            destination = slot_of(part, line, row)
            if which is not None:
                destination = half_of(destination, part, which)
            pltpu.make_async_remote_copy(
                src_ref=destination,
                dst_ref=destination,
                send_sem=send_sems.at[0],
                recv_sem=recv_sems.at[which or 0, part, line, row],
                device_id=sibling,
                device_id_type=MESH_IDS,
            ).wait_recv()

    own = z * 2 + core
    steps = z_order(depth)
    lines = [((z - step) % depth) * 2 + core for step in steps]
    for other in others:
        send(own, dp, place(other, z, core), own=True)
    for step in steps[1:]:
        send(own, dp, place(dp, (z + step) % depth, core), own=True)
    send(own, dp, sibling, own=True)
    keeps = [
        pltpu.make_async_copy(shards[part], slot_of(part, own, dp), own_sems.at[part])
        for part in range(3)
    ]
    for keep in keeps:
        keep.start()
    cond_swap.wait_arrivals()
    high, wide = ada_ref.shape
    part = jnp.dot(
        cond_in[:, 0, :high].astype(bfloat), ada_ref[...], preferred_element_type=jnp.float32)
    part_out[:, 0, :wide] = part + jnp.where(dp == 0, ada_bias[...], 0.0)
    part_swap.start()
    for turn in range(depth + 2):
        if 0 < turn < depth:
            line = lines[turn]
            arrive(line, dp)
            for other in others:
                send(line, dp, place(other, z, core))
            send(line, dp, sibling)
        if 1 <= turn <= depth:
            line = lines[turn - 1]
            for position, other in enumerate(others):
                arrive(line, other)
                if rows == 4:
                    send(line, other, place(others[1 - position], z, core), which=position)
                send(line, other, sibling)
        if turn >= 2 and rows == 4:
            line = lines[turn - 2]
            arrive(line, dp ^ 3, 0)
            arrive(line, dp ^ 3, 1)
            send(line, dp ^ 3, sibling)
    for line in lines:
        for row in range(rows):
            arrive(line + 1 - 2 * core, (dp + row) % rows)
    part_swap.wait_arrivals()
    for block in range(columns):
        total = part_in[block]
        for row in range(1, rows):
            total = total + part_in[row * columns + block]
        mod_out[block] = total

    @pl.loop(1, columns)
    def _(step):
        other = lax.rem(column + step, columns)
        bias_copy(other, other).wait_recv()
        bias_copy(other, other).wait_send()

    bias_out[...] = bias_in[...]
    for keep in keeps:
        keep.wait()
    for copy in sends:
        copy.wait_send()
    cond_swap.wait_sends()
    part_swap.wait_sends()


def round_up(width):
    return -(-width // 128) * 128


def gather_shards(shards, cond_rows, ada_weight, ada_bias, bias_row, rows, columns):
    depth = columns // 2
    total = rows * columns
    mod_pad = round_up(ada_weight.shape[1])
    vmem = pl.BlockSpec(memory_space=pltpu.VMEM)
    dma = pltpu.SemaphoreType.DMA
    row_shape = lambda count, width: jax.ShapeDtypeStruct((count, 1, width), jnp.float32)
    row_buffer = lambda count, width: pltpu.VMEM((count, 1, width), jnp.float32)
    count = (depth - 1) + depth * rows + depth * (rows - 1) + (2 * depth if rows == 4 else 0)
    shapes = [
        whole_shape(shard.shape, part == 2, rows, columns) for part, shard in enumerate(shards)
    ]
    return pl.pallas_call(
        functools.partial(gather_kernel, rows, depth),
        out_shape=[jax.ShapeDtypeStruct(shape, bfloat) for shape in shapes]
        + [row_shape(columns, mod_pad), row_shape(columns, bias_row.shape[-1]),
           row_shape(total, cond_rows.shape[-1])],
        in_specs=[pl.BlockSpec(memory_space=pl.ANY)] * 3 + [vmem] * 4,
        out_specs=[pl.BlockSpec(memory_space=pl.ANY)] * 3 + [vmem] * 3,
        scratch_shapes=[
            dma((3,)),
            dma((3 * count,)),
            dma((2, 3, columns, rows)),
            row_buffer(columns, bias_row.shape[-1]),
            row_buffer(total, mod_pad),
            row_buffer(total, mod_pad),
            dma((total,)), dma((total,)), dma((total,)), dma((total,)),
            dma((columns,)), dma((columns,)),
        ],
        compiler_params=pltpu.CompilerParams(
            collective_id=0, has_side_effects=True, vmem_limit_bytes=32 * 2**20),
        name="gather_shards",
    )(*shards, cond_rows, ada_weight, ada_bias, bias_row)


def scatter_kernel(rows, depth, *refs):
    grads = refs[:3]
    leaving, cond_in, ada_ref, slope = refs[3:7]
    outs, ada_grad, sums_out, cond_grad = refs[7:10], refs[10], refs[11], refs[12]
    refs = refs[13:]
    helds, pairs_in, planes_in, crosses_in, alongs_in = (
        refs[3 * kind : 3 + 3 * kind] for kind in range(5)
    )
    (
        load_sems, pair_send, pair_recv, plane_send, plane_recv,
        cross_send, cross_recv, along_send, along_recv,
        all_rows, back_out, back_in, row_send, row_recv, back_send, back_recv,
    ) = refs[15:]
    dp, z, core, others = positions(rows, depth)
    columns = 2 * depth
    me = dp * columns + lax.axis_index("fsdp")
    row_swap = Exchange(
        me, rows, columns, lambda target: leaving.at[lax.rem(target, columns)], all_rows,
        row_send, row_recv)
    back_swap = Exchange(
        me, rows, columns, lambda target: back_out.at[target], back_in, back_send, back_recv)
    sibling = place(dp, z, 1 - core)
    targets = [dp ^ 3, dp ^ 1, dp ^ 2, dp] if rows == 4 else others + [dp]
    steps = z_order(depth)[::-1]
    enter_barrier(me, rows, columns)
    row_swap.start()
    waits = []

    def remote(source, destination, send_sem, recv_sem, target):
        copy = pltpu.make_async_remote_copy(
            src_ref=source, dst_ref=destination, send_sem=send_sem, recv_sem=recv_sem,
            device_id=target, device_id_type=MESH_IDS,
        )
        copy.start()
        waits.append(copy)
        return copy

    def add(first, others_in, length, target):
        chunk = 48 if length % 48 == 0 else 16

        @pl.loop(0, length // chunk)
        def _(index):
            piece = pl.ds(pl.multiple_of(index * chunk, chunk), chunk)
            total = first[piece, :].astype(jnp.float32)
            for other in others_in:
                total = total + other[piece, :].astype(jnp.float32)
            target[piece, :] = total.astype(target.dtype)

    lines = [(z + step) % depth for step in steps]
    pairs, loads, planes, crosses, alongs = {}, {}, {}, {}, {}
    for turn, line in enumerate(lines):
        for slot, target in enumerate(targets):
            for part in range(3):
                key = (part, turn, slot)
                shape = outs[part].shape
                pairs[key] = remote(
                    block_of(grads[part], line * 2 + 1 - core, target, shape, part == 2),
                    pairs_in[part].at[turn, slot], pair_send.at[key], pair_recv.at[key], sibling)
                loads[key] = pltpu.make_async_copy(
                    block_of(grads[part], line * 2 + core, target, shape, part == 2),
                    helds[part].at[turn, slot], load_sems.at[key])
                loads[key].start()
    last = len(targets) - 1
    for turn in range(depth + 2):
        if turn == depth - 1:
            row_swap.wait_arrivals()
            high, wide = ada_ref.shape
            arrived = all_rows[:, 0, :]
            sums_out[...] = jnp.sum(arrived, axis=0, keepdims=True)
            ada_grad[...] = contract_exact(cond_in[:, 0, :high], arrived[:, :wide])
            back_out[:, 0, :high] = lax.dot_general(
                arrived[:, :wide], ada_ref[...].astype(jnp.float32), (((1,), (1,)), ((), ())),
                precision=highest)
            back_swap.start()
        if turn < depth:
            for slot in range(len(targets)):
                for part in range(3):
                    key = (part, turn, slot)
                    height = outs[part].shape[0]
                    half = height // 2
                    loads[key].wait()
                    pairs[key].wait_recv()
                    here = helds[part].at[turn, slot]
                    add(here, [pairs_in[part].at[turn, slot]], height, here)
                    if rows == 4 and slot == 0:
                        for position in range(2):
                            key = (part, turn, position)
                            crosses[key] = remote(
                                helds[part].at[turn, 0, pl.ds((1 - position) * half, half)],
                                crosses_in[part].at[turn, position],
                                cross_send.at[key], cross_recv.at[key],
                                place(others[position], z, core))
                    if rows != 4 and slot < last:
                        planes[key] = remote(
                            here, planes_in[part].at[turn, slot], plane_send.at[key],
                            plane_recv.at[key], place(targets[slot], z, core))
        if rows == 4 and 1 <= turn <= depth:
            now = turn - 1
            for position in range(2):
                for part in range(3):
                    half = outs[part].shape[0] // 2
                    crosses[part, now, 1 - position].wait_recv()
                    piece = helds[part].at[now, 1 + position, pl.ds(position * half, half)]
                    add(piece, [crosses_in[part].at[now, 1 - position]], half, piece)
                    key = (part, now, position)
                    planes[key] = remote(
                        helds[part].at[now, 1 + position], planes_in[part].at[now, position],
                        plane_send.at[key], plane_recv.at[key],
                        place(others[position], z, core))
        if turn >= 2:
            now = turn - 2
            for part in range(3):
                for slot in range(len(others)):
                    planes[part, now, slot].wait_recv()
                here = helds[part].at[now, last]
                arrived = [planes_in[part].at[now, slot] for slot in range(len(others))]
                add(here, arrived, outs[part].shape[0], here)
                if now < depth - 1:
                    key = (part, now)
                    alongs[key] = remote(
                        here, alongs_in[part].at[now], along_send.at[key], along_recv.at[key],
                        place(dp, lines[now], core))
    for part in range(3):
        for now in range(depth - 1):
            alongs[part, now].wait_recv()
        arrived = [alongs_in[part].at[now] for now in range(depth - 1)]
        add(helds[part].at[depth - 1, last], arrived, outs[part].shape[0], outs[part])
    back_swap.wait_arrivals()
    for row in range(rows):
        total = back_in[row * columns]
        for block in range(1, columns):
            total = total + back_in[row * columns + block]
        cond_grad[row] = total * slope[row]
    for copy in waits:
        copy.wait_send()
    row_swap.wait_sends()
    back_swap.wait_sends()


def scatter_shards(grads, leaving, cond_in, ada_weight, slope, shapes, rows, columns):
    depth = columns // 2
    total = rows * columns
    vmem = pl.BlockSpec(memory_space=pltpu.VMEM)
    row_buffer = lambda count, width: pltpu.VMEM((count, 1, width), jnp.float32)
    peers = 2 if rows == 4 else rows - 1
    dma = pltpu.SemaphoreType.DMA
    buffers = []
    for lead in ((depth, rows), (depth, rows), (depth, peers), (depth, 2), (depth - 1,)):
        for height, width in shapes:
            if lead == (depth, 2) and len(buffers) >= 9:
                height = height // 2 if rows == 4 else 16
            buffers.append(pltpu.VMEM(lead + (height, width), bfloat))
    return pl.pallas_call(
        functools.partial(scatter_kernel, rows, depth),
        out_shape=[jax.ShapeDtypeStruct(shape, jnp.float32) for shape in shapes]
        + [jax.ShapeDtypeStruct(ada_weight.shape, jnp.float32),
           jax.ShapeDtypeStruct((1, leaving.shape[-1]), jnp.float32),
           jax.ShapeDtypeStruct(slope.shape, jnp.float32)],
        in_specs=[pl.BlockSpec(memory_space=pl.ANY)] * 3 + [vmem] * 4,
        out_specs=[vmem] * 6,
        scratch_shapes=buffers + [
            dma((3, depth, rows)), dma((3, depth, rows)), dma((3, depth, rows)),
            dma((3, depth, peers)), dma((3, depth, peers)),
            dma((3, depth, 2)), dma((3, depth, 2)),
            dma((3, depth - 1)), dma((3, depth - 1)),
            row_buffer(total, leaving.shape[-1]),
            row_buffer(total, slope.shape[-1]), row_buffer(total, slope.shape[-1]),
            dma((total,)), dma((total,)), dma((total,)), dma((total,)),
        ],
        compiler_params=pltpu.CompilerParams(
            collective_id=1, has_side_effects=True, vmem_limit_bytes=50 * 2**20),
        name="scatter_shards",
    )(*grads, leaving, cond_in, ada_weight, slope)


def normalize_rows(values):
    center = jnp.mean(values, axis=-1, keepdims=True)
    spread = jnp.mean(jnp.square(values - center), axis=-1, keepdims=True)
    inverse = lax.rsqrt(spread + 1e-06)
    return ((values - center) * inverse, inverse)


def norm_backward(grad_normed, normed, inverse):
    centered = grad_normed - jnp.mean(grad_normed, axis=-1, keepdims=True)
    return inverse * (centered - normed * jnp.mean(grad_normed * normed, axis=-1, keepdims=True))


def contract_rows(left_rows, right_rows):
    return lax.dot_general(
        left_rows, right_rows, (((0,), (0,)), ((), ())), preferred_element_type=jnp.float32
    )


def contract_exact(left_rows, right_rows):
    return lax.dot_general(left_rows, right_rows, (((0,), (0,)), ((), ())), precision=highest)


def against_weight(grad_rows, weight):
    return lax.dot_general(
        grad_rows, weight, (((1,), (1,)), ((), ())), preferred_element_type=jnp.float32
    )


def pick(mixed, columns, kind):
    width = mixed.shape[1] // columns
    edge = 3 * width // 4
    low, high = (0, edge) if kind == 0 else (edge, width)
    return jnp.concatenate(
        [mixed[:, block * width + low : block * width + high] for block in range(columns)], axis=1
    )


def spread(rows_in, columns, kind):
    width = rows_in.shape[1] // columns
    rest = width // 3 if kind == 0 else 3 * width
    zeros = jnp.zeros((rows_in.shape[0], rest), rows_in.dtype)
    pieces = []
    for block in range(columns):
        piece = rows_in[:, block * width : (block + 1) * width]
        pieces += [piece, zeros] if kind == 0 else [zeros, piece]
    return jnp.concatenate(pieces, axis=1)


def layer(latent_rows, live, cot_rows, modulation, weights, biases, columns):
    mixed_weight, fc1_weight, fc2_turned = weights
    qv_bias, proj_bias, fc1_bias, fc2_bias = biases
    length = latent_rows.shape[0]
    rows_wide = latent_rows.astype(jnp.float32)
    shift_one, scale_one, gate_one, shift_two, scale_two, gate_two = jnp.split(
        modulation, 6, axis=-1
    )
    normed_one, inverse_one = normalize_rows(rows_wide)
    hidden_one = (normed_one * (1.0 + scale_one) + shift_one).astype(bfloat)
    qkv_bias = jnp.concatenate([qv_bias[:D], jnp.zeros((D,), jnp.float32), qv_bias[D:]])
    projected = (
        pick(jnp.dot(hidden_one, mixed_weight, preferred_element_type=jnp.float32), columns, 0)
        + qkv_bias
    ).astype(bfloat)
    queries = projected[:, :D].reshape(length, HEADS, HEAD)
    key_rows = projected[:, D : 2 * D].reshape(length, HEADS, HEAD)
    values = projected[:, 2 * D :].reshape(length, HEADS, HEAD)
    scale_factor = HEAD ** (-0.5)
    scores = (
        jnp.einsum("qhe,khe->hqk", queries, key_rows, preferred_element_type=jnp.float32)
        * scale_factor
    )
    row_max = jnp.max(scores, axis=-1, keepdims=True)
    shifted = jnp.exp(scores - row_max)
    row_total = jnp.sum(shifted, axis=-1, keepdims=True)
    exact_probability = shifted / row_total
    probability = exact_probability.astype(bfloat)
    attended = jnp.einsum("hqk,khe->qhe", probability, values, preferred_element_type=jnp.float32)
    attended = attended.reshape(length, D).astype(bfloat)
    branch = pick(jnp.dot(attended, mixed_weight, preferred_element_type=jnp.float32), columns, 1)
    branch = branch + proj_bias
    middle = rows_wide + gate_one * branch
    normed_two, inverse_two = normalize_rows(middle)
    hidden_two = (normed_two * (1.0 + scale_two) + shift_two).astype(bfloat)
    pre_gelu = jnp.dot(hidden_two, fc1_weight, preferred_element_type=jnp.float32) + fc1_bias
    activated, gelu_pull = jax.vjp(
        lambda argument: jax.nn.gelu(argument, approximate=True), pre_gelu
    )
    activated = activated.astype(bfloat)
    mlp_out = against_weight(activated, fc2_turned) + fc2_bias
    block_out = (live * (middle + gate_two * mlp_out)).astype(bfloat)

    grad_out = live * cot_rows.astype(jnp.float32)
    gate_two_grad = jnp.sum(grad_out * mlp_out, axis=0, keepdims=True)
    grad_mlp = (gate_two * grad_out).astype(bfloat)
    fc2_bias_grad = jnp.sum(grad_mlp.astype(jnp.float32), axis=0)
    grad_act = jnp.dot(grad_mlp, fc2_turned, preferred_element_type=jnp.float32)
    grad_pre = gelu_pull(grad_act)[0].astype(bfloat)
    fc1_bias_grad = jnp.sum(grad_pre.astype(jnp.float32), axis=0)
    grad_hidden_two = against_weight(grad_pre, fc1_weight)
    shift_two_grad = jnp.sum(grad_hidden_two, axis=0, keepdims=True)
    scale_two_grad = jnp.sum(grad_hidden_two * normed_two, axis=0, keepdims=True)
    grad_middle = grad_out + norm_backward(
        grad_hidden_two * (1.0 + scale_two), normed_two, inverse_two
    )
    gate_one_grad = jnp.sum(grad_middle * branch, axis=0, keepdims=True)
    grad_branch = (gate_one * grad_middle).astype(bfloat)
    proj_bias_grad = jnp.sum(grad_branch.astype(jnp.float32), axis=0)
    spread_branch = spread(grad_branch, columns, 1)
    grad_attended = (
        against_weight(spread_branch, mixed_weight).astype(bfloat).reshape(length, HEADS, HEAD)
    )
    grad_prob = jnp.einsum(
        "qhe,khe->hqk", grad_attended, values, preferred_element_type=jnp.float32
    )
    inner_sum = jnp.sum(exact_probability * grad_prob, axis=-1, keepdims=True)
    grad_scores = (exact_probability * (grad_prob - inner_sum)).astype(bfloat)
    grad_queries = (
        jnp.einsum("hqk,khe->qhe", grad_scores, key_rows, preferred_element_type=jnp.float32)
        * scale_factor
    )
    grad_keys = (
        jnp.einsum("hqk,qhe->khe", grad_scores, queries, preferred_element_type=jnp.float32)
        * scale_factor
    )
    grad_values = jnp.einsum(
        "hqk,qhe->khe", probability, grad_attended, preferred_element_type=jnp.float32
    )
    grad_projected = jnp.concatenate(
        [
            grad_queries.reshape(length, D),
            grad_keys.reshape(length, D),
            grad_values.reshape(length, D),
        ],
        axis=1,
    ).astype(bfloat)
    summed = jnp.sum(grad_projected.astype(jnp.float32), axis=0)
    qv_bias_grad = jnp.concatenate([summed[:D], summed[2 * D :]])
    spread_projected = spread(grad_projected, columns, 0)
    grad_hidden_one = against_weight(spread_projected, mixed_weight)
    shift_one_grad = jnp.sum(grad_hidden_one, axis=0, keepdims=True)
    scale_one_grad = jnp.sum(grad_hidden_one * normed_one, axis=0, keepdims=True)
    latent_grad = (
        grad_middle + norm_backward(grad_hidden_one * (1.0 + scale_one), normed_one, inverse_one)
    ).astype(bfloat)
    mod_grad = jnp.concatenate(
        [
            shift_one_grad,
            scale_one_grad,
            gate_one_grad,
            shift_two_grad,
            scale_two_grad,
            gate_two_grad,
        ],
        axis=-1,
    )
    weight_grads = (
        contract_rows(
            jnp.concatenate([hidden_one, attended]),
            jnp.concatenate([spread_projected, spread_branch]),
        ).astype(bfloat),
        contract_rows(hidden_two, grad_pre).astype(bfloat),
        contract_rows(grad_mlp, activated).astype(bfloat),
    )
    bias_grads = (qv_bias_grad, proj_bias_grad, fc1_bias_grad, fc2_bias_grad)
    return block_out, latent_grad, mod_grad, weight_grads, bias_grads


def flatten_blocks(blocks, turned):
    if blocks.ndim == 2:
        return blocks
    columns, rows, height, width = blocks.shape
    if turned:
        return blocks.transpose(0, 2, 1, 3).reshape(columns * height, rows * width)
    return blocks.transpose(1, 2, 0, 3).reshape(rows * height, columns * width)


def cut_blocks(whole, shape, turned, rows, columns):
    if len(whole_shape(shape, turned, rows, columns)) == 2:
        return whole
    height, width = shape
    if turned:
        return whole.reshape(columns, height, rows, width).transpose(0, 2, 1, 3)
    return whole.reshape(rows, height, columns, width).transpose(2, 0, 1, 3)


def per_device(
    latents,
    conditioning,
    cotangent,
    latent_count,
    ada_weight,
    ada_bias,
    qkv_weight,
    qv_bias,
    proj_weight,
    proj_bias,
    fc1_weight,
    fc1_bias,
    fc2_weight,
    fc2_bias,
):
    rows, columns = lax.axis_size("dp"), lax.axis_size("fsdp")
    live = latent_count[0].astype(jnp.float32)
    depth = ada_weight.shape[0]
    mod_width = ada_weight.shape[1]
    mod_pad = round_up(mod_width)
    own_biases = (qv_bias, proj_bias, fc1_bias, fc2_bias)
    widths = [bias.shape[0] for bias in own_biases]
    cuts = [sum(widths[:place]) for place in range(len(widths))]

    def split_cond(row):
        pad = round_up(depth) - depth
        return jnp.pad(row.reshape(rows, 1, depth), ((0, 0), (0, 0), (0, pad)))

    cond_row = conditioning.astype(jnp.float32)
    cond_act, silu_pull = jax.vjp(jax.nn.silu, cond_row)
    slope = split_cond(silu_pull(jnp.ones_like(cond_row))[0])
    cond_rows = split_cond(cond_act.astype(bfloat).astype(jnp.float32))
    bias_row = jnp.concatenate(own_biases).astype(jnp.float32).reshape(1, -1)

    qkv_width = qkv_weight.shape[1]
    shards = (
        jnp.concatenate([qkv_weight, proj_weight], axis=1),
        fc1_weight,
        fc2_weight.T,
    )
    shapes = [shard.shape for shard in shards]
    *blocks, mod_blocks, bias_blocks, cond_in = gather_shards(
        shards, cond_rows, ada_weight, ada_bias.astype(jnp.float32).reshape(1, -1), bias_row,
        rows, columns)
    modulation = mod_blocks[:, :, :mod_width].reshape(1, -1)
    biases = tuple(
        bias_blocks[:, :, cut : cut + width].reshape(-1) for cut, width in zip(cuts, widths)
    )
    weights = [flatten_blocks(block, part == 2) for part, block in enumerate(blocks)]
    block_out, latent_grad, mod_grad, weight_grads, bias_grads = layer(
        latents[0], live, cotangent[0], modulation, weights, biases, columns
    )
    grads = [
        cut_blocks(grad, shapes[part], part == 2, rows, columns)
        for part, grad in enumerate(weight_grads)
    ]
    leaving = jnp.concatenate(
        [jnp.pad(mod_grad.reshape(columns, -1), ((0, 0), (0, mod_pad - mod_width)))]
        + [grad.reshape(columns, -1) for grad in bias_grads], axis=1
    ).reshape(columns, 1, -1)
    mixed_grad, fc1_grad, fc2_turned_grad, ada_grad, sums, cond_grad = scatter_shards(
        grads, leaving, cond_in, ada_weight, slope, shapes, rows, columns)
    qkv_grad, proj_grad = mixed_grad[:, :qkv_width], mixed_grad[:, qkv_width:]
    fc2_grad = fc2_turned_grad.T
    ada_bias_grad = sums[0, :mod_width]
    bias_sums = [
        sums[0, mod_pad + cut : mod_pad + cut + width] for cut, width in zip(cuts, widths)]
    cond_grad = cond_grad[:, :, :depth].reshape(1, -1)
    return (
        block_out[None],
        latent_grad[None],
        cond_grad,
        ada_grad,
        ada_bias_grad,
        qkv_grad,
        bias_sums[0],
        proj_grad,
        bias_sums[1],
        fc1_grad,
        bias_sums[2],
        fc2_grad,
        bias_sums[3],
    )


def solution(mesh):
    in_specs = (
        P(("dp", "fsdp"), None, None),
        P(("dp", "fsdp"), None),
        P(("dp", "fsdp"), None, None),
        P(("dp", "fsdp")),
        P("dp", "fsdp"),
        P("fsdp"),
        P("dp", "fsdp"),
        P("fsdp"),
        P("dp", "fsdp"),
        P("fsdp"),
        P("dp", "fsdp"),
        P("fsdp"),
        P("dp", "fsdp"),
        P("fsdp"),
    )
    out_specs = (
        P(("dp", "fsdp"), None, None),
        P(("dp", "fsdp"), None, None),
        P(("dp", "fsdp"), None),
        P("dp", "fsdp"),
        P("fsdp"),
        P("dp", "fsdp"),
        P("fsdp"),
        P("dp", "fsdp"),
        P("fsdp"),
        P("dp", "fsdp"),
        P("fsdp"),
        P("dp", "fsdp"),
        P("fsdp"),
    )
    return jax.shard_map(
        per_device, mesh=mesh, in_specs=in_specs, out_specs=out_specs, check_vma=False
    )
```

```python
import functools
import jax
import jax.numpy as jnp
from jax import lax
from jax.sharding import PartitionSpec as P
from jax.experimental import pallas as pl
from jax.experimental.pallas import tpu as pltpu

MESH_IDS = pl.DeviceIdType.MESH
D = 768
HEADS = 12
HEAD = 64
FF = 3072

highest = lax.Precision.HIGHEST
bfloat = jnp.bfloat16


def place(dp_index, z_index, core):
    return (dp_index, z_index * 2 + core)


def z_order(size):
    steps = [0]
    for distance in range(1, size // 2 + 1):
        steps.append(distance)
        if size - distance != distance:
            steps.append(size - distance)
    return steps


def device_of(index, columns):
    return (index // columns, lax.rem(index, columns))


def enter_barrier(me, rows, columns):
    barrier = pltpu.get_barrier_semaphore()
    count = rows * columns

    @pl.loop(1, count)
    def _(step):
        target = device_of(lax.rem(me + step, count), columns)
        pl.semaphore_signal(barrier, inc=1, device_id=target, device_id_type=MESH_IDS)

    pl.semaphore_wait(barrier, count - 1)


class Exchange:
    def __init__(self, me, rows, columns, row_for, landing, send_sems, recv_sems):
        self.me, self.columns, self.count = me, columns, rows * columns
        self.row_for, self.landing = row_for, landing
        self.send_sems, self.recv_sems = send_sems, recv_sems

    def start(self):
        @pl.loop(1, self.count)
        def _(step):
            target = lax.rem(self.me + step, self.count)
            pltpu.make_async_remote_copy(
                src_ref=self.row_for(target),
                dst_ref=self.landing.at[self.me],
                send_sem=self.send_sems.at[target],
                recv_sem=self.recv_sems.at[self.me],
                device_id=device_of(target, self.columns),
                device_id_type=MESH_IDS,
            ).start()

        self.landing[self.me] = self.row_for(self.me)[...]

    def pair(self, other):
        return pltpu.make_async_remote_copy(
            src_ref=self.row_for(other),
            dst_ref=self.landing.at[other],
            send_sem=self.send_sems.at[other],
            recv_sem=self.recv_sems.at[other],
            device_id=device_of(other, self.columns),
            device_id_type=MESH_IDS,
        )

    def wait_arrivals(self):
        @pl.loop(1, self.count)
        def _(step):
            self.pair(lax.rem(self.me + step, self.count)).wait_recv()

    def wait_sends(self):
        @pl.loop(1, self.count)
        def _(step):
            self.pair(lax.rem(self.me + step, self.count)).wait_send()


def positions(rows, depth):
    dp = lax.axis_index("dp")
    column = lax.axis_index("fsdp")
    z, core = column // 2, column % 2
    others = [(dp ^ 1), (dp ^ 2)] if rows == 4 else [(dp + step) % rows for step in range(1, rows)]
    return dp, z, core, others


def block_of(array, line, row, shape, turned):
    if len(array.shape) == 4:
        return array.at[line, row]
    high, wide = (line, row) if turned else (row, line)
    height, width = shape
    return array.at[
        pl.ds(pl.multiple_of(high * height, height), height),
        pl.ds(pl.multiple_of(wide * width, width), width),
    ]


def whole_shape(shape, turned, rows, columns):
    height, width = shape
    if width % 128 == 0 and height % 32 == 0:
        return (columns * height, rows * width) if turned else (rows * height, columns * width)
    return (columns, rows, height, width)


def gather_kernel(rows, depth, *refs):
    shards = refs[:3]
    cond_rows, ada_ref, ada_bias, bias_row = refs[3:7]
    outs, mod_out, bias_out, cond_in = refs[7:10], refs[10], refs[11], refs[12]
    (
        own_sems, send_sems, recv_sems, bias_in, part_out, part_in,
        cond_send, cond_recv, part_send, part_recv, bias_send, bias_recv,
    ) = refs[13:]
    dp, z, core, others = positions(rows, depth)
    columns = 2 * depth
    column = lax.axis_index("fsdp")
    me = dp * columns + column
    sibling = place(dp, z, 1 - core)
    enter_barrier(me, rows, columns)
    sends = []

    cond_swap = Exchange(
        me, rows, columns, lambda target: cond_rows.at[target // columns], cond_in,
        cond_send, cond_recv)
    part_swap = Exchange(
        me, rows, columns, lambda target: part_out.at[target], part_in, part_send, part_recv)
    cond_swap.start()

    def bias_copy(target, slot):
        return pltpu.make_async_remote_copy(
            src_ref=bias_row, dst_ref=bias_in.at[slot], send_sem=bias_send.at[target],
            recv_sem=bias_recv.at[slot], device_id=(dp, target), device_id_type=MESH_IDS)

    @pl.loop(1, columns)
    def _(step):
        bias_copy(lax.rem(column + step, columns), column).start()

    bias_in[column] = bias_row[...]

    def slot_of(part, line, row):
        return block_of(outs[part], line, row, shards[part].shape, part == 2)

    def half_of(ref, part, which):
        half = shards[part].shape[0] // 2
        return ref.at[pl.ds(which * half, half)]

    def send(line, row, target, which=None, own=False):
        for part in range(3):
            destination = slot_of(part, line, row)
            source = shards[part] if own else destination
            if which is not None:
                source, destination = half_of(source, part, which), half_of(destination, part, which)
            copy = pltpu.make_async_remote_copy(
                src_ref=source,
                dst_ref=destination,
                send_sem=send_sems.at[len(sends)],
                recv_sem=recv_sems.at[which or 0, part, line, row],
                device_id=target,
                device_id_type=MESH_IDS,
            )
            copy.start()
            sends.append(copy)

    def arrive(line, row, which=None):
        for part in range(3):
            destination = slot_of(part, line, row)
            if which is not None:
                destination = half_of(destination, part, which)
            pltpu.make_async_remote_copy(
                src_ref=destination,
                dst_ref=destination,
                send_sem=send_sems.at[0],
                recv_sem=recv_sems.at[which or 0, part, line, row],
                device_id=sibling,
                device_id_type=MESH_IDS,
            ).wait_recv()

    own = z * 2 + core
    steps = z_order(depth)
    lines = [((z - step) % depth) * 2 + core for step in steps]
    for other in others:
        send(own, dp, place(other, z, core), own=True)
    for step in steps[1:]:
        send(own, dp, place(dp, (z + step) % depth, core), own=True)
    send(own, dp, sibling, own=True)
    keeps = [
        pltpu.make_async_copy(shards[part], slot_of(part, own, dp), own_sems.at[part])
        for part in range(3)
    ]
    for keep in keeps:
        keep.start()
    cond_swap.wait_arrivals()
    high, wide = ada_ref.shape
    part = jnp.dot(
        cond_in[:, 0, :high].astype(bfloat), ada_ref[...], preferred_element_type=jnp.float32)
    part_out[:, 0, :wide] = part + jnp.where(dp == 0, ada_bias[...], 0.0)
    part_swap.start()
    for turn in range(depth + 2):
        if 0 < turn < depth:
            line = lines[turn]
            arrive(line, dp)
            for other in others:
                send(line, dp, place(other, z, core))
            send(line, dp, sibling)
        if 1 <= turn <= depth:
            line = lines[turn - 1]
            for position, other in enumerate(others):
                arrive(line, other)
                if rows == 4:
                    send(line, other, place(others[1 - position], z, core), which=position)
                send(line, other, sibling)
        if turn >= 2 and rows == 4:
            line = lines[turn - 2]
            arrive(line, dp ^ 3, 0)
            arrive(line, dp ^ 3, 1)
            send(line, dp ^ 3, sibling)
    for line in lines:
        for row in range(rows):
            arrive(line + 1 - 2 * core, (dp + row) % rows)
    part_swap.wait_arrivals()
    for block in range(columns):
        total = part_in[block]
        for row in range(1, rows):
            total = total + part_in[row * columns + block]
        mod_out[block] = total

    @pl.loop(1, columns)
    def _(step):
        other = lax.rem(column + step, columns)
        bias_copy(other, other).wait_recv()
        bias_copy(other, other).wait_send()

    bias_out[...] = bias_in[...]
    for keep in keeps:
        keep.wait()
    for copy in sends:
        copy.wait_send()
    cond_swap.wait_sends()
    part_swap.wait_sends()


def round_up(width):
    return -(-width // 128) * 128


def gather_shards(shards, cond_rows, ada_weight, ada_bias, bias_row, rows, columns):
    depth = columns // 2
    total = rows * columns
    mod_pad = round_up(ada_weight.shape[1])
    vmem = pl.BlockSpec(memory_space=pltpu.VMEM)
    dma = pltpu.SemaphoreType.DMA
    row_shape = lambda count, width: jax.ShapeDtypeStruct((count, 1, width), jnp.float32)
    row_buffer = lambda count, width: pltpu.VMEM((count, 1, width), jnp.float32)
    count = (depth - 1) + depth * rows + depth * (rows - 1) + (2 * depth if rows == 4 else 0)
    shapes = [
        whole_shape(shard.shape, part == 2, rows, columns) for part, shard in enumerate(shards)
    ]
    return pl.pallas_call(
        functools.partial(gather_kernel, rows, depth),
        out_shape=[jax.ShapeDtypeStruct(shape, bfloat) for shape in shapes]
        + [row_shape(columns, mod_pad), row_shape(columns, bias_row.shape[-1]),
           row_shape(total, cond_rows.shape[-1])],
        in_specs=[pl.BlockSpec(memory_space=pl.ANY)] * 3 + [vmem] * 4,
        out_specs=[pl.BlockSpec(memory_space=pl.ANY)] * 3 + [vmem] * 3,
        scratch_shapes=[
            dma((3,)),
            dma((3 * count,)),
            dma((2, 3, columns, rows)),
            row_buffer(columns, bias_row.shape[-1]),
            row_buffer(total, mod_pad),
            row_buffer(total, mod_pad),
            dma((total,)), dma((total,)), dma((total,)), dma((total,)),
            dma((columns,)), dma((columns,)),
        ],
        compiler_params=pltpu.CompilerParams(
            collective_id=0, has_side_effects=True, vmem_limit_bytes=32 * 2**20),
        name="gather_shards",
    )(*shards, cond_rows, ada_weight, ada_bias, bias_row)


def scatter_kernel(rows, depth, *refs):
    grads = refs[:3]
    leaving, cond_in, ada_ref, slope = refs[3:7]
    outs, ada_grad, sums_out, cond_grad = refs[7:10], refs[10], refs[11], refs[12]
    refs = refs[13:]
    helds, pairs_in, planes_in, crosses_in, alongs_in = (
        refs[3 * kind : 3 + 3 * kind] for kind in range(5)
    )
    (
        load_sems, pair_send, pair_recv, plane_send, plane_recv,
        cross_send, cross_recv, along_send, along_recv,
        all_rows, back_out, back_in, row_send, row_recv, back_send, back_recv,
    ) = refs[15:]
    dp, z, core, others = positions(rows, depth)
    columns = 2 * depth
    me = dp * columns + lax.axis_index("fsdp")
    row_swap = Exchange(
        me, rows, columns, lambda target: leaving.at[lax.rem(target, columns)], all_rows,
        row_send, row_recv)
    back_swap = Exchange(
        me, rows, columns, lambda target: back_out.at[target], back_in, back_send, back_recv)
    sibling = place(dp, z, 1 - core)
    targets = [dp ^ 3, dp ^ 1, dp ^ 2, dp] if rows == 4 else others + [dp]
    steps = z_order(depth)[::-1]
    enter_barrier(me, rows, columns)
    row_swap.start()
    waits = []

    def remote(source, destination, send_sem, recv_sem, target):
        copy = pltpu.make_async_remote_copy(
            src_ref=source, dst_ref=destination, send_sem=send_sem, recv_sem=recv_sem,
            device_id=target, device_id_type=MESH_IDS,
        )
        copy.start()
        waits.append(copy)
        return copy

    def add(first, others_in, length, target):
        chunk = 48 if length % 48 == 0 else 16

        @pl.loop(0, length // chunk)
        def _(index):
            piece = pl.ds(pl.multiple_of(index * chunk, chunk), chunk)
            total = first[piece, :].astype(jnp.float32)
            for other in others_in:
                total = total + other[piece, :].astype(jnp.float32)
            target[piece, :] = total.astype(target.dtype)

    lines = [(z + step) % depth for step in steps]
    pairs, loads, planes, crosses, alongs = {}, {}, {}, {}, {}
    for turn, line in enumerate(lines):
        for slot, target in enumerate(targets):
            for part in range(3):
                key = (part, turn, slot)
                shape = outs[part].shape
                pairs[key] = remote(
                    block_of(grads[part], line * 2 + 1 - core, target, shape, part == 2),
                    pairs_in[part].at[turn, slot], pair_send.at[key], pair_recv.at[key], sibling)
                loads[key] = pltpu.make_async_copy(
                    block_of(grads[part], line * 2 + core, target, shape, part == 2),
                    helds[part].at[turn, slot], load_sems.at[key])
                loads[key].start()
    last = len(targets) - 1
    for turn in range(depth + 2):
        if turn == depth - 1:
            row_swap.wait_arrivals()
            high, wide = ada_ref.shape
            arrived = all_rows[:, 0, :]
            sums_out[...] = jnp.sum(arrived, axis=0, keepdims=True)
            ada_grad[...] = contract_exact(cond_in[:, 0, :high], arrived[:, :wide])
            back_out[:, 0, :high] = lax.dot_general(
                arrived[:, :wide], ada_ref[...].astype(jnp.float32), (((1,), (1,)), ((), ())),
                precision=highest)
            back_swap.start()
        if turn < depth:
            for slot in range(len(targets)):
                for part in range(3):
                    key = (part, turn, slot)
                    height = outs[part].shape[0]
                    half = height // 2
                    loads[key].wait()
                    pairs[key].wait_recv()
                    here = helds[part].at[turn, slot]
                    add(here, [pairs_in[part].at[turn, slot]], height, here)
                    if rows == 4 and slot == 0:
                        for position in range(2):
                            key = (part, turn, position)
                            crosses[key] = remote(
                                helds[part].at[turn, 0, pl.ds((1 - position) * half, half)],
                                crosses_in[part].at[turn, position],
                                cross_send.at[key], cross_recv.at[key],
                                place(others[position], z, core))
                    if rows != 4 and slot < last:
                        planes[key] = remote(
                            here, planes_in[part].at[turn, slot], plane_send.at[key],
                            plane_recv.at[key], place(targets[slot], z, core))
        if rows == 4 and 1 <= turn <= depth:
            now = turn - 1
            for position in range(2):
                for part in range(3):
                    half = outs[part].shape[0] // 2
                    crosses[part, now, 1 - position].wait_recv()
                    piece = helds[part].at[now, 1 + position, pl.ds(position * half, half)]
                    add(piece, [crosses_in[part].at[now, 1 - position]], half, piece)
                    key = (part, now, position)
                    planes[key] = remote(
                        helds[part].at[now, 1 + position], planes_in[part].at[now, position],
                        plane_send.at[key], plane_recv.at[key],
                        place(others[position], z, core))
        if turn >= 2:
            now = turn - 2
            for part in range(3):
                for slot in range(len(others)):
                    planes[part, now, slot].wait_recv()
                here = helds[part].at[now, last]
                arrived = [planes_in[part].at[now, slot] for slot in range(len(others))]
                add(here, arrived, outs[part].shape[0], here)
                if now < depth - 1:
                    key = (part, now)
                    alongs[key] = remote(
                        here, alongs_in[part].at[now], along_send.at[key], along_recv.at[key],
                        place(dp, lines[now], core))
    for part in range(3):
        for now in range(depth - 1):
            alongs[part, now].wait_recv()
        arrived = [alongs_in[part].at[now] for now in range(depth - 1)]
        add(helds[part].at[depth - 1, last], arrived, outs[part].shape[0], outs[part])
    back_swap.wait_arrivals()
    for row in range(rows):
        total = back_in[row * columns]
        for block in range(1, columns):
            total = total + back_in[row * columns + block]
        cond_grad[row] = total * slope[row]
    for copy in waits:
        copy.wait_send()
    row_swap.wait_sends()
    back_swap.wait_sends()


def scatter_shards(grads, leaving, cond_in, ada_weight, slope, shapes, rows, columns):
    depth = columns // 2
    total = rows * columns
    vmem = pl.BlockSpec(memory_space=pltpu.VMEM)
    row_buffer = lambda count, width: pltpu.VMEM((count, 1, width), jnp.float32)
    peers = 2 if rows == 4 else rows - 1
    dma = pltpu.SemaphoreType.DMA
    buffers = []
    for lead in ((depth, rows), (depth, rows), (depth, peers), (depth, 2), (depth - 1,)):
        for height, width in shapes:
            if lead == (depth, 2) and len(buffers) >= 9:
                height = height // 2 if rows == 4 else 16
            buffers.append(pltpu.VMEM(lead + (height, width), bfloat))
    return pl.pallas_call(
        functools.partial(scatter_kernel, rows, depth),
        out_shape=[jax.ShapeDtypeStruct(shape, jnp.float32) for shape in shapes]
        + [jax.ShapeDtypeStruct(ada_weight.shape, jnp.float32),
           jax.ShapeDtypeStruct((1, leaving.shape[-1]), jnp.float32),
           jax.ShapeDtypeStruct(slope.shape, jnp.float32)],
        in_specs=[pl.BlockSpec(memory_space=pl.ANY)] * 3 + [vmem] * 4,
        out_specs=[vmem] * 6,
        scratch_shapes=buffers + [
            dma((3, depth, rows)), dma((3, depth, rows)), dma((3, depth, rows)),
            dma((3, depth, peers)), dma((3, depth, peers)),
            dma((3, depth, 2)), dma((3, depth, 2)),
            dma((3, depth - 1)), dma((3, depth - 1)),
            row_buffer(total, leaving.shape[-1]),
            row_buffer(total, slope.shape[-1]), row_buffer(total, slope.shape[-1]),
            dma((total,)), dma((total,)), dma((total,)), dma((total,)),
        ],
        compiler_params=pltpu.CompilerParams(
            collective_id=1, has_side_effects=True, vmem_limit_bytes=50 * 2**20),
        name="scatter_shards",
    )(*grads, leaving, cond_in, ada_weight, slope)


def normalize_rows(values):
    center = jnp.mean(values, axis=-1, keepdims=True)
    spread = jnp.mean(jnp.square(values - center), axis=-1, keepdims=True)
    inverse = lax.rsqrt(spread + 1e-06)
    return ((values - center) * inverse, inverse)


def norm_backward(grad_normed, normed, inverse):
    centered = grad_normed - jnp.mean(grad_normed, axis=-1, keepdims=True)
    return inverse * (centered - normed * jnp.mean(grad_normed * normed, axis=-1, keepdims=True))


def contract_rows(left_rows, right_rows):
    return lax.dot_general(
        left_rows, right_rows, (((0,), (0,)), ((), ())), preferred_element_type=jnp.float32
    )


def contract_exact(left_rows, right_rows):
    return lax.dot_general(left_rows, right_rows, (((0,), (0,)), ((), ())), precision=highest)


def against_weight(grad_rows, weight):
    return lax.dot_general(
        grad_rows, weight, (((1,), (1,)), ((), ())), preferred_element_type=jnp.float32
    )


def dot_plain(left, right):
    return jnp.dot(left, right, preferred_element_type=jnp.float32)


def columns_sum(values):
    return jnp.sum(values, axis=0, keepdims=True)


class Gather:
    def __init__(self, rows, depth, where, shards, outs, own_sems, send_sems, recv_sems):
        self.rows, self.depth = rows, depth
        self.dp, self.z, self.core, self.others = where
        self.shards, self.outs = shards, outs
        self.own_sems, self.send_sems, self.recv_sems = own_sems, send_sems, recv_sems
        self.sibling = place(self.dp, self.z, 1 - self.core)
        self.sends = []
        self.keeps = []
        self.own = self.z * 2 + self.core
        self.steps = z_order(depth)
        self.lines = [((self.z - step) % depth) * 2 + self.core for step in self.steps]
        self.units = [(part, turn) for part in range(3) for turn in range(depth)]

    def slot_of(self, part, line, row):
        return block_of(self.outs[part], line, row, self.shards[part].shape, part == 2)

    def half_of(self, ref, part, which):
        half = self.shards[part].shape[0] // 2
        return ref.at[pl.ds(which * half, half)]

    def send(self, part, line, row, target, which=None, own=False):
        destination = self.slot_of(part, line, row)
        source = self.shards[part] if own else destination
        if which is not None:
            source, destination = (
                self.half_of(source, part, which), self.half_of(destination, part, which))
        copy = pltpu.make_async_remote_copy(
            src_ref=source,
            dst_ref=destination,
            send_sem=self.send_sems.at[len(self.sends)],
            recv_sem=self.recv_sems.at[which or 0, part, line, row],
            device_id=target,
            device_id_type=MESH_IDS,
        )
        copy.start()
        self.sends.append(copy)

    def arrive(self, part, line, row, which=None):
        destination = self.slot_of(part, line, row)
        if which is not None:
            destination = self.half_of(destination, part, which)
        pltpu.make_async_remote_copy(
            src_ref=destination,
            dst_ref=destination,
            send_sem=self.send_sems.at[0],
            recv_sem=self.recv_sems.at[which or 0, part, line, row],
            device_id=self.sibling,
            device_id_type=MESH_IDS,
        ).wait_recv()

    def send_own(self, part):
        dp, z, core = self.dp, self.z, self.core
        for other in self.others:
            self.send(part, self.own, dp, place(other, z, core), own=True)
        for step in self.steps[1:]:
            self.send(part, self.own, dp, place(dp, (z + step) % self.depth, core), own=True)
        self.send(part, self.own, dp, self.sibling, own=True)
        keep = pltpu.make_async_copy(
            self.shards[part], self.slot_of(part, self.own, dp), self.own_sems.at[part])
        keep.start()
        self.keeps.append(keep)

    def turn(self, index):
        dp, z, core = self.dp, self.z, self.core
        count = len(self.units)
        if index < count:
            part, turn = self.units[index]
            line = self.lines[turn]
            if turn:
                self.arrive(part, line, dp)
                for other in self.others:
                    self.send(part, line, dp, place(other, z, core))
                self.send(part, line, dp, self.sibling)
        if 1 <= index <= count:
            part, turn = self.units[index - 1]
            line = self.lines[turn]
            for position, other in enumerate(self.others):
                self.arrive(part, line, other)
                self.send(
                    part, line, other, place(self.others[1 - position], z, core), which=position)
                self.send(part, line, other, self.sibling)
        if 2 <= index:
            part, turn = self.units[index - 2]
            line = self.lines[turn]
            self.arrive(part, line, dp ^ 3, 0)
            self.arrive(part, line, dp ^ 3, 1)
            self.send(part, line, dp ^ 3, self.sibling)

    def finish_part(self, part):
        for line in self.lines:
            for row in range(self.rows):
                self.arrive(part, line + 1 - 2 * self.core, (self.dp + row) % self.rows)
        self.keeps[part].wait()

    def wait_sends(self):
        for copy in self.sends:
            copy.wait_send()


def layer_kernel(rows, depth, *refs):
    shards = refs[:3]
    cond_rows, ada_ref, ada_bias, bias_row, latents, cotangent, live_ref = refs[3:10]
    block_out, latent_grad, leaving, cond_in = refs[10:14]
    grads_out = refs[14:17]
    weights, grads = refs[17:20], refs[20:23]
    (
        own_sems, send_sems, recv_sems, out_sems, bias_in, part_out, part_in,
        cond_send, cond_recv, part_send, part_recv, bias_send, bias_recv,
        mod, qkv_bias, proj_bias, fc1_bias, fc2_bias, mod_grad, qkv_sums, proj_sums, fc1_sums,
        fc2_sums, inverse_one, inverse_two, normed_one, normed_two, middle, branch, wide,
        hidden_one, hidden_one_t, hidden_two, hidden_two_t, attended, attended_t,
        grad_mlp, grad_mlp_t, grad_attended, projected, grad_natural, grad_mixed,
        grad_proj_mixed, activated, grad_pre, probability,
    ) = refs[23:]
    mixed, fc1, fc2_turned = weights
    where = positions(rows, depth)
    dp = where[0]
    columns = 2 * depth
    column = lax.axis_index("fsdp")
    me = dp * columns + column
    length = latents.shape[0]
    qkv_part, proj_part = 3 * D // columns, D // columns
    block = qkv_part + proj_part
    edge = qkv_part // 128 * 128
    rest = block - edge
    lead = qkv_part - edge
    scale_factor = HEAD ** (-0.5)
    enter_barrier(me, rows, columns)
    gather = Gather(rows, depth, where, shards, weights, own_sems, send_sems, recv_sems)

    cond_swap = Exchange(
        me, rows, columns, lambda target: cond_rows.at[target // columns], cond_in,
        cond_send, cond_recv)
    part_swap = Exchange(
        me, rows, columns, lambda target: part_out.at[target], part_in, part_send, part_recv)
    cond_swap.start()
    gather.send_own(0)

    def bias_copy(target, slot):
        return pltpu.make_async_remote_copy(
            src_ref=bias_row, dst_ref=bias_in.at[slot], send_sem=bias_send.at[target],
            recv_sem=bias_recv.at[slot], device_id=(dp, target), device_id_type=MESH_IDS)

    @pl.loop(1, columns)
    def _(step):
        bias_copy(lax.rem(column + step, columns), column).start()

    bias_in[column] = bias_row[...]
    gather.send_own(1)
    gather.send_own(2)

    def piece(kind):
        return mod[:, kind * D : (kind + 1) * D]

    def start_modulation():
        cond_swap.wait_arrivals()
        high, width = ada_ref.shape
        part = dot_plain(cond_in[:, 0, :high].astype(bfloat), ada_ref[...])
        part_out[:, 0, :width] = part + jnp.where(dp == 0, ada_bias[...], 0.0)
        part_swap.start()

    def normalize_first():
        normed, inverse = normalize_rows(latents[...].astype(jnp.float32))
        normed_one[...] = normed
        inverse_one[...] = inverse

    def finish_modulation():
        part_swap.wait_arrivals()
        width = ada_ref.shape[1]
        pieces = []
        for source in range(columns):
            total = part_in[source]
            for row in range(1, rows):
                total = total + part_in[row * columns + source]
            pieces.append(total[:, :width])
        mod[...] = jnp.concatenate(pieces, axis=1)

        @pl.loop(1, columns)
        def _(step):
            other = lax.rem(column + step, columns)
            bias_copy(other, other).wait_recv()
            bias_copy(other, other).wait_send()

        low = 0
        naturals = []
        for width in (2 * D // columns, D // columns, FF // columns, D // columns):
            naturals.append(jnp.concatenate(
                [bias_in[source][:, low : low + width] for source in range(columns)], axis=1))
            low += width
        qkv_bias[:, :D] = naturals[0][:, :D]
        qkv_bias[:, D : 2 * D] = jnp.zeros((1, D), jnp.float32)
        qkv_bias[:, 2 * D :] = naturals[0][:, D:]
        proj_bias[...] = naturals[1]
        fc1_bias[...] = naturals[2]
        fc2_bias[...] = naturals[3]
        hidden = (normed_one[...] * (1.0 + piece(1)) + piece(0)).astype(bfloat)
        hidden_one[...] = hidden
        hidden_one_t[...] = hidden.T
        grad = (piece(5) * (live_ref[...] * cotangent[...].astype(jnp.float32))).astype(bfloat)
        grad_mlp[...] = grad
        grad_mlp_t[...] = grad.T
        fc2_sums[...] = columns_sum(grad.astype(jnp.float32))

    def span(index, width):
        return pl.ds(pl.multiple_of(index * width, width), width)

    def project():
        @pl.loop(0, columns)
        def _(index):
            wide[:, span(index, block)] = dot_plain(hidden_one[...], mixed[:, span(index, block)])

        for index in range(columns):
            natural = slice(index * qkv_part, (index + 1) * qkv_part)
            projected[:, natural] = (
                wide[:, index * block : index * block + qkv_part] + qkv_bias[:, natural]
            ).astype(bfloat)

    def head_slabs(source, pair):
        return [
            source[:, pl.ds(pl.multiple_of(kind * D + pair * 128, 128), 128)] for kind in range(3)]

    def own_lanes(which):
        lane = lax.broadcasted_iota(jnp.int32, (length, 128), 1)
        return lane < HEAD if which == 0 else lane >= HEAD

    def attend(low, high):
        @pl.loop(low, high)
        def _(pair):
            queries, keys, values = head_slabs(projected, pair)
            zero = jnp.zeros_like(queries)
            results = []
            for which in range(2):
                scores = against_weight(
                    jnp.where(own_lanes(which), queries, zero), keys) * scale_factor
                shifted = jnp.exp(scores - jnp.max(scores, axis=-1, keepdims=True))
                exact = shifted / jnp.sum(shifted, axis=-1, keepdims=True)
                probability[2 * pair + which] = exact
                results.append(dot_plain(exact.astype(bfloat), values))
            attended[:, span(pair, 128)] = jnp.where(
                own_lanes(0), results[0], results[1]).astype(bfloat)

    def finish_attention():
        attended_t[...] = attended[...].T

        @pl.loop(0, columns)
        def _(index):
            tail = pl.ds(pl.multiple_of(index * block + edge, 128), rest)
            wide[:, span(index, rest)] = dot_plain(attended[...], mixed[:, tail])

        for index in range(columns):
            natural = slice(index * proj_part, (index + 1) * proj_part)
            branch[:, natural] = (
                wide[:, index * rest + lead : (index + 1) * rest] + proj_bias[:, natural])
        total = latents[...].astype(jnp.float32) + piece(2) * branch[...]
        middle[...] = total
        normed, inverse = normalize_rows(total)
        normed_two[...] = normed
        inverse_two[...] = inverse
        hidden = (normed * (1.0 + piece(4)) + piece(3)).astype(bfloat)
        hidden_two[...] = hidden
        hidden_two_t[...] = hidden.T

    chunk = 384
    chunks = FF // chunk

    def expand(low, high):
        @pl.loop(low, high)
        def _(index):
            part = span(index, chunk)
            value = dot_plain(hidden_two[...], fc1[:, part]) + fc1_bias[:, part]
            root = 0.7978845608028654
            square = value * value
            bend = jnp.tanh(root * (value + 0.044715 * (square * value)))
            activated[:, part] = (0.5 * value * (1.0 + bend)).astype(bfloat)
            wide[:, part] = 0.5 * (1.0 + bend) + 0.5 * value * (1.0 - bend * bend) * (
                root * (1.0 + 3 * 0.044715 * square))

    def fc2_weight_grad(low, high):
        @pl.loop(low, high)
        def _(index):
            part = span(index, chunk)
            grads[2][:, part] = dot_plain(grad_mlp_t[...], activated[:, part]).astype(bfloat)

    def leave(part):
        copy = pltpu.make_async_copy(grads[part], grads_out[part], out_sems.at[part])
        copy.start()
        return copy

    hooks = {
        0: start_modulation,
        1: normalize_first,
        2: finish_modulation,
    }

    def after_part_zero():
        gather.finish_part(0)
        project()

    def after_part_one():
        gather.finish_part(1)
        expand(0, 4)

    hooks[depth + 2] = after_part_zero
    hooks[depth + 3] = lambda: attend(0, 3)
    hooks[depth + 4] = lambda: attend(3, 6)
    hooks[depth + 5] = finish_attention
    hooks[2 * depth + 2] = after_part_one
    hooks[2 * depth + 3] = lambda: expand(4, 8)
    hooks[2 * depth + 4] = lambda: fc2_weight_grad(0, 4)
    hooks[2 * depth + 5] = lambda: fc2_weight_grad(4, 8)
    for index in range(3 * depth + 2):
        gather.turn(index)
        if index in hooks:
            hooks[index]()
    copies = [leave(2)]
    gather.finish_part(2)

    third = 256

    @pl.loop(0, D // third)
    def _(index):
        part = span(index, third)
        branch_part = against_weight(activated[...], fc2_turned[part, :]) + fc2_bias[:, part]
        live_grad = live_ref[:, part] * cotangent[:, part].astype(jnp.float32)
        gate = mod[:, pl.ds(pl.multiple_of(5 * D + index * third, third), third)]
        block_out[:, part] = (
            live_ref[:, part] * (middle[:, part] + gate * branch_part)).astype(bfloat)
        mod_grad[:, pl.ds(pl.multiple_of(5 * D + index * third, third), third)] = columns_sum(
            live_grad * branch_part)

    @pl.loop(0, chunks)
    def _(index):
        part = span(index, chunk)
        grad = (dot_plain(grad_mlp[...], fc2_turned[:, part]) * wide[:, part]).astype(bfloat)
        grad_pre[:, part] = grad
        fc1_sums[:, part] = columns_sum(grad.astype(jnp.float32))
        grads[1][:, part] = dot_plain(hidden_two_t[...], grad).astype(bfloat)

    copies.append(leave(1))

    @pl.loop(0, D // third)
    def _(index):
        part = span(index, third)
        middle[:, part] = against_weight(grad_pre[...], fc1[part, :])

    grad_hidden = middle[...]
    mod_grad[:, 3 * D : 4 * D] = columns_sum(grad_hidden)
    mod_grad[:, 4 * D : 5 * D] = columns_sum(grad_hidden * normed_two[...])
    grad_middle = live_ref[...] * cotangent[...].astype(jnp.float32) + norm_backward(
        grad_hidden * (1.0 + piece(4)), normed_two[...], inverse_two[...])
    mod_grad[:, 2 * D : 3 * D] = columns_sum(grad_middle * branch[...])
    middle[...] = grad_middle
    grad_branch = (piece(2) * grad_middle).astype(bfloat)
    proj_sums[...] = columns_sum(grad_branch.astype(jnp.float32))
    for index in range(columns):
        grad_proj_mixed[:, index * rest : index * rest + lead] = jnp.zeros((length, lead), bfloat)
        grad_proj_mixed[:, index * rest + lead : (index + 1) * rest] = (
            grad_branch[:, index * proj_part : (index + 1) * proj_part])
    total = None
    for index in range(columns):
        term = against_weight(
            grad_proj_mixed[:, index * rest : (index + 1) * rest],
            mixed[:, index * block + edge : (index + 1) * block])
        total = term if total is None else total + term
    grad_attended[...] = total.astype(bfloat)

    @pl.loop(0, HEADS // 2)
    def _(pair):
        queries, keys, values = head_slabs(projected, pair)
        grad_out = grad_attended[:, span(pair, 128)]
        zero = jnp.zeros_like(grad_out)
        results = []
        for which in range(2):
            exact = probability[2 * pair + which]
            grad_prob = against_weight(jnp.where(own_lanes(which), grad_out, zero), values)
            inner = jnp.sum(exact * grad_prob, axis=-1, keepdims=True)
            grad_scores = (exact * (grad_prob - inner)).astype(bfloat)
            results.append((
                dot_plain(grad_scores, keys) * scale_factor,
                contract_rows(grad_scores, queries) * scale_factor,
                contract_rows(exact.astype(bfloat), grad_out)))
        for kind in range(3):
            grad_natural[:, pl.ds(pl.multiple_of(kind * D + pair * 128, 128), 128)] = jnp.where(
                own_lanes(0), results[0][kind], results[1][kind]).astype(bfloat)

    qkv_sums[...] = columns_sum(grad_natural[...].astype(jnp.float32))
    for index in range(columns):
        grad_mixed[:, index * block : index * block + qkv_part] = (
            grad_natural[:, index * qkv_part : (index + 1) * qkv_part])
        grad_mixed[:, index * block + qkv_part : (index + 1) * block] = jnp.zeros(
            (length, proj_part), bfloat)

    @pl.loop(0, columns)
    def _(index):
        low = pl.multiple_of(index * block, 128)
        grads[0][:, pl.ds(low, edge)] = dot_plain(
            hidden_one_t[...], grad_mixed[:, pl.ds(low, edge)]).astype(bfloat)
        tail = pl.ds(pl.multiple_of(index * block + edge, 128), rest)
        grads[0][:, tail] = (
            dot_plain(hidden_one_t[...], grad_mixed[:, tail])
            + dot_plain(attended_t[...], grad_proj_mixed[:, span(index, rest)])).astype(bfloat)

    copies.append(leave(0))

    @pl.loop(0, D // third)
    def _(index):
        part = span(index, third)
        branch[:, part] = against_weight(grad_mixed[...], mixed[part, :])

    grad_hidden = branch[...]
    mod_grad[:, :D] = columns_sum(grad_hidden)
    mod_grad[:, D : 2 * D] = columns_sum(grad_hidden * normed_one[...])
    latent_grad[...] = (middle[...] + norm_backward(
        grad_hidden * (1.0 + piece(1)), normed_one[...], inverse_one[...])).astype(bfloat)
    width = ada_ref.shape[1]
    pad = jnp.zeros((1, round_up(width) - width), jnp.float32)
    qv_sums = jnp.concatenate([qkv_sums[:, :D], qkv_sums[:, 2 * D :]], axis=1)
    rows_of = (qv_sums, proj_sums[...], fc1_sums[...], fc2_sums[...])
    every = mod_grad[...]
    for index in range(columns):
        pieces = [every[:, index * width : (index + 1) * width], pad]
        for row in rows_of:
            share = row.shape[1] // columns
            pieces.append(row[:, index * share : (index + 1) * share])
        leaving[index] = jnp.concatenate(pieces, axis=1)
    for copy in copies:
        copy.wait()
    gather.wait_sends()
    cond_swap.wait_sends()
    part_swap.wait_sends()


def run_layer(shards, cond_rows, ada_weight, ada_bias, bias_row, latents, cotangent, live,
              rows, columns):
    depth = columns // 2
    count = (depth - 1) + depth * rows + depth * (rows - 1) + 2 * depth
    total = rows * columns
    mod_pad = round_up(ada_weight.shape[1])
    bias_width = bias_row.shape[-1]
    length = latents.shape[0]
    vmem = pl.BlockSpec(memory_space=pltpu.VMEM)
    anywhere = pl.BlockSpec(memory_space=pl.ANY)
    dma = pltpu.SemaphoreType.DMA
    shapes = [
        whole_shape(shard.shape, part == 2, rows, columns) for part, shard in enumerate(shards)]
    row_buffer = lambda count, width: pltpu.VMEM((count, 1, width), jnp.float32)
    wide_row = lambda width: pltpu.VMEM((1, width), jnp.float32)
    single = lambda width: pltpu.VMEM((length, width), jnp.float32)
    half = lambda width: pltpu.VMEM((length, width), bfloat)
    turned = pltpu.VMEM((D, length), bfloat)
    rest = 128 * columns
    row_out = lambda count, width: jax.ShapeDtypeStruct((count, 1, width), jnp.float32)
    return pl.pallas_call(
        functools.partial(layer_kernel, rows, depth),
        out_shape=[
            jax.ShapeDtypeStruct((length, D), bfloat),
            jax.ShapeDtypeStruct((length, D), bfloat),
            row_out(columns, mod_pad + bias_width),
            row_out(total, cond_rows.shape[-1]),
        ] + [jax.ShapeDtypeStruct(shape, bfloat) for shape in shapes],
        in_specs=[anywhere] * 3 + [vmem] * 7,
        out_specs=[vmem] * 4 + [anywhere] * 3,
        scratch_shapes=[pltpu.VMEM(shape, bfloat) for shape in shapes] * 2 + [
            dma((3,)), dma((3 * count,)), dma((2, 3, columns, rows)), dma((3,)),
            row_buffer(columns, bias_width), row_buffer(total, mod_pad), row_buffer(total, mod_pad),
            dma((total,)), dma((total,)), dma((total,)), dma((total,)),
            dma((columns,)), dma((columns,)),
            wide_row(6 * D), wide_row(3 * D), wide_row(D), wide_row(FF), wide_row(D),
            wide_row(6 * D), wide_row(3 * D), wide_row(D), wide_row(FF), wide_row(D),
            single(1), single(1), single(D), single(D), single(D), single(D), single(FF),
            half(D), turned, half(D), turned, half(D), turned,
            half(D), turned, half(D), half(3 * D), half(3 * D), half(4 * D),
            half(rest), half(FF), half(FF), pltpu.VMEM((HEADS, length, length), jnp.float32),
        ],
        compiler_params=pltpu.CompilerParams(
            collective_id=2, has_side_effects=True, vmem_limit_bytes=60 * 2**20),
        name="run_layer",
    )(*shards, cond_rows, ada_weight, ada_bias, bias_row, latents, cotangent, live)


def pick(mixed, columns, kind):
    width = mixed.shape[1] // columns
    edge = 3 * width // 4
    low, high = (0, edge) if kind == 0 else (edge, width)
    return jnp.concatenate(
        [mixed[:, block * width + low : block * width + high] for block in range(columns)], axis=1
    )


def spread(rows_in, columns, kind):
    width = rows_in.shape[1] // columns
    rest = width // 3 if kind == 0 else 3 * width
    zeros = jnp.zeros((rows_in.shape[0], rest), rows_in.dtype)
    pieces = []
    for block in range(columns):
        piece = rows_in[:, block * width : (block + 1) * width]
        pieces += [piece, zeros] if kind == 0 else [zeros, piece]
    return jnp.concatenate(pieces, axis=1)


def layer(latent_rows, live, cot_rows, modulation, weights, biases, columns):
    mixed_weight, fc1_weight, fc2_turned = weights
    qv_bias, proj_bias, fc1_bias, fc2_bias = biases
    length = latent_rows.shape[0]
    rows_wide = latent_rows.astype(jnp.float32)
    shift_one, scale_one, gate_one, shift_two, scale_two, gate_two = jnp.split(
        modulation, 6, axis=-1
    )
    normed_one, inverse_one = normalize_rows(rows_wide)
    hidden_one = (normed_one * (1.0 + scale_one) + shift_one).astype(bfloat)
    qkv_bias = jnp.concatenate([qv_bias[:D], jnp.zeros((D,), jnp.float32), qv_bias[D:]])
    projected = (
        pick(jnp.dot(hidden_one, mixed_weight, preferred_element_type=jnp.float32), columns, 0)
        + qkv_bias
    ).astype(bfloat)
    queries = projected[:, :D].reshape(length, HEADS, HEAD)
    key_rows = projected[:, D : 2 * D].reshape(length, HEADS, HEAD)
    values = projected[:, 2 * D :].reshape(length, HEADS, HEAD)
    scale_factor = HEAD ** (-0.5)
    scores = (
        jnp.einsum("qhe,khe->hqk", queries, key_rows, preferred_element_type=jnp.float32)
        * scale_factor
    )
    row_max = jnp.max(scores, axis=-1, keepdims=True)
    shifted = jnp.exp(scores - row_max)
    row_total = jnp.sum(shifted, axis=-1, keepdims=True)
    exact_probability = shifted / row_total
    probability = exact_probability.astype(bfloat)
    attended = jnp.einsum("hqk,khe->qhe", probability, values, preferred_element_type=jnp.float32)
    attended = attended.reshape(length, D).astype(bfloat)
    branch = pick(jnp.dot(attended, mixed_weight, preferred_element_type=jnp.float32), columns, 1)
    branch = branch + proj_bias
    middle = rows_wide + gate_one * branch
    normed_two, inverse_two = normalize_rows(middle)
    hidden_two = (normed_two * (1.0 + scale_two) + shift_two).astype(bfloat)
    pre_gelu = jnp.dot(hidden_two, fc1_weight, preferred_element_type=jnp.float32) + fc1_bias
    activated, gelu_pull = jax.vjp(
        lambda argument: jax.nn.gelu(argument, approximate=True), pre_gelu
    )
    activated = activated.astype(bfloat)
    mlp_out = against_weight(activated, fc2_turned) + fc2_bias
    block_out = (live * (middle + gate_two * mlp_out)).astype(bfloat)

    grad_out = live * cot_rows.astype(jnp.float32)
    gate_two_grad = jnp.sum(grad_out * mlp_out, axis=0, keepdims=True)
    grad_mlp = (gate_two * grad_out).astype(bfloat)
    fc2_bias_grad = jnp.sum(grad_mlp.astype(jnp.float32), axis=0)
    grad_act = jnp.dot(grad_mlp, fc2_turned, preferred_element_type=jnp.float32)
    grad_pre = gelu_pull(grad_act)[0].astype(bfloat)
    fc1_bias_grad = jnp.sum(grad_pre.astype(jnp.float32), axis=0)
    grad_hidden_two = against_weight(grad_pre, fc1_weight)
    shift_two_grad = jnp.sum(grad_hidden_two, axis=0, keepdims=True)
    scale_two_grad = jnp.sum(grad_hidden_two * normed_two, axis=0, keepdims=True)
    grad_middle = grad_out + norm_backward(
        grad_hidden_two * (1.0 + scale_two), normed_two, inverse_two
    )
    gate_one_grad = jnp.sum(grad_middle * branch, axis=0, keepdims=True)
    grad_branch = (gate_one * grad_middle).astype(bfloat)
    proj_bias_grad = jnp.sum(grad_branch.astype(jnp.float32), axis=0)
    spread_branch = spread(grad_branch, columns, 1)
    grad_attended = (
        against_weight(spread_branch, mixed_weight).astype(bfloat).reshape(length, HEADS, HEAD)
    )
    grad_prob = jnp.einsum(
        "qhe,khe->hqk", grad_attended, values, preferred_element_type=jnp.float32
    )
    inner_sum = jnp.sum(exact_probability * grad_prob, axis=-1, keepdims=True)
    grad_scores = (exact_probability * (grad_prob - inner_sum)).astype(bfloat)
    grad_queries = (
        jnp.einsum("hqk,khe->qhe", grad_scores, key_rows, preferred_element_type=jnp.float32)
        * scale_factor
    )
    grad_keys = (
        jnp.einsum("hqk,qhe->khe", grad_scores, queries, preferred_element_type=jnp.float32)
        * scale_factor
    )
    grad_values = jnp.einsum(
        "hqk,qhe->khe", probability, grad_attended, preferred_element_type=jnp.float32
    )
    grad_projected = jnp.concatenate(
        [
            grad_queries.reshape(length, D),
            grad_keys.reshape(length, D),
            grad_values.reshape(length, D),
        ],
        axis=1,
    ).astype(bfloat)
    summed = jnp.sum(grad_projected.astype(jnp.float32), axis=0)
    qv_bias_grad = jnp.concatenate([summed[:D], summed[2 * D :]])
    spread_projected = spread(grad_projected, columns, 0)
    grad_hidden_one = against_weight(spread_projected, mixed_weight)
    shift_one_grad = jnp.sum(grad_hidden_one, axis=0, keepdims=True)
    scale_one_grad = jnp.sum(grad_hidden_one * normed_one, axis=0, keepdims=True)
    latent_grad = (
        grad_middle + norm_backward(grad_hidden_one * (1.0 + scale_one), normed_one, inverse_one)
    ).astype(bfloat)
    mod_grad = jnp.concatenate(
        [
            shift_one_grad,
            scale_one_grad,
            gate_one_grad,
            shift_two_grad,
            scale_two_grad,
            gate_two_grad,
        ],
        axis=-1,
    )
    weight_grads = (
        contract_rows(
            jnp.concatenate([hidden_one, attended]),
            jnp.concatenate([spread_projected, spread_branch]),
        ).astype(bfloat),
        contract_rows(hidden_two, grad_pre).astype(bfloat),
        contract_rows(grad_mlp, activated).astype(bfloat),
    )
    bias_grads = (qv_bias_grad, proj_bias_grad, fc1_bias_grad, fc2_bias_grad)
    return block_out, latent_grad, mod_grad, weight_grads, bias_grads


def flatten_blocks(blocks, turned):
    if blocks.ndim == 2:
        return blocks
    columns, rows, height, width = blocks.shape
    if turned:
        return blocks.transpose(0, 2, 1, 3).reshape(columns * height, rows * width)
    return blocks.transpose(1, 2, 0, 3).reshape(rows * height, columns * width)


def cut_blocks(whole, shape, turned, rows, columns):
    if len(whole_shape(shape, turned, rows, columns)) == 2:
        return whole
    height, width = shape
    if turned:
        return whole.reshape(columns, height, rows, width).transpose(0, 2, 1, 3)
    return whole.reshape(rows, height, columns, width).transpose(2, 0, 1, 3)


def per_device(
    latents,
    conditioning,
    cotangent,
    latent_count,
    ada_weight,
    ada_bias,
    qkv_weight,
    qv_bias,
    proj_weight,
    proj_bias,
    fc1_weight,
    fc1_bias,
    fc2_weight,
    fc2_bias,
):
    rows, columns = lax.axis_size("dp"), lax.axis_size("fsdp")
    live = latent_count[0].astype(jnp.float32)
    depth = ada_weight.shape[0]
    mod_width = ada_weight.shape[1]
    mod_pad = round_up(mod_width)
    own_biases = (qv_bias, proj_bias, fc1_bias, fc2_bias)
    widths = [bias.shape[0] for bias in own_biases]
    cuts = [sum(widths[:place]) for place in range(len(widths))]

    def split_cond(row):
        pad = round_up(depth) - depth
        return jnp.pad(row.reshape(rows, 1, depth), ((0, 0), (0, 0), (0, pad)))

    cond_row = conditioning.astype(jnp.float32)
    cond_act, silu_pull = jax.vjp(jax.nn.silu, cond_row)
    slope = split_cond(silu_pull(jnp.ones_like(cond_row))[0])
    cond_rows = split_cond(cond_act.astype(bfloat).astype(jnp.float32))
    bias_row = jnp.concatenate(own_biases).astype(jnp.float32).reshape(1, -1)

    qkv_width = qkv_weight.shape[1]
    shards = (
        jnp.concatenate([qkv_weight, proj_weight], axis=1),
        fc1_weight,
        fc2_weight.T,
    )
    shapes = [shard.shape for shard in shards]
    ada_row = ada_bias.astype(jnp.float32).reshape(1, -1)
    fused = rows == 4 and columns == 8
    if fused:
        block_out, latent_grad, leaving, cond_in, *grads = run_layer(
            shards, cond_rows, ada_weight, ada_row, bias_row, latents[0], cotangent[0],
            jnp.full((1, D), live), rows, columns)
    else:
        *blocks, mod_blocks, bias_blocks, cond_in = gather_shards(
            shards, cond_rows, ada_weight, ada_row, bias_row,
            rows, columns)
        modulation = mod_blocks[:, :, :mod_width].reshape(1, -1)
        biases = tuple(
            bias_blocks[:, :, cut : cut + width].reshape(-1) for cut, width in zip(cuts, widths)
        )
        weights = [flatten_blocks(block, part == 2) for part, block in enumerate(blocks)]
        block_out, latent_grad, mod_grad, weight_grads, bias_grads = layer(
            latents[0], live, cotangent[0], modulation, weights, biases, columns
        )
        grads = [
            cut_blocks(grad, shapes[part], part == 2, rows, columns)
            for part, grad in enumerate(weight_grads)
        ]
        leaving = jnp.concatenate(
            [jnp.pad(mod_grad.reshape(columns, -1), ((0, 0), (0, mod_pad - mod_width)))]
            + [grad.reshape(columns, -1) for grad in bias_grads], axis=1
        ).reshape(columns, 1, -1)
    mixed_grad, fc1_grad, fc2_turned_grad, ada_grad, sums, cond_grad = scatter_shards(
        grads, leaving, cond_in, ada_weight, slope, shapes, rows, columns)
    qkv_grad, proj_grad = mixed_grad[:, :qkv_width], mixed_grad[:, qkv_width:]
    fc2_grad = fc2_turned_grad.T
    ada_bias_grad = sums[0, :mod_width]
    bias_sums = [
        sums[0, mod_pad + cut : mod_pad + cut + width] for cut, width in zip(cuts, widths)]
    cond_grad = cond_grad[:, :, :depth].reshape(1, -1)
    return (
        block_out[None],
        latent_grad[None],
        cond_grad,
        ada_grad,
        ada_bias_grad,
        qkv_grad,
        bias_sums[0],
        proj_grad,
        bias_sums[1],
        fc1_grad,
        bias_sums[2],
        fc2_grad,
        bias_sums[3],
    )


def solution(mesh):
    in_specs = (
        P(("dp", "fsdp"), None, None),
        P(("dp", "fsdp"), None),
        P(("dp", "fsdp"), None, None),
        P(("dp", "fsdp")),
        P("dp", "fsdp"),
        P("fsdp"),
        P("dp", "fsdp"),
        P("fsdp"),
        P("dp", "fsdp"),
        P("fsdp"),
        P("dp", "fsdp"),
        P("fsdp"),
        P("dp", "fsdp"),
        P("fsdp"),
    )
    out_specs = (
        P(("dp", "fsdp"), None, None),
        P(("dp", "fsdp"), None, None),
        P(("dp", "fsdp"), None),
        P("dp", "fsdp"),
        P("fsdp"),
        P("dp", "fsdp"),
        P("fsdp"),
        P("dp", "fsdp"),
        P("fsdp"),
        P("dp", "fsdp"),
        P("fsdp"),
        P("dp", "fsdp"),
        P("fsdp"),
    )
    return jax.shard_map(
        per_device, mesh=mesh, in_specs=in_specs, out_specs=out_specs, check_vma=False
    )
```

```python
import functools
import jax
import jax.numpy as jnp
from jax import lax
from jax.sharding import PartitionSpec as P
from jax.experimental import pallas as pl
from jax.experimental.pallas import tpu as pltpu

MESH_IDS = pl.DeviceIdType.MESH
D = 768
HEADS = 12
HEAD = 64
FF = 3072

highest = lax.Precision.HIGHEST
bfloat = jnp.bfloat16


def place(dp_index, z_index, core):
    return (dp_index, z_index * 2 + core)


def z_order(size):
    steps = [0]
    for distance in range(1, size // 2 + 1):
        steps.append(distance)
        if size - distance != distance:
            steps.append(size - distance)
    return steps


def device_of(index, columns):
    return (index // columns, lax.rem(index, columns))


def enter_barrier(me, rows, columns):
    barrier = pltpu.get_barrier_semaphore()
    count = rows * columns

    @pl.loop(1, count)
    def _(step):
        target = device_of(lax.rem(me + step, count), columns)
        pl.semaphore_signal(barrier, inc=1, device_id=target, device_id_type=MESH_IDS)

    pl.semaphore_wait(barrier, count - 1)


class Exchange:
    def __init__(self, me, rows, columns, row_for, landing, send_sems, recv_sems):
        self.me, self.columns, self.count = me, columns, rows * columns
        self.row_for, self.landing = row_for, landing
        self.send_sems, self.recv_sems = send_sems, recv_sems

    def start(self):
        @pl.loop(1, self.count)
        def _(step):
            target = lax.rem(self.me + step, self.count)
            pltpu.make_async_remote_copy(
                src_ref=self.row_for(target),
                dst_ref=self.landing.at[self.me],
                send_sem=self.send_sems.at[target],
                recv_sem=self.recv_sems.at[self.me],
                device_id=device_of(target, self.columns),
                device_id_type=MESH_IDS,
            ).start()

        self.landing[self.me] = self.row_for(self.me)[...]

    def pair(self, other):
        return pltpu.make_async_remote_copy(
            src_ref=self.row_for(other),
            dst_ref=self.landing.at[other],
            send_sem=self.send_sems.at[other],
            recv_sem=self.recv_sems.at[other],
            device_id=device_of(other, self.columns),
            device_id_type=MESH_IDS,
        )

    def wait_arrivals(self):
        @pl.loop(1, self.count)
        def _(step):
            self.pair(lax.rem(self.me + step, self.count)).wait_recv()

    def wait_sends(self):
        @pl.loop(1, self.count)
        def _(step):
            self.pair(lax.rem(self.me + step, self.count)).wait_send()


def positions(rows, depth):
    dp = lax.axis_index("dp")
    column = lax.axis_index("fsdp")
    z, core = column // 2, column % 2
    others = [(dp ^ 1), (dp ^ 2)] if rows == 4 else [(dp + step) % rows for step in range(1, rows)]
    return dp, z, core, others


def block_of(array, line, row, shape, turned):
    if len(array.shape) == 4:
        return array.at[line, row]
    high, wide = (line, row) if turned else (row, line)
    height, width = shape
    return array.at[
        pl.ds(pl.multiple_of(high * height, height), height),
        pl.ds(pl.multiple_of(wide * width, width), width),
    ]


def whole_shape(shape, turned, rows, columns):
    height, width = shape
    if width % 128 == 0 and height % 32 == 0:
        return (columns * height, rows * width) if turned else (rows * height, columns * width)
    return (columns, rows, height, width)


def gather_kernel(rows, depth, *refs):
    shards = refs[:3]
    cond_rows, ada_ref, ada_bias, bias_row = refs[3:7]
    outs, mod_out, bias_out, cond_in = refs[7:10], refs[10], refs[11], refs[12]
    (
        own_sems, send_sems, recv_sems, bias_in, part_out, part_in,
        cond_send, cond_recv, part_send, part_recv, bias_send, bias_recv,
    ) = refs[13:]
    dp, z, core, others = positions(rows, depth)
    columns = 2 * depth
    column = lax.axis_index("fsdp")
    me = dp * columns + column
    sibling = place(dp, z, 1 - core)
    enter_barrier(me, rows, columns)
    sends = []

    cond_swap = Exchange(
        me, rows, columns, lambda target: cond_rows.at[target // columns], cond_in,
        cond_send, cond_recv)
    part_swap = Exchange(
        me, rows, columns, lambda target: part_out.at[target], part_in, part_send, part_recv)
    cond_swap.start()

    def bias_copy(target, slot):
        return pltpu.make_async_remote_copy(
            src_ref=bias_row, dst_ref=bias_in.at[slot], send_sem=bias_send.at[target],
            recv_sem=bias_recv.at[slot], device_id=(dp, target), device_id_type=MESH_IDS)

    @pl.loop(1, columns)
    def _(step):
        bias_copy(lax.rem(column + step, columns), column).start()

    bias_in[column] = bias_row[...]

    def slot_of(part, line, row):
        return block_of(outs[part], line, row, shards[part].shape, part == 2)

    def half_of(ref, part, which):
        half = shards[part].shape[0] // 2
        return ref.at[pl.ds(which * half, half)]

    def send(line, row, target, which=None, own=False):
        for part in range(3):
            destination = slot_of(part, line, row)
            source = shards[part] if own else destination
            if which is not None:
                source, destination = half_of(source, part, which), half_of(destination, part, which)
            copy = pltpu.make_async_remote_copy(
                src_ref=source,
                dst_ref=destination,
                send_sem=send_sems.at[len(sends)],
                recv_sem=recv_sems.at[which or 0, part, line, row],
                device_id=target,
                device_id_type=MESH_IDS,
            )
            copy.start()
            sends.append(copy)

    def arrive(line, row, which=None):
        for part in range(3):
            destination = slot_of(part, line, row)
            if which is not None:
                destination = half_of(destination, part, which)
            pltpu.make_async_remote_copy(
                src_ref=destination,
                dst_ref=destination,
                send_sem=send_sems.at[0],
                recv_sem=recv_sems.at[which or 0, part, line, row],
                device_id=sibling,
                device_id_type=MESH_IDS,
            ).wait_recv()

    own = z * 2 + core
    steps = z_order(depth)
    lines = [((z - step) % depth) * 2 + core for step in steps]
    for other in others:
        send(own, dp, place(other, z, core), own=True)
    for step in steps[1:]:
        send(own, dp, place(dp, (z + step) % depth, core), own=True)
    send(own, dp, sibling, own=True)
    keeps = [
        pltpu.make_async_copy(shards[part], slot_of(part, own, dp), own_sems.at[part])
        for part in range(3)
    ]
    for keep in keeps:
        keep.start()
    cond_swap.wait_arrivals()
    high, wide = ada_ref.shape
    part = jnp.dot(
        cond_in[:, 0, :high].astype(bfloat), ada_ref[...], preferred_element_type=jnp.float32)
    part_out[:, 0, :wide] = part + jnp.where(dp == 0, ada_bias[...], 0.0)
    part_swap.start()
    for turn in range(depth + 2):
        if 0 < turn < depth:
            line = lines[turn]
            arrive(line, dp)
            for other in others:
                send(line, dp, place(other, z, core))
            send(line, dp, sibling)
        if 1 <= turn <= depth:
            line = lines[turn - 1]
            for position, other in enumerate(others):
                arrive(line, other)
                if rows == 4:
                    send(line, other, place(others[1 - position], z, core), which=position)
                send(line, other, sibling)
        if turn >= 2 and rows == 4:
            line = lines[turn - 2]
            arrive(line, dp ^ 3, 0)
            arrive(line, dp ^ 3, 1)
            send(line, dp ^ 3, sibling)
    for line in lines:
        for row in range(rows):
            arrive(line + 1 - 2 * core, (dp + row) % rows)
    part_swap.wait_arrivals()
    for block in range(columns):
        total = part_in[block]
        for row in range(1, rows):
            total = total + part_in[row * columns + block]
        mod_out[block] = total

    @pl.loop(1, columns)
    def _(step):
        other = lax.rem(column + step, columns)
        bias_copy(other, other).wait_recv()
        bias_copy(other, other).wait_send()

    bias_out[...] = bias_in[...]
    for keep in keeps:
        keep.wait()
    for copy in sends:
        copy.wait_send()
    cond_swap.wait_sends()
    part_swap.wait_sends()


def round_up(width):
    return -(-width // 128) * 128


def gather_shards(shards, cond_rows, ada_weight, ada_bias, bias_row, rows, columns):
    depth = columns // 2
    total = rows * columns
    mod_pad = round_up(ada_weight.shape[1])
    vmem = pl.BlockSpec(memory_space=pltpu.VMEM)
    dma = pltpu.SemaphoreType.DMA
    row_shape = lambda count, width: jax.ShapeDtypeStruct((count, 1, width), jnp.float32)
    row_buffer = lambda count, width: pltpu.VMEM((count, 1, width), jnp.float32)
    count = (depth - 1) + depth * rows + depth * (rows - 1) + (2 * depth if rows == 4 else 0)
    shapes = [
        whole_shape(shard.shape, part == 2, rows, columns) for part, shard in enumerate(shards)
    ]
    return pl.pallas_call(
        functools.partial(gather_kernel, rows, depth),
        out_shape=[jax.ShapeDtypeStruct(shape, bfloat) for shape in shapes]
        + [row_shape(columns, mod_pad), row_shape(columns, bias_row.shape[-1]),
           row_shape(total, cond_rows.shape[-1])],
        in_specs=[pl.BlockSpec(memory_space=pl.ANY)] * 3 + [vmem] * 4,
        out_specs=[pl.BlockSpec(memory_space=pl.ANY)] * 3 + [vmem] * 3,
        scratch_shapes=[
            dma((3,)),
            dma((3 * count,)),
            dma((2, 3, columns, rows)),
            row_buffer(columns, bias_row.shape[-1]),
            row_buffer(total, mod_pad),
            row_buffer(total, mod_pad),
            dma((total,)), dma((total,)), dma((total,)), dma((total,)),
            dma((columns,)), dma((columns,)),
        ],
        compiler_params=pltpu.CompilerParams(
            collective_id=0, has_side_effects=True, vmem_limit_bytes=32 * 2**20),
        name="gather_shards",
    )(*shards, cond_rows, ada_weight, ada_bias, bias_row)


def scatter_kernel(rows, depth, *refs):
    grads = refs[:3]
    leaving, cond_in, ada_ref, slope = refs[3:7]
    outs, ada_grad, sums_out, cond_grad = refs[7:10], refs[10], refs[11], refs[12]
    refs = refs[13:]
    helds, pairs_in, planes_in, crosses_in, alongs_in = (
        refs[3 * kind : 3 + 3 * kind] for kind in range(5)
    )
    (
        load_sems, pair_send, pair_recv, plane_send, plane_recv,
        cross_send, cross_recv, along_send, along_recv,
        all_rows, back_out, back_in, row_send, row_recv, back_send, back_recv,
    ) = refs[15:]
    dp, z, core, others = positions(rows, depth)
    columns = 2 * depth
    me = dp * columns + lax.axis_index("fsdp")
    row_swap = Exchange(
        me, rows, columns, lambda target: leaving.at[lax.rem(target, columns)], all_rows,
        row_send, row_recv)
    back_swap = Exchange(
        me, rows, columns, lambda target: back_out.at[target], back_in, back_send, back_recv)
    sibling = place(dp, z, 1 - core)
    targets = [dp ^ 3, dp ^ 1, dp ^ 2, dp] if rows == 4 else others + [dp]
    steps = z_order(depth)[::-1]
    enter_barrier(me, rows, columns)
    row_swap.start()
    waits = []

    def remote(source, destination, send_sem, recv_sem, target):
        copy = pltpu.make_async_remote_copy(
            src_ref=source, dst_ref=destination, send_sem=send_sem, recv_sem=recv_sem,
            device_id=target, device_id_type=MESH_IDS,
        )
        copy.start()
        waits.append(copy)
        return copy

    def add(first, others_in, length, target):
        chunk = 48 if length % 48 == 0 else 16

        @pl.loop(0, length // chunk)
        def _(index):
            piece = pl.ds(pl.multiple_of(index * chunk, chunk), chunk)
            total = first[piece, :].astype(jnp.float32)
            for other in others_in:
                total = total + other[piece, :].astype(jnp.float32)
            target[piece, :] = total.astype(target.dtype)

    lines = [(z + step) % depth for step in steps]
    pairs, loads, planes, crosses, alongs = {}, {}, {}, {}, {}
    for turn, line in enumerate(lines):
        for slot, target in enumerate(targets):
            for part in range(3):
                key = (part, turn, slot)
                shape = outs[part].shape
                pairs[key] = remote(
                    block_of(grads[part], line * 2 + 1 - core, target, shape, part == 2),
                    pairs_in[part].at[turn, slot], pair_send.at[key], pair_recv.at[key], sibling)
                loads[key] = pltpu.make_async_copy(
                    block_of(grads[part], line * 2 + core, target, shape, part == 2),
                    helds[part].at[turn, slot], load_sems.at[key])
                loads[key].start()
    last = len(targets) - 1
    for turn in range(depth + 2):
        if turn == depth - 1:
            row_swap.wait_arrivals()
            high, wide = ada_ref.shape
            arrived = all_rows[:, 0, :]
            sums_out[...] = jnp.sum(arrived, axis=0, keepdims=True)
            ada_grad[...] = contract_exact(cond_in[:, 0, :high], arrived[:, :wide])
            back_out[:, 0, :high] = lax.dot_general(
                arrived[:, :wide], ada_ref[...].astype(jnp.float32), (((1,), (1,)), ((), ())),
                precision=highest)
            back_swap.start()
        if turn < depth:
            for slot in range(len(targets)):
                for part in range(3):
                    key = (part, turn, slot)
                    height = outs[part].shape[0]
                    half = height // 2
                    loads[key].wait()
                    pairs[key].wait_recv()
                    here = helds[part].at[turn, slot]
                    add(here, [pairs_in[part].at[turn, slot]], height, here)
                    if rows == 4 and slot == 0:
                        for position in range(2):
                            key = (part, turn, position)
                            crosses[key] = remote(
                                helds[part].at[turn, 0, pl.ds((1 - position) * half, half)],
                                crosses_in[part].at[turn, position],
                                cross_send.at[key], cross_recv.at[key],
                                place(others[position], z, core))
                    if rows != 4 and slot < last:
                        planes[key] = remote(
                            here, planes_in[part].at[turn, slot], plane_send.at[key],
                            plane_recv.at[key], place(targets[slot], z, core))
        if rows == 4 and 1 <= turn <= depth:
            now = turn - 1
            for position in range(2):
                for part in range(3):
                    half = outs[part].shape[0] // 2
                    crosses[part, now, 1 - position].wait_recv()
                    piece = helds[part].at[now, 1 + position, pl.ds(position * half, half)]
                    add(piece, [crosses_in[part].at[now, 1 - position]], half, piece)
                    key = (part, now, position)
                    planes[key] = remote(
                        helds[part].at[now, 1 + position], planes_in[part].at[now, position],
                        plane_send.at[key], plane_recv.at[key],
                        place(others[position], z, core))
        if turn >= 2:
            now = turn - 2
            for part in range(3):
                for slot in range(len(others)):
                    planes[part, now, slot].wait_recv()
                here = helds[part].at[now, last]
                arrived = [planes_in[part].at[now, slot] for slot in range(len(others))]
                add(here, arrived, outs[part].shape[0], here)
                if now < depth - 1:
                    key = (part, now)
                    alongs[key] = remote(
                        here, alongs_in[part].at[now], along_send.at[key], along_recv.at[key],
                        place(dp, lines[now], core))
    for part in range(3):
        for now in range(depth - 1):
            alongs[part, now].wait_recv()
        arrived = [alongs_in[part].at[now] for now in range(depth - 1)]
        add(helds[part].at[depth - 1, last], arrived, outs[part].shape[0], outs[part])
    back_swap.wait_arrivals()
    for row in range(rows):
        total = back_in[row * columns]
        for block in range(1, columns):
            total = total + back_in[row * columns + block]
        cond_grad[row] = total * slope[row]
    for copy in waits:
        copy.wait_send()
    row_swap.wait_sends()
    back_swap.wait_sends()


def scatter_shards(grads, leaving, cond_in, ada_weight, slope, shapes, rows, columns):
    depth = columns // 2
    total = rows * columns
    vmem = pl.BlockSpec(memory_space=pltpu.VMEM)
    row_buffer = lambda count, width: pltpu.VMEM((count, 1, width), jnp.float32)
    peers = 2 if rows == 4 else rows - 1
    dma = pltpu.SemaphoreType.DMA
    buffers = []
    for lead in ((depth, rows), (depth, rows), (depth, peers), (depth, 2), (depth - 1,)):
        for height, width in shapes:
            if lead == (depth, 2) and len(buffers) >= 9:
                height = height // 2 if rows == 4 else 16
            buffers.append(pltpu.VMEM(lead + (height, width), bfloat))
    return pl.pallas_call(
        functools.partial(scatter_kernel, rows, depth),
        out_shape=[jax.ShapeDtypeStruct(shape, jnp.float32) for shape in shapes]
        + [jax.ShapeDtypeStruct(ada_weight.shape, jnp.float32),
           jax.ShapeDtypeStruct((1, leaving.shape[-1]), jnp.float32),
           jax.ShapeDtypeStruct(slope.shape, jnp.float32)],
        in_specs=[pl.BlockSpec(memory_space=pl.ANY)] * 3 + [vmem] * 4,
        out_specs=[vmem] * 6,
        scratch_shapes=buffers + [
            dma((3, depth, rows)), dma((3, depth, rows)), dma((3, depth, rows)),
            dma((3, depth, peers)), dma((3, depth, peers)),
            dma((3, depth, 2)), dma((3, depth, 2)),
            dma((3, depth - 1)), dma((3, depth - 1)),
            row_buffer(total, leaving.shape[-1]),
            row_buffer(total, slope.shape[-1]), row_buffer(total, slope.shape[-1]),
            dma((total,)), dma((total,)), dma((total,)), dma((total,)),
        ],
        compiler_params=pltpu.CompilerParams(
            collective_id=1, has_side_effects=True, vmem_limit_bytes=50 * 2**20),
        name="scatter_shards",
    )(*grads, leaving, cond_in, ada_weight, slope)


def normalize_rows(values):
    center = jnp.mean(values, axis=-1, keepdims=True)
    spread = jnp.mean(jnp.square(values - center), axis=-1, keepdims=True)
    inverse = lax.rsqrt(spread + 1e-06)
    return ((values - center) * inverse, inverse)


def norm_backward(grad_normed, normed, inverse):
    centered = grad_normed - jnp.mean(grad_normed, axis=-1, keepdims=True)
    return inverse * (centered - normed * jnp.mean(grad_normed * normed, axis=-1, keepdims=True))


def contract_rows(left_rows, right_rows):
    return lax.dot_general(
        left_rows, right_rows, (((0,), (0,)), ((), ())), preferred_element_type=jnp.float32
    )


def contract_exact(left_rows, right_rows):
    return lax.dot_general(left_rows, right_rows, (((0,), (0,)), ((), ())), precision=highest)


def against_weight(grad_rows, weight):
    return lax.dot_general(
        grad_rows, weight, (((1,), (1,)), ((), ())), preferred_element_type=jnp.float32
    )


def dot_plain(left, right):
    return jnp.dot(left, right, preferred_element_type=jnp.float32)


def columns_sum(values):
    return jnp.sum(values, axis=0, keepdims=True)


class Gather:
    def __init__(self, rows, depth, where, shards, outs, own_sems, send_sems, recv_sems):
        self.rows, self.depth = rows, depth
        self.dp, self.z, self.core, self.others = where
        self.shards, self.outs = shards, outs
        self.own_sems, self.send_sems, self.recv_sems = own_sems, send_sems, recv_sems
        self.sibling = place(self.dp, self.z, 1 - self.core)
        self.sends = []
        self.keeps = []
        self.own = self.z * 2 + self.core
        self.steps = z_order(depth)
        self.lines = [((self.z - step) % depth) * 2 + self.core for step in self.steps]
        self.units = [(part, turn) for part in range(3) for turn in range(depth)]

    def slot_of(self, part, line, row):
        return block_of(self.outs[part], line, row, self.shards[part].shape, part == 2)

    def half_of(self, ref, part, which):
        half = self.shards[part].shape[0] // 2
        return ref.at[pl.ds(which * half, half)]

    def send(self, part, line, row, target, which=None, own=False):
        destination = self.slot_of(part, line, row)
        source = self.shards[part] if own else destination
        if which is not None:
            source, destination = (
                self.half_of(source, part, which), self.half_of(destination, part, which))
        copy = pltpu.make_async_remote_copy(
            src_ref=source,
            dst_ref=destination,
            send_sem=self.send_sems.at[len(self.sends)],
            recv_sem=self.recv_sems.at[which or 0, part, line, row],
            device_id=target,
            device_id_type=MESH_IDS,
        )
        copy.start()
        self.sends.append(copy)

    def arrive(self, part, line, row, which=None):
        destination = self.slot_of(part, line, row)
        if which is not None:
            destination = self.half_of(destination, part, which)
        pltpu.make_async_remote_copy(
            src_ref=destination,
            dst_ref=destination,
            send_sem=self.send_sems.at[0],
            recv_sem=self.recv_sems.at[which or 0, part, line, row],
            device_id=self.sibling,
            device_id_type=MESH_IDS,
        ).wait_recv()

    def send_own(self, part):
        dp, z, core = self.dp, self.z, self.core
        for other in self.others:
            self.send(part, self.own, dp, place(other, z, core), own=True)
        for step in self.steps[1:]:
            self.send(part, self.own, dp, place(dp, (z + step) % self.depth, core), own=True)
        self.send(part, self.own, dp, self.sibling, own=True)
        keep = pltpu.make_async_copy(
            self.shards[part], self.slot_of(part, self.own, dp), self.own_sems.at[part])
        keep.start()
        self.keeps.append(keep)

    def turn(self, index):
        dp, z, core = self.dp, self.z, self.core
        count = len(self.units)
        if index < count:
            part, turn = self.units[index]
            line = self.lines[turn]
            if turn:
                self.arrive(part, line, dp)
                for other in self.others:
                    self.send(part, line, dp, place(other, z, core))
                self.send(part, line, dp, self.sibling)
        if 1 <= index <= count:
            part, turn = self.units[index - 1]
            line = self.lines[turn]
            for position, other in enumerate(self.others):
                self.arrive(part, line, other)
                self.send(
                    part, line, other, place(self.others[1 - position], z, core), which=position)
                self.send(part, line, other, self.sibling)
        if 2 <= index:
            part, turn = self.units[index - 2]
            line = self.lines[turn]
            self.arrive(part, line, dp ^ 3, 0)
            self.arrive(part, line, dp ^ 3, 1)
            self.send(part, line, dp ^ 3, self.sibling)

    def finish_part(self, part):
        for line in self.lines:
            for row in range(self.rows):
                self.arrive(part, line + 1 - 2 * self.core, (self.dp + row) % self.rows)
        self.keeps[part].wait()

    def wait_sends(self):
        for copy in self.sends:
            copy.wait_send()


class Scatter:
    def __init__(self, rows, depth, where, shapes, grads, buffers, sems):
        self.rows, self.depth, self.shapes, self.grads = rows, depth, shapes, grads
        self.dp, self.z, self.core, self.others = where
        self.held, self.planes_in, self.crosses_in, self.alongs_in = (
            buffers[3 * kind : 3 * kind + 3] for kind in range(4))
        (
            self.pair_send, self.pair_recv, self.plane_send, self.plane_recv,
            self.cross_send, self.cross_recv, self.along_send, self.along_recv,
        ) = sems
        self.sibling = place(self.dp, self.z, 1 - self.core)
        self.targets = [self.dp ^ 3, self.dp ^ 1, self.dp ^ 2, self.dp]
        self.lines = [(self.z + step) % depth for step in z_order(depth)[::-1]]
        self.units = [(part, turn) for part in (2, 1, 0) for turn in range(depth)]
        self.pairs, self.planes, self.crosses, self.alongs = {}, {}, {}, {}

    def remote(self, source, destination, send_sem, recv_sem, target):
        copy = pltpu.make_async_remote_copy(
            src_ref=source, dst_ref=destination, send_sem=send_sem, recv_sem=recv_sem,
            device_id=target, device_id_type=MESH_IDS)
        copy.start()
        return copy

    def block(self, part, line, target):
        return block_of(self.grads[part], line, target, self.shapes[part], part == 2)

    def add(self, first, others_in, length, target):
        chunk = 48

        @pl.loop(0, length // chunk)
        def _(index):
            piece = pl.ds(pl.multiple_of(index * chunk, chunk), chunk)
            total = first[piece, :].astype(jnp.float32)
            for other in others_in:
                total = total + other[piece, :].astype(jnp.float32)
            target[piece, :] = total.astype(target.dtype)

    def start_pairs(self, part):
        for turn, line in enumerate(self.lines):
            for slot, target in enumerate(self.targets):
                key = (part, turn, slot)
                self.pairs[key] = self.remote(
                    self.block(part, line * 2 + 1 - self.core, target),
                    self.held[part].at[turn, slot], self.pair_send.at[key],
                    self.pair_recv.at[key], self.sibling)

    def wait_pairs_sent(self, part):
        for turn in range(self.depth):
            for slot in range(self.rows):
                self.pairs[part, turn, slot].wait_send()

    def turn(self, index):
        last = self.rows - 1
        count = len(self.units)
        if index < count:
            part, turn = self.units[index]
            height = self.shapes[part][0]
            half = height // 2
            for slot, target in enumerate(self.targets):
                self.pairs[part, turn, slot].wait_recv()
                here = self.held[part].at[turn, slot]
                own = self.block(part, self.lines[turn] * 2 + self.core, target)
                self.add(own, [here], height, here)
                if slot == 0:
                    for position in range(2):
                        key = (part, turn, position)
                        self.crosses[key] = self.remote(
                            self.held[part].at[turn, 0, pl.ds((1 - position) * half, half)],
                            self.crosses_in[part].at[turn, position],
                            self.cross_send.at[key], self.cross_recv.at[key],
                            place(self.others[position], self.z, self.core))
        if 1 <= index <= count:
            part, turn = self.units[index - 1]
            half = self.shapes[part][0] // 2
            for position in range(2):
                self.crosses[part, turn, 1 - position].wait_recv()
                piece = self.held[part].at[turn, 1 + position, pl.ds(position * half, half)]
                self.add(piece, [self.crosses_in[part].at[turn, 1 - position]], half, piece)
                key = (part, turn, position)
                self.planes[key] = self.remote(
                    self.held[part].at[turn, 1 + position], self.planes_in[part].at[turn, position],
                    self.plane_send.at[key], self.plane_recv.at[key],
                    place(self.others[position], self.z, self.core))
        if 2 <= index:
            part, turn = self.units[index - 2]
            for position in range(2):
                self.planes[part, turn, position].wait_recv()
            here = self.held[part].at[turn, last]
            arrived = [self.planes_in[part].at[turn, position] for position in range(2)]
            self.add(here, arrived, self.shapes[part][0], here)
            if turn < self.depth - 1:
                key = (part, turn)
                self.alongs[key] = self.remote(
                    here, self.alongs_in[part].at[turn], self.along_send.at[key],
                    self.along_recv.at[key], place(self.dp, self.lines[turn], self.core))

    def finish_part(self, part):
        total = self.held[part][self.depth - 1, self.rows - 1].astype(jnp.float32)
        for turn in range(self.depth - 1):
            self.alongs[part, turn].wait_recv()
            total = total + self.alongs_in[part][turn].astype(jnp.float32)
        return total

    def wait_sends(self):
        for copies in (self.planes, self.crosses, self.alongs):
            for copy in copies.values():
                copy.wait_send()


def layer_kernel(rows, depth, *refs):
    shards = refs[:3]
    cond_rows, slope, ada_ref, ada_bias, bias_row, latents, cotangent, live_ref = refs[3:11]
    (
        block_out, latent_grad, cond_grad, ada_grad, ada_bias_grad, qkv_grad, qv_bias_grad,
        proj_grad, proj_bias_grad, fc1_grad, fc1_bias_grad, fc2_grad, fc2_bias_grad,
    ) = refs[11:24]
    refs = refs[24:]
    weights, grads = refs[:3], (refs[3], refs[4], refs[3])
    scatter_buffers, scatter_sems = refs[5:17], refs[17:25]
    (
        own_sems, send_sems, recv_sems, bias_in, part_out, part_in,
        cond_send, cond_recv, part_send, part_recv, bias_send, bias_recv,
        leaving, cond_in, all_rows, back_out, back_in, row_send, row_recv, back_send, back_recv,
        mod, qkv_bias, proj_bias, fc1_bias, fc2_bias, mod_grad, qkv_sums, proj_sums, fc1_sums,
        fc2_sums, inverse_one, inverse_two, normed_one, normed_two, middle, branch, wide,
        hidden_one, hidden_one_t, hidden_two, hidden_two_t, attended, attended_t,
        grad_mlp, grad_mlp_t, grad_attended, projected,
        grad_proj_mixed, activated, grad_pre, probability,
    ) = refs[25:]
    grad_natural, grad_mixed = activated, grad_pre
    mixed, fc1, fc2_turned = weights
    where = positions(rows, depth)
    dp = where[0]
    columns = 2 * depth
    column = lax.axis_index("fsdp")
    me = dp * columns + column
    length = latents.shape[0]
    qkv_part, proj_part = 3 * D // columns, D // columns
    block = qkv_part + proj_part
    edge = qkv_part // 128 * 128
    rest = block - edge
    lead = qkv_part - edge
    scale_factor = HEAD ** (-0.5)
    ada_rows, mod_width = ada_ref.shape
    mod_pad = round_up(mod_width)
    enter_barrier(me, rows, columns)
    gather = Gather(rows, depth, where, shards, weights, own_sems, send_sems, recv_sems)
    scatter = Scatter(
        rows, depth, where, [shard.shape for shard in shards], grads, scatter_buffers, scatter_sems)
    row_swap = Exchange(
        me, rows, columns, lambda target: leaving.at[lax.rem(target, columns)], all_rows,
        row_send, row_recv)
    back_swap = Exchange(
        me, rows, columns, lambda target: back_out.at[target], back_in, back_send, back_recv)

    cond_swap = Exchange(
        me, rows, columns, lambda target: cond_rows.at[target // columns], cond_in,
        cond_send, cond_recv)
    part_swap = Exchange(
        me, rows, columns, lambda target: part_out.at[target], part_in, part_send, part_recv)
    cond_swap.start()
    gather.send_own(0)

    def bias_copy(target, slot):
        return pltpu.make_async_remote_copy(
            src_ref=bias_row, dst_ref=bias_in.at[slot], send_sem=bias_send.at[target],
            recv_sem=bias_recv.at[slot], device_id=(dp, target), device_id_type=MESH_IDS)

    @pl.loop(1, columns)
    def _(step):
        bias_copy(lax.rem(column + step, columns), column).start()

    bias_in[column] = bias_row[...]
    gather.send_own(1)
    gather.send_own(2)

    def piece(kind):
        return mod[:, kind * D : (kind + 1) * D]

    def start_modulation():
        cond_swap.wait_arrivals()
        high, width = ada_ref.shape
        part = dot_plain(cond_in[:, 0, :high].astype(bfloat), ada_ref[...])
        part_out[:, 0, :width] = part + jnp.where(dp == 0, ada_bias[...], 0.0)
        part_swap.start()

    def normalize_first():
        normed, inverse = normalize_rows(latents[...].astype(jnp.float32))
        normed_one[...] = normed
        inverse_one[...] = inverse

    def finish_modulation():
        part_swap.wait_arrivals()
        width = ada_ref.shape[1]
        pieces = []
        for source in range(columns):
            total = part_in[source]
            for row in range(1, rows):
                total = total + part_in[row * columns + source]
            pieces.append(total[:, :width])
        mod[...] = jnp.concatenate(pieces, axis=1)

        @pl.loop(1, columns)
        def _(step):
            other = lax.rem(column + step, columns)
            bias_copy(other, other).wait_recv()
            bias_copy(other, other).wait_send()

        low = 0
        naturals = []
        for width in (2 * D // columns, D // columns, FF // columns, D // columns):
            naturals.append(jnp.concatenate(
                [bias_in[source][:, low : low + width] for source in range(columns)], axis=1))
            low += width
        qkv_bias[:, :D] = naturals[0][:, :D]
        qkv_bias[:, D : 2 * D] = jnp.zeros((1, D), jnp.float32)
        qkv_bias[:, 2 * D :] = naturals[0][:, D:]
        proj_bias[...] = naturals[1]
        fc1_bias[...] = naturals[2]
        fc2_bias[...] = naturals[3]
        hidden = (normed_one[...] * (1.0 + piece(1)) + piece(0)).astype(bfloat)
        hidden_one[...] = hidden
        hidden_one_t[...] = hidden.T
        grad = (piece(5) * (live_ref[...] * cotangent[...].astype(jnp.float32))).astype(bfloat)
        grad_mlp[...] = grad
        grad_mlp_t[...] = grad.T
        fc2_sums[...] = columns_sum(grad.astype(jnp.float32))

    def span(index, width):
        return pl.ds(pl.multiple_of(index * width, width), width)

    def project():
        @pl.loop(0, columns)
        def _(index):
            wide[:, span(index, block)] = dot_plain(hidden_one[...], mixed[:, span(index, block)])

        for index in range(columns):
            natural = slice(index * qkv_part, (index + 1) * qkv_part)
            projected[:, natural] = (
                wide[:, index * block : index * block + qkv_part] + qkv_bias[:, natural]
            ).astype(bfloat)

    def head_slabs(source, pair):
        return [
            source[:, pl.ds(pl.multiple_of(kind * D + pair * 128, 128), 128)] for kind in range(3)]

    def own_lanes(which):
        lane = lax.broadcasted_iota(jnp.int32, (length, 128), 1)
        return lane < HEAD if which == 0 else lane >= HEAD

    def attend(low, high):
        @pl.loop(low, high)
        def _(pair):
            queries, keys, values = head_slabs(projected, pair)
            zero = jnp.zeros_like(queries)
            results = []
            for which in range(2):
                scores = against_weight(
                    jnp.where(own_lanes(which), queries, zero), keys) * scale_factor
                shifted = jnp.exp(scores - jnp.max(scores, axis=-1, keepdims=True))
                exact = shifted / jnp.sum(shifted, axis=-1, keepdims=True)
                probability[2 * pair + which] = exact
                results.append(dot_plain(exact.astype(bfloat), values))
            attended[:, span(pair, 128)] = jnp.where(
                own_lanes(0), results[0], results[1]).astype(bfloat)

    def finish_attention():
        attended_t[...] = attended[...].T

        @pl.loop(0, columns)
        def _(index):
            tail = pl.ds(pl.multiple_of(index * block + edge, 128), rest)
            wide[:, span(index, rest)] = dot_plain(attended[...], mixed[:, tail])

        for index in range(columns):
            natural = slice(index * proj_part, (index + 1) * proj_part)
            branch[:, natural] = (
                wide[:, index * rest + lead : (index + 1) * rest] + proj_bias[:, natural])
        total = latents[...].astype(jnp.float32) + piece(2) * branch[...]
        middle[...] = total
        normed, inverse = normalize_rows(total)
        normed_two[...] = normed
        inverse_two[...] = inverse
        hidden = (normed * (1.0 + piece(4)) + piece(3)).astype(bfloat)
        hidden_two[...] = hidden
        hidden_two_t[...] = hidden.T

    chunk = 384
    chunks = FF // chunk

    def expand(low, high):
        @pl.loop(low, high)
        def _(index):
            part = span(index, chunk)
            value = dot_plain(hidden_two[...], fc1[:, part]) + fc1_bias[:, part]
            root = 0.7978845608028654
            square = value * value
            bend = jnp.tanh(root * (value + 0.044715 * (square * value)))
            activated[:, part] = (0.5 * value * (1.0 + bend)).astype(bfloat)
            wide[:, part] = 0.5 * (1.0 + bend) + 0.5 * value * (1.0 - bend * bend) * (
                root * (1.0 + 3 * 0.044715 * square))

    def fc2_weight_grad(low, high):
        @pl.loop(low, high)
        def _(index):
            part = span(index, chunk)
            grads[2][:, part] = dot_plain(grad_mlp_t[...], activated[:, part]).astype(bfloat)

    hooks = {
        0: start_modulation,
        1: normalize_first,
        2: finish_modulation,
    }

    def after_part_zero():
        gather.finish_part(0)
        project()

    def after_part_one():
        gather.finish_part(1)
        expand(0, 4)

    hooks[depth + 2] = after_part_zero
    hooks[depth + 3] = lambda: attend(0, 3)
    hooks[depth + 4] = lambda: attend(3, 6)
    hooks[depth + 5] = finish_attention
    hooks[2 * depth + 2] = after_part_one
    hooks[2 * depth + 3] = lambda: expand(4, 8)
    hooks[2 * depth + 4] = lambda: fc2_weight_grad(0, 4)
    hooks[2 * depth + 5] = lambda: fc2_weight_grad(4, 8)
    for index in range(3 * depth + 2):
        gather.turn(index)
        if index in hooks:
            hooks[index]()
    scatter.start_pairs(2)
    gather.finish_part(2)
    third = 256

    def finish_forward():
        @pl.loop(0, D // third)
        def _(index):
            part = span(index, third)
            branch_part = against_weight(activated[...], fc2_turned[part, :]) + fc2_bias[:, part]
            live_grad = live_ref[:, part] * cotangent[:, part].astype(jnp.float32)
            last = pl.ds(pl.multiple_of(5 * D + index * third, third), third)
            block_out[:, part] = (
                live_ref[:, part] * (middle[:, part] + mod[:, last] * branch_part)).astype(bfloat)
            mod_grad[:, last] = columns_sum(live_grad * branch_part)

    def fc1_weight_grad(low, high):
        @pl.loop(low, high)
        def _(index):
            part = span(index, chunk)
            grad = (dot_plain(grad_mlp[...], fc2_turned[:, part]) * wide[:, part]).astype(bfloat)
            grad_pre[:, part] = grad
            fc1_sums[:, part] = columns_sum(grad.astype(jnp.float32))
            grads[1][:, part] = dot_plain(hidden_two_t[...], grad).astype(bfloat)

    def hidden_two_back():
        @pl.loop(0, D // third)
        def _(index):
            part = span(index, third)
            middle[:, part] = against_weight(grad_pre[...], fc1[part, :])

    def middle_back():
        grad_hidden = middle[...]
        mod_grad[:, 3 * D : 4 * D] = columns_sum(grad_hidden)
        mod_grad[:, 4 * D : 5 * D] = columns_sum(grad_hidden * normed_two[...])
        grad_middle = live_ref[...] * cotangent[...].astype(jnp.float32) + norm_backward(
            grad_hidden * (1.0 + piece(4)), normed_two[...], inverse_two[...])
        mod_grad[:, 2 * D : 3 * D] = columns_sum(grad_middle * branch[...])
        middle[...] = grad_middle
        grad_branch = (piece(2) * grad_middle).astype(bfloat)
        proj_sums[...] = columns_sum(grad_branch.astype(jnp.float32))
        for index in range(columns):
            grad_proj_mixed[:, index * rest : index * rest + lead] = jnp.zeros(
                (length, lead), bfloat)
            grad_proj_mixed[:, index * rest + lead : (index + 1) * rest] = (
                grad_branch[:, index * proj_part : (index + 1) * proj_part])
        total = None
        for index in range(columns):
            term = against_weight(
                grad_proj_mixed[:, index * rest : (index + 1) * rest],
                mixed[:, index * block + edge : (index + 1) * block])
            total = term if total is None else total + term
        grad_attended[...] = total.astype(bfloat)

    def attend_back(low, high):
        @pl.loop(low, high)
        def _(pair):
            queries, keys, values = head_slabs(projected, pair)
            grad_out = grad_attended[:, span(pair, 128)]
            zero = jnp.zeros_like(grad_out)
            results = []
            for which in range(2):
                exact = probability[2 * pair + which]
                grad_prob = against_weight(jnp.where(own_lanes(which), grad_out, zero), values)
                inner = jnp.sum(exact * grad_prob, axis=-1, keepdims=True)
                grad_scores = (exact * (grad_prob - inner)).astype(bfloat)
                results.append((
                    dot_plain(grad_scores, keys) * scale_factor,
                    contract_rows(grad_scores, queries) * scale_factor,
                    contract_rows(exact.astype(bfloat), grad_out)))
            for kind in range(3):
                grad_natural[:, pl.ds(pl.multiple_of(kind * D + pair * 128, 128), 128)] = jnp.where(
                    own_lanes(0), results[0][kind], results[1][kind]).astype(bfloat)

    def mixed_weight_grad():
        qkv_sums[...] = columns_sum(grad_natural[:, : 3 * D].astype(jnp.float32))
        for index in range(columns):
            grad_mixed[:, index * block : index * block + qkv_part] = (
                grad_natural[:, index * qkv_part : (index + 1) * qkv_part])
            grad_mixed[:, index * block + qkv_part : (index + 1) * block] = jnp.zeros(
                (length, proj_part), bfloat)
        scatter.wait_pairs_sent(2)

        @pl.loop(0, columns)
        def _(index):
            low = pl.multiple_of(index * block, 128)
            grads[0][:, pl.ds(low, edge)] = dot_plain(
                hidden_one_t[...], grad_mixed[:, pl.ds(low, edge)]).astype(bfloat)
            tail = pl.ds(pl.multiple_of(index * block + edge, 128), rest)
            grads[0][:, tail] = (
                dot_plain(hidden_one_t[...], grad_mixed[:, tail])
                + dot_plain(attended_t[...], grad_proj_mixed[:, span(index, rest)])).astype(bfloat)

    def finish_backward():
        @pl.loop(0, D // third)
        def _(index):
            part = span(index, third)
            branch[:, part] = against_weight(grad_mixed[...], mixed[part, :])

        grad_hidden = branch[...]
        mod_grad[:, :D] = columns_sum(grad_hidden)
        mod_grad[:, D : 2 * D] = columns_sum(grad_hidden * normed_one[...])
        latent_grad[...] = (middle[...] + norm_backward(
            grad_hidden * (1.0 + piece(1)), normed_one[...], inverse_one[...])).astype(bfloat)
        pad = jnp.zeros((1, mod_pad - mod_width), jnp.float32)
        qv_sums = jnp.concatenate([qkv_sums[:, :D], qkv_sums[:, 2 * D :]], axis=1)
        rows_of = (qv_sums, proj_sums[...], fc1_sums[...], fc2_sums[...])
        every = mod_grad[...]
        for index in range(columns):
            pieces = [every[:, index * mod_width : (index + 1) * mod_width], pad]
            for row in rows_of:
                share = row.shape[1] // columns
                pieces.append(row[:, index * share : (index + 1) * share])
            leaving[index] = jnp.concatenate(pieces, axis=1)
        row_swap.start()

    def own_sums():
        row_swap.wait_arrivals()
        arrived = all_rows[:, 0, :]
        sums = columns_sum(arrived)
        ada_bias_grad[...] = sums[:, :mod_width]
        low = mod_pad
        for out in (qv_bias_grad, proj_bias_grad, fc1_bias_grad, fc2_bias_grad):
            out[...] = sums[:, low : low + out.shape[1]]
            low += out.shape[1]
        ada_grad[...] = contract_exact(cond_in[:, 0, :ada_rows], arrived[:, :mod_width])
        back_out[:, 0, :ada_rows] = lax.dot_general(
            arrived[:, :mod_width], ada_ref[...].astype(jnp.float32), (((1,), (1,)), ((), ())),
            precision=highest)
        back_swap.start()

    fc1_weight_grad(0, 4)
    scatter.turn(0)
    fc1_weight_grad(4, 8)
    scatter.start_pairs(1)
    scatter.turn(1)
    finish_forward()
    hidden_two_back()
    scatter.turn(2)
    middle_back()
    scatter.turn(3)
    attend_back(0, 2)
    scatter.turn(4)
    attend_back(2, 4)
    scatter.turn(5)
    attend_back(4, 6)
    scatter.turn(6)
    mixed_weight_grad()
    scatter.start_pairs(0)
    scatter.turn(7)
    finish_backward()
    fc2_grad[...] = scatter.finish_part(2).T
    scatter.turn(8)
    scatter.turn(9)
    own_sums()
    scatter.turn(10)
    fc1_grad[...] = scatter.finish_part(1)
    scatter.turn(11)
    scatter.turn(12)
    back_swap.wait_arrivals()
    terms = []
    for row in range(rows):
        total = back_in[row * columns]
        for source in range(1, columns):
            total = total + back_in[row * columns + source]
        terms.append(total[:, :ada_rows])
    cond_grad[...] = jnp.concatenate(terms, axis=1) * slope[...]
    scatter.turn(13)
    total = scatter.finish_part(0)
    qkv_grad[...] = total[:, :qkv_part]
    proj_grad[...] = total[:, qkv_part:]
    scatter.wait_pairs_sent(1)
    scatter.wait_pairs_sent(0)
    scatter.wait_sends()
    gather.wait_sends()
    for swap in (cond_swap, part_swap, row_swap, back_swap):
        swap.wait_sends()


def run_layer(shards, cond_rows, slope, ada_weight, ada_bias, bias_row, latents, cotangent, live,
              widths, rows, columns):
    depth = columns // 2
    count = (depth - 1) + depth * rows + depth * (rows - 1) + 2 * depth
    total = rows * columns
    ada_rows, mod_width = ada_weight.shape
    mod_pad = round_up(mod_width)
    bias_width = bias_row.shape[-1]
    length = latents.shape[0]
    vmem = pl.BlockSpec(memory_space=pltpu.VMEM)
    anywhere = pl.BlockSpec(memory_space=pl.ANY)
    dma = pltpu.SemaphoreType.DMA
    shapes = [
        whole_shape(shard.shape, part == 2, rows, columns) for part, shard in enumerate(shards)]
    row_buffer = lambda count, width: pltpu.VMEM((count, 1, width), jnp.float32)
    wide_row = lambda width: pltpu.VMEM((1, width), jnp.float32)
    single = lambda width: pltpu.VMEM((length, width), jnp.float32)
    half = lambda width: pltpu.VMEM((length, width), bfloat)
    turned = pltpu.VMEM((D, length), bfloat)
    rest = 128 * columns
    buffers = []
    for lead in ((depth, rows), (depth, 2), (depth, 2), (depth - 1,)):
        for shard in shards:
            height, width = shard.shape
            height = height // 2 if 6 <= len(buffers) < 9 else height
            buffers.append(pltpu.VMEM(lead + (height, width), bfloat))
    float_out = lambda *shape: jax.ShapeDtypeStruct(shape, jnp.float32)
    qkv_part, proj_part = 3 * D // columns, D // columns
    height = shards[0].shape[0]
    return pl.pallas_call(
        functools.partial(layer_kernel, rows, depth),
        out_shape=[
            jax.ShapeDtypeStruct((length, D), bfloat),
            jax.ShapeDtypeStruct((length, D), bfloat),
            float_out(1, D),
            float_out(ada_rows, mod_width), float_out(1, mod_width),
            float_out(height, qkv_part), float_out(1, widths[0]),
            float_out(height, proj_part), float_out(1, widths[1]),
            float_out(*shards[1].shape), float_out(1, widths[2]),
            float_out(*shards[2].shape[::-1]), float_out(1, widths[3]),
        ],
        in_specs=[anywhere] * 3 + [vmem] * 8,
        out_specs=[vmem] * 13,
        scratch_shapes=[pltpu.VMEM(shape, bfloat) for shape in shapes + shapes[:2]]
        + buffers + [
            dma((3, depth, rows)), dma((3, depth, rows)),
            dma((3, depth, 2)), dma((3, depth, 2)), dma((3, depth, 2)), dma((3, depth, 2)),
            dma((3, depth - 1)), dma((3, depth - 1)),
            dma((3,)), dma((3 * count,)), dma((2, 3, columns, rows)),
            row_buffer(columns, bias_width), row_buffer(total, mod_pad), row_buffer(total, mod_pad),
            dma((total,)), dma((total,)), dma((total,)), dma((total,)),
            dma((columns,)), dma((columns,)),
            row_buffer(columns, mod_pad + bias_width), row_buffer(total, cond_rows.shape[-1]),
            row_buffer(total, mod_pad + bias_width),
            row_buffer(total, round_up(ada_rows)), row_buffer(total, round_up(ada_rows)),
            dma((total,)), dma((total,)), dma((total,)), dma((total,)),
            wide_row(6 * D), wide_row(3 * D), wide_row(D), wide_row(FF), wide_row(D),
            wide_row(6 * D), wide_row(3 * D), wide_row(D), wide_row(FF), wide_row(D),
            single(1), single(1), single(D), single(D), single(D), single(D), single(FF),
            half(D), turned, half(D), turned, half(D), turned,
            half(D), turned, half(D), half(3 * D),
            half(rest), half(FF), half(FF), pltpu.VMEM((HEADS, length, length), jnp.float32),
        ],
        compiler_params=pltpu.CompilerParams(
            collective_id=2, has_side_effects=True, vmem_limit_bytes=62 * 2**20),
        name="run_layer",
    )(*shards, cond_rows, slope, ada_weight, ada_bias, bias_row, latents, cotangent, live)


def pick(mixed, columns, kind):
    width = mixed.shape[1] // columns
    edge = 3 * width // 4
    low, high = (0, edge) if kind == 0 else (edge, width)
    return jnp.concatenate(
        [mixed[:, block * width + low : block * width + high] for block in range(columns)], axis=1
    )


def spread(rows_in, columns, kind):
    width = rows_in.shape[1] // columns
    rest = width // 3 if kind == 0 else 3 * width
    zeros = jnp.zeros((rows_in.shape[0], rest), rows_in.dtype)
    pieces = []
    for block in range(columns):
        piece = rows_in[:, block * width : (block + 1) * width]
        pieces += [piece, zeros] if kind == 0 else [zeros, piece]
    return jnp.concatenate(pieces, axis=1)


def layer(latent_rows, live, cot_rows, modulation, weights, biases, columns):
    mixed_weight, fc1_weight, fc2_turned = weights
    qv_bias, proj_bias, fc1_bias, fc2_bias = biases
    length = latent_rows.shape[0]
    rows_wide = latent_rows.astype(jnp.float32)
    shift_one, scale_one, gate_one, shift_two, scale_two, gate_two = jnp.split(
        modulation, 6, axis=-1
    )
    normed_one, inverse_one = normalize_rows(rows_wide)
    hidden_one = (normed_one * (1.0 + scale_one) + shift_one).astype(bfloat)
    qkv_bias = jnp.concatenate([qv_bias[:D], jnp.zeros((D,), jnp.float32), qv_bias[D:]])
    projected = (
        pick(jnp.dot(hidden_one, mixed_weight, preferred_element_type=jnp.float32), columns, 0)
        + qkv_bias
    ).astype(bfloat)
    queries = projected[:, :D].reshape(length, HEADS, HEAD)
    key_rows = projected[:, D : 2 * D].reshape(length, HEADS, HEAD)
    values = projected[:, 2 * D :].reshape(length, HEADS, HEAD)
    scale_factor = HEAD ** (-0.5)
    scores = (
        jnp.einsum("qhe,khe->hqk", queries, key_rows, preferred_element_type=jnp.float32)
        * scale_factor
    )
    row_max = jnp.max(scores, axis=-1, keepdims=True)
    shifted = jnp.exp(scores - row_max)
    row_total = jnp.sum(shifted, axis=-1, keepdims=True)
    exact_probability = shifted / row_total
    probability = exact_probability.astype(bfloat)
    attended = jnp.einsum("hqk,khe->qhe", probability, values, preferred_element_type=jnp.float32)
    attended = attended.reshape(length, D).astype(bfloat)
    branch = pick(jnp.dot(attended, mixed_weight, preferred_element_type=jnp.float32), columns, 1)
    branch = branch + proj_bias
    middle = rows_wide + gate_one * branch
    normed_two, inverse_two = normalize_rows(middle)
    hidden_two = (normed_two * (1.0 + scale_two) + shift_two).astype(bfloat)
    pre_gelu = jnp.dot(hidden_two, fc1_weight, preferred_element_type=jnp.float32) + fc1_bias
    activated, gelu_pull = jax.vjp(
        lambda argument: jax.nn.gelu(argument, approximate=True), pre_gelu
    )
    activated = activated.astype(bfloat)
    mlp_out = against_weight(activated, fc2_turned) + fc2_bias
    block_out = (live * (middle + gate_two * mlp_out)).astype(bfloat)

    grad_out = live * cot_rows.astype(jnp.float32)
    gate_two_grad = jnp.sum(grad_out * mlp_out, axis=0, keepdims=True)
    grad_mlp = (gate_two * grad_out).astype(bfloat)
    fc2_bias_grad = jnp.sum(grad_mlp.astype(jnp.float32), axis=0)
    grad_act = jnp.dot(grad_mlp, fc2_turned, preferred_element_type=jnp.float32)
    grad_pre = gelu_pull(grad_act)[0].astype(bfloat)
    fc1_bias_grad = jnp.sum(grad_pre.astype(jnp.float32), axis=0)
    grad_hidden_two = against_weight(grad_pre, fc1_weight)
    shift_two_grad = jnp.sum(grad_hidden_two, axis=0, keepdims=True)
    scale_two_grad = jnp.sum(grad_hidden_two * normed_two, axis=0, keepdims=True)
    grad_middle = grad_out + norm_backward(
        grad_hidden_two * (1.0 + scale_two), normed_two, inverse_two
    )
    gate_one_grad = jnp.sum(grad_middle * branch, axis=0, keepdims=True)
    grad_branch = (gate_one * grad_middle).astype(bfloat)
    proj_bias_grad = jnp.sum(grad_branch.astype(jnp.float32), axis=0)
    spread_branch = spread(grad_branch, columns, 1)
    grad_attended = (
        against_weight(spread_branch, mixed_weight).astype(bfloat).reshape(length, HEADS, HEAD)
    )
    grad_prob = jnp.einsum(
        "qhe,khe->hqk", grad_attended, values, preferred_element_type=jnp.float32
    )
    inner_sum = jnp.sum(exact_probability * grad_prob, axis=-1, keepdims=True)
    grad_scores = (exact_probability * (grad_prob - inner_sum)).astype(bfloat)
    grad_queries = (
        jnp.einsum("hqk,khe->qhe", grad_scores, key_rows, preferred_element_type=jnp.float32)
        * scale_factor
    )
    grad_keys = (
        jnp.einsum("hqk,qhe->khe", grad_scores, queries, preferred_element_type=jnp.float32)
        * scale_factor
    )
    grad_values = jnp.einsum(
        "hqk,qhe->khe", probability, grad_attended, preferred_element_type=jnp.float32
    )
    grad_projected = jnp.concatenate(
        [
            grad_queries.reshape(length, D),
            grad_keys.reshape(length, D),
            grad_values.reshape(length, D),
        ],
        axis=1,
    ).astype(bfloat)
    summed = jnp.sum(grad_projected.astype(jnp.float32), axis=0)
    qv_bias_grad = jnp.concatenate([summed[:D], summed[2 * D :]])
    spread_projected = spread(grad_projected, columns, 0)
    grad_hidden_one = against_weight(spread_projected, mixed_weight)
    shift_one_grad = jnp.sum(grad_hidden_one, axis=0, keepdims=True)
    scale_one_grad = jnp.sum(grad_hidden_one * normed_one, axis=0, keepdims=True)
    latent_grad = (
        grad_middle + norm_backward(grad_hidden_one * (1.0 + scale_one), normed_one, inverse_one)
    ).astype(bfloat)
    mod_grad = jnp.concatenate(
        [
            shift_one_grad,
            scale_one_grad,
            gate_one_grad,
            shift_two_grad,
            scale_two_grad,
            gate_two_grad,
        ],
        axis=-1,
    )
    weight_grads = (
        contract_rows(
            jnp.concatenate([hidden_one, attended]),
            jnp.concatenate([spread_projected, spread_branch]),
        ).astype(bfloat),
        contract_rows(hidden_two, grad_pre).astype(bfloat),
        contract_rows(grad_mlp, activated).astype(bfloat),
    )
    bias_grads = (qv_bias_grad, proj_bias_grad, fc1_bias_grad, fc2_bias_grad)
    return block_out, latent_grad, mod_grad, weight_grads, bias_grads


def flatten_blocks(blocks, turned):
    if blocks.ndim == 2:
        return blocks
    columns, rows, height, width = blocks.shape
    if turned:
        return blocks.transpose(0, 2, 1, 3).reshape(columns * height, rows * width)
    return blocks.transpose(1, 2, 0, 3).reshape(rows * height, columns * width)


def cut_blocks(whole, shape, turned, rows, columns):
    if len(whole_shape(shape, turned, rows, columns)) == 2:
        return whole
    height, width = shape
    if turned:
        return whole.reshape(columns, height, rows, width).transpose(0, 2, 1, 3)
    return whole.reshape(rows, height, columns, width).transpose(2, 0, 1, 3)


def per_device(
    latents,
    conditioning,
    cotangent,
    latent_count,
    ada_weight,
    ada_bias,
    qkv_weight,
    qv_bias,
    proj_weight,
    proj_bias,
    fc1_weight,
    fc1_bias,
    fc2_weight,
    fc2_bias,
):
    rows, columns = lax.axis_size("dp"), lax.axis_size("fsdp")
    live = latent_count[0].astype(jnp.float32)
    depth = ada_weight.shape[0]
    mod_width = ada_weight.shape[1]
    mod_pad = round_up(mod_width)
    own_biases = (qv_bias, proj_bias, fc1_bias, fc2_bias)
    widths = [bias.shape[0] for bias in own_biases]
    cuts = [sum(widths[:place]) for place in range(len(widths))]

    def split_cond(row):
        pad = round_up(depth) - depth
        return jnp.pad(row.reshape(rows, 1, depth), ((0, 0), (0, 0), (0, pad)))

    cond_row = conditioning.astype(jnp.float32)
    cond_act, silu_pull = jax.vjp(jax.nn.silu, cond_row)
    slope = silu_pull(jnp.ones_like(cond_row))[0]
    cond_rows = split_cond(cond_act.astype(bfloat).astype(jnp.float32))
    bias_row = jnp.concatenate(own_biases).astype(jnp.float32).reshape(1, -1)

    qkv_width = qkv_weight.shape[1]
    shards = (
        jnp.concatenate([qkv_weight, proj_weight], axis=1),
        fc1_weight,
        fc2_weight.T,
    )
    shapes = [shard.shape for shard in shards]
    ada_row = ada_bias.astype(jnp.float32).reshape(1, -1)
    fused = rows == 4 and columns == 8
    if fused:
        block_out, latent_grad, *param_grads = run_layer(
            shards, cond_rows, slope, ada_weight, ada_row, bias_row, latents[0], cotangent[0],
            jnp.full((1, D), live), widths, rows, columns)
        param_grads = [
            grad.reshape(-1) if 0 < place < 11 and place % 2 == 0 else grad
            for place, grad in enumerate(param_grads)]
        return (block_out[None], latent_grad[None], *param_grads)
    *blocks, mod_blocks, bias_blocks, cond_in = gather_shards(
        shards, cond_rows, ada_weight, ada_row, bias_row,
        rows, columns)
    modulation = mod_blocks[:, :, :mod_width].reshape(1, -1)
    biases = tuple(
        bias_blocks[:, :, cut : cut + width].reshape(-1) for cut, width in zip(cuts, widths)
    )
    weights = [flatten_blocks(block, part == 2) for part, block in enumerate(blocks)]
    block_out, latent_grad, mod_grad, weight_grads, bias_grads = layer(
        latents[0], live, cotangent[0], modulation, weights, biases, columns
    )
    grads = [
        cut_blocks(grad, shapes[part], part == 2, rows, columns)
        for part, grad in enumerate(weight_grads)
    ]
    leaving = jnp.concatenate(
        [jnp.pad(mod_grad.reshape(columns, -1), ((0, 0), (0, mod_pad - mod_width)))]
        + [grad.reshape(columns, -1) for grad in bias_grads], axis=1
    ).reshape(columns, 1, -1)
    mixed_grad, fc1_grad, fc2_turned_grad, ada_grad, sums, cond_grad = scatter_shards(
        grads, leaving, cond_in, ada_weight, split_cond(slope), shapes, rows, columns)
    qkv_grad, proj_grad = mixed_grad[:, :qkv_width], mixed_grad[:, qkv_width:]
    fc2_grad = fc2_turned_grad.T
    ada_bias_grad = sums[0, :mod_width]
    bias_sums = [
        sums[0, mod_pad + cut : mod_pad + cut + width] for cut, width in zip(cuts, widths)]
    cond_grad = cond_grad[:, :, :depth].reshape(1, -1)
    return (
        block_out[None],
        latent_grad[None],
        cond_grad,
        ada_grad,
        ada_bias_grad,
        qkv_grad,
        bias_sums[0],
        proj_grad,
        bias_sums[1],
        fc1_grad,
        bias_sums[2],
        fc2_grad,
        bias_sums[3],
    )


def solution(mesh):
    in_specs = (
        P(("dp", "fsdp"), None, None),
        P(("dp", "fsdp"), None),
        P(("dp", "fsdp"), None, None),
        P(("dp", "fsdp")),
        P("dp", "fsdp"),
        P("fsdp"),
        P("dp", "fsdp"),
        P("fsdp"),
        P("dp", "fsdp"),
        P("fsdp"),
        P("dp", "fsdp"),
        P("fsdp"),
        P("dp", "fsdp"),
        P("fsdp"),
    )
    out_specs = (
        P(("dp", "fsdp"), None, None),
        P(("dp", "fsdp"), None, None),
        P(("dp", "fsdp"), None),
        P("dp", "fsdp"),
        P("fsdp"),
        P("dp", "fsdp"),
        P("fsdp"),
        P("dp", "fsdp"),
        P("fsdp"),
        P("dp", "fsdp"),
        P("fsdp"),
        P("dp", "fsdp"),
        P("fsdp"),
    )
    return jax.shard_map(
        per_device, mesh=mesh, in_specs=in_specs, out_specs=out_specs, check_vma=False
    )
```

```python
import functools
import jax
import jax.numpy as jnp
from jax import lax
from jax.sharding import PartitionSpec as P
from jax.experimental import pallas as pl
from jax.experimental.pallas import tpu as pltpu

MESH_IDS = pl.DeviceIdType.MESH
D = 768
HEADS = 12
HEAD = 64
FF = 3072

highest = lax.Precision.HIGHEST
bfloat = jnp.bfloat16
LAG = 2
AHEAD = 3


def place(dp_index, z_index, core):
    return (dp_index, z_index * 2 + core)


def z_order(size):
    steps = [0]
    for distance in range(1, size // 2 + 1):
        steps.append(distance)
        if size - distance != distance:
            steps.append(size - distance)
    return steps


def device_of(index, columns):
    return (index // columns, lax.rem(index, columns))


def enter_barrier(me, rows, columns):
    barrier = pltpu.get_barrier_semaphore()
    count = rows * columns

    @pl.loop(1, count)
    def _(step):
        target = device_of(lax.rem(me + step, count), columns)
        pl.semaphore_signal(barrier, inc=1, device_id=target, device_id_type=MESH_IDS)

    pl.semaphore_wait(barrier, count - 1)


class Exchange:
    def __init__(self, me, rows, columns, row_for, landing, send_sems, recv_sems):
        self.me, self.columns, self.count = me, columns, rows * columns
        self.row_for, self.landing = row_for, landing
        self.send_sems, self.recv_sems = send_sems, recv_sems

    def start(self):
        @pl.loop(1, self.count)
        def _(step):
            target = lax.rem(self.me + step, self.count)
            pltpu.make_async_remote_copy(
                src_ref=self.row_for(target),
                dst_ref=self.landing.at[self.me],
                send_sem=self.send_sems.at[target],
                recv_sem=self.recv_sems.at[self.me],
                device_id=device_of(target, self.columns),
                device_id_type=MESH_IDS,
            ).start()

        self.landing[self.me] = self.row_for(self.me)[...]

    def pair(self, other):
        return pltpu.make_async_remote_copy(
            src_ref=self.row_for(other),
            dst_ref=self.landing.at[other],
            send_sem=self.send_sems.at[other],
            recv_sem=self.recv_sems.at[other],
            device_id=device_of(other, self.columns),
            device_id_type=MESH_IDS,
        )

    def wait_arrivals(self):
        @pl.loop(1, self.count)
        def _(step):
            self.pair(lax.rem(self.me + step, self.count)).wait_recv()

    def wait_sends(self):
        @pl.loop(1, self.count)
        def _(step):
            self.pair(lax.rem(self.me + step, self.count)).wait_send()


def positions(rows, depth):
    dp = lax.axis_index("dp")
    column = lax.axis_index("fsdp")
    z, core = column // 2, column % 2
    others = [(dp ^ 1), (dp ^ 2)] if rows == 4 else [(dp + step) % rows for step in range(1, rows)]
    return dp, z, core, others


def block_of(array, line, row, shape, turned):
    if len(array.shape) == 4:
        return array.at[line, row]
    high, wide = (line, row) if turned else (row, line)
    height, width = shape
    return array.at[
        pl.ds(pl.multiple_of(high * height, height), height),
        pl.ds(pl.multiple_of(wide * width, width), width),
    ]


def whole_shape(shape, turned, rows, columns):
    height, width = shape
    if width % 128 == 0 and height % 32 == 0:
        return (columns * height, rows * width) if turned else (rows * height, columns * width)
    return (columns, rows, height, width)


def gather_kernel(rows, depth, *refs):
    shards = refs[:3]
    cond_rows, ada_ref, ada_bias, bias_row = refs[3:7]
    outs, mod_out, bias_out, cond_in = refs[7:10], refs[10], refs[11], refs[12]
    (
        own_sems, send_sems, recv_sems, bias_in, part_out, part_in,
        cond_send, cond_recv, part_send, part_recv, bias_send, bias_recv,
    ) = refs[13:]
    dp, z, core, others = positions(rows, depth)
    columns = 2 * depth
    column = lax.axis_index("fsdp")
    me = dp * columns + column
    sibling = place(dp, z, 1 - core)
    enter_barrier(me, rows, columns)
    sends = []

    cond_swap = Exchange(
        me, rows, columns, lambda target: cond_rows.at[target // columns], cond_in,
        cond_send, cond_recv)
    part_swap = Exchange(
        me, rows, columns, lambda target: part_out.at[target], part_in, part_send, part_recv)
    cond_swap.start()

    def bias_copy(target, slot):
        return pltpu.make_async_remote_copy(
            src_ref=bias_row, dst_ref=bias_in.at[slot], send_sem=bias_send.at[target],
            recv_sem=bias_recv.at[slot], device_id=(dp, target), device_id_type=MESH_IDS)

    @pl.loop(1, columns)
    def _(step):
        bias_copy(lax.rem(column + step, columns), column).start()

    bias_in[column] = bias_row[...]

    def slot_of(part, line, row):
        return block_of(outs[part], line, row, shards[part].shape, part == 2)

    def half_of(ref, part, which):
        half = shards[part].shape[0] // 2
        return ref.at[pl.ds(which * half, half)]

    def send(line, row, target, which=None, own=False):
        for part in range(3):
            destination = slot_of(part, line, row)
            source = shards[part] if own else destination
            if which is not None:
                source, destination = half_of(source, part, which), half_of(destination, part, which)
            copy = pltpu.make_async_remote_copy(
                src_ref=source,
                dst_ref=destination,
                send_sem=send_sems.at[len(sends)],
                recv_sem=recv_sems.at[which or 0, part, line, row],
                device_id=target,
                device_id_type=MESH_IDS,
            )
            copy.start()
            sends.append(copy)

    def arrive(line, row, which=None):
        for part in range(3):
            destination = slot_of(part, line, row)
            if which is not None:
                destination = half_of(destination, part, which)
            pltpu.make_async_remote_copy(
                src_ref=destination,
                dst_ref=destination,
                send_sem=send_sems.at[0],
                recv_sem=recv_sems.at[which or 0, part, line, row],
                device_id=sibling,
                device_id_type=MESH_IDS,
            ).wait_recv()

    own = z * 2 + core
    steps = z_order(depth)
    lines = [((z - step) % depth) * 2 + core for step in steps]
    for other in others:
        send(own, dp, place(other, z, core), own=True)
    for step in steps[1:]:
        send(own, dp, place(dp, (z + step) % depth, core), own=True)
    send(own, dp, sibling, own=True)
    keeps = [
        pltpu.make_async_copy(shards[part], slot_of(part, own, dp), own_sems.at[part])
        for part in range(3)
    ]
    for keep in keeps:
        keep.start()
    cond_swap.wait_arrivals()
    high, wide = ada_ref.shape
    part = jnp.dot(
        cond_in[:, 0, :high].astype(bfloat), ada_ref[...], preferred_element_type=jnp.float32)
    part_out[:, 0, :wide] = part + jnp.where(dp == 0, ada_bias[...], 0.0)
    part_swap.start()
    for turn in range(depth + 2):
        if 0 < turn < depth:
            line = lines[turn]
            arrive(line, dp)
            for other in others:
                send(line, dp, place(other, z, core))
            send(line, dp, sibling)
        if 1 <= turn <= depth:
            line = lines[turn - 1]
            for position, other in enumerate(others):
                arrive(line, other)
                if rows == 4:
                    send(line, other, place(others[1 - position], z, core), which=position)
                send(line, other, sibling)
        if turn >= 2 and rows == 4:
            line = lines[turn - 2]
            arrive(line, dp ^ 3, 0)
            arrive(line, dp ^ 3, 1)
            send(line, dp ^ 3, sibling)
    for line in lines:
        for row in range(rows):
            arrive(line + 1 - 2 * core, (dp + row) % rows)
    part_swap.wait_arrivals()
    for block in range(columns):
        total = part_in[block]
        for row in range(1, rows):
            total = total + part_in[row * columns + block]
        mod_out[block] = total

    @pl.loop(1, columns)
    def _(step):
        other = lax.rem(column + step, columns)
        bias_copy(other, other).wait_recv()
        bias_copy(other, other).wait_send()

    bias_out[...] = bias_in[...]
    for keep in keeps:
        keep.wait()
    for copy in sends:
        copy.wait_send()
    cond_swap.wait_sends()
    part_swap.wait_sends()


def round_up(width):
    return -(-width // 128) * 128


def gather_shards(shards, cond_rows, ada_weight, ada_bias, bias_row, rows, columns):
    depth = columns // 2
    total = rows * columns
    mod_pad = round_up(ada_weight.shape[1])
    vmem = pl.BlockSpec(memory_space=pltpu.VMEM)
    dma = pltpu.SemaphoreType.DMA
    row_shape = lambda count, width: jax.ShapeDtypeStruct((count, 1, width), jnp.float32)
    row_buffer = lambda count, width: pltpu.VMEM((count, 1, width), jnp.float32)
    count = (depth - 1) + depth * rows + depth * (rows - 1) + (2 * depth if rows == 4 else 0)
    shapes = [
        whole_shape(shard.shape, part == 2, rows, columns) for part, shard in enumerate(shards)
    ]
    return pl.pallas_call(
        functools.partial(gather_kernel, rows, depth),
        out_shape=[jax.ShapeDtypeStruct(shape, bfloat) for shape in shapes]
        + [row_shape(columns, mod_pad), row_shape(columns, bias_row.shape[-1]),
           row_shape(total, cond_rows.shape[-1])],
        in_specs=[pl.BlockSpec(memory_space=pl.ANY)] * 3 + [vmem] * 4,
        out_specs=[pl.BlockSpec(memory_space=pl.ANY)] * 3 + [vmem] * 3,
        scratch_shapes=[
            dma((3,)),
            dma((3 * count,)),
            dma((2, 3, columns, rows)),
            row_buffer(columns, bias_row.shape[-1]),
            row_buffer(total, mod_pad),
            row_buffer(total, mod_pad),
            dma((total,)), dma((total,)), dma((total,)), dma((total,)),
            dma((columns,)), dma((columns,)),
        ],
        compiler_params=pltpu.CompilerParams(
            collective_id=0, has_side_effects=True, vmem_limit_bytes=32 * 2**20),
        name="gather_shards",
    )(*shards, cond_rows, ada_weight, ada_bias, bias_row)


def scatter_kernel(rows, depth, *refs):
    grads = refs[:3]
    leaving, cond_in, ada_ref, slope = refs[3:7]
    outs, ada_grad, sums_out, cond_grad = refs[7:10], refs[10], refs[11], refs[12]
    refs = refs[13:]
    helds, pairs_in, planes_in, crosses_in, alongs_in = (
        refs[3 * kind : 3 + 3 * kind] for kind in range(5)
    )
    (
        load_sems, pair_send, pair_recv, plane_send, plane_recv,
        cross_send, cross_recv, along_send, along_recv,
        all_rows, back_out, back_in, row_send, row_recv, back_send, back_recv,
    ) = refs[15:]
    dp, z, core, others = positions(rows, depth)
    columns = 2 * depth
    me = dp * columns + lax.axis_index("fsdp")
    row_swap = Exchange(
        me, rows, columns, lambda target: leaving.at[lax.rem(target, columns)], all_rows,
        row_send, row_recv)
    back_swap = Exchange(
        me, rows, columns, lambda target: back_out.at[target], back_in, back_send, back_recv)
    sibling = place(dp, z, 1 - core)
    targets = [dp ^ 3, dp ^ 1, dp ^ 2, dp] if rows == 4 else others + [dp]
    steps = z_order(depth)[::-1]
    enter_barrier(me, rows, columns)
    row_swap.start()
    waits = []

    def remote(source, destination, send_sem, recv_sem, target):
        copy = pltpu.make_async_remote_copy(
            src_ref=source, dst_ref=destination, send_sem=send_sem, recv_sem=recv_sem,
            device_id=target, device_id_type=MESH_IDS,
        )
        copy.start()
        waits.append(copy)
        return copy

    def add(first, others_in, length, target):
        chunk = 48 if length % 48 == 0 else 16

        @pl.loop(0, length // chunk)
        def _(index):
            piece = pl.ds(pl.multiple_of(index * chunk, chunk), chunk)
            total = first[piece, :].astype(jnp.float32)
            for other in others_in:
                total = total + other[piece, :].astype(jnp.float32)
            target[piece, :] = total.astype(target.dtype)

    lines = [(z + step) % depth for step in steps]
    pairs, loads, planes, crosses, alongs = {}, {}, {}, {}, {}
    for turn, line in enumerate(lines):
        for slot, target in enumerate(targets):
            for part in range(3):
                key = (part, turn, slot)
                shape = outs[part].shape
                pairs[key] = remote(
                    block_of(grads[part], line * 2 + 1 - core, target, shape, part == 2),
                    pairs_in[part].at[turn, slot], pair_send.at[key], pair_recv.at[key], sibling)
                loads[key] = pltpu.make_async_copy(
                    block_of(grads[part], line * 2 + core, target, shape, part == 2),
                    helds[part].at[turn, slot], load_sems.at[key])
                loads[key].start()
    last = len(targets) - 1
    for turn in range(depth + 2):
        if turn == depth - 1:
            row_swap.wait_arrivals()
            high, wide = ada_ref.shape
            arrived = all_rows[:, 0, :]
            sums_out[...] = jnp.sum(arrived, axis=0, keepdims=True)
            ada_grad[...] = contract_exact(cond_in[:, 0, :high], arrived[:, :wide])
            back_out[:, 0, :high] = lax.dot_general(
                arrived[:, :wide], ada_ref[...].astype(jnp.float32), (((1,), (1,)), ((), ())),
                precision=highest)
            back_swap.start()
        if turn < depth:
            for slot in range(len(targets)):
                for part in range(3):
                    key = (part, turn, slot)
                    height = outs[part].shape[0]
                    half = height // 2
                    loads[key].wait()
                    pairs[key].wait_recv()
                    here = helds[part].at[turn, slot]
                    add(here, [pairs_in[part].at[turn, slot]], height, here)
                    if rows == 4 and slot == 0:
                        for position in range(2):
                            key = (part, turn, position)
                            crosses[key] = remote(
                                helds[part].at[turn, 0, pl.ds((1 - position) * half, half)],
                                crosses_in[part].at[turn, position],
                                cross_send.at[key], cross_recv.at[key],
                                place(others[position], z, core))
                    if rows != 4 and slot < last:
                        planes[key] = remote(
                            here, planes_in[part].at[turn, slot], plane_send.at[key],
                            plane_recv.at[key], place(targets[slot], z, core))
        if rows == 4 and 1 <= turn <= depth:
            now = turn - 1
            for position in range(2):
                for part in range(3):
                    half = outs[part].shape[0] // 2
                    crosses[part, now, 1 - position].wait_recv()
                    piece = helds[part].at[now, 1 + position, pl.ds(position * half, half)]
                    add(piece, [crosses_in[part].at[now, 1 - position]], half, piece)
                    key = (part, now, position)
                    planes[key] = remote(
                        helds[part].at[now, 1 + position], planes_in[part].at[now, position],
                        plane_send.at[key], plane_recv.at[key],
                        place(others[position], z, core))
        if turn >= 2:
            now = turn - 2
            for part in range(3):
                for slot in range(len(others)):
                    planes[part, now, slot].wait_recv()
                here = helds[part].at[now, last]
                arrived = [planes_in[part].at[now, slot] for slot in range(len(others))]
                add(here, arrived, outs[part].shape[0], here)
                if now < depth - 1:
                    key = (part, now)
                    alongs[key] = remote(
                        here, alongs_in[part].at[now], along_send.at[key], along_recv.at[key],
                        place(dp, lines[now], core))
    for part in range(3):
        for now in range(depth - 1):
            alongs[part, now].wait_recv()
        arrived = [alongs_in[part].at[now] for now in range(depth - 1)]
        add(helds[part].at[depth - 1, last], arrived, outs[part].shape[0], outs[part])
    back_swap.wait_arrivals()
    for row in range(rows):
        total = back_in[row * columns]
        for block in range(1, columns):
            total = total + back_in[row * columns + block]
        cond_grad[row] = total * slope[row]
    for copy in waits:
        copy.wait_send()
    row_swap.wait_sends()
    back_swap.wait_sends()


def scatter_shards(grads, leaving, cond_in, ada_weight, slope, shapes, rows, columns):
    depth = columns // 2
    total = rows * columns
    vmem = pl.BlockSpec(memory_space=pltpu.VMEM)
    row_buffer = lambda count, width: pltpu.VMEM((count, 1, width), jnp.float32)
    peers = 2 if rows == 4 else rows - 1
    dma = pltpu.SemaphoreType.DMA
    buffers = []
    for lead in ((depth, rows), (depth, rows), (depth, peers), (depth, 2), (depth - 1,)):
        for height, width in shapes:
            if lead == (depth, 2) and len(buffers) >= 9:
                height = height // 2 if rows == 4 else 16
            buffers.append(pltpu.VMEM(lead + (height, width), bfloat))
    return pl.pallas_call(
        functools.partial(scatter_kernel, rows, depth),
        out_shape=[jax.ShapeDtypeStruct(shape, jnp.float32) for shape in shapes]
        + [jax.ShapeDtypeStruct(ada_weight.shape, jnp.float32),
           jax.ShapeDtypeStruct((1, leaving.shape[-1]), jnp.float32),
           jax.ShapeDtypeStruct(slope.shape, jnp.float32)],
        in_specs=[pl.BlockSpec(memory_space=pl.ANY)] * 3 + [vmem] * 4,
        out_specs=[vmem] * 6,
        scratch_shapes=buffers + [
            dma((3, depth, rows)), dma((3, depth, rows)), dma((3, depth, rows)),
            dma((3, depth, peers)), dma((3, depth, peers)),
            dma((3, depth, 2)), dma((3, depth, 2)),
            dma((3, depth - 1)), dma((3, depth - 1)),
            row_buffer(total, leaving.shape[-1]),
            row_buffer(total, slope.shape[-1]), row_buffer(total, slope.shape[-1]),
            dma((total,)), dma((total,)), dma((total,)), dma((total,)),
        ],
        compiler_params=pltpu.CompilerParams(
            collective_id=1, has_side_effects=True, vmem_limit_bytes=50 * 2**20),
        name="scatter_shards",
    )(*grads, leaving, cond_in, ada_weight, slope)


def normalize_rows(values):
    center = jnp.mean(values, axis=-1, keepdims=True)
    spread = jnp.mean(jnp.square(values - center), axis=-1, keepdims=True)
    inverse = lax.rsqrt(spread + 1e-06)
    return ((values - center) * inverse, inverse)


def norm_backward(grad_normed, normed, inverse):
    centered = grad_normed - jnp.mean(grad_normed, axis=-1, keepdims=True)
    return inverse * (centered - normed * jnp.mean(grad_normed * normed, axis=-1, keepdims=True))


def contract_rows(left_rows, right_rows):
    return lax.dot_general(
        left_rows, right_rows, (((0,), (0,)), ((), ())), preferred_element_type=jnp.float32
    )


def contract_exact(left_rows, right_rows):
    return lax.dot_general(left_rows, right_rows, (((0,), (0,)), ((), ())), precision=highest)


def against_weight(grad_rows, weight):
    return lax.dot_general(
        grad_rows, weight, (((1,), (1,)), ((), ())), preferred_element_type=jnp.float32
    )


def dot_plain(left, right):
    return jnp.dot(left, right, preferred_element_type=jnp.float32)


def columns_sum(values):
    return jnp.sum(values, axis=0, keepdims=True)


class Swap:
    def __init__(self, me, size, device, row_for, landing, send_sems, recv_sems):
        self.me, self.size, self.device = me, size, device
        self.row_for, self.landing = row_for, landing
        self.send_sems, self.recv_sems = send_sems, recv_sems
        self.copies = []

    def start(self):
        for step in range(1, self.size):
            other = lax.rem(self.me + step, self.size)
            copy = pltpu.make_async_remote_copy(
                src_ref=self.row_for(other),
                dst_ref=self.landing.at[self.me],
                send_sem=self.send_sems.at[step],
                recv_sem=self.recv_sems.at[step],
                device_id=self.device(other),
                device_id_type=MESH_IDS,
            )
            copy.start()
            self.copies.append(copy)
        self.landing[self.me] = self.row_for(self.me)[...]

    def wait_arrivals(self):
        for copy in self.copies:
            copy.wait_recv()

    def wait_sends(self):
        for copy in self.copies:
            copy.wait_send()


class Gather:
    def __init__(self, rows, depth, where, shards, outs, own_sems, send_sems, recv_sems):
        self.rows, self.depth = rows, depth
        self.dp, self.z, self.core, self.others = where
        self.shards, self.outs = shards, outs
        self.own_sems, self.send_sems, self.recv_sems = own_sems, send_sems, recv_sems
        self.sibling = place(self.dp, self.z, 1 - self.core)
        self.sends = []
        self.keeps = []
        self.own = self.z * 2 + self.core
        self.lines = [(self.z ^ step) * 2 + self.core for step in range(depth)]
        self.units = [(part, turn) for part in range(3) for turn in range(depth)]

    def slot_of(self, part, line, row):
        return block_of(self.outs[part], line, row, self.shards[part].shape, part == 2)

    def half_of(self, ref, part, which):
        half = self.shards[part].shape[0] // 2
        return ref.at[pl.ds(which * half, half)]

    def send(self, part, line, row, target, which=None, own=False):
        destination = self.slot_of(part, line, row)
        source = self.shards[part] if own else destination
        if which is not None:
            source, destination = (
                self.half_of(source, part, which), self.half_of(destination, part, which))
        copy = pltpu.make_async_remote_copy(
            src_ref=source,
            dst_ref=destination,
            send_sem=self.send_sems.at[len(self.sends)],
            recv_sem=self.recv_sems.at[which or 0, part, line, row],
            device_id=target,
            device_id_type=MESH_IDS,
        )
        copy.start()
        self.sends.append(copy)

    def arrive(self, part, line, row, which=None):
        destination = self.slot_of(part, line, row)
        if which is not None:
            destination = self.half_of(destination, part, which)
        pltpu.make_async_remote_copy(
            src_ref=destination,
            dst_ref=destination,
            send_sem=self.send_sems.at[0],
            recv_sem=self.recv_sems.at[which or 0, part, line, row],
            device_id=self.sibling,
            device_id_type=MESH_IDS,
        ).wait_recv()

    def send_own(self, part):
        for other in self.others:
            self.send(part, self.own, self.dp, place(other, self.z, self.core), own=True)
        self.send(part, self.own, self.dp, self.sibling, own=True)
        keep = pltpu.make_async_copy(
            self.shards[part], self.slot_of(part, self.own, self.dp), self.own_sems.at[part])
        keep.start()
        self.keeps.append(keep)

    def send_deep(self, index):
        if index < len(self.units):
            part, step = self.units[index]
            if step:
                target = place(self.dp, self.z ^ step, self.core)
                self.send(part, self.own, self.dp, target, own=True)

    def turn(self, index):
        dp, z, core = self.dp, self.z, self.core
        count = len(self.units)
        self.send_deep(index + AHEAD)
        if index in (1, 2):
            self.send_own(index)
        if index < count:
            part, turn = self.units[index]
            line = self.lines[turn]
            if turn:
                self.arrive(part, line, dp)
                for other in self.others:
                    self.send(part, line, dp, place(other, z, core))
                self.send(part, line, dp, self.sibling)
        if LAG <= index < count + LAG:
            part, turn = self.units[index - LAG]
            line = self.lines[turn]
            for position, other in enumerate(self.others):
                self.arrive(part, line, other)
                self.send(
                    part, line, other, place(self.others[1 - position], z, core), which=position)
                self.send(part, line, other, self.sibling)
        if 2 * LAG <= index:
            part, turn = self.units[index - 2 * LAG]
            line = self.lines[turn]
            self.arrive(part, line, dp ^ 3, 0)
            self.arrive(part, line, dp ^ 3, 1)
            self.send(part, line, dp ^ 3, self.sibling)

    def finish_part(self, part):
        for line in self.lines:
            for row in range(self.rows):
                self.arrive(part, line + 1 - 2 * self.core, (self.dp + row) % self.rows)
        self.keeps[part].wait()

    def wait_sends(self):
        for copy in self.sends:
            copy.wait_send()


class Scatter:
    def __init__(self, rows, depth, where, shapes, grads, buffers, sems):
        self.rows, self.depth, self.shapes, self.grads = rows, depth, shapes, grads
        self.dp, self.z, self.core, self.others = where
        self.held, self.planes_in, self.crosses_in, self.alongs_in = (
            buffers[3 * kind : 3 * kind + 3] for kind in range(4))
        (
            self.pair_send, self.pair_recv, self.plane_send, self.plane_recv,
            self.cross_send, self.cross_recv, self.along_send, self.along_recv,
        ) = sems
        self.sibling = place(self.dp, self.z, 1 - self.core)
        self.targets = [self.dp ^ 3, self.dp ^ 1, self.dp ^ 2, self.dp]
        self.lines = [self.z ^ step for step in reversed(range(depth))]
        self.units = [(part, turn) for part in (2, 1, 0) for turn in range(depth)]
        self.pairs, self.planes, self.crosses, self.alongs = {}, {}, {}, {}

    def remote(self, source, destination, send_sem, recv_sem, target):
        copy = pltpu.make_async_remote_copy(
            src_ref=source, dst_ref=destination, send_sem=send_sem, recv_sem=recv_sem,
            device_id=target, device_id_type=MESH_IDS)
        copy.start()
        return copy

    def block(self, part, line, target):
        return block_of(self.grads[part], line, target, self.shapes[part], part == 2)

    def add(self, first, others_in, length, target):
        chunk = 48

        @pl.loop(0, length // chunk)
        def _(index):
            piece = pl.ds(pl.multiple_of(index * chunk, chunk), chunk)
            total = first[piece, :].astype(jnp.float32)
            for other in others_in:
                total = total + other[piece, :].astype(jnp.float32)
            target[piece, :] = total.astype(target.dtype)

    def start_pairs(self, part):
        for turn, line in enumerate(self.lines):
            for slot, target in enumerate(self.targets):
                key = (part, turn, slot)
                self.pairs[key] = self.remote(
                    self.block(part, line * 2 + 1 - self.core, target),
                    self.held[part].at[turn, slot], self.pair_send.at[key],
                    self.pair_recv.at[key], self.sibling)

    def wait_pairs_sent(self, part):
        for turn in range(self.depth):
            for slot in range(self.rows):
                self.pairs[part, turn, slot].wait_send()

    def turn(self, index):
        last = self.rows - 1
        count = len(self.units)
        if index < count:
            part, turn = self.units[index]
            height = self.shapes[part][0]
            half = height // 2
            for slot, target in enumerate(self.targets):
                self.pairs[part, turn, slot].wait_recv()
                here = self.held[part].at[turn, slot]
                own = self.block(part, self.lines[turn] * 2 + self.core, target)
                self.add(own, [here], height, here)
                if slot == 0:
                    for position in range(2):
                        key = (part, turn, position)
                        self.crosses[key] = self.remote(
                            self.held[part].at[turn, 0, pl.ds((1 - position) * half, half)],
                            self.crosses_in[part].at[turn, position],
                            self.cross_send.at[key], self.cross_recv.at[key],
                            place(self.others[position], self.z, self.core))
        if LAG <= index < count + LAG:
            part, turn = self.units[index - LAG]
            half = self.shapes[part][0] // 2
            for position in range(2):
                self.crosses[part, turn, 1 - position].wait_recv()
                piece = self.held[part].at[turn, 1 + position, pl.ds(position * half, half)]
                self.add(piece, [self.crosses_in[part].at[turn, 1 - position]], half, piece)
                key = (part, turn, position)
                self.planes[key] = self.remote(
                    self.held[part].at[turn, 1 + position], self.planes_in[part].at[turn, position],
                    self.plane_send.at[key], self.plane_recv.at[key],
                    place(self.others[position], self.z, self.core))
        if 2 * LAG <= index:
            part, turn = self.units[index - 2 * LAG]
            for position in range(2):
                self.planes[part, turn, position].wait_recv()
            here = self.held[part].at[turn, last]
            arrived = [self.planes_in[part].at[turn, position] for position in range(2)]
            self.add(here, arrived, self.shapes[part][0], here)
            if turn < self.depth - 1:
                key = (part, turn)
                self.alongs[key] = self.remote(
                    here, self.alongs_in[part].at[turn], self.along_send.at[key],
                    self.along_recv.at[key], place(self.dp, self.lines[turn], self.core))

    def finish_part(self, part):
        total = self.held[part][self.depth - 1, self.rows - 1].astype(jnp.float32)
        for turn in range(self.depth - 1):
            self.alongs[part, turn].wait_recv()
            total = total + self.alongs_in[part][turn].astype(jnp.float32)
        return total

    def wait_sends(self):
        for copies in (self.planes, self.crosses, self.alongs):
            for copy in copies.values():
                copy.wait_send()


def layer_kernel(rows, depth, *refs):
    shards = refs[:3]
    cond_rows, slope, ada_ref, ada_bias, bias_rows, latents, cotangent, live_ref = refs[3:11]
    (
        block_out, latent_grad, cond_grad, ada_grad, ada_bias_grad, qkv_grad, qv_bias_grad,
        proj_grad, proj_bias_grad, fc1_grad, fc1_bias_grad, fc2_grad, fc2_bias_grad,
    ) = refs[11:24]
    refs = refs[24:]
    weights, grads = refs[:3], (refs[3], refs[4], refs[3])
    scatter_buffers, scatter_sems = refs[5:17], refs[17:25]
    (
        own_sems, send_sems, recv_sems, swap_send, swap_recv,
        cond_across, cond_own, cond_along, cond_in, part_out, part_across, part_row, part_along,
        leaving, rows_along, rows_across, back_out, back_across, back_row, back_along,
        mod, qkv_bias, proj_bias, fc1_bias, fc2_bias, mod_grad, qkv_sums, proj_sums, fc1_sums,
        fc2_sums, inverse_one, inverse_two, normed_one, normed_two, middle, branch, wide,
        hidden_one, hidden_one_t, hidden_two, hidden_two_t, attended, attended_t,
        grad_mlp, grad_mlp_t, grad_attended, projected,
        grad_proj_mixed, activated, grad_pre, grad_natural, grad_state, probability,
    ) = refs[25:]
    grad_mixed = grad_pre
    mixed, fc1, fc2_turned = weights
    where = positions(rows, depth)
    dp = where[0]
    columns = 2 * depth
    column = lax.axis_index("fsdp")
    length = latents.shape[0]
    qkv_part, proj_part = 3 * D // columns, D // columns
    block = qkv_part + proj_part
    edge = qkv_part // 128 * 128
    rest = block - edge
    lead = qkv_part - edge
    scale_factor = HEAD ** (-0.5)
    ada_rows, mod_width = ada_ref.shape
    mod_pad = round_up(mod_width)
    barrier = pltpu.get_barrier_semaphore()
    partners = [(lax.rem(dp + step, rows), column) for step in range(1, rows)]
    partners += [(dp, lax.rem(column + step, columns)) for step in range(1, columns)]
    for partner in partners:
        pl.semaphore_signal(barrier, inc=1, device_id=partner, device_id_type=MESH_IDS)
    pl.semaphore_wait(barrier, len(partners))
    gather = Gather(rows, depth, where, shards, weights, own_sems, send_sems, recv_sems)
    scatter = Scatter(
        rows, depth, where, [shard.shape for shard in shards], grads, scatter_buffers, scatter_sems)
    swaps = []

    def swap_across(row_for, landing):
        at = len(swaps)
        swaps.append(Swap(
            dp, rows, lambda other: (other, column), row_for, landing,
            swap_send.at[at], swap_recv.at[at]))
        return swaps[-1]

    def swap_along(row_for, landing):
        at = len(swaps)
        swaps.append(Swap(
            column, columns, lambda other: (dp, other), row_for, landing,
            swap_send.at[at], swap_recv.at[at]))
        return swaps[-1]

    cond_first = swap_across(
        lambda other: cond_rows.at[other], cond_across)
    cond_second = swap_along(lambda other: cond_own, cond_along)
    part_first = swap_across(lambda other: part_out.at[other], part_across)
    part_second = swap_along(lambda other: part_row.at[other], part_along)
    rows_first = swap_along(lambda other: leaving.at[other], rows_along)
    rows_second = swap_across(lambda other: rows_along, rows_across)
    back_first = swap_across(lambda other: back_out.at[other], back_across)
    back_second = swap_along(lambda other: back_row.at[other], back_along)
    cond_first.start()
    for index in range(AHEAD):
        gather.send_deep(index)
    gather.send_own(0)

    def piece(kind):
        return mod[:, kind * D : (kind + 1) * D]

    def share_condition():
        cond_first.wait_arrivals()
        cond_own[:rows] = cond_across[...]
        cond_own[rows:] = bias_rows[...]
        cond_second.start()

    def start_modulation():
        cond_second.wait_arrivals()
        cond_in[...] = jnp.concatenate(
            [cond_along[source, row] for row in range(rows) for source in range(columns)], axis=0)
        part = dot_plain(cond_in[:, :ada_rows].astype(bfloat), ada_ref[...])
        part = part + jnp.where(dp == 0, ada_bias[...], 0.0)
        for row in range(rows):
            part_out[row, :, :mod_width] = part[row * columns : (row + 1) * columns]
        part_first.start()

    def sum_modulation():
        part_first.wait_arrivals()
        total = part_across[0]
        for row in range(1, rows):
            total = total + part_across[row]
        part_row[:, 0, :] = total
        part_second.start()

    def normalize_first():
        normed, inverse = normalize_rows(latents[...].astype(jnp.float32))
        normed_one[...] = normed
        inverse_one[...] = inverse

    def finish_modulation():
        part_second.wait_arrivals()
        mod[...] = jnp.concatenate(
            [part_along[source][:, :mod_width] for source in range(columns)], axis=1)
        bias_parts = [
            jnp.concatenate(
                [cond_along[source, row] for row in range(rows, cond_along.shape[1])], axis=1)
            for source in range(columns)]
        low = 0
        naturals = []
        for width in (2 * D // columns, D // columns, FF // columns, D // columns):
            naturals.append(jnp.concatenate(
                [part[:, low : low + width] for part in bias_parts], axis=1))
            low += width
        qkv_bias[:, :D] = naturals[0][:, :D]
        qkv_bias[:, D : 2 * D] = jnp.zeros((1, D), jnp.float32)
        qkv_bias[:, 2 * D :] = naturals[0][:, D:]
        proj_bias[...] = naturals[1]
        fc1_bias[...] = naturals[2]
        fc2_bias[...] = naturals[3]
        hidden = (normed_one[...] * (1.0 + piece(1)) + piece(0)).astype(bfloat)
        hidden_one[...] = hidden
        hidden_one_t[...] = hidden.T

    def start_gradient():
        grad = (piece(5) * (live_ref[...] * cotangent[...].astype(jnp.float32))).astype(bfloat)
        grad_mlp[...] = grad
        grad_mlp_t[...] = grad.T
        fc2_sums[...] = columns_sum(grad.astype(jnp.float32))

    def span(index, width):
        return pl.ds(pl.multiple_of(index * width, width), width)

    def project():
        @pl.loop(0, columns)
        def _(index):
            wide[:, span(index, block)] = dot_plain(hidden_one[...], mixed[:, span(index, block)])

        for index in range(columns):
            natural = slice(index * qkv_part, (index + 1) * qkv_part)
            projected[:, natural] = (
                wide[:, index * block : index * block + qkv_part] + qkv_bias[:, natural]
            ).astype(bfloat)

    def head_slabs(source, pair):
        return [
            source[:, pl.ds(pl.multiple_of(kind * D + pair * 128, 128), 128)] for kind in range(3)]

    def own_lanes(which):
        lane = lax.broadcasted_iota(jnp.int32, (length, 128), 1)
        return lane < HEAD if which == 0 else lane >= HEAD

    def attend(low, high):
        @pl.loop(low, high)
        def _(pair):
            queries, keys, values = head_slabs(projected, pair)
            zero = jnp.zeros_like(queries)
            results = []
            for which in range(2):
                scores = against_weight(
                    jnp.where(own_lanes(which), queries, zero), keys) * scale_factor
                shifted = jnp.exp(scores - jnp.max(scores, axis=-1, keepdims=True))
                exact = shifted / jnp.sum(shifted, axis=-1, keepdims=True)
                probability[2 * pair + which] = exact
                results.append(dot_plain(exact.astype(bfloat), values))
            attended[:, span(pair, 128)] = jnp.where(
                own_lanes(0), results[0], results[1]).astype(bfloat)

    def finish_attention():
        attended_t[...] = attended[...].T

        @pl.loop(0, columns)
        def _(index):
            tail = pl.ds(pl.multiple_of(index * block + edge, 128), rest)
            wide[:, span(index, rest)] = dot_plain(attended[...], mixed[:, tail])

        for index in range(columns):
            natural = slice(index * proj_part, (index + 1) * proj_part)
            branch[:, natural] = (
                wide[:, index * rest + lead : (index + 1) * rest] + proj_bias[:, natural])
        total = latents[...].astype(jnp.float32) + piece(2) * branch[...]
        middle[...] = total
        normed, inverse = normalize_rows(total)
        normed_two[...] = normed
        inverse_two[...] = inverse
        hidden = (normed * (1.0 + piece(4)) + piece(3)).astype(bfloat)
        hidden_two[...] = hidden
        hidden_two_t[...] = hidden.T

    chunk = 384
    chunks = FF // chunk

    def expand(low, high):
        @pl.loop(low, high)
        def _(index):
            part = span(index, chunk)
            value = dot_plain(hidden_two[...], fc1[:, part]) + fc1_bias[:, part]
            root = 0.7978845608028654
            square = value * value
            bend = jnp.tanh(root * (value + 0.044715 * (square * value)))
            activated[:, part] = (0.5 * value * (1.0 + bend)).astype(bfloat)
            wide[:, part] = 0.5 * (1.0 + bend) + 0.5 * value * (1.0 - bend * bend) * (
                root * (1.0 + 3 * 0.044715 * square))

    def fc2_weight_grad(low, high):
        @pl.loop(low, high)
        def _(index):
            part = span(index, chunk)
            grads[2][:, part] = dot_plain(grad_mlp_t[...], activated[:, part]).astype(bfloat)

    def after_part_zero():
        gather.finish_part(0)
        project()

    def after_part_one():
        gather.finish_part(1)
        expand(0, 4)

    def send_fc2_grad():
        fc2_weight_grad(4, 8)
        scatter.start_pairs(2)

    hooks = [
        share_condition, normalize_first, start_modulation, None, sum_modulation, None,
        finish_modulation, start_gradient, after_part_zero, lambda: attend(0, 3),
        lambda: attend(3, 6), finish_attention, after_part_one, lambda: expand(4, 8),
        lambda: fc2_weight_grad(0, 4), send_fc2_grad,
    ]
    for index, hook in enumerate(hooks):
        gather.turn(index)
        if hook is not None:
            hook()
    scatter.turn(0)
    gather.finish_part(2)
    third = 256

    def finish_forward():
        @pl.loop(0, D // third)
        def _(index):
            part = span(index, third)
            branch_part = against_weight(activated[...], fc2_turned[part, :]) + fc2_bias[:, part]
            live_grad = live_ref[:, part] * cotangent[:, part].astype(jnp.float32)
            last = pl.ds(pl.multiple_of(5 * D + index * third, third), third)
            block_out[:, part] = (
                live_ref[:, part] * (middle[:, part] + mod[:, last] * branch_part)).astype(bfloat)
            mod_grad[:, last] = columns_sum(live_grad * branch_part)

    def fc1_weight_grad(low, high):
        @pl.loop(low, high)
        def _(index):
            part = span(index, chunk)
            grad = (dot_plain(grad_mlp[...], fc2_turned[:, part]) * wide[:, part]).astype(bfloat)
            grad_pre[:, part] = grad
            fc1_sums[:, part] = columns_sum(grad.astype(jnp.float32))
            grads[1][:, part] = dot_plain(hidden_two_t[...], grad).astype(bfloat)

    def hidden_two_back():
        @pl.loop(0, D // third)
        def _(index):
            part = span(index, third)
            grad_state[:, part] = against_weight(grad_pre[...], fc1[part, :])

    def middle_back():
        grad_hidden = grad_state[...]
        mod_grad[:, 3 * D : 4 * D] = columns_sum(grad_hidden)
        mod_grad[:, 4 * D : 5 * D] = columns_sum(grad_hidden * normed_two[...])
        grad_middle = live_ref[...] * cotangent[...].astype(jnp.float32) + norm_backward(
            grad_hidden * (1.0 + piece(4)), normed_two[...], inverse_two[...])
        mod_grad[:, 2 * D : 3 * D] = columns_sum(grad_middle * branch[...])
        grad_state[...] = grad_middle
        grad_branch = (piece(2) * grad_middle).astype(bfloat)
        proj_sums[...] = columns_sum(grad_branch.astype(jnp.float32))
        for index in range(columns):
            grad_proj_mixed[:, index * rest : index * rest + lead] = jnp.zeros(
                (length, lead), bfloat)
            grad_proj_mixed[:, index * rest + lead : (index + 1) * rest] = (
                grad_branch[:, index * proj_part : (index + 1) * proj_part])
        total = None
        for index in range(columns):
            term = against_weight(
                grad_proj_mixed[:, index * rest : (index + 1) * rest],
                mixed[:, index * block + edge : (index + 1) * block])
            total = term if total is None else total + term
        grad_attended[...] = total.astype(bfloat)

    def attend_back(low, high):
        @pl.loop(low, high)
        def _(pair):
            queries, keys, values = head_slabs(projected, pair)
            grad_out = grad_attended[:, span(pair, 128)]
            zero = jnp.zeros_like(grad_out)
            results = []
            for which in range(2):
                exact = probability[2 * pair + which]
                grad_prob = against_weight(jnp.where(own_lanes(which), grad_out, zero), values)
                inner = jnp.sum(exact * grad_prob, axis=-1, keepdims=True)
                grad_scores = (exact * (grad_prob - inner)).astype(bfloat)
                results.append((
                    dot_plain(grad_scores, keys) * scale_factor,
                    contract_rows(grad_scores, queries) * scale_factor,
                    contract_rows(exact.astype(bfloat), grad_out)))
            for kind in range(3):
                grad_natural[:, pl.ds(pl.multiple_of(kind * D + pair * 128, 128), 128)] = jnp.where(
                    own_lanes(0), results[0][kind], results[1][kind]).astype(bfloat)

    def mixed_weight_grad():
        qkv_sums[...] = columns_sum(grad_natural[...].astype(jnp.float32))
        for index in range(columns):
            grad_mixed[:, index * block : index * block + qkv_part] = (
                grad_natural[:, index * qkv_part : (index + 1) * qkv_part])
            grad_mixed[:, index * block + qkv_part : (index + 1) * block] = jnp.zeros(
                (length, proj_part), bfloat)
        scatter.wait_pairs_sent(2)

        @pl.loop(0, columns)
        def _(index):
            low = pl.multiple_of(index * block, 128)
            grads[0][:, pl.ds(low, edge)] = dot_plain(
                hidden_one_t[...], grad_mixed[:, pl.ds(low, edge)]).astype(bfloat)
            tail = pl.ds(pl.multiple_of(index * block + edge, 128), rest)
            grads[0][:, tail] = (
                dot_plain(hidden_one_t[...], grad_mixed[:, tail])
                + dot_plain(attended_t[...], grad_proj_mixed[:, span(index, rest)])).astype(bfloat)

    def finish_backward():
        @pl.loop(0, D // third)
        def _(index):
            part = span(index, third)
            branch[:, part] = against_weight(grad_mixed[...], mixed[part, :])

        grad_hidden = branch[...]
        mod_grad[:, :D] = columns_sum(grad_hidden)
        mod_grad[:, D : 2 * D] = columns_sum(grad_hidden * normed_one[...])
        latent_grad[...] = (grad_state[...] + norm_backward(
            grad_hidden * (1.0 + piece(1)), normed_one[...], inverse_one[...])).astype(bfloat)
        pad = jnp.zeros((1, mod_pad - mod_width), jnp.float32)
        qv_sums = jnp.concatenate([qkv_sums[:, :D], qkv_sums[:, 2 * D :]], axis=1)
        rows_of = (qv_sums, proj_sums[...], fc1_sums[...], fc2_sums[...])
        every = mod_grad[...]
        for index in range(columns):
            pieces = [every[:, index * mod_width : (index + 1) * mod_width], pad]
            for row in rows_of:
                share = row.shape[1] // columns
                pieces.append(row[:, index * share : (index + 1) * share])
            leaving[index] = jnp.concatenate(pieces, axis=1)
        rows_first.start()

    def share_rows():
        rows_first.wait_arrivals()
        rows_second.start()

    def own_sums():
        rows_second.wait_arrivals()
        arrived = jnp.concatenate([rows_across[row, :, 0, :] for row in range(rows)], axis=0)
        sums = columns_sum(arrived)
        ada_bias_grad[...] = sums[:, :mod_width]
        low = mod_pad
        for out in (qv_bias_grad, proj_bias_grad, fc1_bias_grad, fc2_bias_grad):
            out[...] = sums[:, low : low + out.shape[1]]
            low += out.shape[1]
        ada_grad[...] = contract_exact(cond_in[:, :ada_rows], arrived[:, :mod_width])
        back = lax.dot_general(
            arrived[:, :mod_width], ada_ref[...].astype(jnp.float32), (((1,), (1,)), ((), ())),
            precision=highest)
        for row in range(rows):
            back_out[row, :, :ada_rows] = back[row * columns : (row + 1) * columns]
        back_first.start()

    def share_back():
        back_first.wait_arrivals()
        for row in range(rows):
            back_row[:, row, 0, :] = back_across[row]
        back_second.start()

    def finish_condition():
        back_second.wait_arrivals()
        total = back_along[0]
        for source in range(1, columns):
            total = total + back_along[source]
        cond_grad[...] = jnp.concatenate(
            [total[row][:, :ada_rows] for row in range(rows)], axis=1) * slope[...]

    def finish_fc2():
        fc2_grad[...] = scatter.finish_part(2).T

    def finish_fc1():
        fc1_grad[...] = scatter.finish_part(1)

    def send_fc1_grad():
        fc1_weight_grad(4, 8)
        scatter.start_pairs(1)

    def send_mixed_grad():
        mixed_weight_grad()
        scatter.start_pairs(0)

    hooks = [
        lambda: fc1_weight_grad(0, 4), send_fc1_grad, hidden_two_back, middle_back,
        lambda: attend_back(0, 3), lambda: attend_back(3, 6), send_mixed_grad,
        finish_forward, finish_backward, finish_fc2, share_rows, own_sums, finish_fc1,
        share_back, finish_condition,
    ]
    for index, hook in enumerate(hooks):
        hook()
        scatter.turn(index + 1)
    total = scatter.finish_part(0)
    qkv_grad[...] = total[:, :qkv_part]
    proj_grad[...] = total[:, qkv_part:]
    scatter.wait_pairs_sent(1)
    scatter.wait_pairs_sent(0)
    scatter.wait_sends()
    gather.wait_sends()
    for swap in swaps:
        swap.wait_sends()


def run_layer(shards, cond_rows, slope, ada_weight, ada_bias, bias_row, latents, cotangent, live,
              widths, rows, columns):
    depth = columns // 2
    cond_pad = cond_rows.shape[-1]
    group = rows + bias_row.shape[-1] // cond_pad
    count = (depth - 1) + depth * rows + depth * (rows - 1) + 2 * depth
    total = rows * columns
    ada_rows, mod_width = ada_weight.shape
    mod_pad = round_up(mod_width)
    bias_rows = bias_row.reshape(-1, 1, cond_rows.shape[-1])
    bias_width = bias_row.shape[-1]
    length = latents.shape[0]
    vmem = pl.BlockSpec(memory_space=pltpu.VMEM)
    anywhere = pl.BlockSpec(memory_space=pl.ANY)
    dma = pltpu.SemaphoreType.DMA
    shapes = [
        whole_shape(shard.shape, part == 2, rows, columns) for part, shard in enumerate(shards)]
    row_buffer = lambda count, width: pltpu.VMEM((count, 1, width), jnp.float32)
    wide_row = lambda width: pltpu.VMEM((1, width), jnp.float32)
    single = lambda width: pltpu.VMEM((length, width), jnp.float32)
    half = lambda width: pltpu.VMEM((length, width), bfloat)
    turned = pltpu.VMEM((D, length), bfloat)
    rest = 128 * columns
    buffers = []
    for lead in ((depth, rows), (depth, 2), (depth, 2), (depth - 1,)):
        for shard in shards:
            height, width = shard.shape
            height = height // 2 if 6 <= len(buffers) < 9 else height
            buffers.append(pltpu.VMEM(lead + (height, width), bfloat))
    float_out = lambda *shape: jax.ShapeDtypeStruct(shape, jnp.float32)
    qkv_part, proj_part = 3 * D // columns, D // columns
    height = shards[0].shape[0]
    return pl.pallas_call(
        functools.partial(layer_kernel, rows, depth),
        out_shape=[
            jax.ShapeDtypeStruct((length, D), bfloat),
            jax.ShapeDtypeStruct((length, D), bfloat),
            float_out(1, D),
            float_out(ada_rows, mod_width), float_out(1, mod_width),
            float_out(height, qkv_part), float_out(1, widths[0]),
            float_out(height, proj_part), float_out(1, widths[1]),
            float_out(*shards[1].shape), float_out(1, widths[2]),
            float_out(*shards[2].shape[::-1]), float_out(1, widths[3]),
        ],
        in_specs=[anywhere] * 3 + [vmem] * 8,
        out_specs=[vmem] * 13,
        scratch_shapes=[pltpu.VMEM(shape, bfloat) for shape in shapes + shapes[:2]]
        + buffers + [
            dma((3, depth, rows)), dma((3, depth, rows)),
            dma((3, depth, 2)), dma((3, depth, 2)), dma((3, depth, 2)), dma((3, depth, 2)),
            dma((3, depth - 1)), dma((3, depth - 1)),
            dma((3,)), dma((3 * count,)), dma((2, 3, columns, rows)),
            dma((8, columns)), dma((8, columns)),
            row_buffer(rows, cond_pad), row_buffer(group, cond_pad),
            pltpu.VMEM((columns, group, 1, cond_pad), jnp.float32),
            pltpu.VMEM((total, cond_pad), jnp.float32),
            pltpu.VMEM((rows, columns, mod_pad), jnp.float32),
            pltpu.VMEM((rows, columns, mod_pad), jnp.float32),
            row_buffer(columns, mod_pad), row_buffer(columns, mod_pad),
            row_buffer(columns, mod_pad + bias_width), row_buffer(columns, mod_pad + bias_width),
            pltpu.VMEM((rows, columns, 1, mod_pad + bias_width), jnp.float32),
            pltpu.VMEM((rows, columns, cond_pad), jnp.float32),
            pltpu.VMEM((rows, columns, cond_pad), jnp.float32),
            pltpu.VMEM((columns, rows, 1, cond_pad), jnp.float32),
            pltpu.VMEM((columns, rows, 1, cond_pad), jnp.float32),
            wide_row(6 * D), wide_row(3 * D), wide_row(D), wide_row(FF), wide_row(D),
            wide_row(6 * D), wide_row(3 * D), wide_row(D), wide_row(FF), wide_row(D),
            single(1), single(1), single(D), single(D), single(D), single(D), single(FF),
            half(D), turned, half(D), turned, half(D), turned,
            half(D), turned, half(D), half(3 * D),
            half(rest), half(FF), half(FF), half(3 * D), single(D), pltpu.VMEM((HEADS, length, length), jnp.float32),
        ],
        compiler_params=pltpu.CompilerParams(
            collective_id=2, has_side_effects=True, vmem_limit_bytes=62 * 2**20),
        name="run_layer",
    )(*shards, cond_rows, slope, ada_weight, ada_bias, bias_rows, latents, cotangent, live)


def pick(mixed, columns, kind):
    width = mixed.shape[1] // columns
    edge = 3 * width // 4
    low, high = (0, edge) if kind == 0 else (edge, width)
    return jnp.concatenate(
        [mixed[:, block * width + low : block * width + high] for block in range(columns)], axis=1
    )


def spread(rows_in, columns, kind):
    width = rows_in.shape[1] // columns
    rest = width // 3 if kind == 0 else 3 * width
    zeros = jnp.zeros((rows_in.shape[0], rest), rows_in.dtype)
    pieces = []
    for block in range(columns):
        piece = rows_in[:, block * width : (block + 1) * width]
        pieces += [piece, zeros] if kind == 0 else [zeros, piece]
    return jnp.concatenate(pieces, axis=1)


def layer(latent_rows, live, cot_rows, modulation, weights, biases, columns):
    mixed_weight, fc1_weight, fc2_turned = weights
    qv_bias, proj_bias, fc1_bias, fc2_bias = biases
    length = latent_rows.shape[0]
    rows_wide = latent_rows.astype(jnp.float32)
    shift_one, scale_one, gate_one, shift_two, scale_two, gate_two = jnp.split(
        modulation, 6, axis=-1
    )
    normed_one, inverse_one = normalize_rows(rows_wide)
    hidden_one = (normed_one * (1.0 + scale_one) + shift_one).astype(bfloat)
    qkv_bias = jnp.concatenate([qv_bias[:D], jnp.zeros((D,), jnp.float32), qv_bias[D:]])
    projected = (
        pick(jnp.dot(hidden_one, mixed_weight, preferred_element_type=jnp.float32), columns, 0)
        + qkv_bias
    ).astype(bfloat)
    queries = projected[:, :D].reshape(length, HEADS, HEAD)
    key_rows = projected[:, D : 2 * D].reshape(length, HEADS, HEAD)
    values = projected[:, 2 * D :].reshape(length, HEADS, HEAD)
    scale_factor = HEAD ** (-0.5)
    scores = (
        jnp.einsum("qhe,khe->hqk", queries, key_rows, preferred_element_type=jnp.float32)
        * scale_factor
    )
    row_max = jnp.max(scores, axis=-1, keepdims=True)
    shifted = jnp.exp(scores - row_max)
    row_total = jnp.sum(shifted, axis=-1, keepdims=True)
    exact_probability = shifted / row_total
    probability = exact_probability.astype(bfloat)
    attended = jnp.einsum("hqk,khe->qhe", probability, values, preferred_element_type=jnp.float32)
    attended = attended.reshape(length, D).astype(bfloat)
    branch = pick(jnp.dot(attended, mixed_weight, preferred_element_type=jnp.float32), columns, 1)
    branch = branch + proj_bias
    middle = rows_wide + gate_one * branch
    normed_two, inverse_two = normalize_rows(middle)
    hidden_two = (normed_two * (1.0 + scale_two) + shift_two).astype(bfloat)
    pre_gelu = jnp.dot(hidden_two, fc1_weight, preferred_element_type=jnp.float32) + fc1_bias
    activated, gelu_pull = jax.vjp(
        lambda argument: jax.nn.gelu(argument, approximate=True), pre_gelu
    )
    activated = activated.astype(bfloat)
    mlp_out = against_weight(activated, fc2_turned) + fc2_bias
    block_out = (live * (middle + gate_two * mlp_out)).astype(bfloat)

    grad_out = live * cot_rows.astype(jnp.float32)
    gate_two_grad = jnp.sum(grad_out * mlp_out, axis=0, keepdims=True)
    grad_mlp = (gate_two * grad_out).astype(bfloat)
    fc2_bias_grad = jnp.sum(grad_mlp.astype(jnp.float32), axis=0)
    grad_act = jnp.dot(grad_mlp, fc2_turned, preferred_element_type=jnp.float32)
    grad_pre = gelu_pull(grad_act)[0].astype(bfloat)
    fc1_bias_grad = jnp.sum(grad_pre.astype(jnp.float32), axis=0)
    grad_hidden_two = against_weight(grad_pre, fc1_weight)
    shift_two_grad = jnp.sum(grad_hidden_two, axis=0, keepdims=True)
    scale_two_grad = jnp.sum(grad_hidden_two * normed_two, axis=0, keepdims=True)
    grad_middle = grad_out + norm_backward(
        grad_hidden_two * (1.0 + scale_two), normed_two, inverse_two
    )
    gate_one_grad = jnp.sum(grad_middle * branch, axis=0, keepdims=True)
    grad_branch = (gate_one * grad_middle).astype(bfloat)
    proj_bias_grad = jnp.sum(grad_branch.astype(jnp.float32), axis=0)
    spread_branch = spread(grad_branch, columns, 1)
    grad_attended = (
        against_weight(spread_branch, mixed_weight).astype(bfloat).reshape(length, HEADS, HEAD)
    )
    grad_prob = jnp.einsum(
        "qhe,khe->hqk", grad_attended, values, preferred_element_type=jnp.float32
    )
    inner_sum = jnp.sum(exact_probability * grad_prob, axis=-1, keepdims=True)
    grad_scores = (exact_probability * (grad_prob - inner_sum)).astype(bfloat)
    grad_queries = (
        jnp.einsum("hqk,khe->qhe", grad_scores, key_rows, preferred_element_type=jnp.float32)
        * scale_factor
    )
    grad_keys = (
        jnp.einsum("hqk,qhe->khe", grad_scores, queries, preferred_element_type=jnp.float32)
        * scale_factor
    )
    grad_values = jnp.einsum(
        "hqk,qhe->khe", probability, grad_attended, preferred_element_type=jnp.float32
    )
    grad_projected = jnp.concatenate(
        [
            grad_queries.reshape(length, D),
            grad_keys.reshape(length, D),
            grad_values.reshape(length, D),
        ],
        axis=1,
    ).astype(bfloat)
    summed = jnp.sum(grad_projected.astype(jnp.float32), axis=0)
    qv_bias_grad = jnp.concatenate([summed[:D], summed[2 * D :]])
    spread_projected = spread(grad_projected, columns, 0)
    grad_hidden_one = against_weight(spread_projected, mixed_weight)
    shift_one_grad = jnp.sum(grad_hidden_one, axis=0, keepdims=True)
    scale_one_grad = jnp.sum(grad_hidden_one * normed_one, axis=0, keepdims=True)
    latent_grad = (
        grad_middle + norm_backward(grad_hidden_one * (1.0 + scale_one), normed_one, inverse_one)
    ).astype(bfloat)
    mod_grad = jnp.concatenate(
        [
            shift_one_grad,
            scale_one_grad,
            gate_one_grad,
            shift_two_grad,
            scale_two_grad,
            gate_two_grad,
        ],
        axis=-1,
    )
    weight_grads = (
        contract_rows(
            jnp.concatenate([hidden_one, attended]),
            jnp.concatenate([spread_projected, spread_branch]),
        ).astype(bfloat),
        contract_rows(hidden_two, grad_pre).astype(bfloat),
        contract_rows(grad_mlp, activated).astype(bfloat),
    )
    bias_grads = (qv_bias_grad, proj_bias_grad, fc1_bias_grad, fc2_bias_grad)
    return block_out, latent_grad, mod_grad, weight_grads, bias_grads


def flatten_blocks(blocks, turned):
    if blocks.ndim == 2:
        return blocks
    columns, rows, height, width = blocks.shape
    if turned:
        return blocks.transpose(0, 2, 1, 3).reshape(columns * height, rows * width)
    return blocks.transpose(1, 2, 0, 3).reshape(rows * height, columns * width)


def cut_blocks(whole, shape, turned, rows, columns):
    if len(whole_shape(shape, turned, rows, columns)) == 2:
        return whole
    height, width = shape
    if turned:
        return whole.reshape(columns, height, rows, width).transpose(0, 2, 1, 3)
    return whole.reshape(rows, height, columns, width).transpose(2, 0, 1, 3)


def per_device(
    latents,
    conditioning,
    cotangent,
    latent_count,
    ada_weight,
    ada_bias,
    qkv_weight,
    qv_bias,
    proj_weight,
    proj_bias,
    fc1_weight,
    fc1_bias,
    fc2_weight,
    fc2_bias,
):
    rows, columns = lax.axis_size("dp"), lax.axis_size("fsdp")
    live = latent_count[0].astype(jnp.float32)
    depth = ada_weight.shape[0]
    mod_width = ada_weight.shape[1]
    mod_pad = round_up(mod_width)
    own_biases = (qv_bias, proj_bias, fc1_bias, fc2_bias)
    widths = [bias.shape[0] for bias in own_biases]
    cuts = [sum(widths[:place]) for place in range(len(widths))]

    def split_cond(row):
        pad = round_up(depth) - depth
        return jnp.pad(row.reshape(rows, 1, depth), ((0, 0), (0, 0), (0, pad)))

    cond_row = conditioning.astype(jnp.float32)
    cond_act, silu_pull = jax.vjp(jax.nn.silu, cond_row)
    slope = silu_pull(jnp.ones_like(cond_row))[0]
    cond_rows = split_cond(cond_act.astype(bfloat).astype(jnp.float32))
    bias_row = jnp.concatenate(own_biases).astype(jnp.float32).reshape(1, -1)

    qkv_width = qkv_weight.shape[1]
    shards = (
        jnp.concatenate([qkv_weight, proj_weight], axis=1),
        fc1_weight,
        fc2_weight.T,
    )
    shapes = [shard.shape for shard in shards]
    ada_row = ada_bias.astype(jnp.float32).reshape(1, -1)
    fused = rows == 4 and columns == 8
    if fused:
        block_out, latent_grad, *param_grads = run_layer(
            shards, cond_rows, slope, ada_weight, ada_row, bias_row, latents[0], cotangent[0],
            jnp.full((1, D), live), widths, rows, columns)
        param_grads = [
            grad.reshape(-1) if 0 < place < 11 and place % 2 == 0 else grad
            for place, grad in enumerate(param_grads)]
        return (block_out[None], latent_grad[None], *param_grads)
    *blocks, mod_blocks, bias_blocks, cond_in = gather_shards(
        shards, cond_rows, ada_weight, ada_row, bias_row,
        rows, columns)
    modulation = mod_blocks[:, :, :mod_width].reshape(1, -1)
    biases = tuple(
        bias_blocks[:, :, cut : cut + width].reshape(-1) for cut, width in zip(cuts, widths)
    )
    weights = [flatten_blocks(block, part == 2) for part, block in enumerate(blocks)]
    block_out, latent_grad, mod_grad, weight_grads, bias_grads = layer(
        latents[0], live, cotangent[0], modulation, weights, biases, columns
    )
    grads = [
        cut_blocks(grad, shapes[part], part == 2, rows, columns)
        for part, grad in enumerate(weight_grads)
    ]
    leaving = jnp.concatenate(
        [jnp.pad(mod_grad.reshape(columns, -1), ((0, 0), (0, mod_pad - mod_width)))]
        + [grad.reshape(columns, -1) for grad in bias_grads], axis=1
    ).reshape(columns, 1, -1)
    mixed_grad, fc1_grad, fc2_turned_grad, ada_grad, sums, cond_grad = scatter_shards(
        grads, leaving, cond_in, ada_weight, split_cond(slope), shapes, rows, columns)
    qkv_grad, proj_grad = mixed_grad[:, :qkv_width], mixed_grad[:, qkv_width:]
    fc2_grad = fc2_turned_grad.T
    ada_bias_grad = sums[0, :mod_width]
    bias_sums = [
        sums[0, mod_pad + cut : mod_pad + cut + width] for cut, width in zip(cuts, widths)]
    cond_grad = cond_grad[:, :, :depth].reshape(1, -1)
    return (
        block_out[None],
        latent_grad[None],
        cond_grad,
        ada_grad,
        ada_bias_grad,
        qkv_grad,
        bias_sums[0],
        proj_grad,
        bias_sums[1],
        fc1_grad,
        bias_sums[2],
        fc2_grad,
        bias_sums[3],
    )


def solution(mesh):
    in_specs = (
        P(("dp", "fsdp"), None, None),
        P(("dp", "fsdp"), None),
        P(("dp", "fsdp"), None, None),
        P(("dp", "fsdp")),
        P("dp", "fsdp"),
        P("fsdp"),
        P("dp", "fsdp"),
        P("fsdp"),
        P("dp", "fsdp"),
        P("fsdp"),
        P("dp", "fsdp"),
        P("fsdp"),
        P("dp", "fsdp"),
        P("fsdp"),
    )
    out_specs = (
        P(("dp", "fsdp"), None, None),
        P(("dp", "fsdp"), None, None),
        P(("dp", "fsdp"), None),
        P("dp", "fsdp"),
        P("fsdp"),
        P("dp", "fsdp"),
        P("fsdp"),
        P("dp", "fsdp"),
        P("fsdp"),
        P("dp", "fsdp"),
        P("fsdp"),
        P("dp", "fsdp"),
        P("fsdp"),
    )
    return jax.shard_map(
        per_device, mesh=mesh, in_specs=in_specs, out_specs=out_specs, check_vma=False
    )
```

```python
import functools
import jax
import jax.numpy as jnp
from jax import lax
from jax.sharding import PartitionSpec as P
from jax.experimental import pallas as pl
from jax.experimental.pallas import tpu as pltpu

MESH_IDS = pl.DeviceIdType.MESH
D = 768
HEADS = 12
HEAD = 64
FF = 3072

highest = lax.Precision.HIGHEST
bfloat = jnp.bfloat16
LAG = 2
AHEAD = 3


def place(dp_index, z_index, core):
    return (dp_index, z_index * 2 + core)


def z_order(size):
    steps = [0]
    for distance in range(1, size // 2 + 1):
        steps.append(distance)
        if size - distance != distance:
            steps.append(size - distance)
    return steps


def device_of(index, columns):
    return (index // columns, lax.rem(index, columns))


def enter_barrier(me, rows, columns):
    barrier = pltpu.get_barrier_semaphore()
    count = rows * columns

    @pl.loop(1, count)
    def _(step):
        target = device_of(lax.rem(me + step, count), columns)
        pl.semaphore_signal(barrier, inc=1, device_id=target, device_id_type=MESH_IDS)

    pl.semaphore_wait(barrier, count - 1)


class Exchange:
    def __init__(self, me, rows, columns, row_for, landing, send_sems, recv_sems):
        self.me, self.columns, self.count = me, columns, rows * columns
        self.row_for, self.landing = row_for, landing
        self.send_sems, self.recv_sems = send_sems, recv_sems

    def start(self):
        @pl.loop(1, self.count)
        def _(step):
            target = lax.rem(self.me + step, self.count)
            pltpu.make_async_remote_copy(
                src_ref=self.row_for(target),
                dst_ref=self.landing.at[self.me],
                send_sem=self.send_sems.at[target],
                recv_sem=self.recv_sems.at[self.me],
                device_id=device_of(target, self.columns),
                device_id_type=MESH_IDS,
            ).start()

        self.landing[self.me] = self.row_for(self.me)[...]

    def pair(self, other):
        return pltpu.make_async_remote_copy(
            src_ref=self.row_for(other),
            dst_ref=self.landing.at[other],
            send_sem=self.send_sems.at[other],
            recv_sem=self.recv_sems.at[other],
            device_id=device_of(other, self.columns),
            device_id_type=MESH_IDS,
        )

    def wait_arrivals(self):
        @pl.loop(1, self.count)
        def _(step):
            self.pair(lax.rem(self.me + step, self.count)).wait_recv()

    def wait_sends(self):
        @pl.loop(1, self.count)
        def _(step):
            self.pair(lax.rem(self.me + step, self.count)).wait_send()


def positions(rows, depth):
    dp = lax.axis_index("dp")
    column = lax.axis_index("fsdp")
    z, core = column // 2, column % 2
    others = [(dp ^ 1), (dp ^ 2)] if rows == 4 else [(dp + step) % rows for step in range(1, rows)]
    return dp, z, core, others


def block_of(array, line, row, shape, turned):
    if len(array.shape) == 4:
        return array.at[line, row]
    high, wide = (line, row) if turned else (row, line)
    height, width = shape
    return array.at[
        pl.ds(pl.multiple_of(high * height, height), height),
        pl.ds(pl.multiple_of(wide * width, width), width),
    ]


def whole_shape(shape, turned, rows, columns):
    height, width = shape
    if width % 128 == 0 and height % 32 == 0:
        return (columns * height, rows * width) if turned else (rows * height, columns * width)
    return (columns, rows, height, width)


def gather_kernel(rows, depth, *refs):
    shards = refs[:3]
    cond_rows, ada_ref, ada_bias, bias_row = refs[3:7]
    outs, mod_out, bias_out, cond_in = refs[7:10], refs[10], refs[11], refs[12]
    (
        own_sems, send_sems, recv_sems, bias_in, part_out, part_in,
        cond_send, cond_recv, part_send, part_recv, bias_send, bias_recv,
    ) = refs[13:]
    dp, z, core, others = positions(rows, depth)
    columns = 2 * depth
    column = lax.axis_index("fsdp")
    me = dp * columns + column
    sibling = place(dp, z, 1 - core)
    enter_barrier(me, rows, columns)
    sends = []

    cond_swap = Exchange(
        me, rows, columns, lambda target: cond_rows.at[target // columns], cond_in,
        cond_send, cond_recv)
    part_swap = Exchange(
        me, rows, columns, lambda target: part_out.at[target], part_in, part_send, part_recv)
    cond_swap.start()

    def bias_copy(target, slot):
        return pltpu.make_async_remote_copy(
            src_ref=bias_row, dst_ref=bias_in.at[slot], send_sem=bias_send.at[target],
            recv_sem=bias_recv.at[slot], device_id=(dp, target), device_id_type=MESH_IDS)

    @pl.loop(1, columns)
    def _(step):
        bias_copy(lax.rem(column + step, columns), column).start()

    bias_in[column] = bias_row[...]

    def slot_of(part, line, row):
        return block_of(outs[part], line, row, shards[part].shape, part == 2)

    def half_of(ref, part, which):
        half = shards[part].shape[0] // 2
        return ref.at[pl.ds(which * half, half)]

    def send(line, row, target, which=None, own=False):
        for part in range(3):
            destination = slot_of(part, line, row)
            source = shards[part] if own else destination
            if which is not None:
                source, destination = half_of(source, part, which), half_of(destination, part, which)
            copy = pltpu.make_async_remote_copy(
                src_ref=source,
                dst_ref=destination,
                send_sem=send_sems.at[len(sends)],
                recv_sem=recv_sems.at[which or 0, part, line, row],
                device_id=target,
                device_id_type=MESH_IDS,
            )
            copy.start()
            sends.append(copy)

    def arrive(line, row, which=None):
        for part in range(3):
            destination = slot_of(part, line, row)
            if which is not None:
                destination = half_of(destination, part, which)
            pltpu.make_async_remote_copy(
                src_ref=destination,
                dst_ref=destination,
                send_sem=send_sems.at[0],
                recv_sem=recv_sems.at[which or 0, part, line, row],
                device_id=sibling,
                device_id_type=MESH_IDS,
            ).wait_recv()

    own = z * 2 + core
    steps = z_order(depth)
    lines = [((z - step) % depth) * 2 + core for step in steps]
    for other in others:
        send(own, dp, place(other, z, core), own=True)
    for step in steps[1:]:
        send(own, dp, place(dp, (z + step) % depth, core), own=True)
    send(own, dp, sibling, own=True)
    keeps = [
        pltpu.make_async_copy(shards[part], slot_of(part, own, dp), own_sems.at[part])
        for part in range(3)
    ]
    for keep in keeps:
        keep.start()
    cond_swap.wait_arrivals()
    high, wide = ada_ref.shape
    part = jnp.dot(
        cond_in[:, 0, :high].astype(bfloat), ada_ref[...], preferred_element_type=jnp.float32)
    part_out[:, 0, :wide] = part + jnp.where(dp == 0, ada_bias[...], 0.0)
    part_swap.start()
    for turn in range(depth + 2):
        if 0 < turn < depth:
            line = lines[turn]
            arrive(line, dp)
            for other in others:
                send(line, dp, place(other, z, core))
            send(line, dp, sibling)
        if 1 <= turn <= depth:
            line = lines[turn - 1]
            for position, other in enumerate(others):
                arrive(line, other)
                if rows == 4:
                    send(line, other, place(others[1 - position], z, core), which=position)
                send(line, other, sibling)
        if turn >= 2 and rows == 4:
            line = lines[turn - 2]
            arrive(line, dp ^ 3, 0)
            arrive(line, dp ^ 3, 1)
            send(line, dp ^ 3, sibling)
    for line in lines:
        for row in range(rows):
            arrive(line + 1 - 2 * core, (dp + row) % rows)
    part_swap.wait_arrivals()
    for block in range(columns):
        total = part_in[block]
        for row in range(1, rows):
            total = total + part_in[row * columns + block]
        mod_out[block] = total

    @pl.loop(1, columns)
    def _(step):
        other = lax.rem(column + step, columns)
        bias_copy(other, other).wait_recv()
        bias_copy(other, other).wait_send()

    bias_out[...] = bias_in[...]
    for keep in keeps:
        keep.wait()
    for copy in sends:
        copy.wait_send()
    cond_swap.wait_sends()
    part_swap.wait_sends()


def round_up(width):
    return -(-width // 128) * 128


def gather_shards(shards, cond_rows, ada_weight, ada_bias, bias_row, rows, columns):
    depth = columns // 2
    total = rows * columns
    mod_pad = round_up(ada_weight.shape[1])
    vmem = pl.BlockSpec(memory_space=pltpu.VMEM)
    dma = pltpu.SemaphoreType.DMA
    row_shape = lambda count, width: jax.ShapeDtypeStruct((count, 1, width), jnp.float32)
    row_buffer = lambda count, width: pltpu.VMEM((count, 1, width), jnp.float32)
    count = (depth - 1) + depth * rows + depth * (rows - 1) + (2 * depth if rows == 4 else 0)
    shapes = [
        whole_shape(shard.shape, part == 2, rows, columns) for part, shard in enumerate(shards)
    ]
    return pl.pallas_call(
        functools.partial(gather_kernel, rows, depth),
        out_shape=[jax.ShapeDtypeStruct(shape, bfloat) for shape in shapes]
        + [row_shape(columns, mod_pad), row_shape(columns, bias_row.shape[-1]),
           row_shape(total, cond_rows.shape[-1])],
        in_specs=[pl.BlockSpec(memory_space=pl.ANY)] * 3 + [vmem] * 4,
        out_specs=[pl.BlockSpec(memory_space=pl.ANY)] * 3 + [vmem] * 3,
        scratch_shapes=[
            dma((3,)),
            dma((3 * count,)),
            dma((2, 3, columns, rows)),
            row_buffer(columns, bias_row.shape[-1]),
            row_buffer(total, mod_pad),
            row_buffer(total, mod_pad),
            dma((total,)), dma((total,)), dma((total,)), dma((total,)),
            dma((columns,)), dma((columns,)),
        ],
        compiler_params=pltpu.CompilerParams(
            collective_id=0, has_side_effects=True, vmem_limit_bytes=32 * 2**20),
        name="gather_shards",
    )(*shards, cond_rows, ada_weight, ada_bias, bias_row)


def scatter_kernel(rows, depth, *refs):
    grads = refs[:3]
    leaving, cond_in, ada_ref, slope = refs[3:7]
    outs, ada_grad, sums_out, cond_grad = refs[7:10], refs[10], refs[11], refs[12]
    refs = refs[13:]
    helds, pairs_in, planes_in, crosses_in, alongs_in = (
        refs[3 * kind : 3 + 3 * kind] for kind in range(5)
    )
    (
        load_sems, pair_send, pair_recv, plane_send, plane_recv,
        cross_send, cross_recv, along_send, along_recv,
        all_rows, back_out, back_in, row_send, row_recv, back_send, back_recv,
    ) = refs[15:]
    dp, z, core, others = positions(rows, depth)
    columns = 2 * depth
    me = dp * columns + lax.axis_index("fsdp")
    row_swap = Exchange(
        me, rows, columns, lambda target: leaving.at[lax.rem(target, columns)], all_rows,
        row_send, row_recv)
    back_swap = Exchange(
        me, rows, columns, lambda target: back_out.at[target], back_in, back_send, back_recv)
    sibling = place(dp, z, 1 - core)
    targets = [dp ^ 3, dp ^ 1, dp ^ 2, dp] if rows == 4 else others + [dp]
    steps = z_order(depth)[::-1]
    enter_barrier(me, rows, columns)
    row_swap.start()
    waits = []

    def remote(source, destination, send_sem, recv_sem, target):
        copy = pltpu.make_async_remote_copy(
            src_ref=source, dst_ref=destination, send_sem=send_sem, recv_sem=recv_sem,
            device_id=target, device_id_type=MESH_IDS,
        )
        copy.start()
        waits.append(copy)
        return copy

    def add(first, others_in, length, target):
        chunk = 48 if length % 48 == 0 else 16

        @pl.loop(0, length // chunk)
        def _(index):
            piece = pl.ds(pl.multiple_of(index * chunk, chunk), chunk)
            total = first[piece, :].astype(jnp.float32)
            for other in others_in:
                total = total + other[piece, :].astype(jnp.float32)
            target[piece, :] = total.astype(target.dtype)

    lines = [(z + step) % depth for step in steps]
    pairs, loads, planes, crosses, alongs = {}, {}, {}, {}, {}
    for turn, line in enumerate(lines):
        for slot, target in enumerate(targets):
            for part in range(3):
                key = (part, turn, slot)
                shape = outs[part].shape
                pairs[key] = remote(
                    block_of(grads[part], line * 2 + 1 - core, target, shape, part == 2),
                    pairs_in[part].at[turn, slot], pair_send.at[key], pair_recv.at[key], sibling)
                loads[key] = pltpu.make_async_copy(
                    block_of(grads[part], line * 2 + core, target, shape, part == 2),
                    helds[part].at[turn, slot], load_sems.at[key])
                loads[key].start()
    last = len(targets) - 1
    for turn in range(depth + 2):
        if turn == depth - 1:
            row_swap.wait_arrivals()
            high, wide = ada_ref.shape
            arrived = all_rows[:, 0, :]
            sums_out[...] = jnp.sum(arrived, axis=0, keepdims=True)
            ada_grad[...] = contract_exact(cond_in[:, 0, :high], arrived[:, :wide])
            back_out[:, 0, :high] = lax.dot_general(
                arrived[:, :wide], ada_ref[...].astype(jnp.float32), (((1,), (1,)), ((), ())),
                precision=highest)
            back_swap.start()
        if turn < depth:
            for slot in range(len(targets)):
                for part in range(3):
                    key = (part, turn, slot)
                    height = outs[part].shape[0]
                    half = height // 2
                    loads[key].wait()
                    pairs[key].wait_recv()
                    here = helds[part].at[turn, slot]
                    add(here, [pairs_in[part].at[turn, slot]], height, here)
                    if rows == 4 and slot == 0:
                        for position in range(2):
                            key = (part, turn, position)
                            crosses[key] = remote(
                                helds[part].at[turn, 0, pl.ds((1 - position) * half, half)],
                                crosses_in[part].at[turn, position],
                                cross_send.at[key], cross_recv.at[key],
                                place(others[position], z, core))
                    if rows != 4 and slot < last:
                        planes[key] = remote(
                            here, planes_in[part].at[turn, slot], plane_send.at[key],
                            plane_recv.at[key], place(targets[slot], z, core))
        if rows == 4 and 1 <= turn <= depth:
            now = turn - 1
            for position in range(2):
                for part in range(3):
                    half = outs[part].shape[0] // 2
                    crosses[part, now, 1 - position].wait_recv()
                    piece = helds[part].at[now, 1 + position, pl.ds(position * half, half)]
                    add(piece, [crosses_in[part].at[now, 1 - position]], half, piece)
                    key = (part, now, position)
                    planes[key] = remote(
                        helds[part].at[now, 1 + position], planes_in[part].at[now, position],
                        plane_send.at[key], plane_recv.at[key],
                        place(others[position], z, core))
        if turn >= 2:
            now = turn - 2
            for part in range(3):
                for slot in range(len(others)):
                    planes[part, now, slot].wait_recv()
                here = helds[part].at[now, last]
                arrived = [planes_in[part].at[now, slot] for slot in range(len(others))]
                add(here, arrived, outs[part].shape[0], here)
                if now < depth - 1:
                    key = (part, now)
                    alongs[key] = remote(
                        here, alongs_in[part].at[now], along_send.at[key], along_recv.at[key],
                        place(dp, lines[now], core))
    for part in range(3):
        for now in range(depth - 1):
            alongs[part, now].wait_recv()
        arrived = [alongs_in[part].at[now] for now in range(depth - 1)]
        add(helds[part].at[depth - 1, last], arrived, outs[part].shape[0], outs[part])
    back_swap.wait_arrivals()
    for row in range(rows):
        total = back_in[row * columns]
        for block in range(1, columns):
            total = total + back_in[row * columns + block]
        cond_grad[row] = total * slope[row]
    for copy in waits:
        copy.wait_send()
    row_swap.wait_sends()
    back_swap.wait_sends()


def scatter_shards(grads, leaving, cond_in, ada_weight, slope, shapes, rows, columns):
    depth = columns // 2
    total = rows * columns
    vmem = pl.BlockSpec(memory_space=pltpu.VMEM)
    row_buffer = lambda count, width: pltpu.VMEM((count, 1, width), jnp.float32)
    peers = 2 if rows == 4 else rows - 1
    dma = pltpu.SemaphoreType.DMA
    buffers = []
    for lead in ((depth, rows), (depth, rows), (depth, peers), (depth, 2), (depth - 1,)):
        for height, width in shapes:
            if lead == (depth, 2) and len(buffers) >= 9:
                height = height // 2 if rows == 4 else 16
            buffers.append(pltpu.VMEM(lead + (height, width), bfloat))
    return pl.pallas_call(
        functools.partial(scatter_kernel, rows, depth),
        out_shape=[jax.ShapeDtypeStruct(shape, jnp.float32) for shape in shapes]
        + [jax.ShapeDtypeStruct(ada_weight.shape, jnp.float32),
           jax.ShapeDtypeStruct((1, leaving.shape[-1]), jnp.float32),
           jax.ShapeDtypeStruct(slope.shape, jnp.float32)],
        in_specs=[pl.BlockSpec(memory_space=pl.ANY)] * 3 + [vmem] * 4,
        out_specs=[vmem] * 6,
        scratch_shapes=buffers + [
            dma((3, depth, rows)), dma((3, depth, rows)), dma((3, depth, rows)),
            dma((3, depth, peers)), dma((3, depth, peers)),
            dma((3, depth, 2)), dma((3, depth, 2)),
            dma((3, depth - 1)), dma((3, depth - 1)),
            row_buffer(total, leaving.shape[-1]),
            row_buffer(total, slope.shape[-1]), row_buffer(total, slope.shape[-1]),
            dma((total,)), dma((total,)), dma((total,)), dma((total,)),
        ],
        compiler_params=pltpu.CompilerParams(
            collective_id=1, has_side_effects=True, vmem_limit_bytes=50 * 2**20),
        name="scatter_shards",
    )(*grads, leaving, cond_in, ada_weight, slope)


def normalize_rows(values):
    center = jnp.mean(values, axis=-1, keepdims=True)
    spread = jnp.mean(jnp.square(values - center), axis=-1, keepdims=True)
    inverse = lax.rsqrt(spread + 1e-06)
    return ((values - center) * inverse, inverse)


def norm_backward(grad_normed, normed, inverse):
    centered = grad_normed - jnp.mean(grad_normed, axis=-1, keepdims=True)
    return inverse * (centered - normed * jnp.mean(grad_normed * normed, axis=-1, keepdims=True))


def contract_rows(left_rows, right_rows):
    return lax.dot_general(
        left_rows, right_rows, (((0,), (0,)), ((), ())), preferred_element_type=jnp.float32
    )


def contract_exact(left_rows, right_rows):
    return lax.dot_general(left_rows, right_rows, (((0,), (0,)), ((), ())), precision=highest)


def against_weight(grad_rows, weight):
    return lax.dot_general(
        grad_rows, weight, (((1,), (1,)), ((), ())), preferred_element_type=jnp.float32
    )


def dot_plain(left, right):
    return jnp.dot(left, right, preferred_element_type=jnp.float32)


def columns_sum(values):
    return jnp.sum(values, axis=0, keepdims=True)


class Swap:
    def __init__(self, me, size, device, row_for, landing, send_sems, recv_sems):
        self.me, self.size, self.device = me, size, device
        self.row_for, self.landing = row_for, landing
        self.send_sems, self.recv_sems = send_sems, recv_sems
        self.copies = []

    def start(self):
        for step in range(1, self.size):
            other = lax.rem(self.me + step, self.size)
            copy = pltpu.make_async_remote_copy(
                src_ref=self.row_for(other),
                dst_ref=self.landing.at[self.me],
                send_sem=self.send_sems.at[step],
                recv_sem=self.recv_sems.at[step],
                device_id=self.device(other),
                device_id_type=MESH_IDS,
            )
            copy.start()
            self.copies.append(copy)
        self.landing[self.me] = self.row_for(self.me)[...]

    def wait_arrivals(self):
        for copy in self.copies:
            copy.wait_recv()

    def wait_sends(self):
        for copy in self.copies:
            copy.wait_send()


class Gather:
    def __init__(self, rows, depth, where, shards, outs, own_sems, send_sems, recv_sems):
        self.rows, self.depth = rows, depth
        self.dp, self.z, self.core, self.others = where
        self.shards, self.outs = shards, outs
        self.own_sems, self.send_sems, self.recv_sems = own_sems, send_sems, recv_sems
        self.sibling = place(self.dp, self.z, 1 - self.core)
        self.sends = []
        self.keeps = []
        self.own = self.z * 2 + self.core
        self.lines = [(self.z ^ step) * 2 + self.core for step in range(depth)]
        self.units = [(part, turn) for part in range(3) for turn in range(depth)]

    def slot_of(self, part, line, row):
        return block_of(self.outs[part], line, row, self.shards[part].shape, part == 2)

    def half_of(self, ref, part, which):
        half = self.shards[part].shape[0] // 2
        return ref.at[pl.ds(which * half, half)]

    def send(self, part, line, row, target, which=None, own=False):
        destination = self.slot_of(part, line, row)
        source = self.shards[part] if own else destination
        if which is not None:
            source, destination = (
                self.half_of(source, part, which), self.half_of(destination, part, which))
        copy = pltpu.make_async_remote_copy(
            src_ref=source,
            dst_ref=destination,
            send_sem=self.send_sems.at[len(self.sends)],
            recv_sem=self.recv_sems.at[which or 0, part, line, row],
            device_id=target,
            device_id_type=MESH_IDS,
        )
        copy.start()
        self.sends.append(copy)

    def arrive(self, part, line, row, which=None):
        destination = self.slot_of(part, line, row)
        if which is not None:
            destination = self.half_of(destination, part, which)
        pltpu.make_async_remote_copy(
            src_ref=destination,
            dst_ref=destination,
            send_sem=self.send_sems.at[0],
            recv_sem=self.recv_sems.at[which or 0, part, line, row],
            device_id=self.sibling,
            device_id_type=MESH_IDS,
        ).wait_recv()

    def send_own(self, part):
        for other in self.others:
            self.send(part, self.own, self.dp, place(other, self.z, self.core), own=True)
        self.send(part, self.own, self.dp, self.sibling, own=True)
        keep = pltpu.make_async_copy(
            self.shards[part], self.slot_of(part, self.own, self.dp), self.own_sems.at[part])
        keep.start()
        self.keeps.append(keep)

    def send_deep(self, index):
        if index < len(self.units):
            part, step = self.units[index]
            if step:
                target = place(self.dp, self.z ^ step, self.core)
                self.send(part, self.own, self.dp, target, own=True)

    def turn(self, index):
        dp, z, core = self.dp, self.z, self.core
        count = len(self.units)
        self.send_deep(index + AHEAD)
        if index in (1, 2):
            self.send_own(index)
        if index < count:
            part, turn = self.units[index]
            line = self.lines[turn]
            if turn:
                self.arrive(part, line, dp)
                for other in self.others:
                    self.send(part, line, dp, place(other, z, core))
                self.send(part, line, dp, self.sibling)
        if LAG <= index < count + LAG:
            part, turn = self.units[index - LAG]
            line = self.lines[turn]
            for position, other in enumerate(self.others):
                self.arrive(part, line, other)
                self.send(
                    part, line, other, place(self.others[1 - position], z, core), which=position)
                self.send(part, line, other, self.sibling)
        if 2 * LAG <= index:
            part, turn = self.units[index - 2 * LAG]
            line = self.lines[turn]
            self.arrive(part, line, dp ^ 3, 0)
            self.arrive(part, line, dp ^ 3, 1)
            self.send(part, line, dp ^ 3, self.sibling)

    def finish_part(self, part):
        for line in self.lines:
            for row in range(self.rows):
                self.arrive(part, line + 1 - 2 * self.core, (self.dp + row) % self.rows)
        self.keeps[part].wait()

    def wait_sends(self):
        for copy in self.sends:
            copy.wait_send()


class Scatter:
    def __init__(self, rows, depth, where, shapes, grads, buffers, sems):
        self.rows, self.depth, self.shapes, self.grads = rows, depth, shapes, grads
        self.dp, self.z, self.core, self.others = where
        self.held, self.planes_in, self.crosses_in, self.alongs_in = (
            buffers[3 * kind : 3 * kind + 3] for kind in range(4))
        (
            self.pair_send, self.pair_recv, self.plane_send, self.plane_recv,
            self.cross_send, self.cross_recv, self.along_send, self.along_recv,
        ) = sems
        self.sibling = place(self.dp, self.z, 1 - self.core)
        self.targets = [self.dp ^ 3, self.dp ^ 1, self.dp ^ 2, self.dp]
        self.lines = [self.z ^ step for step in reversed(range(depth))]
        self.units = [(part, turn) for part in (2, 1, 0) for turn in range(depth)]
        self.pairs, self.planes, self.crosses, self.alongs = {}, {}, {}, {}

    def remote(self, source, destination, send_sem, recv_sem, target):
        copy = pltpu.make_async_remote_copy(
            src_ref=source, dst_ref=destination, send_sem=send_sem, recv_sem=recv_sem,
            device_id=target, device_id_type=MESH_IDS)
        copy.start()
        return copy

    def block(self, part, line, target):
        return block_of(self.grads[part], line, target, self.shapes[part], part == 2)

    def add(self, first, others_in, length, target):
        chunk = 48

        @pl.loop(0, length // chunk)
        def _(index):
            piece = pl.ds(pl.multiple_of(index * chunk, chunk), chunk)
            total = first[piece, :].astype(jnp.float32)
            for other in others_in:
                total = total + other[piece, :].astype(jnp.float32)
            target[piece, :] = total.astype(target.dtype)

    def start_pairs(self, part):
        for turn, line in enumerate(self.lines):
            for slot, target in enumerate(self.targets):
                key = (part, turn, slot)
                self.pairs[key] = self.remote(
                    self.block(part, line * 2 + 1 - self.core, target),
                    self.held[part].at[turn, slot], self.pair_send.at[key],
                    self.pair_recv.at[key], self.sibling)

    def wait_pairs_sent(self, part):
        for turn in range(self.depth):
            for slot in range(self.rows):
                self.pairs[part, turn, slot].wait_send()

    def turn(self, index):
        last = self.rows - 1
        count = len(self.units)
        if index < count:
            part, turn = self.units[index]
            height = self.shapes[part][0]
            half = height // 2
            for slot, target in enumerate(self.targets):
                self.pairs[part, turn, slot].wait_recv()
                here = self.held[part].at[turn, slot]
                own = self.block(part, self.lines[turn] * 2 + self.core, target)
                self.add(own, [here], height, here)
                if slot == 0:
                    for position in range(2):
                        key = (part, turn, position)
                        self.crosses[key] = self.remote(
                            self.held[part].at[turn, 0, pl.ds((1 - position) * half, half)],
                            self.crosses_in[part].at[turn, position],
                            self.cross_send.at[key], self.cross_recv.at[key],
                            place(self.others[position], self.z, self.core))
        if LAG <= index < count + LAG:
            part, turn = self.units[index - LAG]
            half = self.shapes[part][0] // 2
            for position in range(2):
                self.crosses[part, turn, 1 - position].wait_recv()
                piece = self.held[part].at[turn, 1 + position, pl.ds(position * half, half)]
                self.add(piece, [self.crosses_in[part].at[turn, 1 - position]], half, piece)
                key = (part, turn, position)
                self.planes[key] = self.remote(
                    self.held[part].at[turn, 1 + position], self.planes_in[part].at[turn, position],
                    self.plane_send.at[key], self.plane_recv.at[key],
                    place(self.others[position], self.z, self.core))
        if 2 * LAG <= index:
            part, turn = self.units[index - 2 * LAG]
            for position in range(2):
                self.planes[part, turn, position].wait_recv()
            here = self.held[part].at[turn, last]
            arrived = [self.planes_in[part].at[turn, position] for position in range(2)]
            self.add(here, arrived, self.shapes[part][0], here)
            if turn < self.depth - 1:
                key = (part, turn)
                self.alongs[key] = self.remote(
                    here, self.alongs_in[part].at[turn], self.along_send.at[key],
                    self.along_recv.at[key], place(self.dp, self.lines[turn], self.core))

    def finish_part(self, part):
        total = self.held[part][self.depth - 1, self.rows - 1].astype(jnp.float32)
        for turn in range(self.depth - 1):
            self.alongs[part, turn].wait_recv()
            total = total + self.alongs_in[part][turn].astype(jnp.float32)
        return total

    def wait_sends(self):
        for copies in (self.planes, self.crosses, self.alongs):
            for copy in copies.values():
                copy.wait_send()


def layer_kernel(rows, depth, *refs):
    sources, live_ref, outs = refs[2:13], refs[13], refs[14:22]
    landed, results = refs[22:33], refs[33:41]
    (
        latents, cotangent, conditioning, ada_ref, ada_bias, qkv_shard, qv_shard, proj_shard,
        proj_bias_shard, fc1_bias_shard, fc2_bias_shard,
    ) = landed
    block_out, latent_grad, ada_grad, qkv_grad, proj_grad, fc1_grad, fc2_grad, small = results
    mixed_shard, cond_rows, slope, load_sems, store_sems = refs[41:46]
    shards = (mixed_shard, refs[0], refs[1])
    refs = refs[46:]
    weights, grads = refs[:3], (refs[3], refs[4], refs[3])
    scatter_buffers, scatter_sems = refs[5:17], refs[17:25]
    (
        own_sems, send_sems, recv_sems, swap_send, swap_recv,
        cond_across, cond_own, cond_along, cond_in, part_out, part_across, part_row, part_along,
        leaving, rows_along, rows_across, back_out, back_across, back_row, back_along,
        mod, qkv_bias, proj_bias, fc1_bias, fc2_bias, mod_grad, qkv_sums, proj_sums, fc1_sums,
        fc2_sums, inverse_one, inverse_two, normed_one, normed_two, middle, branch, wide,
        hidden_one, hidden_one_t, hidden_two, hidden_two_t, attended, attended_t,
        grad_mlp, grad_mlp_t, grad_attended, projected,
        grad_proj_mixed, activated, grad_pre, grad_natural, grad_state, probability,
    ) = refs[25:]
    grad_mixed = grad_pre
    mixed, fc1, fc2_turned = weights
    where = positions(rows, depth)
    dp = where[0]
    columns = 2 * depth
    column = lax.axis_index("fsdp")
    length = latents.shape[0]
    qkv_part, proj_part = 3 * D // columns, D // columns
    block = qkv_part + proj_part
    edge = qkv_part // 128 * 128
    rest = block - edge
    lead = qkv_part - edge
    scale_factor = HEAD ** (-0.5)
    ada_rows, mod_width = ada_ref.shape
    mod_pad = round_up(mod_width)
    loads = [
        pltpu.make_async_copy(source, target, load_sems.at[at])
        for at, (source, target) in enumerate(zip(sources, landed))]
    for at in (2, 5, 7, 6, 8, 9, 10, 0, 3, 4, 1):
        loads[at].start()
    stores = []

    def store(at):
        copy = pltpu.make_async_copy(results[at], outs[at], store_sems.at[at])
        copy.start()
        stores.append(copy)

    barrier = pltpu.get_barrier_semaphore()
    partners = [(lax.rem(dp + step, rows), column) for step in range(1, rows)]
    partners += [(dp, lax.rem(column + step, columns)) for step in range(1, columns)]
    for partner in partners:
        pl.semaphore_signal(barrier, inc=1, device_id=partner, device_id_type=MESH_IDS)
    live = live_ref[0].astype(jnp.float32)
    loads[2].wait()
    cond_value = conditioning[...].astype(jnp.float32)
    logistic = 1.0 / (1.0 + jnp.exp(-cond_value))
    slope[...] = logistic * (1.0 + cond_value * (1.0 - logistic))
    cond_act = (cond_value * logistic).astype(bfloat).astype(jnp.float32)
    for row in range(rows):
        cond_rows[row, :, :ada_rows] = cond_act[:, row * ada_rows : (row + 1) * ada_rows]
    pl.semaphore_wait(barrier, len(partners))
    gather = Gather(rows, depth, where, shards, weights, own_sems, send_sems, recv_sems)
    scatter = Scatter(
        rows, depth, where, [shard.shape for shard in shards], grads, scatter_buffers, scatter_sems)
    swaps = []

    def swap_across(row_for, landing):
        at = len(swaps)
        swaps.append(Swap(
            dp, rows, lambda other: (other, column), row_for, landing,
            swap_send.at[at], swap_recv.at[at]))
        return swaps[-1]

    def swap_along(row_for, landing):
        at = len(swaps)
        swaps.append(Swap(
            column, columns, lambda other: (dp, other), row_for, landing,
            swap_send.at[at], swap_recv.at[at]))
        return swaps[-1]

    cond_first = swap_across(
        lambda other: cond_rows.at[other], cond_across)
    cond_second = swap_along(lambda other: cond_own, cond_along)
    part_first = swap_across(lambda other: part_out.at[other], part_across)
    part_second = swap_along(lambda other: part_row.at[other], part_along)
    rows_first = swap_along(lambda other: leaving.at[other], rows_along)
    rows_second = swap_across(lambda other: rows_along, rows_across)
    back_first = swap_across(lambda other: back_out.at[other], back_across)
    back_second = swap_along(lambda other: back_row.at[other], back_along)
    cond_first.start()
    loads[5].wait()
    loads[7].wait()
    mixed_shard[:, :qkv_part] = qkv_shard[...]
    mixed_shard[:, qkv_part:] = proj_shard[...]
    for index in range(AHEAD):
        gather.send_deep(index)
    gather.send_own(0)

    def piece(kind):
        return mod[:, kind * D : (kind + 1) * D]

    def share_condition():
        cond_first.wait_arrivals()
        cond_own[:rows] = cond_across[...]
        bias_row = []
        for at in (6, 8, 9, 10):
            loads[at].wait()
            bias_row.append(landed[at][...].astype(jnp.float32).reshape(1, -1))
        bias_row = jnp.concatenate(bias_row, axis=1)
        pad = cond_own.shape[-1]
        for at in range(bias_row.shape[1] // pad):
            cond_own[rows + at] = bias_row[:, at * pad : (at + 1) * pad]
        cond_second.start()

    def start_modulation():
        cond_second.wait_arrivals()
        cond_in[...] = jnp.concatenate(
            [cond_along[source, row] for row in range(rows) for source in range(columns)], axis=0)
        loads[3].wait()
        loads[4].wait()
        part = dot_plain(cond_in[:, :ada_rows].astype(bfloat), ada_ref[...])
        own_bias = ada_bias[...].astype(jnp.float32).reshape(1, -1)
        part = part + jnp.where(dp == 0, own_bias, 0.0)
        for row in range(rows):
            part_out[row, :, :mod_width] = part[row * columns : (row + 1) * columns]
        part_first.start()

    def sum_modulation():
        part_first.wait_arrivals()
        total = part_across[0]
        for row in range(1, rows):
            total = total + part_across[row]
        part_row[:, 0, :] = total
        part_second.start()

    def normalize_first():
        loads[0].wait()
        normed, inverse = normalize_rows(latents[...].astype(jnp.float32))
        normed_one[...] = normed
        inverse_one[...] = inverse

    def finish_modulation():
        part_second.wait_arrivals()
        mod[...] = jnp.concatenate(
            [part_along[source][:, :mod_width] for source in range(columns)], axis=1)
        bias_parts = [
            jnp.concatenate(
                [cond_along[source, row] for row in range(rows, cond_along.shape[1])], axis=1)
            for source in range(columns)]
        low = 0
        naturals = []
        for width in (2 * D // columns, D // columns, FF // columns, D // columns):
            naturals.append(jnp.concatenate(
                [part[:, low : low + width] for part in bias_parts], axis=1))
            low += width
        qkv_bias[:, :D] = naturals[0][:, :D]
        qkv_bias[:, D : 2 * D] = jnp.zeros((1, D), jnp.float32)
        qkv_bias[:, 2 * D :] = naturals[0][:, D:]
        proj_bias[...] = naturals[1]
        fc1_bias[...] = naturals[2]
        fc2_bias[...] = naturals[3]
        hidden = (normed_one[...] * (1.0 + piece(1)) + piece(0)).astype(bfloat)
        hidden_one[...] = hidden
        hidden_one_t[...] = hidden.T

    def start_gradient():
        loads[1].wait()
        grad = (piece(5) * (live * cotangent[...].astype(jnp.float32))).astype(bfloat)
        grad_mlp[...] = grad
        grad_mlp_t[...] = grad.T
        fc2_sums[...] = columns_sum(grad.astype(jnp.float32))

    def span(index, width):
        return pl.ds(pl.multiple_of(index * width, width), width)

    def project():
        @pl.loop(0, columns)
        def _(index):
            wide[:, span(index, block)] = dot_plain(hidden_one[...], mixed[:, span(index, block)])

        for index in range(columns):
            natural = slice(index * qkv_part, (index + 1) * qkv_part)
            projected[:, natural] = (
                wide[:, index * block : index * block + qkv_part] + qkv_bias[:, natural]
            ).astype(bfloat)

    def head_slabs(source, pair):
        return [
            source[:, pl.ds(pl.multiple_of(kind * D + pair * 128, 128), 128)] for kind in range(3)]

    def own_lanes(which):
        lane = lax.broadcasted_iota(jnp.int32, (length, 128), 1)
        return lane < HEAD if which == 0 else lane >= HEAD

    def attend(low, high):
        @pl.loop(low, high)
        def _(pair):
            queries, keys, values = head_slabs(projected, pair)
            zero = jnp.zeros_like(queries)
            results = []
            for which in range(2):
                scores = against_weight(
                    jnp.where(own_lanes(which), queries, zero), keys) * scale_factor
                shifted = jnp.exp(scores - jnp.max(scores, axis=-1, keepdims=True))
                exact = shifted / jnp.sum(shifted, axis=-1, keepdims=True)
                probability[2 * pair + which] = exact
                results.append(dot_plain(exact.astype(bfloat), values))
            attended[:, span(pair, 128)] = jnp.where(
                own_lanes(0), results[0], results[1]).astype(bfloat)

    def finish_attention():
        attended_t[...] = attended[...].T

        @pl.loop(0, columns)
        def _(index):
            tail = pl.ds(pl.multiple_of(index * block + edge, 128), rest)
            wide[:, span(index, rest)] = dot_plain(attended[...], mixed[:, tail])

        for index in range(columns):
            natural = slice(index * proj_part, (index + 1) * proj_part)
            branch[:, natural] = (
                wide[:, index * rest + lead : (index + 1) * rest] + proj_bias[:, natural])
        total = latents[...].astype(jnp.float32) + piece(2) * branch[...]
        middle[...] = total
        normed, inverse = normalize_rows(total)
        normed_two[...] = normed
        inverse_two[...] = inverse
        hidden = (normed * (1.0 + piece(4)) + piece(3)).astype(bfloat)
        hidden_two[...] = hidden
        hidden_two_t[...] = hidden.T

    chunk = 384
    chunks = FF // chunk

    def expand(low, high):
        @pl.loop(low, high)
        def _(index):
            part = span(index, chunk)
            value = dot_plain(hidden_two[...], fc1[:, part]) + fc1_bias[:, part]
            root = 0.7978845608028654
            square = value * value
            bend = jnp.tanh(root * (value + 0.044715 * (square * value)))
            activated[:, part] = (0.5 * value * (1.0 + bend)).astype(bfloat)
            wide[:, part] = 0.5 * (1.0 + bend) + 0.5 * value * (1.0 - bend * bend) * (
                root * (1.0 + 3 * 0.044715 * square))

    def fc2_weight_grad(low, high):
        @pl.loop(low, high)
        def _(index):
            part = span(index, chunk)
            grads[2][:, part] = dot_plain(grad_mlp_t[...], activated[:, part]).astype(bfloat)

    def after_part_zero():
        gather.finish_part(0)
        project()

    def after_part_one():
        gather.finish_part(1)
        expand(0, 4)

    def send_fc2_grad():
        fc2_weight_grad(4, 8)
        scatter.start_pairs(2)

    hooks = [
        share_condition, normalize_first, start_modulation, None, sum_modulation, None,
        finish_modulation, start_gradient, after_part_zero, lambda: attend(0, 3),
        lambda: attend(3, 6), finish_attention, after_part_one, lambda: expand(4, 8),
        lambda: fc2_weight_grad(0, 4), send_fc2_grad,
    ]
    for index, hook in enumerate(hooks):
        gather.turn(index)
        if hook is not None:
            hook()
    scatter.turn(0)
    gather.finish_part(2)
    third = 256

    def finish_forward():
        @pl.loop(0, D // third)
        def _(index):
            part = span(index, third)
            branch_part = against_weight(activated[...], fc2_turned[part, :]) + fc2_bias[:, part]
            live_grad = live * cotangent[:, part].astype(jnp.float32)
            last = pl.ds(pl.multiple_of(5 * D + index * third, third), third)
            block_out[:, part] = (
                live * (middle[:, part] + mod[:, last] * branch_part)).astype(bfloat)
            mod_grad[:, last] = columns_sum(live_grad * branch_part)

        store(0)

    def fc1_weight_grad(low, high):
        @pl.loop(low, high)
        def _(index):
            part = span(index, chunk)
            grad = (dot_plain(grad_mlp[...], fc2_turned[:, part]) * wide[:, part]).astype(bfloat)
            grad_pre[:, part] = grad
            fc1_sums[:, part] = columns_sum(grad.astype(jnp.float32))
            grads[1][:, part] = dot_plain(hidden_two_t[...], grad).astype(bfloat)

    def hidden_two_back():
        @pl.loop(0, D // third)
        def _(index):
            part = span(index, third)
            grad_state[:, part] = against_weight(grad_pre[...], fc1[part, :])

    def middle_back():
        grad_hidden = grad_state[...]
        mod_grad[:, 3 * D : 4 * D] = columns_sum(grad_hidden)
        mod_grad[:, 4 * D : 5 * D] = columns_sum(grad_hidden * normed_two[...])
        grad_middle = live * cotangent[...].astype(jnp.float32) + norm_backward(
            grad_hidden * (1.0 + piece(4)), normed_two[...], inverse_two[...])
        mod_grad[:, 2 * D : 3 * D] = columns_sum(grad_middle * branch[...])
        grad_state[...] = grad_middle
        grad_branch = (piece(2) * grad_middle).astype(bfloat)
        proj_sums[...] = columns_sum(grad_branch.astype(jnp.float32))
        for index in range(columns):
            grad_proj_mixed[:, index * rest : index * rest + lead] = jnp.zeros(
                (length, lead), bfloat)
            grad_proj_mixed[:, index * rest + lead : (index + 1) * rest] = (
                grad_branch[:, index * proj_part : (index + 1) * proj_part])
        total = None
        for index in range(columns):
            term = against_weight(
                grad_proj_mixed[:, index * rest : (index + 1) * rest],
                mixed[:, index * block + edge : (index + 1) * block])
            total = term if total is None else total + term
        grad_attended[...] = total.astype(bfloat)

    def attend_back(low, high):
        @pl.loop(low, high)
        def _(pair):
            queries, keys, values = head_slabs(projected, pair)
            grad_out = grad_attended[:, span(pair, 128)]
            zero = jnp.zeros_like(grad_out)
            results = []
            for which in range(2):
                exact = probability[2 * pair + which]
                grad_prob = against_weight(jnp.where(own_lanes(which), grad_out, zero), values)
                inner = jnp.sum(exact * grad_prob, axis=-1, keepdims=True)
                grad_scores = (exact * (grad_prob - inner)).astype(bfloat)
                results.append((
                    dot_plain(grad_scores, keys) * scale_factor,
                    contract_rows(grad_scores, queries) * scale_factor,
                    contract_rows(exact.astype(bfloat), grad_out)))
            for kind in range(3):
                grad_natural[:, pl.ds(pl.multiple_of(kind * D + pair * 128, 128), 128)] = jnp.where(
                    own_lanes(0), results[0][kind], results[1][kind]).astype(bfloat)

    def mixed_weight_grad():
        qkv_sums[...] = columns_sum(grad_natural[...].astype(jnp.float32))
        for index in range(columns):
            grad_mixed[:, index * block : index * block + qkv_part] = (
                grad_natural[:, index * qkv_part : (index + 1) * qkv_part])
            grad_mixed[:, index * block + qkv_part : (index + 1) * block] = jnp.zeros(
                (length, proj_part), bfloat)
        scatter.wait_pairs_sent(2)

        @pl.loop(0, columns)
        def _(index):
            low = pl.multiple_of(index * block, 128)
            grads[0][:, pl.ds(low, edge)] = dot_plain(
                hidden_one_t[...], grad_mixed[:, pl.ds(low, edge)]).astype(bfloat)
            tail = pl.ds(pl.multiple_of(index * block + edge, 128), rest)
            grads[0][:, tail] = (
                dot_plain(hidden_one_t[...], grad_mixed[:, tail])
                + dot_plain(attended_t[...], grad_proj_mixed[:, span(index, rest)])).astype(bfloat)

    def finish_backward():
        @pl.loop(0, D // third)
        def _(index):
            part = span(index, third)
            branch[:, part] = against_weight(grad_mixed[...], mixed[part, :])

        grad_hidden = branch[...]
        mod_grad[:, :D] = columns_sum(grad_hidden)
        mod_grad[:, D : 2 * D] = columns_sum(grad_hidden * normed_one[...])
        latent_grad[...] = (grad_state[...] + norm_backward(
            grad_hidden * (1.0 + piece(1)), normed_one[...], inverse_one[...])).astype(bfloat)
        store(1)
        pad = jnp.zeros((1, mod_pad - mod_width), jnp.float32)
        qv_sums = jnp.concatenate([qkv_sums[:, :D], qkv_sums[:, 2 * D :]], axis=1)
        rows_of = (qv_sums, proj_sums[...], fc1_sums[...], fc2_sums[...])
        every = mod_grad[...]
        for index in range(columns):
            pieces = [every[:, index * mod_width : (index + 1) * mod_width], pad]
            for row in rows_of:
                share = row.shape[1] // columns
                pieces.append(row[:, index * share : (index + 1) * share])
            leaving[index] = jnp.concatenate(pieces, axis=1)
        rows_first.start()

    def share_rows():
        rows_first.wait_arrivals()
        rows_second.start()

    def own_sums():
        rows_second.wait_arrivals()
        arrived = jnp.concatenate([rows_across[row, :, 0, :] for row in range(rows)], axis=0)
        small[:, D:] = columns_sum(arrived)
        ada_grad[...] = contract_exact(cond_in[:, :ada_rows], arrived[:, :mod_width])
        store(2)
        back = lax.dot_general(
            arrived[:, :mod_width], ada_ref[...].astype(jnp.float32), (((1,), (1,)), ((), ())),
            precision=highest)
        for row in range(rows):
            back_out[row, :, :ada_rows] = back[row * columns : (row + 1) * columns]
        back_first.start()

    def share_back():
        back_first.wait_arrivals()
        for row in range(rows):
            back_row[:, row, 0, :] = back_across[row]
        back_second.start()

    def finish_condition():
        back_second.wait_arrivals()
        total = back_along[0]
        for source in range(1, columns):
            total = total + back_along[source]
        small[:, :D] = jnp.concatenate(
            [total[row][:, :ada_rows] for row in range(rows)], axis=1) * slope[...]
        store(7)

    def finish_fc2():
        fc2_grad[...] = scatter.finish_part(2)
        store(6)

    def finish_fc1():
        fc1_grad[...] = scatter.finish_part(1)
        store(5)

    def send_fc1_grad():
        fc1_weight_grad(4, 8)
        scatter.start_pairs(1)

    def send_mixed_grad():
        mixed_weight_grad()
        scatter.start_pairs(0)

    hooks = [
        lambda: fc1_weight_grad(0, 4), send_fc1_grad, hidden_two_back, middle_back,
        lambda: attend_back(0, 3), lambda: attend_back(3, 6), send_mixed_grad,
        finish_forward, finish_backward, finish_fc2, share_rows, own_sums, finish_fc1,
        share_back, finish_condition,
    ]
    for index, hook in enumerate(hooks):
        hook()
        scatter.turn(index + 1)
    total = scatter.finish_part(0)
    qkv_grad[...] = total[:, :qkv_part]
    proj_grad[...] = total[:, qkv_part:]
    store(3)
    store(4)
    scatter.wait_pairs_sent(1)
    scatter.wait_pairs_sent(0)
    scatter.wait_sends()
    gather.wait_sends()
    for swap in swaps:
        swap.wait_sends()
    for copy in stores:
        copy.wait()


def emit_kernel(*refs):
    small, wholes = refs[0], refs[1:8]
    cond_grad, rows_out, outs, held, sems = refs[8], refs[9:14], refs[14:21], refs[21:28], refs[28]
    loads = [
        pltpu.make_async_copy(whole, hold, sems.at[0, at])
        for at, (whole, hold) in enumerate(zip(wholes, held))]
    stores = [
        pltpu.make_async_copy(hold, out, sems.at[1, at])
        for at, (hold, out) in enumerate(zip(held, outs))]
    for load in loads:
        load.start()
    cond_grad[...] = small[:, :D]
    low = D
    for out in rows_out:
        width = out.shape[0]
        out[...] = small[0, low : low + width]
        low += round_up(width) if low == D else width
    for load, store in zip(loads, stores):
        load.wait()
        store.start()
    for store in stores:
        store.wait()


def emit(small, wholes, widths):
    vmem = pl.BlockSpec(memory_space=pltpu.VMEM)
    anywhere = pl.BlockSpec(memory_space=pl.ANY)
    count = len(wholes)
    return pl.pallas_call(
        emit_kernel,
        out_shape=[jax.ShapeDtypeStruct((1, D), jnp.float32)]
        + [jax.ShapeDtypeStruct((width,), jnp.float32) for width in widths]
        + [jax.ShapeDtypeStruct(whole.shape, whole.dtype) for whole in wholes],
        in_specs=[vmem] + [anywhere] * count,
        out_specs=[vmem] * (1 + len(widths)) + [anywhere] * count,
        scratch_shapes=[pltpu.VMEM(whole.shape, whole.dtype) for whole in wholes]
        + [pltpu.SemaphoreType.DMA((2, count))],
        name="emit",
    )(small, *wholes)


def run_layer(fc1_shard, fc2_turned_shard, sources, latent_count, rows, columns):
    latents, _, conditioning, ada_weight, _, qkv_shard, _, proj_shard = sources[:8]
    depth = columns // 2
    qkv_part, proj_part = qkv_shard.shape[1], proj_shard.shape[1]
    shards = (
        jax.ShapeDtypeStruct((qkv_shard.shape[0], qkv_part + proj_part), bfloat),
        fc1_shard, fc2_turned_shard)
    ada_rows, mod_width = ada_weight.shape
    cond_pad = round_up(ada_rows)
    bias_width = sum(sources[at].shape[0] for at in (6, 8, 9, 10))
    group = rows + bias_width // cond_pad
    count = (depth - 1) + depth * rows + depth * (rows - 1) + 2 * depth
    total = rows * columns
    mod_pad = round_up(mod_width)
    length = latents.shape[0]
    anywhere = pl.BlockSpec(memory_space=pl.ANY)
    dma = pltpu.SemaphoreType.DMA
    shapes = [
        whole_shape(shard.shape, part == 2, rows, columns) for part, shard in enumerate(shards)]
    row_buffer = lambda count, width: pltpu.VMEM((count, 1, width), jnp.float32)
    wide_row = lambda width: pltpu.VMEM((1, width), jnp.float32)
    single = lambda width: pltpu.VMEM((length, width), jnp.float32)
    half = lambda width: pltpu.VMEM((length, width), bfloat)
    turned = pltpu.VMEM((D, length), bfloat)
    rest = 128 * columns
    buffers = []
    for lead in ((depth, rows), (depth, 2), (depth, 2), (depth - 1,)):
        for shard in shards:
            height, width = shard.shape
            height = height // 2 if 6 <= len(buffers) < 9 else height
            buffers.append(pltpu.VMEM(lead + (height, width), bfloat))
    float_out = lambda *shape: jax.ShapeDtypeStruct(shape, jnp.float32)
    outs = [
        jax.ShapeDtypeStruct((length, D), bfloat),
        jax.ShapeDtypeStruct((length, D), bfloat),
        float_out(ada_rows, mod_width),
        float_out(qkv_shard.shape[0], qkv_part),
        float_out(qkv_shard.shape[0], proj_part),
        float_out(*fc1_shard.shape),
        float_out(*fc2_turned_shard.shape),
        float_out(1, D + mod_pad + bias_width),
    ]
    return pl.pallas_call(
        functools.partial(layer_kernel, rows, depth),
        out_shape=outs,
        in_specs=[anywhere] * 13 + [pl.BlockSpec(memory_space=pltpu.SMEM)],
        out_specs=[anywhere] * 8,
        scratch_shapes=[pltpu.VMEM(source.shape, source.dtype) for source in sources]
        + [pltpu.VMEM(out.shape, out.dtype) for out in outs]
        + [
            pltpu.VMEM(shards[0].shape, bfloat), row_buffer(rows, cond_pad), wide_row(D),
            dma((len(sources),)), dma((len(outs),)),
        ]
        + [pltpu.VMEM(shape, bfloat) for shape in shapes + shapes[:2]]
        + buffers + [
            dma((3, depth, rows)), dma((3, depth, rows)),
            dma((3, depth, 2)), dma((3, depth, 2)), dma((3, depth, 2)), dma((3, depth, 2)),
            dma((3, depth - 1)), dma((3, depth - 1)),
            dma((3,)), dma((3 * count,)), dma((2, 3, columns, rows)),
            dma((8, columns)), dma((8, columns)),
            row_buffer(rows, cond_pad), row_buffer(group, cond_pad),
            pltpu.VMEM((columns, group, 1, cond_pad), jnp.float32),
            pltpu.VMEM((total, cond_pad), jnp.float32),
            pltpu.VMEM((rows, columns, mod_pad), jnp.float32),
            pltpu.VMEM((rows, columns, mod_pad), jnp.float32),
            row_buffer(columns, mod_pad), row_buffer(columns, mod_pad),
            row_buffer(columns, mod_pad + bias_width), row_buffer(columns, mod_pad + bias_width),
            pltpu.VMEM((rows, columns, 1, mod_pad + bias_width), jnp.float32),
            pltpu.VMEM((rows, columns, cond_pad), jnp.float32),
            pltpu.VMEM((rows, columns, cond_pad), jnp.float32),
            pltpu.VMEM((columns, rows, 1, cond_pad), jnp.float32),
            pltpu.VMEM((columns, rows, 1, cond_pad), jnp.float32),
            wide_row(6 * D), wide_row(3 * D), wide_row(D), wide_row(FF), wide_row(D),
            wide_row(6 * D), wide_row(3 * D), wide_row(D), wide_row(FF), wide_row(D),
            single(1), single(1), single(D), single(D), single(D), single(D), single(FF),
            half(D), turned, half(D), turned, half(D), turned,
            half(D), turned, half(D), half(3 * D),
            half(rest), half(FF), half(FF), half(3 * D), single(D), pltpu.VMEM((HEADS, length, length), jnp.float32),
        ],
        compiler_params=pltpu.CompilerParams(
            collective_id=2, has_side_effects=True, vmem_limit_bytes=62 * 2**20),
        name="run_layer",
    )(fc1_shard, fc2_turned_shard, *sources, latent_count)


def pick(mixed, columns, kind):
    width = mixed.shape[1] // columns
    edge = 3 * width // 4
    low, high = (0, edge) if kind == 0 else (edge, width)
    return jnp.concatenate(
        [mixed[:, block * width + low : block * width + high] for block in range(columns)], axis=1
    )


def spread(rows_in, columns, kind):
    width = rows_in.shape[1] // columns
    rest = width // 3 if kind == 0 else 3 * width
    zeros = jnp.zeros((rows_in.shape[0], rest), rows_in.dtype)
    pieces = []
    for block in range(columns):
        piece = rows_in[:, block * width : (block + 1) * width]
        pieces += [piece, zeros] if kind == 0 else [zeros, piece]
    return jnp.concatenate(pieces, axis=1)


def layer(latent_rows, live, cot_rows, modulation, weights, biases, columns):
    mixed_weight, fc1_weight, fc2_turned = weights
    qv_bias, proj_bias, fc1_bias, fc2_bias = biases
    length = latent_rows.shape[0]
    rows_wide = latent_rows.astype(jnp.float32)
    shift_one, scale_one, gate_one, shift_two, scale_two, gate_two = jnp.split(
        modulation, 6, axis=-1
    )
    normed_one, inverse_one = normalize_rows(rows_wide)
    hidden_one = (normed_one * (1.0 + scale_one) + shift_one).astype(bfloat)
    qkv_bias = jnp.concatenate([qv_bias[:D], jnp.zeros((D,), jnp.float32), qv_bias[D:]])
    projected = (
        pick(jnp.dot(hidden_one, mixed_weight, preferred_element_type=jnp.float32), columns, 0)
        + qkv_bias
    ).astype(bfloat)
    queries = projected[:, :D].reshape(length, HEADS, HEAD)
    key_rows = projected[:, D : 2 * D].reshape(length, HEADS, HEAD)
    values = projected[:, 2 * D :].reshape(length, HEADS, HEAD)
    scale_factor = HEAD ** (-0.5)
    scores = (
        jnp.einsum("qhe,khe->hqk", queries, key_rows, preferred_element_type=jnp.float32)
        * scale_factor
    )
    row_max = jnp.max(scores, axis=-1, keepdims=True)
    shifted = jnp.exp(scores - row_max)
    row_total = jnp.sum(shifted, axis=-1, keepdims=True)
    exact_probability = shifted / row_total
    probability = exact_probability.astype(bfloat)
    attended = jnp.einsum("hqk,khe->qhe", probability, values, preferred_element_type=jnp.float32)
    attended = attended.reshape(length, D).astype(bfloat)
    branch = pick(jnp.dot(attended, mixed_weight, preferred_element_type=jnp.float32), columns, 1)
    branch = branch + proj_bias
    middle = rows_wide + gate_one * branch
    normed_two, inverse_two = normalize_rows(middle)
    hidden_two = (normed_two * (1.0 + scale_two) + shift_two).astype(bfloat)
    pre_gelu = jnp.dot(hidden_two, fc1_weight, preferred_element_type=jnp.float32) + fc1_bias
    activated, gelu_pull = jax.vjp(
        lambda argument: jax.nn.gelu(argument, approximate=True), pre_gelu
    )
    activated = activated.astype(bfloat)
    mlp_out = against_weight(activated, fc2_turned) + fc2_bias
    block_out = (live * (middle + gate_two * mlp_out)).astype(bfloat)

    grad_out = live * cot_rows.astype(jnp.float32)
    gate_two_grad = jnp.sum(grad_out * mlp_out, axis=0, keepdims=True)
    grad_mlp = (gate_two * grad_out).astype(bfloat)
    fc2_bias_grad = jnp.sum(grad_mlp.astype(jnp.float32), axis=0)
    grad_act = jnp.dot(grad_mlp, fc2_turned, preferred_element_type=jnp.float32)
    grad_pre = gelu_pull(grad_act)[0].astype(bfloat)
    fc1_bias_grad = jnp.sum(grad_pre.astype(jnp.float32), axis=0)
    grad_hidden_two = against_weight(grad_pre, fc1_weight)
    shift_two_grad = jnp.sum(grad_hidden_two, axis=0, keepdims=True)
    scale_two_grad = jnp.sum(grad_hidden_two * normed_two, axis=0, keepdims=True)
    grad_middle = grad_out + norm_backward(
        grad_hidden_two * (1.0 + scale_two), normed_two, inverse_two
    )
    gate_one_grad = jnp.sum(grad_middle * branch, axis=0, keepdims=True)
    grad_branch = (gate_one * grad_middle).astype(bfloat)
    proj_bias_grad = jnp.sum(grad_branch.astype(jnp.float32), axis=0)
    spread_branch = spread(grad_branch, columns, 1)
    grad_attended = (
        against_weight(spread_branch, mixed_weight).astype(bfloat).reshape(length, HEADS, HEAD)
    )
    grad_prob = jnp.einsum(
        "qhe,khe->hqk", grad_attended, values, preferred_element_type=jnp.float32
    )
    inner_sum = jnp.sum(exact_probability * grad_prob, axis=-1, keepdims=True)
    grad_scores = (exact_probability * (grad_prob - inner_sum)).astype(bfloat)
    grad_queries = (
        jnp.einsum("hqk,khe->qhe", grad_scores, key_rows, preferred_element_type=jnp.float32)
        * scale_factor
    )
    grad_keys = (
        jnp.einsum("hqk,qhe->khe", grad_scores, queries, preferred_element_type=jnp.float32)
        * scale_factor
    )
    grad_values = jnp.einsum(
        "hqk,qhe->khe", probability, grad_attended, preferred_element_type=jnp.float32
    )
    grad_projected = jnp.concatenate(
        [
            grad_queries.reshape(length, D),
            grad_keys.reshape(length, D),
            grad_values.reshape(length, D),
        ],
        axis=1,
    ).astype(bfloat)
    summed = jnp.sum(grad_projected.astype(jnp.float32), axis=0)
    qv_bias_grad = jnp.concatenate([summed[:D], summed[2 * D :]])
    spread_projected = spread(grad_projected, columns, 0)
    grad_hidden_one = against_weight(spread_projected, mixed_weight)
    shift_one_grad = jnp.sum(grad_hidden_one, axis=0, keepdims=True)
    scale_one_grad = jnp.sum(grad_hidden_one * normed_one, axis=0, keepdims=True)
    latent_grad = (
        grad_middle + norm_backward(grad_hidden_one * (1.0 + scale_one), normed_one, inverse_one)
    ).astype(bfloat)
    mod_grad = jnp.concatenate(
        [
            shift_one_grad,
            scale_one_grad,
            gate_one_grad,
            shift_two_grad,
            scale_two_grad,
            gate_two_grad,
        ],
        axis=-1,
    )
    weight_grads = (
        contract_rows(
            jnp.concatenate([hidden_one, attended]),
            jnp.concatenate([spread_projected, spread_branch]),
        ).astype(bfloat),
        contract_rows(hidden_two, grad_pre).astype(bfloat),
        contract_rows(grad_mlp, activated).astype(bfloat),
    )
    bias_grads = (qv_bias_grad, proj_bias_grad, fc1_bias_grad, fc2_bias_grad)
    return block_out, latent_grad, mod_grad, weight_grads, bias_grads


def flatten_blocks(blocks, turned):
    if blocks.ndim == 2:
        return blocks
    columns, rows, height, width = blocks.shape
    if turned:
        return blocks.transpose(0, 2, 1, 3).reshape(columns * height, rows * width)
    return blocks.transpose(1, 2, 0, 3).reshape(rows * height, columns * width)


def cut_blocks(whole, shape, turned, rows, columns):
    if len(whole_shape(shape, turned, rows, columns)) == 2:
        return whole
    height, width = shape
    if turned:
        return whole.reshape(columns, height, rows, width).transpose(0, 2, 1, 3)
    return whole.reshape(rows, height, columns, width).transpose(2, 0, 1, 3)


def per_device(
    latents,
    conditioning,
    cotangent,
    latent_count,
    ada_weight,
    ada_bias,
    qkv_weight,
    qv_bias,
    proj_weight,
    proj_bias,
    fc1_weight,
    fc1_bias,
    fc2_weight,
    fc2_bias,
):
    rows, columns = lax.axis_size("dp"), lax.axis_size("fsdp")
    if rows == 4 and columns == 8:
        sources = (
            latents[0], cotangent[0], conditioning, ada_weight, ada_bias, qkv_weight, qv_bias,
            proj_weight, proj_bias, fc1_bias, fc2_bias)
        *wholes, small = run_layer(
            fc1_weight, fc2_weight.T, sources, latent_count, rows, columns)
        widths = [bias.shape[0] for bias in (ada_bias, qv_bias, proj_bias, fc1_bias, fc2_bias)]
        (
            cond_grad, ada_bias_grad, qv_bias_grad, proj_bias_grad, fc1_bias_grad, fc2_bias_grad,
            block_out, latent_grad, ada_grad, qkv_grad, proj_grad, fc1_grad, fc2_turned_grad,
        ) = emit(small, wholes, widths)
        return (
            block_out[None], latent_grad[None], cond_grad, ada_grad, ada_bias_grad, qkv_grad,
            qv_bias_grad, proj_grad, proj_bias_grad, fc1_grad, fc1_bias_grad, fc2_turned_grad.T,
            fc2_bias_grad,
        )
    live = latent_count[0].astype(jnp.float32)
    depth = ada_weight.shape[0]
    mod_width = ada_weight.shape[1]
    mod_pad = round_up(mod_width)
    own_biases = (qv_bias, proj_bias, fc1_bias, fc2_bias)
    widths = [bias.shape[0] for bias in own_biases]
    cuts = [sum(widths[:place]) for place in range(len(widths))]

    def split_cond(row):
        pad = round_up(depth) - depth
        return jnp.pad(row.reshape(rows, 1, depth), ((0, 0), (0, 0), (0, pad)))

    cond_row = conditioning.astype(jnp.float32)
    cond_act, silu_pull = jax.vjp(jax.nn.silu, cond_row)
    slope = silu_pull(jnp.ones_like(cond_row))[0]
    cond_rows = split_cond(cond_act.astype(bfloat).astype(jnp.float32))
    bias_row = jnp.concatenate(own_biases).astype(jnp.float32).reshape(1, -1)

    qkv_width = qkv_weight.shape[1]
    shards = (
        jnp.concatenate([qkv_weight, proj_weight], axis=1),
        fc1_weight,
        fc2_weight.T,
    )
    shapes = [shard.shape for shard in shards]
    ada_row = ada_bias.astype(jnp.float32).reshape(1, -1)
    *blocks, mod_blocks, bias_blocks, cond_in = gather_shards(
        shards, cond_rows, ada_weight, ada_row, bias_row,
        rows, columns)
    modulation = mod_blocks[:, :, :mod_width].reshape(1, -1)
    biases = tuple(
        bias_blocks[:, :, cut : cut + width].reshape(-1) for cut, width in zip(cuts, widths)
    )
    weights = [flatten_blocks(block, part == 2) for part, block in enumerate(blocks)]
    block_out, latent_grad, mod_grad, weight_grads, bias_grads = layer(
        latents[0], live, cotangent[0], modulation, weights, biases, columns
    )
    grads = [
        cut_blocks(grad, shapes[part], part == 2, rows, columns)
        for part, grad in enumerate(weight_grads)
    ]
    leaving = jnp.concatenate(
        [jnp.pad(mod_grad.reshape(columns, -1), ((0, 0), (0, mod_pad - mod_width)))]
        + [grad.reshape(columns, -1) for grad in bias_grads], axis=1
    ).reshape(columns, 1, -1)
    mixed_grad, fc1_grad, fc2_turned_grad, ada_grad, sums, cond_grad = scatter_shards(
        grads, leaving, cond_in, ada_weight, split_cond(slope), shapes, rows, columns)
    qkv_grad, proj_grad = mixed_grad[:, :qkv_width], mixed_grad[:, qkv_width:]
    fc2_grad = fc2_turned_grad.T
    ada_bias_grad = sums[0, :mod_width]
    bias_sums = [
        sums[0, mod_pad + cut : mod_pad + cut + width] for cut, width in zip(cuts, widths)]
    cond_grad = cond_grad[:, :, :depth].reshape(1, -1)
    return (
        block_out[None],
        latent_grad[None],
        cond_grad,
        ada_grad,
        ada_bias_grad,
        qkv_grad,
        bias_sums[0],
        proj_grad,
        bias_sums[1],
        fc1_grad,
        bias_sums[2],
        fc2_grad,
        bias_sums[3],
    )


def solution(mesh):
    in_specs = (
        P(("dp", "fsdp"), None, None),
        P(("dp", "fsdp"), None),
        P(("dp", "fsdp"), None, None),
        P(("dp", "fsdp")),
        P("dp", "fsdp"),
        P("fsdp"),
        P("dp", "fsdp"),
        P("fsdp"),
        P("dp", "fsdp"),
        P("fsdp"),
        P("dp", "fsdp"),
        P("fsdp"),
        P("dp", "fsdp"),
        P("fsdp"),
    )
    out_specs = (
        P(("dp", "fsdp"), None, None),
        P(("dp", "fsdp"), None, None),
        P(("dp", "fsdp"), None),
        P("dp", "fsdp"),
        P("fsdp"),
        P("dp", "fsdp"),
        P("fsdp"),
        P("dp", "fsdp"),
        P("fsdp"),
        P("dp", "fsdp"),
        P("fsdp"),
        P("dp", "fsdp"),
        P("fsdp"),
    )
    return jax.shard_map(
        per_device, mesh=mesh, in_specs=in_specs, out_specs=out_specs, check_vma=False
    )
```

```python
import functools
import jax
import jax.numpy as jnp
from jax import lax
from jax.sharding import PartitionSpec as P
from jax.experimental import pallas as pl
from jax.experimental.pallas import tpu as pltpu

MESH_IDS = pl.DeviceIdType.MESH
D = 768
HEADS = 12
HEAD = 64
FF = 3072

highest = lax.Precision.HIGHEST
bfloat = jnp.bfloat16
LAG = 2
AHEAD = 3


def place(dp_index, z_index, core):
    return (dp_index, z_index * 2 + core)


def z_order(size):
    steps = [0]
    for distance in range(1, size // 2 + 1):
        steps.append(distance)
        if size - distance != distance:
            steps.append(size - distance)
    return steps


def device_of(index, columns):
    return (index // columns, lax.rem(index, columns))


def enter_barrier(me, rows, columns):
    barrier = pltpu.get_barrier_semaphore()
    count = rows * columns

    @pl.loop(1, count)
    def _(step):
        target = device_of(lax.rem(me + step, count), columns)
        pl.semaphore_signal(barrier, inc=1, device_id=target, device_id_type=MESH_IDS)

    pl.semaphore_wait(barrier, count - 1)


class Exchange:
    def __init__(self, me, rows, columns, row_for, landing, send_sems, recv_sems):
        self.me, self.columns, self.count = me, columns, rows * columns
        self.row_for, self.landing = row_for, landing
        self.send_sems, self.recv_sems = send_sems, recv_sems

    def start(self):
        @pl.loop(1, self.count)
        def _(step):
            target = lax.rem(self.me + step, self.count)
            pltpu.make_async_remote_copy(
                src_ref=self.row_for(target),
                dst_ref=self.landing.at[self.me],
                send_sem=self.send_sems.at[target],
                recv_sem=self.recv_sems.at[self.me],
                device_id=device_of(target, self.columns),
                device_id_type=MESH_IDS,
            ).start()

        self.landing[self.me] = self.row_for(self.me)[...]

    def pair(self, other):
        return pltpu.make_async_remote_copy(
            src_ref=self.row_for(other),
            dst_ref=self.landing.at[other],
            send_sem=self.send_sems.at[other],
            recv_sem=self.recv_sems.at[other],
            device_id=device_of(other, self.columns),
            device_id_type=MESH_IDS,
        )

    def wait_arrivals(self):
        @pl.loop(1, self.count)
        def _(step):
            self.pair(lax.rem(self.me + step, self.count)).wait_recv()

    def wait_sends(self):
        @pl.loop(1, self.count)
        def _(step):
            self.pair(lax.rem(self.me + step, self.count)).wait_send()


def positions(rows, depth):
    dp = lax.axis_index("dp")
    column = lax.axis_index("fsdp")
    z, core = column // 2, column % 2
    others = [(dp ^ 1), (dp ^ 2)] if rows == 4 else [(dp + step) % rows for step in range(1, rows)]
    return dp, z, core, others


def block_of(array, line, row, shape, turned):
    if len(array.shape) == 4:
        return array.at[line, row]
    high, wide = (line, row) if turned else (row, line)
    height, width = shape
    return array.at[
        pl.ds(pl.multiple_of(high * height, height), height),
        pl.ds(pl.multiple_of(wide * width, width), width),
    ]


def whole_shape(shape, turned, rows, columns):
    height, width = shape
    if width % 128 == 0 and height % 32 == 0:
        return (columns * height, rows * width) if turned else (rows * height, columns * width)
    return (columns, rows, height, width)


def gather_kernel(rows, depth, *refs):
    shards = refs[:3]
    cond_rows, ada_ref, ada_bias, bias_row = refs[3:7]
    outs, mod_out, bias_out, cond_in = refs[7:10], refs[10], refs[11], refs[12]
    (
        own_sems, send_sems, recv_sems, bias_in, part_out, part_in,
        cond_send, cond_recv, part_send, part_recv, bias_send, bias_recv,
    ) = refs[13:]
    dp, z, core, others = positions(rows, depth)
    columns = 2 * depth
    column = lax.axis_index("fsdp")
    me = dp * columns + column
    sibling = place(dp, z, 1 - core)
    enter_barrier(me, rows, columns)
    sends = []

    cond_swap = Exchange(
        me, rows, columns, lambda target: cond_rows.at[target // columns], cond_in,
        cond_send, cond_recv)
    part_swap = Exchange(
        me, rows, columns, lambda target: part_out.at[target], part_in, part_send, part_recv)
    cond_swap.start()

    def bias_copy(target, slot):
        return pltpu.make_async_remote_copy(
            src_ref=bias_row, dst_ref=bias_in.at[slot], send_sem=bias_send.at[target],
            recv_sem=bias_recv.at[slot], device_id=(dp, target), device_id_type=MESH_IDS)

    @pl.loop(1, columns)
    def _(step):
        bias_copy(lax.rem(column + step, columns), column).start()

    bias_in[column] = bias_row[...]

    def slot_of(part, line, row):
        return block_of(outs[part], line, row, shards[part].shape, part == 2)

    def half_of(ref, part, which):
        half = shards[part].shape[0] // 2
        return ref.at[pl.ds(which * half, half)]

    def send(line, row, target, which=None, own=False):
        for part in range(3):
            destination = slot_of(part, line, row)
            source = shards[part] if own else destination
            if which is not None:
                source, destination = half_of(source, part, which), half_of(destination, part, which)
            copy = pltpu.make_async_remote_copy(
                src_ref=source,
                dst_ref=destination,
                send_sem=send_sems.at[len(sends)],
                recv_sem=recv_sems.at[which or 0, part, line, row],
                device_id=target,
                device_id_type=MESH_IDS,
            )
            copy.start()
            sends.append(copy)

    def arrive(line, row, which=None):
        for part in range(3):
            destination = slot_of(part, line, row)
            if which is not None:
                destination = half_of(destination, part, which)
            pltpu.make_async_remote_copy(
                src_ref=destination,
                dst_ref=destination,
                send_sem=send_sems.at[0],
                recv_sem=recv_sems.at[which or 0, part, line, row],
                device_id=sibling,
                device_id_type=MESH_IDS,
            ).wait_recv()

    own = z * 2 + core
    steps = z_order(depth)
    lines = [((z - step) % depth) * 2 + core for step in steps]
    for other in others:
        send(own, dp, place(other, z, core), own=True)
    for step in steps[1:]:
        send(own, dp, place(dp, (z + step) % depth, core), own=True)
    send(own, dp, sibling, own=True)
    keeps = [
        pltpu.make_async_copy(shards[part], slot_of(part, own, dp), own_sems.at[part])
        for part in range(3)
    ]
    for keep in keeps:
        keep.start()
    cond_swap.wait_arrivals()
    high, wide = ada_ref.shape
    part = jnp.dot(
        cond_in[:, 0, :high].astype(bfloat), ada_ref[...], preferred_element_type=jnp.float32)
    part_out[:, 0, :wide] = part + jnp.where(dp == 0, ada_bias[...], 0.0)
    part_swap.start()
    for turn in range(depth + 2):
        if 0 < turn < depth:
            line = lines[turn]
            arrive(line, dp)
            for other in others:
                send(line, dp, place(other, z, core))
            send(line, dp, sibling)
        if 1 <= turn <= depth:
            line = lines[turn - 1]
            for position, other in enumerate(others):
                arrive(line, other)
                if rows == 4:
                    send(line, other, place(others[1 - position], z, core), which=position)
                send(line, other, sibling)
        if turn >= 2 and rows == 4:
            line = lines[turn - 2]
            arrive(line, dp ^ 3, 0)
            arrive(line, dp ^ 3, 1)
            send(line, dp ^ 3, sibling)
    for line in lines:
        for row in range(rows):
            arrive(line + 1 - 2 * core, (dp + row) % rows)
    part_swap.wait_arrivals()
    for block in range(columns):
        total = part_in[block]
        for row in range(1, rows):
            total = total + part_in[row * columns + block]
        mod_out[block] = total

    @pl.loop(1, columns)
    def _(step):
        other = lax.rem(column + step, columns)
        bias_copy(other, other).wait_recv()
        bias_copy(other, other).wait_send()

    bias_out[...] = bias_in[...]
    for keep in keeps:
        keep.wait()
    for copy in sends:
        copy.wait_send()
    cond_swap.wait_sends()
    part_swap.wait_sends()


def round_up(width):
    return -(-width // 128) * 128


def gather_shards(shards, cond_rows, ada_weight, ada_bias, bias_row, rows, columns):
    depth = columns // 2
    total = rows * columns
    mod_pad = round_up(ada_weight.shape[1])
    vmem = pl.BlockSpec(memory_space=pltpu.VMEM)
    dma = pltpu.SemaphoreType.DMA
    row_shape = lambda count, width: jax.ShapeDtypeStruct((count, 1, width), jnp.float32)
    row_buffer = lambda count, width: pltpu.VMEM((count, 1, width), jnp.float32)
    count = (depth - 1) + depth * rows + depth * (rows - 1) + (2 * depth if rows == 4 else 0)
    shapes = [
        whole_shape(shard.shape, part == 2, rows, columns) for part, shard in enumerate(shards)
    ]
    return pl.pallas_call(
        functools.partial(gather_kernel, rows, depth),
        out_shape=[jax.ShapeDtypeStruct(shape, bfloat) for shape in shapes]
        + [row_shape(columns, mod_pad), row_shape(columns, bias_row.shape[-1]),
           row_shape(total, cond_rows.shape[-1])],
        in_specs=[pl.BlockSpec(memory_space=pl.ANY)] * 3 + [vmem] * 4,
        out_specs=[pl.BlockSpec(memory_space=pl.ANY)] * 3 + [vmem] * 3,
        scratch_shapes=[
            dma((3,)),
            dma((3 * count,)),
            dma((2, 3, columns, rows)),
            row_buffer(columns, bias_row.shape[-1]),
            row_buffer(total, mod_pad),
            row_buffer(total, mod_pad),
            dma((total,)), dma((total,)), dma((total,)), dma((total,)),
            dma((columns,)), dma((columns,)),
        ],
        compiler_params=pltpu.CompilerParams(
            collective_id=0, has_side_effects=True, vmem_limit_bytes=32 * 2**20),
        name="gather_shards",
    )(*shards, cond_rows, ada_weight, ada_bias, bias_row)


def scatter_kernel(rows, depth, *refs):
    grads = refs[:3]
    leaving, cond_in, ada_ref, slope = refs[3:7]
    outs, ada_grad, sums_out, cond_grad = refs[7:10], refs[10], refs[11], refs[12]
    refs = refs[13:]
    helds, pairs_in, planes_in, crosses_in, alongs_in = (
        refs[3 * kind : 3 + 3 * kind] for kind in range(5)
    )
    (
        load_sems, pair_send, pair_recv, plane_send, plane_recv,
        cross_send, cross_recv, along_send, along_recv,
        all_rows, back_out, back_in, row_send, row_recv, back_send, back_recv,
    ) = refs[15:]
    dp, z, core, others = positions(rows, depth)
    columns = 2 * depth
    me = dp * columns + lax.axis_index("fsdp")
    row_swap = Exchange(
        me, rows, columns, lambda target: leaving.at[lax.rem(target, columns)], all_rows,
        row_send, row_recv)
    back_swap = Exchange(
        me, rows, columns, lambda target: back_out.at[target], back_in, back_send, back_recv)
    sibling = place(dp, z, 1 - core)
    targets = [dp ^ 3, dp ^ 1, dp ^ 2, dp] if rows == 4 else others + [dp]
    steps = z_order(depth)[::-1]
    enter_barrier(me, rows, columns)
    row_swap.start()
    waits = []

    def remote(source, destination, send_sem, recv_sem, target):
        copy = pltpu.make_async_remote_copy(
            src_ref=source, dst_ref=destination, send_sem=send_sem, recv_sem=recv_sem,
            device_id=target, device_id_type=MESH_IDS,
        )
        copy.start()
        waits.append(copy)
        return copy

    def add(first, others_in, length, target):
        chunk = 48 if length % 48 == 0 else 16

        @pl.loop(0, length // chunk)
        def _(index):
            piece = pl.ds(pl.multiple_of(index * chunk, chunk), chunk)
            total = first[piece, :].astype(jnp.float32)
            for other in others_in:
                total = total + other[piece, :].astype(jnp.float32)
            target[piece, :] = total.astype(target.dtype)

    lines = [(z + step) % depth for step in steps]
    pairs, loads, planes, crosses, alongs = {}, {}, {}, {}, {}
    for turn, line in enumerate(lines):
        for slot, target in enumerate(targets):
            for part in range(3):
                key = (part, turn, slot)
                shape = outs[part].shape
                pairs[key] = remote(
                    block_of(grads[part], line * 2 + 1 - core, target, shape, part == 2),
                    pairs_in[part].at[turn, slot], pair_send.at[key], pair_recv.at[key], sibling)
                loads[key] = pltpu.make_async_copy(
                    block_of(grads[part], line * 2 + core, target, shape, part == 2),
                    helds[part].at[turn, slot], load_sems.at[key])
                loads[key].start()
    last = len(targets) - 1
    for turn in range(depth + 2):
        if turn == depth - 1:
            row_swap.wait_arrivals()
            high, wide = ada_ref.shape
            arrived = all_rows[:, 0, :]
            sums_out[...] = jnp.sum(arrived, axis=0, keepdims=True)
            ada_grad[...] = contract_exact(cond_in[:, 0, :high], arrived[:, :wide])
            back_out[:, 0, :high] = lax.dot_general(
                arrived[:, :wide], ada_ref[...].astype(jnp.float32), (((1,), (1,)), ((), ())),
                precision=highest)
            back_swap.start()
        if turn < depth:
            for slot in range(len(targets)):
                for part in range(3):
                    key = (part, turn, slot)
                    height = outs[part].shape[0]
                    half = height // 2
                    loads[key].wait()
                    pairs[key].wait_recv()
                    here = helds[part].at[turn, slot]
                    add(here, [pairs_in[part].at[turn, slot]], height, here)
                    if rows == 4 and slot == 0:
                        for position in range(2):
                            key = (part, turn, position)
                            crosses[key] = remote(
                                helds[part].at[turn, 0, pl.ds((1 - position) * half, half)],
                                crosses_in[part].at[turn, position],
                                cross_send.at[key], cross_recv.at[key],
                                place(others[position], z, core))
                    if rows != 4 and slot < last:
                        planes[key] = remote(
                            here, planes_in[part].at[turn, slot], plane_send.at[key],
                            plane_recv.at[key], place(targets[slot], z, core))
        if rows == 4 and 1 <= turn <= depth:
            now = turn - 1
            for position in range(2):
                for part in range(3):
                    half = outs[part].shape[0] // 2
                    crosses[part, now, 1 - position].wait_recv()
                    piece = helds[part].at[now, 1 + position, pl.ds(position * half, half)]
                    add(piece, [crosses_in[part].at[now, 1 - position]], half, piece)
                    key = (part, now, position)
                    planes[key] = remote(
                        helds[part].at[now, 1 + position], planes_in[part].at[now, position],
                        plane_send.at[key], plane_recv.at[key],
                        place(others[position], z, core))
        if turn >= 2:
            now = turn - 2
            for part in range(3):
                for slot in range(len(others)):
                    planes[part, now, slot].wait_recv()
                here = helds[part].at[now, last]
                arrived = [planes_in[part].at[now, slot] for slot in range(len(others))]
                add(here, arrived, outs[part].shape[0], here)
                if now < depth - 1:
                    key = (part, now)
                    alongs[key] = remote(
                        here, alongs_in[part].at[now], along_send.at[key], along_recv.at[key],
                        place(dp, lines[now], core))
    for part in range(3):
        for now in range(depth - 1):
            alongs[part, now].wait_recv()
        arrived = [alongs_in[part].at[now] for now in range(depth - 1)]
        add(helds[part].at[depth - 1, last], arrived, outs[part].shape[0], outs[part])
    back_swap.wait_arrivals()
    for row in range(rows):
        total = back_in[row * columns]
        for block in range(1, columns):
            total = total + back_in[row * columns + block]
        cond_grad[row] = total * slope[row]
    for copy in waits:
        copy.wait_send()
    row_swap.wait_sends()
    back_swap.wait_sends()


def scatter_shards(grads, leaving, cond_in, ada_weight, slope, shapes, rows, columns):
    depth = columns // 2
    total = rows * columns
    vmem = pl.BlockSpec(memory_space=pltpu.VMEM)
    row_buffer = lambda count, width: pltpu.VMEM((count, 1, width), jnp.float32)
    peers = 2 if rows == 4 else rows - 1
    dma = pltpu.SemaphoreType.DMA
    buffers = []
    for lead in ((depth, rows), (depth, rows), (depth, peers), (depth, 2), (depth - 1,)):
        for height, width in shapes:
            if lead == (depth, 2) and len(buffers) >= 9:
                height = height // 2 if rows == 4 else 16
            buffers.append(pltpu.VMEM(lead + (height, width), bfloat))
    return pl.pallas_call(
        functools.partial(scatter_kernel, rows, depth),
        out_shape=[jax.ShapeDtypeStruct(shape, jnp.float32) for shape in shapes]
        + [jax.ShapeDtypeStruct(ada_weight.shape, jnp.float32),
           jax.ShapeDtypeStruct((1, leaving.shape[-1]), jnp.float32),
           jax.ShapeDtypeStruct(slope.shape, jnp.float32)],
        in_specs=[pl.BlockSpec(memory_space=pl.ANY)] * 3 + [vmem] * 4,
        out_specs=[vmem] * 6,
        scratch_shapes=buffers + [
            dma((3, depth, rows)), dma((3, depth, rows)), dma((3, depth, rows)),
            dma((3, depth, peers)), dma((3, depth, peers)),
            dma((3, depth, 2)), dma((3, depth, 2)),
            dma((3, depth - 1)), dma((3, depth - 1)),
            row_buffer(total, leaving.shape[-1]),
            row_buffer(total, slope.shape[-1]), row_buffer(total, slope.shape[-1]),
            dma((total,)), dma((total,)), dma((total,)), dma((total,)),
        ],
        compiler_params=pltpu.CompilerParams(
            collective_id=1, has_side_effects=True, vmem_limit_bytes=50 * 2**20),
        name="scatter_shards",
    )(*grads, leaving, cond_in, ada_weight, slope)


def normalize_rows(values):
    center = jnp.mean(values, axis=-1, keepdims=True)
    spread = jnp.mean(jnp.square(values - center), axis=-1, keepdims=True)
    inverse = lax.rsqrt(spread + 1e-06)
    return ((values - center) * inverse, inverse)


def norm_backward(grad_normed, normed, inverse):
    centered = grad_normed - jnp.mean(grad_normed, axis=-1, keepdims=True)
    return inverse * (centered - normed * jnp.mean(grad_normed * normed, axis=-1, keepdims=True))


def contract_rows(left_rows, right_rows):
    return lax.dot_general(
        left_rows, right_rows, (((0,), (0,)), ((), ())), preferred_element_type=jnp.float32
    )


def contract_exact(left_rows, right_rows):
    return lax.dot_general(left_rows, right_rows, (((0,), (0,)), ((), ())), precision=highest)


def against_weight(grad_rows, weight):
    return lax.dot_general(
        grad_rows, weight, (((1,), (1,)), ((), ())), preferred_element_type=jnp.float32
    )


def dot_plain(left, right):
    return jnp.dot(left, right, preferred_element_type=jnp.float32)


def columns_sum(values):
    return jnp.sum(values, axis=0, keepdims=True)


class Swap:
    def __init__(self, me, size, device, row_for, landing, send_sems, recv_sems):
        self.me, self.size, self.device = me, size, device
        self.row_for, self.landing = row_for, landing
        self.send_sems, self.recv_sems = send_sems, recv_sems
        self.copies = []

    def start(self):
        for step in range(1, self.size):
            other = lax.rem(self.me + step, self.size)
            copy = pltpu.make_async_remote_copy(
                src_ref=self.row_for(other),
                dst_ref=self.landing.at[self.me],
                send_sem=self.send_sems.at[step],
                recv_sem=self.recv_sems.at[step],
                device_id=self.device(other),
                device_id_type=MESH_IDS,
            )
            copy.start()
            self.copies.append(copy)
        self.landing[self.me] = self.row_for(self.me)[...]

    def wait_arrivals(self):
        for copy in self.copies:
            copy.wait_recv()

    def wait_sends(self):
        for copy in self.copies:
            copy.wait_send()


class Gather:
    def __init__(self, rows, depth, where, shards, outs, own_sems, send_sems, recv_sems):
        self.rows, self.depth = rows, depth
        self.dp, self.z, self.core, self.others = where
        self.shards, self.outs = shards, outs
        self.own_sems, self.send_sems, self.recv_sems = own_sems, send_sems, recv_sems
        self.sibling = place(self.dp, self.z, 1 - self.core)
        self.sends = []
        self.keeps = []
        self.own = self.z * 2 + self.core
        self.steps = [0] + list(range(2, depth)) + [1]
        self.lines = [(self.z ^ step) * 2 + self.core for step in self.steps]
        self.units = [(part, turn) for part in range(3) for turn in range(depth)]
        self.helped = depth - 1

    def slot_of(self, part, line, row):
        return block_of(self.outs[part], line, row, self.shards[part].shape, part == 2)

    def half_of(self, ref, part, which):
        half = self.shards[part].shape[0] // 2
        return ref.at[pl.ds(which * half, half)]

    def send(self, part, line, row, target, which=None, own=False):
        destination = self.slot_of(part, line, row)
        source = self.shards[part] if own else destination
        if which is not None:
            source, destination = (
                self.half_of(source, part, which), self.half_of(destination, part, which))
        copy = pltpu.make_async_remote_copy(
            src_ref=source,
            dst_ref=destination,
            send_sem=self.send_sems.at[len(self.sends)],
            recv_sem=self.recv_sems.at[which or 0, part, line, row],
            device_id=target,
            device_id_type=MESH_IDS,
        )
        copy.start()
        self.sends.append(copy)

    def arrive(self, part, line, row, which=None):
        destination = self.slot_of(part, line, row)
        if which is not None:
            destination = self.half_of(destination, part, which)
        pltpu.make_async_remote_copy(
            src_ref=destination,
            dst_ref=destination,
            send_sem=self.send_sems.at[0],
            recv_sem=self.recv_sems.at[which or 0, part, line, row],
            device_id=self.sibling,
            device_id_type=MESH_IDS,
        ).wait_recv()

    def send_own(self, part):
        for other in self.others:
            self.send(part, self.own, self.dp, place(other, self.z, self.core), own=True)
        self.send(part, self.own, self.dp, self.sibling, own=True)
        keep = pltpu.make_async_copy(
            self.shards[part], self.slot_of(part, self.own, self.dp), self.own_sems.at[part])
        keep.start()
        self.keeps.append(keep)

    def send_deep(self, index):
        if index < len(self.units):
            part, turn = self.units[index]
            if turn:
                target = place(self.dp, self.z ^ self.steps[turn], self.core)
                self.send(part, self.own, self.dp, target, own=True)

    def turn(self, index):
        dp, z, core = self.dp, self.z, self.core
        count = len(self.units)
        self.send_deep(index + AHEAD)
        if index in (1, 2):
            self.send_own(index)
        if index < count:
            part, turn = self.units[index]
            line = self.lines[turn]
            if turn:
                self.arrive(part, line, dp)
                which = 0 if turn == self.helped else None
                for other in self.others:
                    self.send(part, line, dp, place(other, z, core), which=which)
                self.send(part, line, dp, self.sibling)
        if LAG <= index < count + LAG:
            part, turn = self.units[index - LAG]
            line = self.lines[turn]
            for position, other in enumerate(self.others):
                if turn == self.helped:
                    self.arrive(part, line, other, 0)
                    self.arrive(part, line, other, 1)
                else:
                    self.arrive(part, line, other)
                    self.send(
                        part, line, other, place(self.others[1 - position], z, core),
                        which=position)
                if turn == 0:
                    self.send(part, line, other, place(dp, z ^ 1, core), which=1)
                self.send(part, line, other, self.sibling)
        if 2 * LAG <= index:
            part, turn = self.units[index - 2 * LAG]
            line = self.lines[turn]
            if turn == self.helped:
                self.arrive(part, line, dp ^ 3)
            else:
                self.arrive(part, line, dp ^ 3, 0)
                self.arrive(part, line, dp ^ 3, 1)
            if turn == 0:
                self.send(part, line, dp ^ 3, place(dp, z ^ 1, core))
            self.send(part, line, dp ^ 3, self.sibling)

    def finish_part(self, part):
        for line in self.lines:
            for row in range(self.rows):
                self.arrive(part, line + 1 - 2 * self.core, (self.dp + row) % self.rows)
        self.keeps[part].wait()

    def wait_sends(self):
        for copy in self.sends:
            copy.wait_send()


class Scatter:
    def __init__(self, rows, depth, where, shapes, grads, buffers, sems):
        self.rows, self.depth, self.shapes, self.grads = rows, depth, shapes, grads
        self.dp, self.z, self.core, self.others = where
        (
            self.held, self.planes_in, self.crosses_in, self.alongs_in, self.help_in, self.half_in,
        ) = (buffers[3 * kind : 3 * kind + 3] for kind in range(6))
        (
            self.pair_send, self.pair_recv, self.plane_send, self.plane_recv,
            self.cross_send, self.cross_recv, self.along_send, self.along_recv,
            self.help_send, self.help_recv,
        ) = sems
        self.sibling = place(self.dp, self.z, 1 - self.core)
        self.targets = [self.dp ^ 3, self.dp ^ 1, self.dp ^ 2, self.dp]
        self.lines = [self.z ^ step for step in [1] + list(range(2, depth))[::-1] + [0]]
        self.units = [(part, turn) for part in (2, 1, 0) for turn in range(depth)]
        self.pairs, self.planes, self.crosses, self.alongs, self.helps = {}, {}, {}, {}, {}

    def remote(self, source, destination, send_sem, recv_sem, target):
        copy = pltpu.make_async_remote_copy(
            src_ref=source, dst_ref=destination, send_sem=send_sem, recv_sem=recv_sem,
            device_id=target, device_id_type=MESH_IDS)
        copy.start()
        return copy

    def block(self, part, line, target):
        return block_of(self.grads[part], line, target, self.shapes[part], part == 2)

    def add(self, first, others_in, length, target):
        chunk = 48

        @pl.loop(0, length // chunk)
        def _(index):
            piece = pl.ds(pl.multiple_of(index * chunk, chunk), chunk)
            total = first[piece, :].astype(jnp.float32)
            for other in others_in:
                total = total + other[piece, :].astype(jnp.float32)
            target[piece, :] = total.astype(target.dtype)

    def help(self, part, slot, source, destination):
        self.helps[part, slot] = self.remote(
            source, destination, self.help_send.at[part, slot], self.help_recv.at[part, slot],
            place(self.dp, self.z ^ 1, self.core))

    def start_pairs(self, part):
        for turn, line in enumerate(self.lines):
            for slot, target in enumerate(self.targets):
                key = (part, turn, slot)
                self.pairs[key] = self.remote(
                    self.block(part, line * 2 + 1 - self.core, target),
                    self.held[part].at[turn, slot], self.pair_send.at[key],
                    self.pair_recv.at[key], self.sibling)

    def wait_pairs_sent(self, part):
        for turn in range(self.depth):
            for slot in range(self.rows):
                self.pairs[part, turn, slot].wait_send()

    def turn(self, index):
        last = self.rows - 1
        count = len(self.units)
        if index < count:
            part, turn = self.units[index]
            height = self.shapes[part][0]
            half = height // 2
            for slot, target in enumerate(self.targets):
                self.pairs[part, turn, slot].wait_recv()
                here = self.held[part].at[turn, slot]
                own = self.block(part, self.lines[turn] * 2 + self.core, target)
                arrived = [here]
                if turn == self.depth - 1 and slot == 0:
                    self.helps[part, 0].wait_recv()
                    arrived.append(self.help_in[part])
                self.add(own, arrived, height, here)
                if turn == self.depth - 1 and slot in (1, 2):
                    self.helps[part, slot].wait_recv()
                    piece = self.held[part].at[turn, slot, pl.ds(half, half)]
                    self.add(piece, [self.half_in[part].at[slot - 1]], half, piece)
                if turn == 0 and slot == 0:
                    self.help(part, 0, here, self.help_in[part])
                elif turn == 0 and slot < 3:
                    self.help(
                        part, slot, self.held[part].at[turn, slot, pl.ds(half, half)],
                        self.half_in[part].at[slot - 1])
                    key = (part, turn, slot - 1)
                    self.planes[key] = self.remote(
                        self.held[part].at[turn, slot, pl.ds(0, half)],
                        self.planes_in[part].at[turn, slot - 1, pl.ds(0, half)],
                        self.plane_send.at[key], self.plane_recv.at[key],
                        place(self.others[slot - 1], self.z, self.core))
                elif slot == 0:
                    for position in range(2):
                        key = (part, turn, position)
                        self.crosses[key] = self.remote(
                            self.held[part].at[turn, 0, pl.ds((1 - position) * half, half)],
                            self.crosses_in[part].at[turn, position],
                            self.cross_send.at[key], self.cross_recv.at[key],
                            place(self.others[position], self.z, self.core))
        if LAG <= index < count + LAG:
            part, turn = self.units[index - LAG]
            half = self.shapes[part][0] // 2
            for position in range(2 if turn else 0):
                self.crosses[part, turn, 1 - position].wait_recv()
                piece = self.held[part].at[turn, 1 + position, pl.ds(position * half, half)]
                self.add(piece, [self.crosses_in[part].at[turn, 1 - position]], half, piece)
                key = (part, turn, position)
                self.planes[key] = self.remote(
                    self.held[part].at[turn, 1 + position], self.planes_in[part].at[turn, position],
                    self.plane_send.at[key], self.plane_recv.at[key],
                    place(self.others[position], self.z, self.core))
        if 2 * LAG <= index:
            part, turn = self.units[index - 2 * LAG]
            for position in range(2):
                self.planes[part, turn, position].wait_recv()
            height = self.shapes[part][0] if turn else self.shapes[part][0] // 2
            here = self.held[part].at[turn, last]
            piece = self.held[part].at[turn, last, pl.ds(0, height)]
            arrived = [
                self.planes_in[part].at[turn, position, pl.ds(0, height)] for position in range(2)]
            self.add(piece, arrived, height, piece)
            if turn < self.depth - 1:
                key = (part, turn)
                self.alongs[key] = self.remote(
                    here, self.alongs_in[part].at[turn], self.along_send.at[key],
                    self.along_recv.at[key], place(self.dp, self.lines[turn], self.core))

    def finish_part(self, part):
        total = self.held[part][self.depth - 1, self.rows - 1].astype(jnp.float32)
        for turn in range(self.depth - 1):
            self.alongs[part, turn].wait_recv()
            total = total + self.alongs_in[part][turn].astype(jnp.float32)
        return total

    def wait_sends(self):
        for copies in (self.planes, self.crosses, self.alongs, self.helps):
            for copy in copies.values():
                copy.wait_send()


def layer_kernel(rows, depth, *refs):
    sources, live_ref, outs = refs[2:13], refs[13], refs[14:22]
    landed = refs[22:33]
    results = landed[:2] + refs[33:39]
    (
        latents, cotangent, conditioning, ada_ref, ada_bias, qkv_shard, qv_shard, proj_shard,
        proj_bias_shard, fc1_bias_shard, fc2_bias_shard,
    ) = landed
    block_out, latent_grad, ada_grad, qkv_grad, proj_grad, fc1_grad, fc2_grad, small = results
    mixed_shard, cond_rows, slope, load_sems, store_sems = refs[39:44]
    shards = (mixed_shard, refs[0], refs[1])
    refs = refs[44:]
    weights, grads = refs[:3], (refs[3], refs[4], refs[3])
    scatter_buffers, scatter_sems = refs[5:23], refs[23:33]
    (
        own_sems, send_sems, recv_sems, swap_send, swap_recv,
        cond_across, cond_own, cond_along, cond_in, part_out, part_across, part_row, part_along,
        leaving, rows_along, rows_across, back_out, back_across, back_row, back_along,
        mod, qkv_bias, proj_bias, fc1_bias, fc2_bias, mod_grad, qkv_sums, proj_sums, fc1_sums,
        fc2_sums, inverse_one, inverse_two, normed_one, normed_two, middle, branch, wide,
        hidden_one, hidden_one_t, hidden_two, hidden_two_t, attended, attended_t,
        grad_mlp, grad_mlp_t, projected,
        grad_proj_mixed, activated, grad_pre, grad_natural, grad_state, probability,
    ) = refs[33:]
    grad_mixed, grad_attended = grad_pre, hidden_one
    mixed, fc1, fc2_turned = weights
    where = positions(rows, depth)
    dp = where[0]
    columns = 2 * depth
    column = lax.axis_index("fsdp")
    length = latents.shape[0]
    qkv_part, proj_part = 3 * D // columns, D // columns
    block = qkv_part + proj_part
    edge = qkv_part // 128 * 128
    rest = block - edge
    lead = qkv_part - edge
    scale_factor = HEAD ** (-0.5)
    ada_rows, mod_width = ada_ref.shape
    mod_pad = round_up(mod_width)
    loads = [
        pltpu.make_async_copy(source, target, load_sems.at[at])
        for at, (source, target) in enumerate(zip(sources, landed))]
    for at in (2, 5, 7, 6, 8, 9, 10, 0, 3, 4, 1):
        loads[at].start()
    stores = []

    def store(at):
        copy = pltpu.make_async_copy(results[at], outs[at], store_sems.at[at])
        copy.start()
        stores.append(copy)

    barrier = pltpu.get_barrier_semaphore()
    partners = [(lax.rem(dp + step, rows), column) for step in range(1, rows)]
    partners += [(dp, lax.rem(column + step, columns)) for step in range(1, columns)]
    for partner in partners:
        pl.semaphore_signal(barrier, inc=1, device_id=partner, device_id_type=MESH_IDS)
    live = live_ref[0].astype(jnp.float32)
    loads[2].wait()
    cond_value = conditioning[...].astype(jnp.float32)
    logistic = 1.0 / (1.0 + jnp.exp(-cond_value))
    slope[...] = logistic * (1.0 + cond_value * (1.0 - logistic))
    cond_act = (cond_value * logistic).astype(bfloat).astype(jnp.float32)
    for row in range(rows):
        cond_rows[row, :, :ada_rows] = cond_act[:, row * ada_rows : (row + 1) * ada_rows]
    pl.semaphore_wait(barrier, len(partners))
    gather = Gather(rows, depth, where, shards, weights, own_sems, send_sems, recv_sems)
    scatter = Scatter(
        rows, depth, where, [shard.shape for shard in shards], grads, scatter_buffers, scatter_sems)
    swaps = []

    def swap_across(row_for, landing):
        at = len(swaps)
        swaps.append(Swap(
            dp, rows, lambda other: (other, column), row_for, landing,
            swap_send.at[at], swap_recv.at[at]))
        return swaps[-1]

    def swap_along(row_for, landing):
        at = len(swaps)
        swaps.append(Swap(
            column, columns, lambda other: (dp, other), row_for, landing,
            swap_send.at[at], swap_recv.at[at]))
        return swaps[-1]

    cond_first = swap_across(
        lambda other: cond_rows.at[other], cond_across)
    cond_second = swap_along(lambda other: cond_own, cond_along)
    part_first = swap_across(lambda other: part_out.at[other], part_across)
    part_second = swap_along(lambda other: part_row.at[other], part_along)
    rows_first = swap_along(lambda other: leaving.at[other], rows_along)
    rows_second = swap_across(lambda other: rows_along, rows_across)
    back_first = swap_across(lambda other: back_out.at[other], back_across)
    back_second = swap_along(lambda other: back_row.at[other], back_along)
    cond_first.start()
    loads[5].wait()
    loads[7].wait()
    mixed_shard[:, :qkv_part] = qkv_shard[...]
    mixed_shard[:, qkv_part:] = proj_shard[...]
    for index in range(AHEAD):
        gather.send_deep(index)
    gather.send_own(0)

    def piece(kind):
        return mod[:, kind * D : (kind + 1) * D]

    def share_condition():
        cond_first.wait_arrivals()
        cond_own[:rows] = cond_across[...]
        bias_row = []
        for at in (6, 8, 9, 10):
            loads[at].wait()
            bias_row.append(landed[at][...].astype(jnp.float32).reshape(1, -1))
        bias_row = jnp.concatenate(bias_row, axis=1)
        pad = cond_own.shape[-1]
        for at in range(bias_row.shape[1] // pad):
            cond_own[rows + at] = bias_row[:, at * pad : (at + 1) * pad]
        cond_second.start()

    def start_modulation():
        cond_second.wait_arrivals()
        cond_in[...] = jnp.concatenate(
            [cond_along[source, row] for row in range(rows) for source in range(columns)], axis=0)
        loads[3].wait()
        loads[4].wait()
        part = dot_plain(cond_in[:, :ada_rows].astype(bfloat), ada_ref[...])
        own_bias = ada_bias[...].astype(jnp.float32).reshape(1, -1)
        part = part + jnp.where(dp == 0, own_bias, 0.0)
        for row in range(rows):
            part_out[row, :, :mod_width] = part[row * columns : (row + 1) * columns]
        part_first.start()

    def sum_modulation():
        part_first.wait_arrivals()
        total = part_across[0]
        for row in range(1, rows):
            total = total + part_across[row]
        part_row[:, 0, :] = total
        part_second.start()

    def normalize_first():
        loads[0].wait()
        normed, inverse = normalize_rows(latents[...].astype(jnp.float32))
        normed_one[...] = normed
        inverse_one[...] = inverse

    def finish_modulation():
        part_second.wait_arrivals()
        mod[...] = jnp.concatenate(
            [part_along[source][:, :mod_width] for source in range(columns)], axis=1)
        bias_parts = [
            jnp.concatenate(
                [cond_along[source, row] for row in range(rows, cond_along.shape[1])], axis=1)
            for source in range(columns)]
        low = 0
        naturals = []
        for width in (2 * D // columns, D // columns, FF // columns, D // columns):
            naturals.append(jnp.concatenate(
                [part[:, low : low + width] for part in bias_parts], axis=1))
            low += width
        qkv_bias[:, :D] = naturals[0][:, :D]
        qkv_bias[:, D : 2 * D] = jnp.zeros((1, D), jnp.float32)
        qkv_bias[:, 2 * D :] = naturals[0][:, D:]
        proj_bias[...] = naturals[1]
        fc1_bias[...] = naturals[2]
        fc2_bias[...] = naturals[3]
        hidden = (normed_one[...] * (1.0 + piece(1)) + piece(0)).astype(bfloat)
        hidden_one[...] = hidden
        hidden_one_t[...] = hidden.T

    def start_gradient():
        loads[1].wait()
        grad = (piece(5) * (live * cotangent[...].astype(jnp.float32))).astype(bfloat)
        grad_mlp[...] = grad
        grad_mlp_t[...] = grad.T
        fc2_sums[...] = columns_sum(grad.astype(jnp.float32))

    def span(index, width):
        return pl.ds(pl.multiple_of(index * width, width), width)

    def project():
        @pl.loop(0, columns)
        def _(index):
            wide[:, span(index, block)] = dot_plain(hidden_one[...], mixed[:, span(index, block)])

        for index in range(columns):
            natural = slice(index * qkv_part, (index + 1) * qkv_part)
            projected[:, natural] = (
                wide[:, index * block : index * block + qkv_part] + qkv_bias[:, natural]
            ).astype(bfloat)

    def head_slabs(source, pair):
        return [
            source[:, pl.ds(pl.multiple_of(kind * D + pair * 128, 128), 128)] for kind in range(3)]

    def own_lanes(which):
        lane = lax.broadcasted_iota(jnp.int32, (length, 128), 1)
        return lane < HEAD if which == 0 else lane >= HEAD

    def attend(low, high):
        @pl.loop(low, high)
        def _(pair):
            queries, keys, values = head_slabs(projected, pair)
            zero = jnp.zeros_like(queries)
            results = []
            for which in range(2):
                scores = against_weight(
                    jnp.where(own_lanes(which), queries, zero), keys) * scale_factor
                shifted = jnp.exp(scores - jnp.max(scores, axis=-1, keepdims=True))
                exact = shifted / jnp.sum(shifted, axis=-1, keepdims=True)
                probability[2 * pair + which] = exact
                results.append(dot_plain(exact.astype(bfloat), values))
            attended[:, span(pair, 128)] = jnp.where(
                own_lanes(0), results[0], results[1]).astype(bfloat)

    def finish_attention():
        attended_t[...] = attended[...].T

        @pl.loop(0, columns)
        def _(index):
            tail = pl.ds(pl.multiple_of(index * block + edge, 128), rest)
            wide[:, span(index, rest)] = dot_plain(attended[...], mixed[:, tail])

        for index in range(columns):
            natural = slice(index * proj_part, (index + 1) * proj_part)
            branch[:, natural] = (
                wide[:, index * rest + lead : (index + 1) * rest] + proj_bias[:, natural])
        total = latents[...].astype(jnp.float32) + piece(2) * branch[...]
        middle[...] = total
        normed, inverse = normalize_rows(total)
        normed_two[...] = normed
        inverse_two[...] = inverse
        hidden = (normed * (1.0 + piece(4)) + piece(3)).astype(bfloat)
        hidden_two[...] = hidden
        hidden_two_t[...] = hidden.T

    chunk = 384
    chunks = FF // chunk

    def expand(low, high):
        @pl.loop(low, high)
        def _(index):
            part = span(index, chunk)
            value = dot_plain(hidden_two[...], fc1[:, part]) + fc1_bias[:, part]
            root = 0.7978845608028654
            square = value * value
            bend = jnp.tanh(root * (value + 0.044715 * (square * value)))
            activated[:, part] = (0.5 * value * (1.0 + bend)).astype(bfloat)
            wide[:, part] = 0.5 * (1.0 + bend) + 0.5 * value * (1.0 - bend * bend) * (
                root * (1.0 + 3 * 0.044715 * square))

    def fc2_weight_grad(low, high):
        @pl.loop(low, high)
        def _(index):
            part = span(index, chunk)
            grads[2][:, part] = dot_plain(grad_mlp_t[...], activated[:, part]).astype(bfloat)

    def after_part_zero():
        gather.finish_part(0)
        project()

    def after_part_one():
        gather.finish_part(1)
        expand(0, 4)

    def send_fc2_grad():
        fc2_weight_grad(4, 8)
        scatter.start_pairs(2)

    hooks = [
        share_condition, normalize_first, start_modulation, None, sum_modulation, None,
        finish_modulation, start_gradient, after_part_zero, lambda: attend(0, 3),
        lambda: attend(3, 6), finish_attention, after_part_one, lambda: expand(4, 8),
        lambda: fc2_weight_grad(0, 4), send_fc2_grad,
    ]
    for index, hook in enumerate(hooks):
        gather.turn(index)
        if hook is not None:
            hook()
    scatter.turn(0)
    gather.finish_part(2)
    third = 256

    def finish_forward():
        @pl.loop(0, D // third)
        def _(index):
            part = span(index, third)
            branch_part = against_weight(activated[...], fc2_turned[part, :]) + fc2_bias[:, part]
            live_grad = live * cotangent[:, part].astype(jnp.float32)
            last = pl.ds(pl.multiple_of(5 * D + index * third, third), third)
            block_out[:, part] = (
                live * (middle[:, part] + mod[:, last] * branch_part)).astype(bfloat)
            mod_grad[:, last] = columns_sum(live_grad * branch_part)

        store(0)

    def fc1_weight_grad(low, high):
        @pl.loop(low, high)
        def _(index):
            part = span(index, chunk)
            grad = (dot_plain(grad_mlp[...], fc2_turned[:, part]) * wide[:, part]).astype(bfloat)
            grad_pre[:, part] = grad
            fc1_sums[:, part] = columns_sum(grad.astype(jnp.float32))
            grads[1][:, part] = dot_plain(hidden_two_t[...], grad).astype(bfloat)

    def hidden_two_back():
        @pl.loop(0, D // third)
        def _(index):
            part = span(index, third)
            grad_state[:, part] = against_weight(grad_pre[...], fc1[part, :])

    def middle_back():
        grad_hidden = grad_state[...]
        mod_grad[:, 3 * D : 4 * D] = columns_sum(grad_hidden)
        mod_grad[:, 4 * D : 5 * D] = columns_sum(grad_hidden * normed_two[...])
        grad_middle = live * cotangent[...].astype(jnp.float32) + norm_backward(
            grad_hidden * (1.0 + piece(4)), normed_two[...], inverse_two[...])
        mod_grad[:, 2 * D : 3 * D] = columns_sum(grad_middle * branch[...])
        grad_state[...] = grad_middle
        grad_branch = (piece(2) * grad_middle).astype(bfloat)
        proj_sums[...] = columns_sum(grad_branch.astype(jnp.float32))
        for index in range(columns):
            grad_proj_mixed[:, index * rest : index * rest + lead] = jnp.zeros(
                (length, lead), bfloat)
            grad_proj_mixed[:, index * rest + lead : (index + 1) * rest] = (
                grad_branch[:, index * proj_part : (index + 1) * proj_part])
        total = None
        for index in range(columns):
            term = against_weight(
                grad_proj_mixed[:, index * rest : (index + 1) * rest],
                mixed[:, index * block + edge : (index + 1) * block])
            total = term if total is None else total + term
        grad_attended[...] = total.astype(bfloat)

    def attend_back(low, high):
        @pl.loop(low, high)
        def _(pair):
            queries, keys, values = head_slabs(projected, pair)
            grad_out = grad_attended[:, span(pair, 128)]
            zero = jnp.zeros_like(grad_out)
            results = []
            for which in range(2):
                exact = probability[2 * pair + which]
                grad_prob = against_weight(jnp.where(own_lanes(which), grad_out, zero), values)
                inner = jnp.sum(exact * grad_prob, axis=-1, keepdims=True)
                grad_scores = (exact * (grad_prob - inner)).astype(bfloat)
                results.append((
                    dot_plain(grad_scores, keys) * scale_factor,
                    contract_rows(grad_scores, queries) * scale_factor,
                    contract_rows(exact.astype(bfloat), grad_out)))
            for kind in range(3):
                grad_natural[:, pl.ds(pl.multiple_of(kind * D + pair * 128, 128), 128)] = jnp.where(
                    own_lanes(0), results[0][kind], results[1][kind]).astype(bfloat)

    def mixed_weight_grad():
        qkv_sums[...] = columns_sum(grad_natural[...].astype(jnp.float32))
        for index in range(columns):
            grad_mixed[:, index * block : index * block + qkv_part] = (
                grad_natural[:, index * qkv_part : (index + 1) * qkv_part])
            grad_mixed[:, index * block + qkv_part : (index + 1) * block] = jnp.zeros(
                (length, proj_part), bfloat)
        scatter.wait_pairs_sent(2)

        @pl.loop(0, columns)
        def _(index):
            low = pl.multiple_of(index * block, 128)
            grads[0][:, pl.ds(low, edge)] = dot_plain(
                hidden_one_t[...], grad_mixed[:, pl.ds(low, edge)]).astype(bfloat)
            tail = pl.ds(pl.multiple_of(index * block + edge, 128), rest)
            grads[0][:, tail] = (
                dot_plain(hidden_one_t[...], grad_mixed[:, tail])
                + dot_plain(attended_t[...], grad_proj_mixed[:, span(index, rest)])).astype(bfloat)

    def finish_backward():
        @pl.loop(0, D // third)
        def _(index):
            part = span(index, third)
            branch[:, part] = against_weight(grad_mixed[...], mixed[part, :])

        grad_hidden = branch[...]
        mod_grad[:, :D] = columns_sum(grad_hidden)
        mod_grad[:, D : 2 * D] = columns_sum(grad_hidden * normed_one[...])
        latent_grad[...] = (grad_state[...] + norm_backward(
            grad_hidden * (1.0 + piece(1)), normed_one[...], inverse_one[...])).astype(bfloat)
        store(1)
        pad = jnp.zeros((1, mod_pad - mod_width), jnp.float32)
        qv_sums = jnp.concatenate([qkv_sums[:, :D], qkv_sums[:, 2 * D :]], axis=1)
        rows_of = (qv_sums, proj_sums[...], fc1_sums[...], fc2_sums[...])
        every = mod_grad[...]
        for index in range(columns):
            pieces = [every[:, index * mod_width : (index + 1) * mod_width], pad]
            for row in rows_of:
                share = row.shape[1] // columns
                pieces.append(row[:, index * share : (index + 1) * share])
            leaving[index] = jnp.concatenate(pieces, axis=1)
        rows_first.start()

    def share_rows():
        rows_first.wait_arrivals()
        rows_second.start()

    def own_sums():
        rows_second.wait_arrivals()
        arrived = jnp.concatenate([rows_across[row, :, 0, :] for row in range(rows)], axis=0)
        small[:, D:] = columns_sum(arrived)
        ada_grad[...] = contract_exact(cond_in[:, :ada_rows], arrived[:, :mod_width])
        store(2)
        back = lax.dot_general(
            arrived[:, :mod_width], ada_ref[...].astype(jnp.float32), (((1,), (1,)), ((), ())),
            precision=highest)
        for row in range(rows):
            back_out[row, :, :ada_rows] = back[row * columns : (row + 1) * columns]
        back_first.start()

    def share_back():
        back_first.wait_arrivals()
        for row in range(rows):
            back_row[:, row, 0, :] = back_across[row]
        back_second.start()

    def finish_condition():
        back_second.wait_arrivals()
        total = back_along[0]
        for source in range(1, columns):
            total = total + back_along[source]
        small[:, :D] = jnp.concatenate(
            [total[row][:, :ada_rows] for row in range(rows)], axis=1) * slope[...]
        store(7)

    def finish_fc2():
        fc2_grad[...] = scatter.finish_part(2)
        store(6)

    def finish_fc1():
        fc1_grad[...] = scatter.finish_part(1)
        store(5)

    def send_fc1_grad():
        fc1_weight_grad(4, 8)
        scatter.start_pairs(1)

    def send_mixed_grad():
        mixed_weight_grad()
        scatter.start_pairs(0)

    hooks = [
        lambda: fc1_weight_grad(0, 4), send_fc1_grad, hidden_two_back, middle_back,
        lambda: attend_back(0, 3), lambda: attend_back(3, 6), send_mixed_grad,
        finish_forward, finish_backward, finish_fc2, share_rows, own_sums, finish_fc1,
        share_back, finish_condition,
    ]
    for index, hook in enumerate(hooks):
        hook()
        scatter.turn(index + 1)
    total = scatter.finish_part(0)
    qkv_grad[...] = total[:, :qkv_part]
    proj_grad[...] = total[:, qkv_part:]
    store(3)
    store(4)
    scatter.wait_pairs_sent(1)
    scatter.wait_pairs_sent(0)
    scatter.wait_sends()
    gather.wait_sends()
    for swap in swaps:
        swap.wait_sends()
    for copy in stores:
        copy.wait()


def emit_kernel(*refs):
    small, wholes = refs[0], refs[1:8]
    cond_grad, rows_out, outs, held, sems = refs[8], refs[9:14], refs[14:21], refs[21:28], refs[28]
    loads = [
        pltpu.make_async_copy(whole, hold, sems.at[0, at])
        for at, (whole, hold) in enumerate(zip(wholes, held))]
    stores = [
        pltpu.make_async_copy(hold, out, sems.at[1, at])
        for at, (hold, out) in enumerate(zip(held, outs))]
    for load in loads:
        load.start()
    cond_grad[...] = small[:, :D]
    low = D
    for out in rows_out:
        width = out.shape[0]
        out[...] = small[0, low : low + width]
        low += round_up(width) if low == D else width
    for load, store in zip(loads, stores):
        load.wait()
        store.start()
    for store in stores:
        store.wait()


def emit(small, wholes, widths):
    vmem = pl.BlockSpec(memory_space=pltpu.VMEM)
    anywhere = pl.BlockSpec(memory_space=pl.ANY)
    count = len(wholes)
    return pl.pallas_call(
        emit_kernel,
        out_shape=[jax.ShapeDtypeStruct((1, D), jnp.float32)]
        + [jax.ShapeDtypeStruct((width,), jnp.float32) for width in widths]
        + [jax.ShapeDtypeStruct(whole.shape, whole.dtype) for whole in wholes],
        in_specs=[vmem] + [anywhere] * count,
        out_specs=[vmem] * (1 + len(widths)) + [anywhere] * count,
        scratch_shapes=[pltpu.VMEM(whole.shape, whole.dtype) for whole in wholes]
        + [pltpu.SemaphoreType.DMA((2, count))],
        name="emit",
    )(small, *wholes)


def run_layer(fc1_shard, fc2_turned_shard, sources, latent_count, rows, columns):
    latents, _, conditioning, ada_weight, _, qkv_shard, _, proj_shard = sources[:8]
    depth = columns // 2
    qkv_part, proj_part = qkv_shard.shape[1], proj_shard.shape[1]
    shards = (
        jax.ShapeDtypeStruct((qkv_shard.shape[0], qkv_part + proj_part), bfloat),
        fc1_shard, fc2_turned_shard)
    ada_rows, mod_width = ada_weight.shape
    cond_pad = round_up(ada_rows)
    bias_width = sum(sources[at].shape[0] for at in (6, 8, 9, 10))
    group = rows + bias_width // cond_pad
    count = (depth - 1) + depth * rows + depth * (rows - 1) + 2 * depth
    total = rows * columns
    mod_pad = round_up(mod_width)
    length = latents.shape[0]
    anywhere = pl.BlockSpec(memory_space=pl.ANY)
    dma = pltpu.SemaphoreType.DMA
    shapes = [
        whole_shape(shard.shape, part == 2, rows, columns) for part, shard in enumerate(shards)]
    row_buffer = lambda count, width: pltpu.VMEM((count, 1, width), jnp.float32)
    wide_row = lambda width: pltpu.VMEM((1, width), jnp.float32)
    single = lambda width: pltpu.VMEM((length, width), jnp.float32)
    half = lambda width: pltpu.VMEM((length, width), bfloat)
    turned = pltpu.VMEM((D, length), bfloat)
    rest = 128 * columns
    buffers = []
    for lead in ((depth, rows), (depth, 2), (depth, 2), (depth - 1,), (), (2,)):
        for shard in shards:
            height, width = shard.shape
            height = height // 2 if len(buffers) // 3 in (2, 5) else height
            buffers.append(pltpu.VMEM(lead + (height, width), bfloat))
    float_out = lambda *shape: jax.ShapeDtypeStruct(shape, jnp.float32)
    outs = [
        jax.ShapeDtypeStruct((length, D), bfloat),
        jax.ShapeDtypeStruct((length, D), bfloat),
        float_out(ada_rows, mod_width),
        float_out(qkv_shard.shape[0], qkv_part),
        float_out(qkv_shard.shape[0], proj_part),
        float_out(*fc1_shard.shape),
        float_out(*fc2_turned_shard.shape),
        float_out(1, D + mod_pad + bias_width),
    ]
    return pl.pallas_call(
        functools.partial(layer_kernel, rows, depth),
        out_shape=outs,
        in_specs=[anywhere] * 13 + [pl.BlockSpec(memory_space=pltpu.SMEM)],
        out_specs=[anywhere] * 8,
        scratch_shapes=[pltpu.VMEM(source.shape, source.dtype) for source in sources]
        + [pltpu.VMEM(out.shape, out.dtype) for out in outs[2:]]
        + [
            pltpu.VMEM(shards[0].shape, bfloat), row_buffer(rows, cond_pad), wide_row(D),
            dma((len(sources),)), dma((len(outs),)),
        ]
        + [pltpu.VMEM(shape, bfloat) for shape in shapes + shapes[:2]]
        + buffers + [
            dma((3, depth, rows)), dma((3, depth, rows)),
            dma((3, depth, 2)), dma((3, depth, 2)), dma((3, depth, 2)), dma((3, depth, 2)),
            dma((3, depth - 1)), dma((3, depth - 1)), dma((3, 3)), dma((3, 3)),
            dma((3,)), dma((3 * count,)), dma((2, 3, columns, rows)),
            dma((8, columns)), dma((8, columns)),
            row_buffer(rows, cond_pad), row_buffer(group, cond_pad),
            pltpu.VMEM((columns, group, 1, cond_pad), jnp.float32),
            pltpu.VMEM((total, cond_pad), jnp.float32),
            pltpu.VMEM((rows, columns, mod_pad), jnp.float32),
            pltpu.VMEM((rows, columns, mod_pad), jnp.float32),
            row_buffer(columns, mod_pad), row_buffer(columns, mod_pad),
            row_buffer(columns, mod_pad + bias_width), row_buffer(columns, mod_pad + bias_width),
            pltpu.VMEM((rows, columns, 1, mod_pad + bias_width), jnp.float32),
            pltpu.VMEM((rows, columns, cond_pad), jnp.float32),
            pltpu.VMEM((rows, columns, cond_pad), jnp.float32),
            pltpu.VMEM((columns, rows, 1, cond_pad), jnp.float32),
            pltpu.VMEM((columns, rows, 1, cond_pad), jnp.float32),
            wide_row(6 * D), wide_row(3 * D), wide_row(D), wide_row(FF), wide_row(D),
            wide_row(6 * D), wide_row(3 * D), wide_row(D), wide_row(FF), wide_row(D),
            single(1), single(1), single(D), single(D), single(D), single(D), single(FF),
            half(D), turned, half(D), turned, half(D), turned,
            half(D), turned, half(3 * D),
            half(rest), half(FF), half(FF), half(3 * D), single(D), pltpu.VMEM((HEADS, length, length), jnp.float32),
        ],
        compiler_params=pltpu.CompilerParams(
            collective_id=2, has_side_effects=True, vmem_limit_bytes=62 * 2**20),
        name="run_layer",
    )(fc1_shard, fc2_turned_shard, *sources, latent_count)


def pick(mixed, columns, kind):
    width = mixed.shape[1] // columns
    edge = 3 * width // 4
    low, high = (0, edge) if kind == 0 else (edge, width)
    return jnp.concatenate(
        [mixed[:, block * width + low : block * width + high] for block in range(columns)], axis=1
    )


def spread(rows_in, columns, kind):
    width = rows_in.shape[1] // columns
    rest = width // 3 if kind == 0 else 3 * width
    zeros = jnp.zeros((rows_in.shape[0], rest), rows_in.dtype)
    pieces = []
    for block in range(columns):
        piece = rows_in[:, block * width : (block + 1) * width]
        pieces += [piece, zeros] if kind == 0 else [zeros, piece]
    return jnp.concatenate(pieces, axis=1)


def layer(latent_rows, live, cot_rows, modulation, weights, biases, columns):
    mixed_weight, fc1_weight, fc2_turned = weights
    qv_bias, proj_bias, fc1_bias, fc2_bias = biases
    length = latent_rows.shape[0]
    rows_wide = latent_rows.astype(jnp.float32)
    shift_one, scale_one, gate_one, shift_two, scale_two, gate_two = jnp.split(
        modulation, 6, axis=-1
    )
    normed_one, inverse_one = normalize_rows(rows_wide)
    hidden_one = (normed_one * (1.0 + scale_one) + shift_one).astype(bfloat)
    qkv_bias = jnp.concatenate([qv_bias[:D], jnp.zeros((D,), jnp.float32), qv_bias[D:]])
    projected = (
        pick(jnp.dot(hidden_one, mixed_weight, preferred_element_type=jnp.float32), columns, 0)
        + qkv_bias
    ).astype(bfloat)
    queries = projected[:, :D].reshape(length, HEADS, HEAD)
    key_rows = projected[:, D : 2 * D].reshape(length, HEADS, HEAD)
    values = projected[:, 2 * D :].reshape(length, HEADS, HEAD)
    scale_factor = HEAD ** (-0.5)
    scores = (
        jnp.einsum("qhe,khe->hqk", queries, key_rows, preferred_element_type=jnp.float32)
        * scale_factor
    )
    row_max = jnp.max(scores, axis=-1, keepdims=True)
    shifted = jnp.exp(scores - row_max)
    row_total = jnp.sum(shifted, axis=-1, keepdims=True)
    exact_probability = shifted / row_total
    probability = exact_probability.astype(bfloat)
    attended = jnp.einsum("hqk,khe->qhe", probability, values, preferred_element_type=jnp.float32)
    attended = attended.reshape(length, D).astype(bfloat)
    branch = pick(jnp.dot(attended, mixed_weight, preferred_element_type=jnp.float32), columns, 1)
    branch = branch + proj_bias
    middle = rows_wide + gate_one * branch
    normed_two, inverse_two = normalize_rows(middle)
    hidden_two = (normed_two * (1.0 + scale_two) + shift_two).astype(bfloat)
    pre_gelu = jnp.dot(hidden_two, fc1_weight, preferred_element_type=jnp.float32) + fc1_bias
    activated, gelu_pull = jax.vjp(
        lambda argument: jax.nn.gelu(argument, approximate=True), pre_gelu
    )
    activated = activated.astype(bfloat)
    mlp_out = against_weight(activated, fc2_turned) + fc2_bias
    block_out = (live * (middle + gate_two * mlp_out)).astype(bfloat)

    grad_out = live * cot_rows.astype(jnp.float32)
    gate_two_grad = jnp.sum(grad_out * mlp_out, axis=0, keepdims=True)
    grad_mlp = (gate_two * grad_out).astype(bfloat)
    fc2_bias_grad = jnp.sum(grad_mlp.astype(jnp.float32), axis=0)
    grad_act = jnp.dot(grad_mlp, fc2_turned, preferred_element_type=jnp.float32)
    grad_pre = gelu_pull(grad_act)[0].astype(bfloat)
    fc1_bias_grad = jnp.sum(grad_pre.astype(jnp.float32), axis=0)
    grad_hidden_two = against_weight(grad_pre, fc1_weight)
    shift_two_grad = jnp.sum(grad_hidden_two, axis=0, keepdims=True)
    scale_two_grad = jnp.sum(grad_hidden_two * normed_two, axis=0, keepdims=True)
    grad_middle = grad_out + norm_backward(
        grad_hidden_two * (1.0 + scale_two), normed_two, inverse_two
    )
    gate_one_grad = jnp.sum(grad_middle * branch, axis=0, keepdims=True)
    grad_branch = (gate_one * grad_middle).astype(bfloat)
    proj_bias_grad = jnp.sum(grad_branch.astype(jnp.float32), axis=0)
    spread_branch = spread(grad_branch, columns, 1)
    grad_attended = (
        against_weight(spread_branch, mixed_weight).astype(bfloat).reshape(length, HEADS, HEAD)
    )
    grad_prob = jnp.einsum(
        "qhe,khe->hqk", grad_attended, values, preferred_element_type=jnp.float32
    )
    inner_sum = jnp.sum(exact_probability * grad_prob, axis=-1, keepdims=True)
    grad_scores = (exact_probability * (grad_prob - inner_sum)).astype(bfloat)
    grad_queries = (
        jnp.einsum("hqk,khe->qhe", grad_scores, key_rows, preferred_element_type=jnp.float32)
        * scale_factor
    )
    grad_keys = (
        jnp.einsum("hqk,qhe->khe", grad_scores, queries, preferred_element_type=jnp.float32)
        * scale_factor
    )
    grad_values = jnp.einsum(
        "hqk,qhe->khe", probability, grad_attended, preferred_element_type=jnp.float32
    )
    grad_projected = jnp.concatenate(
        [
            grad_queries.reshape(length, D),
            grad_keys.reshape(length, D),
            grad_values.reshape(length, D),
        ],
        axis=1,
    ).astype(bfloat)
    summed = jnp.sum(grad_projected.astype(jnp.float32), axis=0)
    qv_bias_grad = jnp.concatenate([summed[:D], summed[2 * D :]])
    spread_projected = spread(grad_projected, columns, 0)
    grad_hidden_one = against_weight(spread_projected, mixed_weight)
    shift_one_grad = jnp.sum(grad_hidden_one, axis=0, keepdims=True)
    scale_one_grad = jnp.sum(grad_hidden_one * normed_one, axis=0, keepdims=True)
    latent_grad = (
        grad_middle + norm_backward(grad_hidden_one * (1.0 + scale_one), normed_one, inverse_one)
    ).astype(bfloat)
    mod_grad = jnp.concatenate(
        [
            shift_one_grad,
            scale_one_grad,
            gate_one_grad,
            shift_two_grad,
            scale_two_grad,
            gate_two_grad,
        ],
        axis=-1,
    )
    weight_grads = (
        contract_rows(
            jnp.concatenate([hidden_one, attended]),
            jnp.concatenate([spread_projected, spread_branch]),
        ).astype(bfloat),
        contract_rows(hidden_two, grad_pre).astype(bfloat),
        contract_rows(grad_mlp, activated).astype(bfloat),
    )
    bias_grads = (qv_bias_grad, proj_bias_grad, fc1_bias_grad, fc2_bias_grad)
    return block_out, latent_grad, mod_grad, weight_grads, bias_grads


def flatten_blocks(blocks, turned):
    if blocks.ndim == 2:
        return blocks
    columns, rows, height, width = blocks.shape
    if turned:
        return blocks.transpose(0, 2, 1, 3).reshape(columns * height, rows * width)
    return blocks.transpose(1, 2, 0, 3).reshape(rows * height, columns * width)


def cut_blocks(whole, shape, turned, rows, columns):
    if len(whole_shape(shape, turned, rows, columns)) == 2:
        return whole
    height, width = shape
    if turned:
        return whole.reshape(columns, height, rows, width).transpose(0, 2, 1, 3)
    return whole.reshape(rows, height, columns, width).transpose(2, 0, 1, 3)


def per_device(
    latents,
    conditioning,
    cotangent,
    latent_count,
    ada_weight,
    ada_bias,
    qkv_weight,
    qv_bias,
    proj_weight,
    proj_bias,
    fc1_weight,
    fc1_bias,
    fc2_weight,
    fc2_bias,
):
    rows, columns = lax.axis_size("dp"), lax.axis_size("fsdp")
    if rows == 4 and columns == 8:
        sources = (
            latents[0], cotangent[0], conditioning, ada_weight, ada_bias, qkv_weight, qv_bias,
            proj_weight, proj_bias, fc1_bias, fc2_bias)
        *wholes, small = run_layer(
            fc1_weight, fc2_weight.T, sources, latent_count, rows, columns)
        widths = [bias.shape[0] for bias in (ada_bias, qv_bias, proj_bias, fc1_bias, fc2_bias)]
        (
            cond_grad, ada_bias_grad, qv_bias_grad, proj_bias_grad, fc1_bias_grad, fc2_bias_grad,
            block_out, latent_grad, ada_grad, qkv_grad, proj_grad, fc1_grad, fc2_turned_grad,
        ) = emit(small, wholes, widths)
        return (
            block_out[None], latent_grad[None], cond_grad, ada_grad, ada_bias_grad, qkv_grad,
            qv_bias_grad, proj_grad, proj_bias_grad, fc1_grad, fc1_bias_grad, fc2_turned_grad.T,
            fc2_bias_grad,
        )
    live = latent_count[0].astype(jnp.float32)
    depth = ada_weight.shape[0]
    mod_width = ada_weight.shape[1]
    mod_pad = round_up(mod_width)
    own_biases = (qv_bias, proj_bias, fc1_bias, fc2_bias)
    widths = [bias.shape[0] for bias in own_biases]
    cuts = [sum(widths[:place]) for place in range(len(widths))]

    def split_cond(row):
        pad = round_up(depth) - depth
        return jnp.pad(row.reshape(rows, 1, depth), ((0, 0), (0, 0), (0, pad)))

    cond_row = conditioning.astype(jnp.float32)
    cond_act, silu_pull = jax.vjp(jax.nn.silu, cond_row)
    slope = silu_pull(jnp.ones_like(cond_row))[0]
    cond_rows = split_cond(cond_act.astype(bfloat).astype(jnp.float32))
    bias_row = jnp.concatenate(own_biases).astype(jnp.float32).reshape(1, -1)

    qkv_width = qkv_weight.shape[1]
    shards = (
        jnp.concatenate([qkv_weight, proj_weight], axis=1),
        fc1_weight,
        fc2_weight.T,
    )
    shapes = [shard.shape for shard in shards]
    ada_row = ada_bias.astype(jnp.float32).reshape(1, -1)
    *blocks, mod_blocks, bias_blocks, cond_in = gather_shards(
        shards, cond_rows, ada_weight, ada_row, bias_row,
        rows, columns)
    modulation = mod_blocks[:, :, :mod_width].reshape(1, -1)
    biases = tuple(
        bias_blocks[:, :, cut : cut + width].reshape(-1) for cut, width in zip(cuts, widths)
    )
    weights = [flatten_blocks(block, part == 2) for part, block in enumerate(blocks)]
    block_out, latent_grad, mod_grad, weight_grads, bias_grads = layer(
        latents[0], live, cotangent[0], modulation, weights, biases, columns
    )
    grads = [
        cut_blocks(grad, shapes[part], part == 2, rows, columns)
        for part, grad in enumerate(weight_grads)
    ]
    leaving = jnp.concatenate(
        [jnp.pad(mod_grad.reshape(columns, -1), ((0, 0), (0, mod_pad - mod_width)))]
        + [grad.reshape(columns, -1) for grad in bias_grads], axis=1
    ).reshape(columns, 1, -1)
    mixed_grad, fc1_grad, fc2_turned_grad, ada_grad, sums, cond_grad = scatter_shards(
        grads, leaving, cond_in, ada_weight, split_cond(slope), shapes, rows, columns)
    qkv_grad, proj_grad = mixed_grad[:, :qkv_width], mixed_grad[:, qkv_width:]
    fc2_grad = fc2_turned_grad.T
    ada_bias_grad = sums[0, :mod_width]
    bias_sums = [
        sums[0, mod_pad + cut : mod_pad + cut + width] for cut, width in zip(cuts, widths)]
    cond_grad = cond_grad[:, :, :depth].reshape(1, -1)
    return (
        block_out[None],
        latent_grad[None],
        cond_grad,
        ada_grad,
        ada_bias_grad,
        qkv_grad,
        bias_sums[0],
        proj_grad,
        bias_sums[1],
        fc1_grad,
        bias_sums[2],
        fc2_grad,
        bias_sums[3],
    )


def solution(mesh):
    in_specs = (
        P(("dp", "fsdp"), None, None),
        P(("dp", "fsdp"), None),
        P(("dp", "fsdp"), None, None),
        P(("dp", "fsdp")),
        P("dp", "fsdp"),
        P("fsdp"),
        P("dp", "fsdp"),
        P("fsdp"),
        P("dp", "fsdp"),
        P("fsdp"),
        P("dp", "fsdp"),
        P("fsdp"),
        P("dp", "fsdp"),
        P("fsdp"),
    )
    out_specs = (
        P(("dp", "fsdp"), None, None),
        P(("dp", "fsdp"), None, None),
        P(("dp", "fsdp"), None),
        P("dp", "fsdp"),
        P("fsdp"),
        P("dp", "fsdp"),
        P("fsdp"),
        P("dp", "fsdp"),
        P("fsdp"),
        P("dp", "fsdp"),
        P("fsdp"),
        P("dp", "fsdp"),
        P("fsdp"),
    )
    return jax.shard_map(
        per_device, mesh=mesh, in_specs=in_specs, out_specs=out_specs, check_vma=False
    )
```

```python
import functools
import jax
import jax.numpy as jnp
from jax import lax
from jax.sharding import PartitionSpec as P
from jax.experimental import pallas as pl
from jax.experimental.pallas import tpu as pltpu

MESH_IDS = pl.DeviceIdType.MESH
D = 768
HEADS = 12
HEAD = 64
FF = 3072

highest = lax.Precision.HIGHEST
bfloat = jnp.bfloat16
LAG = 2
AHEAD = 3


def place(dp_index, z_index, core):
    return (dp_index, z_index * 2 + core)


def z_order(size):
    steps = [0]
    for distance in range(1, size // 2 + 1):
        steps.append(distance)
        if size - distance != distance:
            steps.append(size - distance)
    return steps


def device_of(index, columns):
    return (index // columns, lax.rem(index, columns))


def enter_barrier(me, rows, columns):
    barrier = pltpu.get_barrier_semaphore()
    count = rows * columns

    @pl.loop(1, count)
    def _(step):
        target = device_of(lax.rem(me + step, count), columns)
        pl.semaphore_signal(barrier, inc=1, device_id=target, device_id_type=MESH_IDS)

    pl.semaphore_wait(barrier, count - 1)


class Exchange:
    def __init__(self, me, rows, columns, row_for, landing, send_sems, recv_sems):
        self.me, self.columns, self.count = me, columns, rows * columns
        self.row_for, self.landing = row_for, landing
        self.send_sems, self.recv_sems = send_sems, recv_sems

    def start(self):
        @pl.loop(1, self.count)
        def _(step):
            target = lax.rem(self.me + step, self.count)
            pltpu.make_async_remote_copy(
                src_ref=self.row_for(target),
                dst_ref=self.landing.at[self.me],
                send_sem=self.send_sems.at[target],
                recv_sem=self.recv_sems.at[self.me],
                device_id=device_of(target, self.columns),
                device_id_type=MESH_IDS,
            ).start()

        self.landing[self.me] = self.row_for(self.me)[...]

    def pair(self, other):
        return pltpu.make_async_remote_copy(
            src_ref=self.row_for(other),
            dst_ref=self.landing.at[other],
            send_sem=self.send_sems.at[other],
            recv_sem=self.recv_sems.at[other],
            device_id=device_of(other, self.columns),
            device_id_type=MESH_IDS,
        )

    def wait_arrivals(self):
        @pl.loop(1, self.count)
        def _(step):
            self.pair(lax.rem(self.me + step, self.count)).wait_recv()

    def wait_sends(self):
        @pl.loop(1, self.count)
        def _(step):
            self.pair(lax.rem(self.me + step, self.count)).wait_send()


def positions(rows, depth):
    dp = lax.axis_index("dp")
    column = lax.axis_index("fsdp")
    z, core = column // 2, column % 2
    others = [(dp ^ 1), (dp ^ 2)] if rows == 4 else [(dp + step) % rows for step in range(1, rows)]
    return dp, z, core, others


def block_of(array, line, row, shape, turned):
    if len(array.shape) == 4:
        return array.at[line, row]
    high, wide = (line, row) if turned else (row, line)
    height, width = shape
    return array.at[
        pl.ds(pl.multiple_of(high * height, height), height),
        pl.ds(pl.multiple_of(wide * width, width), width),
    ]


def whole_shape(shape, turned, rows, columns):
    height, width = shape
    if width % 128 == 0 and height % 32 == 0:
        return (columns * height, rows * width) if turned else (rows * height, columns * width)
    return (columns, rows, height, width)


def gather_kernel(rows, depth, *refs):
    shards = refs[:3]
    cond_rows, ada_ref, ada_bias, bias_row = refs[3:7]
    outs, mod_out, bias_out, cond_in = refs[7:10], refs[10], refs[11], refs[12]
    (
        own_sems, send_sems, recv_sems, bias_in, part_out, part_in,
        cond_send, cond_recv, part_send, part_recv, bias_send, bias_recv,
    ) = refs[13:]
    dp, z, core, others = positions(rows, depth)
    columns = 2 * depth
    column = lax.axis_index("fsdp")
    me = dp * columns + column
    sibling = place(dp, z, 1 - core)
    enter_barrier(me, rows, columns)
    sends = []

    cond_swap = Exchange(
        me, rows, columns, lambda target: cond_rows.at[target // columns], cond_in,
        cond_send, cond_recv)
    part_swap = Exchange(
        me, rows, columns, lambda target: part_out.at[target], part_in, part_send, part_recv)
    cond_swap.start()

    def bias_copy(target, slot):
        return pltpu.make_async_remote_copy(
            src_ref=bias_row, dst_ref=bias_in.at[slot], send_sem=bias_send.at[target],
            recv_sem=bias_recv.at[slot], device_id=(dp, target), device_id_type=MESH_IDS)

    @pl.loop(1, columns)
    def _(step):
        bias_copy(lax.rem(column + step, columns), column).start()

    bias_in[column] = bias_row[...]

    def slot_of(part, line, row):
        return block_of(outs[part], line, row, shards[part].shape, part == 2)

    def half_of(ref, part, which):
        half = shards[part].shape[0] // 2
        return ref.at[pl.ds(which * half, half)]

    def send(line, row, target, which=None, own=False):
        for part in range(3):
            destination = slot_of(part, line, row)
            source = shards[part] if own else destination
            if which is not None:
                source, destination = half_of(source, part, which), half_of(destination, part, which)
            copy = pltpu.make_async_remote_copy(
                src_ref=source,
                dst_ref=destination,
                send_sem=send_sems.at[len(sends)],
                recv_sem=recv_sems.at[which or 0, part, line, row],
                device_id=target,
                device_id_type=MESH_IDS,
            )
            copy.start()
            sends.append(copy)

    def arrive(line, row, which=None):
        for part in range(3):
            destination = slot_of(part, line, row)
            if which is not None:
                destination = half_of(destination, part, which)
            pltpu.make_async_remote_copy(
                src_ref=destination,
                dst_ref=destination,
                send_sem=send_sems.at[0],
                recv_sem=recv_sems.at[which or 0, part, line, row],
                device_id=sibling,
                device_id_type=MESH_IDS,
            ).wait_recv()

    own = z * 2 + core
    steps = z_order(depth)
    lines = [((z - step) % depth) * 2 + core for step in steps]
    for other in others:
        send(own, dp, place(other, z, core), own=True)
    for step in steps[1:]:
        send(own, dp, place(dp, (z + step) % depth, core), own=True)
    send(own, dp, sibling, own=True)
    keeps = [
        pltpu.make_async_copy(shards[part], slot_of(part, own, dp), own_sems.at[part])
        for part in range(3)
    ]
    for keep in keeps:
        keep.start()
    cond_swap.wait_arrivals()
    high, wide = ada_ref.shape
    part = jnp.dot(
        cond_in[:, 0, :high].astype(bfloat), ada_ref[...], preferred_element_type=jnp.float32)
    part_out[:, 0, :wide] = part + jnp.where(dp == 0, ada_bias[...], 0.0)
    part_swap.start()
    for turn in range(depth + 2):
        if 0 < turn < depth:
            line = lines[turn]
            arrive(line, dp)
            for other in others:
                send(line, dp, place(other, z, core))
            send(line, dp, sibling)
        if 1 <= turn <= depth:
            line = lines[turn - 1]
            for position, other in enumerate(others):
                arrive(line, other)
                if rows == 4:
                    send(line, other, place(others[1 - position], z, core), which=position)
                send(line, other, sibling)
        if turn >= 2 and rows == 4:
            line = lines[turn - 2]
            arrive(line, dp ^ 3, 0)
            arrive(line, dp ^ 3, 1)
            send(line, dp ^ 3, sibling)
    for line in lines:
        for row in range(rows):
            arrive(line + 1 - 2 * core, (dp + row) % rows)
    part_swap.wait_arrivals()
    for block in range(columns):
        total = part_in[block]
        for row in range(1, rows):
            total = total + part_in[row * columns + block]
        mod_out[block] = total

    @pl.loop(1, columns)
    def _(step):
        other = lax.rem(column + step, columns)
        bias_copy(other, other).wait_recv()
        bias_copy(other, other).wait_send()

    bias_out[...] = bias_in[...]
    for keep in keeps:
        keep.wait()
    for copy in sends:
        copy.wait_send()
    cond_swap.wait_sends()
    part_swap.wait_sends()


def round_up(width):
    return -(-width // 128) * 128


def gather_shards(shards, cond_rows, ada_weight, ada_bias, bias_row, rows, columns):
    depth = columns // 2
    total = rows * columns
    mod_pad = round_up(ada_weight.shape[1])
    vmem = pl.BlockSpec(memory_space=pltpu.VMEM)
    dma = pltpu.SemaphoreType.DMA
    row_shape = lambda count, width: jax.ShapeDtypeStruct((count, 1, width), jnp.float32)
    row_buffer = lambda count, width: pltpu.VMEM((count, 1, width), jnp.float32)
    count = (depth - 1) + depth * rows + depth * (rows - 1) + (2 * depth if rows == 4 else 0)
    shapes = [
        whole_shape(shard.shape, part == 2, rows, columns) for part, shard in enumerate(shards)
    ]
    return pl.pallas_call(
        functools.partial(gather_kernel, rows, depth),
        out_shape=[jax.ShapeDtypeStruct(shape, bfloat) for shape in shapes]
        + [row_shape(columns, mod_pad), row_shape(columns, bias_row.shape[-1]),
           row_shape(total, cond_rows.shape[-1])],
        in_specs=[pl.BlockSpec(memory_space=pl.ANY)] * 3 + [vmem] * 4,
        out_specs=[pl.BlockSpec(memory_space=pl.ANY)] * 3 + [vmem] * 3,
        scratch_shapes=[
            dma((3,)),
            dma((3 * count,)),
            dma((2, 3, columns, rows)),
            row_buffer(columns, bias_row.shape[-1]),
            row_buffer(total, mod_pad),
            row_buffer(total, mod_pad),
            dma((total,)), dma((total,)), dma((total,)), dma((total,)),
            dma((columns,)), dma((columns,)),
        ],
        compiler_params=pltpu.CompilerParams(
            collective_id=0, has_side_effects=True, vmem_limit_bytes=32 * 2**20),
        name="gather_shards",
    )(*shards, cond_rows, ada_weight, ada_bias, bias_row)


def scatter_kernel(rows, depth, *refs):
    grads = refs[:3]
    leaving, cond_in, ada_ref, slope = refs[3:7]
    outs, ada_grad, sums_out, cond_grad = refs[7:10], refs[10], refs[11], refs[12]
    refs = refs[13:]
    helds, pairs_in, planes_in, crosses_in, alongs_in = (
        refs[3 * kind : 3 + 3 * kind] for kind in range(5)
    )
    (
        load_sems, pair_send, pair_recv, plane_send, plane_recv,
        cross_send, cross_recv, along_send, along_recv,
        all_rows, back_out, back_in, row_send, row_recv, back_send, back_recv,
    ) = refs[15:]
    dp, z, core, others = positions(rows, depth)
    columns = 2 * depth
    me = dp * columns + lax.axis_index("fsdp")
    row_swap = Exchange(
        me, rows, columns, lambda target: leaving.at[lax.rem(target, columns)], all_rows,
        row_send, row_recv)
    back_swap = Exchange(
        me, rows, columns, lambda target: back_out.at[target], back_in, back_send, back_recv)
    sibling = place(dp, z, 1 - core)
    targets = [dp ^ 3, dp ^ 1, dp ^ 2, dp] if rows == 4 else others + [dp]
    steps = z_order(depth)[::-1]
    enter_barrier(me, rows, columns)
    row_swap.start()
    waits = []

    def remote(source, destination, send_sem, recv_sem, target):
        copy = pltpu.make_async_remote_copy(
            src_ref=source, dst_ref=destination, send_sem=send_sem, recv_sem=recv_sem,
            device_id=target, device_id_type=MESH_IDS,
        )
        copy.start()
        waits.append(copy)
        return copy

    def add(first, others_in, length, target):
        chunk = 48 if length % 48 == 0 else 16

        @pl.loop(0, length // chunk)
        def _(index):
            piece = pl.ds(pl.multiple_of(index * chunk, chunk), chunk)
            total = first[piece, :].astype(jnp.float32)
            for other in others_in:
                total = total + other[piece, :].astype(jnp.float32)
            target[piece, :] = total.astype(target.dtype)

    lines = [(z + step) % depth for step in steps]
    pairs, loads, planes, crosses, alongs = {}, {}, {}, {}, {}
    for turn, line in enumerate(lines):
        for slot, target in enumerate(targets):
            for part in range(3):
                key = (part, turn, slot)
                shape = outs[part].shape
                pairs[key] = remote(
                    block_of(grads[part], line * 2 + 1 - core, target, shape, part == 2),
                    pairs_in[part].at[turn, slot], pair_send.at[key], pair_recv.at[key], sibling)
                loads[key] = pltpu.make_async_copy(
                    block_of(grads[part], line * 2 + core, target, shape, part == 2),
                    helds[part].at[turn, slot], load_sems.at[key])
                loads[key].start()
    last = len(targets) - 1
    for turn in range(depth + 2):
        if turn == depth - 1:
            row_swap.wait_arrivals()
            high, wide = ada_ref.shape
            arrived = all_rows[:, 0, :]
            sums_out[...] = jnp.sum(arrived, axis=0, keepdims=True)
            ada_grad[...] = contract_exact(cond_in[:, 0, :high], arrived[:, :wide])
            back_out[:, 0, :high] = lax.dot_general(
                arrived[:, :wide], ada_ref[...].astype(jnp.float32), (((1,), (1,)), ((), ())),
                precision=highest)
            back_swap.start()
        if turn < depth:
            for slot in range(len(targets)):
                for part in range(3):
                    key = (part, turn, slot)
                    height = outs[part].shape[0]
                    half = height // 2
                    loads[key].wait()
                    pairs[key].wait_recv()
                    here = helds[part].at[turn, slot]
                    add(here, [pairs_in[part].at[turn, slot]], height, here)
                    if rows == 4 and slot == 0:
                        for position in range(2):
                            key = (part, turn, position)
                            crosses[key] = remote(
                                helds[part].at[turn, 0, pl.ds((1 - position) * half, half)],
                                crosses_in[part].at[turn, position],
                                cross_send.at[key], cross_recv.at[key],
                                place(others[position], z, core))
                    if rows != 4 and slot < last:
                        planes[key] = remote(
                            here, planes_in[part].at[turn, slot], plane_send.at[key],
                            plane_recv.at[key], place(targets[slot], z, core))
        if rows == 4 and 1 <= turn <= depth:
            now = turn - 1
            for position in range(2):
                for part in range(3):
                    half = outs[part].shape[0] // 2
                    crosses[part, now, 1 - position].wait_recv()
                    piece = helds[part].at[now, 1 + position, pl.ds(position * half, half)]
                    add(piece, [crosses_in[part].at[now, 1 - position]], half, piece)
                    key = (part, now, position)
                    planes[key] = remote(
                        helds[part].at[now, 1 + position], planes_in[part].at[now, position],
                        plane_send.at[key], plane_recv.at[key],
                        place(others[position], z, core))
        if turn >= 2:
            now = turn - 2
            for part in range(3):
                for slot in range(len(others)):
                    planes[part, now, slot].wait_recv()
                here = helds[part].at[now, last]
                arrived = [planes_in[part].at[now, slot] for slot in range(len(others))]
                add(here, arrived, outs[part].shape[0], here)
                if now < depth - 1:
                    key = (part, now)
                    alongs[key] = remote(
                        here, alongs_in[part].at[now], along_send.at[key], along_recv.at[key],
                        place(dp, lines[now], core))
    for part in range(3):
        for now in range(depth - 1):
            alongs[part, now].wait_recv()
        arrived = [alongs_in[part].at[now] for now in range(depth - 1)]
        add(helds[part].at[depth - 1, last], arrived, outs[part].shape[0], outs[part])
    back_swap.wait_arrivals()
    for row in range(rows):
        total = back_in[row * columns]
        for block in range(1, columns):
            total = total + back_in[row * columns + block]
        cond_grad[row] = total * slope[row]
    for copy in waits:
        copy.wait_send()
    row_swap.wait_sends()
    back_swap.wait_sends()


def scatter_shards(grads, leaving, cond_in, ada_weight, slope, shapes, rows, columns):
    depth = columns // 2
    total = rows * columns
    vmem = pl.BlockSpec(memory_space=pltpu.VMEM)
    row_buffer = lambda count, width: pltpu.VMEM((count, 1, width), jnp.float32)
    peers = 2 if rows == 4 else rows - 1
    dma = pltpu.SemaphoreType.DMA
    buffers = []
    for lead in ((depth, rows), (depth, rows), (depth, peers), (depth, 2), (depth - 1,)):
        for height, width in shapes:
            if lead == (depth, 2) and len(buffers) >= 9:
                height = height // 2 if rows == 4 else 16
            buffers.append(pltpu.VMEM(lead + (height, width), bfloat))
    return pl.pallas_call(
        functools.partial(scatter_kernel, rows, depth),
        out_shape=[jax.ShapeDtypeStruct(shape, jnp.float32) for shape in shapes]
        + [jax.ShapeDtypeStruct(ada_weight.shape, jnp.float32),
           jax.ShapeDtypeStruct((1, leaving.shape[-1]), jnp.float32),
           jax.ShapeDtypeStruct(slope.shape, jnp.float32)],
        in_specs=[pl.BlockSpec(memory_space=pl.ANY)] * 3 + [vmem] * 4,
        out_specs=[vmem] * 6,
        scratch_shapes=buffers + [
            dma((3, depth, rows)), dma((3, depth, rows)), dma((3, depth, rows)),
            dma((3, depth, peers)), dma((3, depth, peers)),
            dma((3, depth, 2)), dma((3, depth, 2)),
            dma((3, depth - 1)), dma((3, depth - 1)),
            row_buffer(total, leaving.shape[-1]),
            row_buffer(total, slope.shape[-1]), row_buffer(total, slope.shape[-1]),
            dma((total,)), dma((total,)), dma((total,)), dma((total,)),
        ],
        compiler_params=pltpu.CompilerParams(
            collective_id=1, has_side_effects=True, vmem_limit_bytes=50 * 2**20),
        name="scatter_shards",
    )(*grads, leaving, cond_in, ada_weight, slope)


def normalize_rows(values):
    center = jnp.mean(values, axis=-1, keepdims=True)
    spread = jnp.mean(jnp.square(values - center), axis=-1, keepdims=True)
    inverse = lax.rsqrt(spread + 1e-06)
    return ((values - center) * inverse, inverse)


def norm_backward(grad_normed, normed, inverse):
    centered = grad_normed - jnp.mean(grad_normed, axis=-1, keepdims=True)
    return inverse * (centered - normed * jnp.mean(grad_normed * normed, axis=-1, keepdims=True))


def contract_rows(left_rows, right_rows):
    return lax.dot_general(
        left_rows, right_rows, (((0,), (0,)), ((), ())), preferred_element_type=jnp.float32
    )


def contract_exact(left_rows, right_rows):
    return lax.dot_general(left_rows, right_rows, (((0,), (0,)), ((), ())), precision=highest)


def against_weight(grad_rows, weight):
    return lax.dot_general(
        grad_rows, weight, (((1,), (1,)), ((), ())), preferred_element_type=jnp.float32
    )


def dot_plain(left, right):
    return jnp.dot(left, right, preferred_element_type=jnp.float32)


def columns_sum(values):
    return jnp.sum(values, axis=0, keepdims=True)


class Swap:
    def __init__(self, me, size, device, row_for, landing, send_sems, recv_sems):
        self.me, self.size, self.device = me, size, device
        self.row_for, self.landing = row_for, landing
        self.send_sems, self.recv_sems = send_sems, recv_sems
        self.copies = []

    def start(self):
        for step in range(1, self.size):
            other = lax.rem(self.me + step, self.size)
            copy = pltpu.make_async_remote_copy(
                src_ref=self.row_for(other),
                dst_ref=self.landing.at[self.me],
                send_sem=self.send_sems.at[step],
                recv_sem=self.recv_sems.at[step],
                device_id=self.device(other),
                device_id_type=MESH_IDS,
            )
            copy.start()
            self.copies.append(copy)
        self.landing[self.me] = self.row_for(self.me)[...]

    def wait_arrivals(self):
        for copy in self.copies:
            copy.wait_recv()

    def wait_sends(self):
        for copy in self.copies:
            copy.wait_send()


class Gather:
    def __init__(self, rows, depth, where, shards, outs, own_sems, send_sems, recv_sems):
        self.rows, self.depth = rows, depth
        self.dp, self.z, self.core, self.others = where
        self.shards, self.outs = shards, outs
        self.own_sems, self.send_sems, self.recv_sems = own_sems, send_sems, recv_sems
        self.sibling = place(self.dp, self.z, 1 - self.core)
        self.sends = []
        self.keeps = []
        self.own = self.z * 2 + self.core
        self.steps = [0] + list(range(2, depth)) + [1]
        self.lines = [(self.z ^ step) * 2 + self.core for step in self.steps]
        self.units = [(part, turn) for part in range(3) for turn in range(depth)]
        self.helped = depth - 1

    def slot_of(self, part, line, row):
        return block_of(self.outs[part], line, row, self.shards[part].shape, part == 2)

    def half_of(self, ref, part, which):
        half = self.shards[part].shape[0] // 2
        return ref.at[pl.ds(which * half, half)]

    def send(self, part, line, row, target, which=None, own=False):
        destination = self.slot_of(part, line, row)
        source = self.shards[part] if own else destination
        if which is not None:
            source, destination = (
                self.half_of(source, part, which), self.half_of(destination, part, which))
        copy = pltpu.make_async_remote_copy(
            src_ref=source,
            dst_ref=destination,
            send_sem=self.send_sems.at[len(self.sends)],
            recv_sem=self.recv_sems.at[which or 0, part, line, row],
            device_id=target,
            device_id_type=MESH_IDS,
        )
        copy.start()
        self.sends.append(copy)

    def arrive(self, part, line, row, which=None):
        destination = self.slot_of(part, line, row)
        if which is not None:
            destination = self.half_of(destination, part, which)
        pltpu.make_async_remote_copy(
            src_ref=destination,
            dst_ref=destination,
            send_sem=self.send_sems.at[0],
            recv_sem=self.recv_sems.at[which or 0, part, line, row],
            device_id=self.sibling,
            device_id_type=MESH_IDS,
        ).wait_recv()

    def send_own(self, part):
        for other in self.others:
            self.send(part, self.own, self.dp, place(other, self.z, self.core), own=True)
        self.send(part, self.own, self.dp, self.sibling, own=True)
        keep = pltpu.make_async_copy(
            self.shards[part], self.slot_of(part, self.own, self.dp), self.own_sems.at[part])
        keep.start()
        self.keeps.append(keep)

    def send_deep(self, index):
        if index < len(self.units):
            part, turn = self.units[index]
            if turn:
                target = place(self.dp, self.z ^ self.steps[turn], self.core)
                self.send(part, self.own, self.dp, target, own=True)

    def turn(self, index):
        dp, z, core = self.dp, self.z, self.core
        count = len(self.units)
        self.send_deep(index + AHEAD)
        if index in (1, 2):
            self.send_own(index)
        if index < count:
            part, turn = self.units[index]
            line = self.lines[turn]
            if turn:
                self.arrive(part, line, dp)
                which = 0 if turn == self.helped else None
                for other in self.others:
                    self.send(part, line, dp, place(other, z, core), which=which)
                self.send(part, line, dp, self.sibling)
        if LAG <= index < count + LAG:
            part, turn = self.units[index - LAG]
            line = self.lines[turn]
            for position, other in enumerate(self.others):
                if turn == self.helped:
                    self.arrive(part, line, other, 0)
                    self.arrive(part, line, other, 1)
                else:
                    self.arrive(part, line, other)
                    self.send(
                        part, line, other, place(self.others[1 - position], z, core),
                        which=position)
                if turn == 0:
                    self.send(part, line, other, place(dp, z ^ 1, core), which=1)
                self.send(part, line, other, self.sibling)
        if 2 * LAG <= index:
            part, turn = self.units[index - 2 * LAG]
            line = self.lines[turn]
            if turn == self.helped:
                self.arrive(part, line, dp ^ 3)
            else:
                self.arrive(part, line, dp ^ 3, 0)
                self.arrive(part, line, dp ^ 3, 1)
            if turn == 0:
                self.send(part, line, dp ^ 3, place(dp, z ^ 1, core))
            self.send(part, line, dp ^ 3, self.sibling)

    def finish_part(self, part):
        for line in self.lines:
            for row in range(self.rows):
                self.arrive(part, line + 1 - 2 * self.core, (self.dp + row) % self.rows)
        self.keeps[part].wait()

    def wait_sends(self):
        for copy in self.sends:
            copy.wait_send()


class Scatter:
    def __init__(self, rows, depth, where, shapes, grads, buffers, sems):
        self.rows, self.depth, self.shapes, self.grads = rows, depth, shapes, grads
        self.dp, self.z, self.core, self.others = where
        (
            self.held, self.planes_in, self.crosses_in, self.alongs_in, self.help_in, self.half_in,
        ) = (buffers[3 * kind : 3 * kind + 3] for kind in range(6))
        (
            self.pair_send, self.pair_recv, self.plane_send, self.plane_recv,
            self.cross_send, self.cross_recv, self.along_send, self.along_recv,
            self.help_send, self.help_recv,
        ) = sems
        self.sibling = place(self.dp, self.z, 1 - self.core)
        self.targets = [self.dp ^ 3, self.dp ^ 1, self.dp ^ 2, self.dp]
        self.lines = [self.z ^ step for step in [1] + list(range(2, depth))[::-1] + [0]]
        self.units = [(part, turn) for part in (2, 1, 0) for turn in range(depth)]
        self.pairs, self.planes, self.crosses, self.alongs, self.helps = {}, {}, {}, {}, {}

    def remote(self, source, destination, send_sem, recv_sem, target):
        copy = pltpu.make_async_remote_copy(
            src_ref=source, dst_ref=destination, send_sem=send_sem, recv_sem=recv_sem,
            device_id=target, device_id_type=MESH_IDS)
        copy.start()
        return copy

    def block(self, part, line, target):
        return block_of(self.grads[part], line, target, self.shapes[part], part == 2)

    def add(self, first, others_in, length, target):
        chunk = 48

        @pl.loop(0, length // chunk)
        def _(index):
            piece = pl.ds(pl.multiple_of(index * chunk, chunk), chunk)
            total = first[piece, :].astype(jnp.float32)
            for other in others_in:
                total = total + other[piece, :].astype(jnp.float32)
            target[piece, :] = total.astype(target.dtype)

    def help(self, part, slot, source, destination):
        self.helps[part, slot] = self.remote(
            source, destination, self.help_send.at[part, slot], self.help_recv.at[part, slot],
            place(self.dp, self.z ^ 1, self.core))

    def start_pairs(self, part):
        for turn, line in enumerate(self.lines):
            for slot, target in enumerate(self.targets):
                key = (part, turn, slot)
                self.pairs[key] = self.remote(
                    self.block(part, line * 2 + 1 - self.core, target),
                    self.held[part].at[turn, slot], self.pair_send.at[key],
                    self.pair_recv.at[key], self.sibling)

    def wait_pairs_sent(self, part):
        for turn in range(self.depth):
            for slot in range(self.rows):
                self.pairs[part, turn, slot].wait_send()

    def turn(self, index):
        last = self.rows - 1
        count = len(self.units)
        if index < count:
            part, turn = self.units[index]
            height = self.shapes[part][0]
            half = height // 2
            for slot, target in enumerate(self.targets):
                self.pairs[part, turn, slot].wait_recv()
                here = self.held[part].at[turn, slot]
                own = self.block(part, self.lines[turn] * 2 + self.core, target)
                arrived = [here]
                if turn == self.depth - 1 and slot == 0:
                    self.helps[part, 0].wait_recv()
                    arrived.append(self.help_in[part])
                self.add(own, arrived, height, here)
                if turn == self.depth - 1 and slot in (1, 2):
                    self.helps[part, slot].wait_recv()
                    piece = self.held[part].at[turn, slot, pl.ds(half, half)]
                    self.add(piece, [self.half_in[part].at[slot - 1]], half, piece)
                if turn == 0 and slot == 0:
                    self.help(part, 0, here, self.help_in[part])
                elif turn == 0 and slot < 3:
                    self.help(
                        part, slot, self.held[part].at[turn, slot, pl.ds(half, half)],
                        self.half_in[part].at[slot - 1])
                    key = (part, turn, slot - 1)
                    self.planes[key] = self.remote(
                        self.held[part].at[turn, slot, pl.ds(0, half)],
                        self.planes_in[part].at[turn, slot - 1, pl.ds(0, half)],
                        self.plane_send.at[key], self.plane_recv.at[key],
                        place(self.others[slot - 1], self.z, self.core))
                elif slot == 0:
                    for position in range(2):
                        key = (part, turn, position)
                        self.crosses[key] = self.remote(
                            self.held[part].at[turn, 0, pl.ds((1 - position) * half, half)],
                            self.crosses_in[part].at[turn, position],
                            self.cross_send.at[key], self.cross_recv.at[key],
                            place(self.others[position], self.z, self.core))
        if LAG <= index < count + LAG:
            part, turn = self.units[index - LAG]
            half = self.shapes[part][0] // 2
            for position in range(2 if turn else 0):
                self.crosses[part, turn, 1 - position].wait_recv()
                piece = self.held[part].at[turn, 1 + position, pl.ds(position * half, half)]
                self.add(piece, [self.crosses_in[part].at[turn, 1 - position]], half, piece)
                key = (part, turn, position)
                self.planes[key] = self.remote(
                    self.held[part].at[turn, 1 + position], self.planes_in[part].at[turn, position],
                    self.plane_send.at[key], self.plane_recv.at[key],
                    place(self.others[position], self.z, self.core))
        if 2 * LAG <= index:
            part, turn = self.units[index - 2 * LAG]
            for position in range(2):
                self.planes[part, turn, position].wait_recv()
            height = self.shapes[part][0] if turn else self.shapes[part][0] // 2
            here = self.held[part].at[turn, last]
            piece = self.held[part].at[turn, last, pl.ds(0, height)]
            arrived = [
                self.planes_in[part].at[turn, position, pl.ds(0, height)] for position in range(2)]
            self.add(piece, arrived, height, piece)
            if turn < self.depth - 1:
                key = (part, turn)
                self.alongs[key] = self.remote(
                    here, self.alongs_in[part].at[turn], self.along_send.at[key],
                    self.along_recv.at[key], place(self.dp, self.lines[turn], self.core))

    def finish_part(self, part):
        total = self.held[part][self.depth - 1, self.rows - 1].astype(jnp.float32)
        for turn in range(self.depth - 1):
            self.alongs[part, turn].wait_recv()
            total = total + self.alongs_in[part][turn].astype(jnp.float32)
        return total

    def wait_sends(self):
        for copies in (self.planes, self.crosses, self.alongs, self.helps):
            for copy in copies.values():
                copy.wait_send()


def layer_kernel(rows, depth, *refs):
    sources, live_ref, outs = refs[2:13], refs[13], refs[14:22]
    landed = refs[22:33]
    results = landed[:2] + refs[33:39]
    (
        latents, cotangent, conditioning, ada_ref, ada_bias, qkv_shard, qv_shard, proj_shard,
        proj_bias_shard, fc1_bias_shard, fc2_bias_shard,
    ) = landed
    block_out, latent_grad, ada_grad, qkv_grad, proj_grad, fc1_grad, fc2_grad, small = results
    mixed_shard, cond_rows, slope, load_sems, store_sems = refs[39:44]
    shards = (mixed_shard, refs[0], refs[1])
    refs = refs[44:]
    weights, grads = refs[:3], (refs[3], refs[4], refs[3])
    scatter_buffers, scatter_sems = refs[5:23], refs[23:33]
    (
        own_sems, send_sems, recv_sems, swap_send, swap_recv,
        cond_across, cond_own, cond_along, cond_in, part_out, part_across, part_row, part_along,
        leaving, rows_along, rows_across, back_out, back_across, back_row, back_along,
        mod, qkv_bias, proj_bias, fc1_bias, fc2_bias, mod_grad, qkv_sums, proj_sums, fc1_sums,
        fc2_sums, inverse_one, inverse_two, normed_one, normed_two, middle, branch, wide,
        hidden_one, hidden_one_t, hidden_two, hidden_two_t, attended, attended_t,
        grad_mlp, grad_mlp_t, projected,
        grad_proj_mixed, activated, grad_pre, grad_natural, grad_state, probability,
    ) = refs[33:]
    grad_mixed, grad_attended = grad_pre, hidden_one
    mixed, fc1, fc2_turned = weights
    where = positions(rows, depth)
    dp = where[0]
    columns = 2 * depth
    column = lax.axis_index("fsdp")
    length = latents.shape[0]
    qkv_part, proj_part = 3 * D // columns, D // columns
    block = qkv_part + proj_part
    edge = qkv_part // 128 * 128
    rest = block - edge
    lead = qkv_part - edge
    scale_factor = HEAD ** (-0.5)
    ada_rows, mod_width = ada_ref.shape
    mod_pad = round_up(mod_width)
    loads = [
        pltpu.make_async_copy(source, target, load_sems.at[at])
        for at, (source, target) in enumerate(zip(sources, landed))]
    for at in (2, 5, 7, 6, 8, 9, 10, 0, 3, 4, 1):
        loads[at].start()
    stores = []

    def store(at):
        copy = pltpu.make_async_copy(results[at], outs[at], store_sems.at[at])
        copy.start()
        stores.append(copy)

    barrier = pltpu.get_barrier_semaphore()
    partners = [(lax.rem(dp + step, rows), column) for step in range(1, rows)]
    partners += [(dp, lax.rem(column + step, columns)) for step in range(1, columns)]
    for partner in partners:
        pl.semaphore_signal(barrier, inc=1, device_id=partner, device_id_type=MESH_IDS)
    live = live_ref[0].astype(jnp.float32)
    loads[2].wait()
    cond_value = conditioning[...].astype(jnp.float32)
    logistic = 1.0 / (1.0 + jnp.exp(-cond_value))
    slope[...] = logistic * (1.0 + cond_value * (1.0 - logistic))
    cond_act = (cond_value * logistic).astype(bfloat).astype(jnp.float32)
    for row in range(rows):
        cond_rows[row, :, :ada_rows] = cond_act[:, row * ada_rows : (row + 1) * ada_rows]
    pl.semaphore_wait(barrier, len(partners))
    gather = Gather(rows, depth, where, shards, weights, own_sems, send_sems, recv_sems)
    scatter = Scatter(
        rows, depth, where, [shard.shape for shard in shards], grads, scatter_buffers, scatter_sems)
    swaps = []

    def swap_across(row_for, landing):
        at = len(swaps)
        swaps.append(Swap(
            dp, rows, lambda other: (other, column), row_for, landing,
            swap_send.at[at], swap_recv.at[at]))
        return swaps[-1]

    def swap_along(row_for, landing):
        at = len(swaps)
        swaps.append(Swap(
            column, columns, lambda other: (dp, other), row_for, landing,
            swap_send.at[at], swap_recv.at[at]))
        return swaps[-1]

    cond_first = swap_across(
        lambda other: cond_rows.at[other], cond_across)
    cond_second = swap_along(lambda other: cond_own, cond_along)
    part_first = swap_across(lambda other: part_out.at[other], part_across)
    part_second = swap_along(lambda other: part_row.at[other], part_along)
    rows_first = swap_along(lambda other: leaving.at[other], rows_along)
    rows_second = swap_across(lambda other: rows_along, rows_across)
    back_first = swap_across(lambda other: back_out.at[other], back_across)
    back_second = swap_along(lambda other: back_row.at[other], back_along)
    cond_first.start()
    loads[5].wait()
    loads[7].wait()
    mixed_shard[:, :qkv_part] = qkv_shard[...]
    mixed_shard[:, qkv_part:] = proj_shard[...]
    for index in range(AHEAD):
        gather.send_deep(index)
    gather.send_own(0)

    def piece(kind):
        return mod[:, kind * D : (kind + 1) * D]

    def share_condition():
        cond_first.wait_arrivals()
        cond_own[:rows] = cond_across[...]
        bias_row = []
        for at in (6, 8, 9, 10):
            loads[at].wait()
            bias_row.append(landed[at][...].astype(jnp.float32).reshape(1, -1))
        bias_row = jnp.concatenate(bias_row, axis=1)
        pad = cond_own.shape[-1]
        for at in range(bias_row.shape[1] // pad):
            cond_own[rows + at] = bias_row[:, at * pad : (at + 1) * pad]
        cond_second.start()

    def start_modulation():
        cond_second.wait_arrivals()
        cond_in[...] = jnp.concatenate(
            [cond_along[source, row] for row in range(rows) for source in range(columns)], axis=0)
        loads[3].wait()
        loads[4].wait()
        part = dot_plain(cond_in[:, :ada_rows].astype(bfloat), ada_ref[...])
        own_bias = ada_bias[...].astype(jnp.float32).reshape(1, -1)
        part = part + jnp.where(dp == 0, own_bias, 0.0)
        for row in range(rows):
            part_out[row, :, :mod_width] = part[row * columns : (row + 1) * columns]
        part_first.start()

    def sum_modulation():
        part_first.wait_arrivals()
        total = part_across[0]
        for row in range(1, rows):
            total = total + part_across[row]
        part_row[:, 0, :] = total
        part_second.start()

    def normalize_first():
        loads[0].wait()
        normed, inverse = normalize_rows(latents[...].astype(jnp.float32))
        normed_one[...] = normed
        inverse_one[...] = inverse

    def finish_modulation():
        part_second.wait_arrivals()
        mod[...] = jnp.concatenate(
            [part_along[source][:, :mod_width] for source in range(columns)], axis=1)
        bias_parts = [
            jnp.concatenate(
                [cond_along[source, row] for row in range(rows, cond_along.shape[1])], axis=1)
            for source in range(columns)]
        low = 0
        naturals = []
        for width in (2 * D // columns, D // columns, FF // columns, D // columns):
            naturals.append(jnp.concatenate(
                [part[:, low : low + width] for part in bias_parts], axis=1))
            low += width
        qkv_bias[:, :D] = naturals[0][:, :D]
        qkv_bias[:, D : 2 * D] = jnp.zeros((1, D), jnp.float32)
        qkv_bias[:, 2 * D :] = naturals[0][:, D:]
        proj_bias[...] = naturals[1]
        fc1_bias[...] = naturals[2]
        fc2_bias[...] = naturals[3]
        hidden = (normed_one[...] * (1.0 + piece(1)) + piece(0)).astype(bfloat)
        hidden_one[...] = hidden
        hidden_one_t[...] = hidden.T

    def start_gradient():
        loads[1].wait()
        grad = (piece(5) * (live * cotangent[...].astype(jnp.float32))).astype(bfloat)
        grad_mlp[...] = grad
        grad_mlp_t[...] = grad.T
        fc2_sums[...] = columns_sum(grad.astype(jnp.float32))

    def span(index, width):
        return pl.ds(pl.multiple_of(index * width, width), width)

    def project():
        @pl.loop(0, columns)
        def _(index):
            wide[:, span(index, block)] = dot_plain(hidden_one[...], mixed[:, span(index, block)])

        for index in range(columns):
            natural = slice(index * qkv_part, (index + 1) * qkv_part)
            projected[:, natural] = (
                wide[:, index * block : index * block + qkv_part] + qkv_bias[:, natural]
            ).astype(bfloat)

    def head_slabs(source, pair):
        return [
            source[:, pl.ds(pl.multiple_of(kind * D + pair * 128, 128), 128)] for kind in range(3)]

    def own_lanes(which):
        lane = lax.broadcasted_iota(jnp.int32, (length, 128), 1)
        return lane < HEAD if which == 0 else lane >= HEAD

    def attend(low, high):
        @pl.loop(low, high)
        def _(pair):
            queries, keys, values = head_slabs(projected, pair)
            zero = jnp.zeros_like(queries)
            results = []
            for which in range(2):
                scores = against_weight(
                    jnp.where(own_lanes(which), queries, zero), keys) * scale_factor
                shifted = jnp.exp(scores - jnp.max(scores, axis=-1, keepdims=True))
                exact = shifted / jnp.sum(shifted, axis=-1, keepdims=True)
                probability[2 * pair + which] = exact
                results.append(dot_plain(exact.astype(bfloat), values))
            attended[:, span(pair, 128)] = jnp.where(
                own_lanes(0), results[0], results[1]).astype(bfloat)

    def finish_attention():
        attended_t[...] = attended[...].T

        @pl.loop(0, columns)
        def _(index):
            tail = pl.ds(pl.multiple_of(index * block + edge, 128), rest)
            wide[:, span(index, rest)] = dot_plain(attended[...], mixed[:, tail])

        for index in range(columns):
            natural = slice(index * proj_part, (index + 1) * proj_part)
            branch[:, natural] = (
                wide[:, index * rest + lead : (index + 1) * rest] + proj_bias[:, natural])
        total = latents[...].astype(jnp.float32) + piece(2) * branch[...]
        middle[...] = total
        normed, inverse = normalize_rows(total)
        normed_two[...] = normed
        inverse_two[...] = inverse
        hidden = (normed * (1.0 + piece(4)) + piece(3)).astype(bfloat)
        hidden_two[...] = hidden
        hidden_two_t[...] = hidden.T

    chunk = 1536
    chunks = FF // chunk

    def expand(low, high):
        @pl.loop(low, high)
        def _(index):
            part = span(index, chunk)
            value = dot_plain(hidden_two[...], fc1[:, part]) + fc1_bias[:, part]
            root = 0.7978845608028654
            square = value * value
            bend = jnp.tanh(root * (value + 0.044715 * (square * value)))
            activated[:, part] = (0.5 * value * (1.0 + bend)).astype(bfloat)
            wide[:, part] = 0.5 * (1.0 + bend) + 0.5 * value * (1.0 - bend * bend) * (
                root * (1.0 + 3 * 0.044715 * square))

    def fc2_weight_grad(low, high):
        @pl.loop(low, high)
        def _(index):
            part = span(index, chunk)
            grads[2][:, part] = dot_plain(grad_mlp_t[...], activated[:, part]).astype(bfloat)

    def after_part_zero():
        gather.finish_part(0)
        project()

    def after_part_one():
        gather.finish_part(1)
        expand(0, 1)

    def send_fc2_grad():
        fc2_weight_grad(1, 2)
        scatter.start_pairs(2)

    hooks = [
        share_condition, normalize_first, start_modulation, None, sum_modulation, None,
        finish_modulation, start_gradient, after_part_zero, lambda: attend(0, 3),
        lambda: attend(3, 6), finish_attention, after_part_one, lambda: expand(1, 2),
        lambda: fc2_weight_grad(0, 1), send_fc2_grad,
    ]
    for index, hook in enumerate(hooks):
        gather.turn(index)
        if hook is not None:
            hook()
    scatter.turn(0)
    gather.finish_part(2)
    third = 256

    def finish_forward():
        @pl.loop(0, D // third)
        def _(index):
            part = span(index, third)
            branch_part = against_weight(activated[...], fc2_turned[part, :]) + fc2_bias[:, part]
            live_grad = live * cotangent[:, part].astype(jnp.float32)
            last = pl.ds(pl.multiple_of(5 * D + index * third, third), third)
            block_out[:, part] = (
                live * (middle[:, part] + mod[:, last] * branch_part)).astype(bfloat)
            mod_grad[:, last] = columns_sum(live_grad * branch_part)

        store(0)

    def fc1_weight_grad(low, high):
        @pl.loop(low, high)
        def _(index):
            part = span(index, chunk)
            grad = (dot_plain(grad_mlp[...], fc2_turned[:, part]) * wide[:, part]).astype(bfloat)
            grad_pre[:, part] = grad
            fc1_sums[:, part] = columns_sum(grad.astype(jnp.float32))
            grads[1][:, part] = dot_plain(hidden_two_t[...], grad).astype(bfloat)

    def hidden_two_back():
        @pl.loop(0, D // third)
        def _(index):
            part = span(index, third)
            grad_state[:, part] = against_weight(grad_pre[...], fc1[part, :])

    def middle_back():
        grad_hidden = grad_state[...]
        mod_grad[:, 3 * D : 4 * D] = columns_sum(grad_hidden)
        mod_grad[:, 4 * D : 5 * D] = columns_sum(grad_hidden * normed_two[...])
        grad_middle = live * cotangent[...].astype(jnp.float32) + norm_backward(
            grad_hidden * (1.0 + piece(4)), normed_two[...], inverse_two[...])
        mod_grad[:, 2 * D : 3 * D] = columns_sum(grad_middle * branch[...])
        grad_state[...] = grad_middle
        grad_branch = (piece(2) * grad_middle).astype(bfloat)
        proj_sums[...] = columns_sum(grad_branch.astype(jnp.float32))
        for index in range(columns):
            grad_proj_mixed[:, index * rest : index * rest + lead] = jnp.zeros(
                (length, lead), bfloat)
            grad_proj_mixed[:, index * rest + lead : (index + 1) * rest] = (
                grad_branch[:, index * proj_part : (index + 1) * proj_part])
        total = None
        for index in range(columns):
            term = against_weight(
                grad_proj_mixed[:, index * rest : (index + 1) * rest],
                mixed[:, index * block + edge : (index + 1) * block])
            total = term if total is None else total + term
        grad_attended[...] = total.astype(bfloat)

    def attend_back(low, high):
        @pl.loop(low, high)
        def _(pair):
            queries, keys, values = head_slabs(projected, pair)
            grad_out = grad_attended[:, span(pair, 128)]
            zero = jnp.zeros_like(grad_out)
            results = []
            for which in range(2):
                exact = probability[2 * pair + which]
                grad_prob = against_weight(jnp.where(own_lanes(which), grad_out, zero), values)
                inner = jnp.sum(exact * grad_prob, axis=-1, keepdims=True)
                grad_scores = (exact * (grad_prob - inner)).astype(bfloat)
                results.append((
                    dot_plain(grad_scores, keys) * scale_factor,
                    contract_rows(grad_scores, queries) * scale_factor,
                    contract_rows(exact.astype(bfloat), grad_out)))
            for kind in range(3):
                grad_natural[:, pl.ds(pl.multiple_of(kind * D + pair * 128, 128), 128)] = jnp.where(
                    own_lanes(0), results[0][kind], results[1][kind]).astype(bfloat)

    def mixed_weight_grad():
        qkv_sums[...] = columns_sum(grad_natural[...].astype(jnp.float32))
        for index in range(columns):
            grad_mixed[:, index * block : index * block + qkv_part] = (
                grad_natural[:, index * qkv_part : (index + 1) * qkv_part])
            grad_mixed[:, index * block + qkv_part : (index + 1) * block] = jnp.zeros(
                (length, proj_part), bfloat)
        scatter.wait_pairs_sent(2)

        @pl.loop(0, columns)
        def _(index):
            low = pl.multiple_of(index * block, 128)
            grads[0][:, pl.ds(low, edge)] = dot_plain(
                hidden_one_t[...], grad_mixed[:, pl.ds(low, edge)]).astype(bfloat)
            tail = pl.ds(pl.multiple_of(index * block + edge, 128), rest)
            grads[0][:, tail] = (
                dot_plain(hidden_one_t[...], grad_mixed[:, tail])
                + dot_plain(attended_t[...], grad_proj_mixed[:, span(index, rest)])).astype(bfloat)

    def finish_backward():
        @pl.loop(0, D // third)
        def _(index):
            part = span(index, third)
            branch[:, part] = against_weight(grad_mixed[...], mixed[part, :])

        grad_hidden = branch[...]
        mod_grad[:, :D] = columns_sum(grad_hidden)
        mod_grad[:, D : 2 * D] = columns_sum(grad_hidden * normed_one[...])
        latent_grad[...] = (grad_state[...] + norm_backward(
            grad_hidden * (1.0 + piece(1)), normed_one[...], inverse_one[...])).astype(bfloat)
        store(1)
        pad = jnp.zeros((1, mod_pad - mod_width), jnp.float32)
        qv_sums = jnp.concatenate([qkv_sums[:, :D], qkv_sums[:, 2 * D :]], axis=1)
        rows_of = (qv_sums, proj_sums[...], fc1_sums[...], fc2_sums[...])
        every = mod_grad[...]
        for index in range(columns):
            pieces = [every[:, index * mod_width : (index + 1) * mod_width], pad]
            for row in rows_of:
                share = row.shape[1] // columns
                pieces.append(row[:, index * share : (index + 1) * share])
            leaving[index] = jnp.concatenate(pieces, axis=1)
        rows_first.start()

    def share_rows():
        rows_first.wait_arrivals()
        rows_second.start()

    def own_sums():
        rows_second.wait_arrivals()
        arrived = jnp.concatenate([rows_across[row, :, 0, :] for row in range(rows)], axis=0)
        small[:, D:] = columns_sum(arrived)
        ada_grad[...] = contract_exact(cond_in[:, :ada_rows], arrived[:, :mod_width])
        store(2)
        back = lax.dot_general(
            arrived[:, :mod_width], ada_ref[...].astype(jnp.float32), (((1,), (1,)), ((), ())),
            precision=highest)
        for row in range(rows):
            back_out[row, :, :ada_rows] = back[row * columns : (row + 1) * columns]
        back_first.start()

    def share_back():
        back_first.wait_arrivals()
        for row in range(rows):
            back_row[:, row, 0, :] = back_across[row]
        back_second.start()

    def finish_condition():
        back_second.wait_arrivals()
        total = back_along[0]
        for source in range(1, columns):
            total = total + back_along[source]
        small[:, :D] = jnp.concatenate(
            [total[row][:, :ada_rows] for row in range(rows)], axis=1) * slope[...]
        store(7)

    def finish_fc2():
        fc2_grad[...] = scatter.finish_part(2)
        store(6)

    def finish_fc1():
        fc1_grad[...] = scatter.finish_part(1)
        store(5)

    def send_fc1_grad():
        fc1_weight_grad(1, 2)
        scatter.start_pairs(1)

    def send_mixed_grad():
        mixed_weight_grad()
        scatter.start_pairs(0)

    hooks = [
        lambda: fc1_weight_grad(0, 1), send_fc1_grad, hidden_two_back, middle_back,
        lambda: attend_back(0, 3), lambda: attend_back(3, 6), send_mixed_grad,
        finish_forward, finish_backward, finish_fc2, share_rows, own_sums, finish_fc1,
        share_back, finish_condition,
    ]
    for index, hook in enumerate(hooks):
        hook()
        scatter.turn(index + 1)
    total = scatter.finish_part(0)
    qkv_grad[...] = total[:, :qkv_part]
    proj_grad[...] = total[:, qkv_part:]
    store(3)
    store(4)
    scatter.wait_pairs_sent(1)
    scatter.wait_pairs_sent(0)
    scatter.wait_sends()
    gather.wait_sends()
    for swap in swaps:
        swap.wait_sends()
    for copy in stores:
        copy.wait()


def emit_kernel(*refs):
    small, wholes = refs[0], refs[1:8]
    cond_grad, rows_out, outs, held, sems = refs[8], refs[9:14], refs[14:21], refs[21:28], refs[28]
    loads = [
        pltpu.make_async_copy(whole, hold, sems.at[0, at])
        for at, (whole, hold) in enumerate(zip(wholes, held))]
    stores = [
        pltpu.make_async_copy(hold, out, sems.at[1, at])
        for at, (hold, out) in enumerate(zip(held, outs))]
    for load in loads:
        load.start()
    cond_grad[...] = small[:, :D]
    low = D
    for out in rows_out:
        width = out.shape[0]
        out[...] = small[0, low : low + width]
        low += round_up(width) if low == D else width
    for load, store in zip(loads, stores):
        load.wait()
        store.start()
    for store in stores:
        store.wait()


def emit(small, wholes, widths):
    vmem = pl.BlockSpec(memory_space=pltpu.VMEM)
    anywhere = pl.BlockSpec(memory_space=pl.ANY)
    count = len(wholes)
    return pl.pallas_call(
        emit_kernel,
        out_shape=[jax.ShapeDtypeStruct((1, D), jnp.float32)]
        + [jax.ShapeDtypeStruct((width,), jnp.float32) for width in widths]
        + [jax.ShapeDtypeStruct(whole.shape, whole.dtype) for whole in wholes],
        in_specs=[vmem] + [anywhere] * count,
        out_specs=[vmem] * (1 + len(widths)) + [anywhere] * count,
        scratch_shapes=[pltpu.VMEM(whole.shape, whole.dtype) for whole in wholes]
        + [pltpu.SemaphoreType.DMA((2, count))],
        name="emit",
    )(small, *wholes)


def run_layer(fc1_shard, fc2_turned_shard, sources, latent_count, rows, columns):
    latents, _, conditioning, ada_weight, _, qkv_shard, _, proj_shard = sources[:8]
    depth = columns // 2
    qkv_part, proj_part = qkv_shard.shape[1], proj_shard.shape[1]
    shards = (
        jax.ShapeDtypeStruct((qkv_shard.shape[0], qkv_part + proj_part), bfloat),
        fc1_shard, fc2_turned_shard)
    ada_rows, mod_width = ada_weight.shape
    cond_pad = round_up(ada_rows)
    bias_width = sum(sources[at].shape[0] for at in (6, 8, 9, 10))
    group = rows + bias_width // cond_pad
    count = (depth - 1) + depth * rows + depth * (rows - 1) + 2 * depth
    total = rows * columns
    mod_pad = round_up(mod_width)
    length = latents.shape[0]
    anywhere = pl.BlockSpec(memory_space=pl.ANY)
    dma = pltpu.SemaphoreType.DMA
    shapes = [
        whole_shape(shard.shape, part == 2, rows, columns) for part, shard in enumerate(shards)]
    row_buffer = lambda count, width: pltpu.VMEM((count, 1, width), jnp.float32)
    wide_row = lambda width: pltpu.VMEM((1, width), jnp.float32)
    single = lambda width: pltpu.VMEM((length, width), jnp.float32)
    half = lambda width: pltpu.VMEM((length, width), bfloat)
    turned = pltpu.VMEM((D, length), bfloat)
    rest = 128 * columns
    buffers = []
    for lead in ((depth, rows), (depth, 2), (depth, 2), (depth - 1,), (), (2,)):
        for shard in shards:
            height, width = shard.shape
            height = height // 2 if len(buffers) // 3 in (2, 5) else height
            buffers.append(pltpu.VMEM(lead + (height, width), bfloat))
    float_out = lambda *shape: jax.ShapeDtypeStruct(shape, jnp.float32)
    outs = [
        jax.ShapeDtypeStruct((length, D), bfloat),
        jax.ShapeDtypeStruct((length, D), bfloat),
        float_out(ada_rows, mod_width),
        float_out(qkv_shard.shape[0], qkv_part),
        float_out(qkv_shard.shape[0], proj_part),
        float_out(*fc1_shard.shape),
        float_out(*fc2_turned_shard.shape),
        float_out(1, D + mod_pad + bias_width),
    ]
    return pl.pallas_call(
        functools.partial(layer_kernel, rows, depth),
        out_shape=outs,
        in_specs=[anywhere] * 13 + [pl.BlockSpec(memory_space=pltpu.SMEM)],
        out_specs=[anywhere] * 8,
        scratch_shapes=[pltpu.VMEM(source.shape, source.dtype) for source in sources]
        + [pltpu.VMEM(out.shape, out.dtype) for out in outs[2:]]
        + [
            pltpu.VMEM(shards[0].shape, bfloat), row_buffer(rows, cond_pad), wide_row(D),
            dma((len(sources),)), dma((len(outs),)),
        ]
        + [pltpu.VMEM(shape, bfloat) for shape in shapes + shapes[:2]]
        + buffers + [
            dma((3, depth, rows)), dma((3, depth, rows)),
            dma((3, depth, 2)), dma((3, depth, 2)), dma((3, depth, 2)), dma((3, depth, 2)),
            dma((3, depth - 1)), dma((3, depth - 1)), dma((3, 3)), dma((3, 3)),
            dma((3,)), dma((3 * count,)), dma((2, 3, columns, rows)),
            dma((8, columns)), dma((8, columns)),
            row_buffer(rows, cond_pad), row_buffer(group, cond_pad),
            pltpu.VMEM((columns, group, 1, cond_pad), jnp.float32),
            pltpu.VMEM((total, cond_pad), jnp.float32),
            pltpu.VMEM((rows, columns, mod_pad), jnp.float32),
            pltpu.VMEM((rows, columns, mod_pad), jnp.float32),
            row_buffer(columns, mod_pad), row_buffer(columns, mod_pad),
            row_buffer(columns, mod_pad + bias_width), row_buffer(columns, mod_pad + bias_width),
            pltpu.VMEM((rows, columns, 1, mod_pad + bias_width), jnp.float32),
            pltpu.VMEM((rows, columns, cond_pad), jnp.float32),
            pltpu.VMEM((rows, columns, cond_pad), jnp.float32),
            pltpu.VMEM((columns, rows, 1, cond_pad), jnp.float32),
            pltpu.VMEM((columns, rows, 1, cond_pad), jnp.float32),
            wide_row(6 * D), wide_row(3 * D), wide_row(D), wide_row(FF), wide_row(D),
            wide_row(6 * D), wide_row(3 * D), wide_row(D), wide_row(FF), wide_row(D),
            single(1), single(1), single(D), single(D), single(D), single(D), single(FF),
            half(D), turned, half(D), turned, half(D), turned,
            half(D), turned, half(3 * D),
            half(rest), half(FF), half(FF), half(3 * D), single(D), pltpu.VMEM((HEADS, length, length), jnp.float32),
        ],
        compiler_params=pltpu.CompilerParams(
            collective_id=2, has_side_effects=True, vmem_limit_bytes=62 * 2**20),
        name="run_layer",
    )(fc1_shard, fc2_turned_shard, *sources, latent_count)


def pick(mixed, columns, kind):
    width = mixed.shape[1] // columns
    edge = 3 * width // 4
    low, high = (0, edge) if kind == 0 else (edge, width)
    return jnp.concatenate(
        [mixed[:, block * width + low : block * width + high] for block in range(columns)], axis=1
    )


def spread(rows_in, columns, kind):
    width = rows_in.shape[1] // columns
    rest = width // 3 if kind == 0 else 3 * width
    zeros = jnp.zeros((rows_in.shape[0], rest), rows_in.dtype)
    pieces = []
    for block in range(columns):
        piece = rows_in[:, block * width : (block + 1) * width]
        pieces += [piece, zeros] if kind == 0 else [zeros, piece]
    return jnp.concatenate(pieces, axis=1)


def layer(latent_rows, live, cot_rows, modulation, weights, biases, columns):
    mixed_weight, fc1_weight, fc2_turned = weights
    qv_bias, proj_bias, fc1_bias, fc2_bias = biases
    length = latent_rows.shape[0]
    rows_wide = latent_rows.astype(jnp.float32)
    shift_one, scale_one, gate_one, shift_two, scale_two, gate_two = jnp.split(
        modulation, 6, axis=-1
    )
    normed_one, inverse_one = normalize_rows(rows_wide)
    hidden_one = (normed_one * (1.0 + scale_one) + shift_one).astype(bfloat)
    qkv_bias = jnp.concatenate([qv_bias[:D], jnp.zeros((D,), jnp.float32), qv_bias[D:]])
    projected = (
        pick(jnp.dot(hidden_one, mixed_weight, preferred_element_type=jnp.float32), columns, 0)
        + qkv_bias
    ).astype(bfloat)
    queries = projected[:, :D].reshape(length, HEADS, HEAD)
    key_rows = projected[:, D : 2 * D].reshape(length, HEADS, HEAD)
    values = projected[:, 2 * D :].reshape(length, HEADS, HEAD)
    scale_factor = HEAD ** (-0.5)
    scores = (
        jnp.einsum("qhe,khe->hqk", queries, key_rows, preferred_element_type=jnp.float32)
        * scale_factor
    )
    row_max = jnp.max(scores, axis=-1, keepdims=True)
    shifted = jnp.exp(scores - row_max)
    row_total = jnp.sum(shifted, axis=-1, keepdims=True)
    exact_probability = shifted / row_total
    probability = exact_probability.astype(bfloat)
    attended = jnp.einsum("hqk,khe->qhe", probability, values, preferred_element_type=jnp.float32)
    attended = attended.reshape(length, D).astype(bfloat)
    branch = pick(jnp.dot(attended, mixed_weight, preferred_element_type=jnp.float32), columns, 1)
    branch = branch + proj_bias
    middle = rows_wide + gate_one * branch
    normed_two, inverse_two = normalize_rows(middle)
    hidden_two = (normed_two * (1.0 + scale_two) + shift_two).astype(bfloat)
    pre_gelu = jnp.dot(hidden_two, fc1_weight, preferred_element_type=jnp.float32) + fc1_bias
    activated, gelu_pull = jax.vjp(
        lambda argument: jax.nn.gelu(argument, approximate=True), pre_gelu
    )
    activated = activated.astype(bfloat)
    mlp_out = against_weight(activated, fc2_turned) + fc2_bias
    block_out = (live * (middle + gate_two * mlp_out)).astype(bfloat)

    grad_out = live * cot_rows.astype(jnp.float32)
    gate_two_grad = jnp.sum(grad_out * mlp_out, axis=0, keepdims=True)
    grad_mlp = (gate_two * grad_out).astype(bfloat)
    fc2_bias_grad = jnp.sum(grad_mlp.astype(jnp.float32), axis=0)
    grad_act = jnp.dot(grad_mlp, fc2_turned, preferred_element_type=jnp.float32)
    grad_pre = gelu_pull(grad_act)[0].astype(bfloat)
    fc1_bias_grad = jnp.sum(grad_pre.astype(jnp.float32), axis=0)
    grad_hidden_two = against_weight(grad_pre, fc1_weight)
    shift_two_grad = jnp.sum(grad_hidden_two, axis=0, keepdims=True)
    scale_two_grad = jnp.sum(grad_hidden_two * normed_two, axis=0, keepdims=True)
    grad_middle = grad_out + norm_backward(
        grad_hidden_two * (1.0 + scale_two), normed_two, inverse_two
    )
    gate_one_grad = jnp.sum(grad_middle * branch, axis=0, keepdims=True)
    grad_branch = (gate_one * grad_middle).astype(bfloat)
    proj_bias_grad = jnp.sum(grad_branch.astype(jnp.float32), axis=0)
    spread_branch = spread(grad_branch, columns, 1)
    grad_attended = (
        against_weight(spread_branch, mixed_weight).astype(bfloat).reshape(length, HEADS, HEAD)
    )
    grad_prob = jnp.einsum(
        "qhe,khe->hqk", grad_attended, values, preferred_element_type=jnp.float32
    )
    inner_sum = jnp.sum(exact_probability * grad_prob, axis=-1, keepdims=True)
    grad_scores = (exact_probability * (grad_prob - inner_sum)).astype(bfloat)
    grad_queries = (
        jnp.einsum("hqk,khe->qhe", grad_scores, key_rows, preferred_element_type=jnp.float32)
        * scale_factor
    )
    grad_keys = (
        jnp.einsum("hqk,qhe->khe", grad_scores, queries, preferred_element_type=jnp.float32)
        * scale_factor
    )
    grad_values = jnp.einsum(
        "hqk,qhe->khe", probability, grad_attended, preferred_element_type=jnp.float32
    )
    grad_projected = jnp.concatenate(
        [
            grad_queries.reshape(length, D),
            grad_keys.reshape(length, D),
            grad_values.reshape(length, D),
        ],
        axis=1,
    ).astype(bfloat)
    summed = jnp.sum(grad_projected.astype(jnp.float32), axis=0)
    qv_bias_grad = jnp.concatenate([summed[:D], summed[2 * D :]])
    spread_projected = spread(grad_projected, columns, 0)
    grad_hidden_one = against_weight(spread_projected, mixed_weight)
    shift_one_grad = jnp.sum(grad_hidden_one, axis=0, keepdims=True)
    scale_one_grad = jnp.sum(grad_hidden_one * normed_one, axis=0, keepdims=True)
    latent_grad = (
        grad_middle + norm_backward(grad_hidden_one * (1.0 + scale_one), normed_one, inverse_one)
    ).astype(bfloat)
    mod_grad = jnp.concatenate(
        [
            shift_one_grad,
            scale_one_grad,
            gate_one_grad,
            shift_two_grad,
            scale_two_grad,
            gate_two_grad,
        ],
        axis=-1,
    )
    weight_grads = (
        contract_rows(
            jnp.concatenate([hidden_one, attended]),
            jnp.concatenate([spread_projected, spread_branch]),
        ).astype(bfloat),
        contract_rows(hidden_two, grad_pre).astype(bfloat),
        contract_rows(grad_mlp, activated).astype(bfloat),
    )
    bias_grads = (qv_bias_grad, proj_bias_grad, fc1_bias_grad, fc2_bias_grad)
    return block_out, latent_grad, mod_grad, weight_grads, bias_grads


def flatten_blocks(blocks, turned):
    if blocks.ndim == 2:
        return blocks
    columns, rows, height, width = blocks.shape
    if turned:
        return blocks.transpose(0, 2, 1, 3).reshape(columns * height, rows * width)
    return blocks.transpose(1, 2, 0, 3).reshape(rows * height, columns * width)


def cut_blocks(whole, shape, turned, rows, columns):
    if len(whole_shape(shape, turned, rows, columns)) == 2:
        return whole
    height, width = shape
    if turned:
        return whole.reshape(columns, height, rows, width).transpose(0, 2, 1, 3)
    return whole.reshape(rows, height, columns, width).transpose(2, 0, 1, 3)


def per_device(
    latents,
    conditioning,
    cotangent,
    latent_count,
    ada_weight,
    ada_bias,
    qkv_weight,
    qv_bias,
    proj_weight,
    proj_bias,
    fc1_weight,
    fc1_bias,
    fc2_weight,
    fc2_bias,
):
    rows, columns = lax.axis_size("dp"), lax.axis_size("fsdp")
    if rows == 4 and columns == 8:
        sources = (
            latents[0], cotangent[0], conditioning, ada_weight, ada_bias, qkv_weight, qv_bias,
            proj_weight, proj_bias, fc1_bias, fc2_bias)
        *wholes, small = run_layer(
            fc1_weight, fc2_weight.T, sources, latent_count, rows, columns)
        widths = [bias.shape[0] for bias in (ada_bias, qv_bias, proj_bias, fc1_bias, fc2_bias)]
        (
            cond_grad, ada_bias_grad, qv_bias_grad, proj_bias_grad, fc1_bias_grad, fc2_bias_grad,
            block_out, latent_grad, ada_grad, qkv_grad, proj_grad, fc1_grad, fc2_turned_grad,
        ) = emit(small, wholes, widths)
        return (
            block_out[None], latent_grad[None], cond_grad, ada_grad, ada_bias_grad, qkv_grad,
            qv_bias_grad, proj_grad, proj_bias_grad, fc1_grad, fc1_bias_grad, fc2_turned_grad.T,
            fc2_bias_grad,
        )
    live = latent_count[0].astype(jnp.float32)
    depth = ada_weight.shape[0]
    mod_width = ada_weight.shape[1]
    mod_pad = round_up(mod_width)
    own_biases = (qv_bias, proj_bias, fc1_bias, fc2_bias)
    widths = [bias.shape[0] for bias in own_biases]
    cuts = [sum(widths[:place]) for place in range(len(widths))]

    def split_cond(row):
        pad = round_up(depth) - depth
        return jnp.pad(row.reshape(rows, 1, depth), ((0, 0), (0, 0), (0, pad)))

    cond_row = conditioning.astype(jnp.float32)
    cond_act, silu_pull = jax.vjp(jax.nn.silu, cond_row)
    slope = silu_pull(jnp.ones_like(cond_row))[0]
    cond_rows = split_cond(cond_act.astype(bfloat).astype(jnp.float32))
    bias_row = jnp.concatenate(own_biases).astype(jnp.float32).reshape(1, -1)

    qkv_width = qkv_weight.shape[1]
    shards = (
        jnp.concatenate([qkv_weight, proj_weight], axis=1),
        fc1_weight,
        fc2_weight.T,
    )
    shapes = [shard.shape for shard in shards]
    ada_row = ada_bias.astype(jnp.float32).reshape(1, -1)
    *blocks, mod_blocks, bias_blocks, cond_in = gather_shards(
        shards, cond_rows, ada_weight, ada_row, bias_row,
        rows, columns)
    modulation = mod_blocks[:, :, :mod_width].reshape(1, -1)
    biases = tuple(
        bias_blocks[:, :, cut : cut + width].reshape(-1) for cut, width in zip(cuts, widths)
    )
    weights = [flatten_blocks(block, part == 2) for part, block in enumerate(blocks)]
    block_out, latent_grad, mod_grad, weight_grads, bias_grads = layer(
        latents[0], live, cotangent[0], modulation, weights, biases, columns
    )
    grads = [
        cut_blocks(grad, shapes[part], part == 2, rows, columns)
        for part, grad in enumerate(weight_grads)
    ]
    leaving = jnp.concatenate(
        [jnp.pad(mod_grad.reshape(columns, -1), ((0, 0), (0, mod_pad - mod_width)))]
        + [grad.reshape(columns, -1) for grad in bias_grads], axis=1
    ).reshape(columns, 1, -1)
    mixed_grad, fc1_grad, fc2_turned_grad, ada_grad, sums, cond_grad = scatter_shards(
        grads, leaving, cond_in, ada_weight, split_cond(slope), shapes, rows, columns)
    qkv_grad, proj_grad = mixed_grad[:, :qkv_width], mixed_grad[:, qkv_width:]
    fc2_grad = fc2_turned_grad.T
    ada_bias_grad = sums[0, :mod_width]
    bias_sums = [
        sums[0, mod_pad + cut : mod_pad + cut + width] for cut, width in zip(cuts, widths)]
    cond_grad = cond_grad[:, :, :depth].reshape(1, -1)
    return (
        block_out[None],
        latent_grad[None],
        cond_grad,
        ada_grad,
        ada_bias_grad,
        qkv_grad,
        bias_sums[0],
        proj_grad,
        bias_sums[1],
        fc1_grad,
        bias_sums[2],
        fc2_grad,
        bias_sums[3],
    )


def solution(mesh):
    in_specs = (
        P(("dp", "fsdp"), None, None),
        P(("dp", "fsdp"), None),
        P(("dp", "fsdp"), None, None),
        P(("dp", "fsdp")),
        P("dp", "fsdp"),
        P("fsdp"),
        P("dp", "fsdp"),
        P("fsdp"),
        P("dp", "fsdp"),
        P("fsdp"),
        P("dp", "fsdp"),
        P("fsdp"),
        P("dp", "fsdp"),
        P("fsdp"),
    )
    out_specs = (
        P(("dp", "fsdp"), None, None),
        P(("dp", "fsdp"), None, None),
        P(("dp", "fsdp"), None),
        P("dp", "fsdp"),
        P("fsdp"),
        P("dp", "fsdp"),
        P("fsdp"),
        P("dp", "fsdp"),
        P("fsdp"),
        P("dp", "fsdp"),
        P("fsdp"),
        P("dp", "fsdp"),
        P("fsdp"),
    )
    return jax.shard_map(
        per_device, mesh=mesh, in_specs=in_specs, out_specs=out_specs, check_vma=False
    )
```

```python
import functools
import jax
import jax.numpy as jnp
from jax import lax
from jax.sharding import PartitionSpec as P
from jax.experimental import pallas as pl
from jax.experimental.pallas import tpu as pltpu

MESH_IDS = pl.DeviceIdType.MESH
D = 768
HEADS = 12
HEAD = 64
FF = 3072

highest = lax.Precision.HIGHEST
bfloat = jnp.bfloat16
LAG = 2
AHEAD = 3


def place(dp_index, z_index, core):
    return (dp_index, z_index * 2 + core)


def z_order(size):
    steps = [0]
    for distance in range(1, size // 2 + 1):
        steps.append(distance)
        if size - distance != distance:
            steps.append(size - distance)
    return steps


def device_of(index, columns):
    return (index // columns, lax.rem(index, columns))


def enter_barrier(me, rows, columns):
    barrier = pltpu.get_barrier_semaphore()
    count = rows * columns

    @pl.loop(1, count)
    def _(step):
        target = device_of(lax.rem(me + step, count), columns)
        pl.semaphore_signal(barrier, inc=1, device_id=target, device_id_type=MESH_IDS)

    pl.semaphore_wait(barrier, count - 1)


class Exchange:
    def __init__(self, me, rows, columns, row_for, landing, send_sems, recv_sems):
        self.me, self.columns, self.count = me, columns, rows * columns
        self.row_for, self.landing = row_for, landing
        self.send_sems, self.recv_sems = send_sems, recv_sems

    def start(self):
        @pl.loop(1, self.count)
        def _(step):
            target = lax.rem(self.me + step, self.count)
            pltpu.make_async_remote_copy(
                src_ref=self.row_for(target),
                dst_ref=self.landing.at[self.me],
                send_sem=self.send_sems.at[target],
                recv_sem=self.recv_sems.at[self.me],
                device_id=device_of(target, self.columns),
                device_id_type=MESH_IDS,
            ).start()

        self.landing[self.me] = self.row_for(self.me)[...]

    def pair(self, other):
        return pltpu.make_async_remote_copy(
            src_ref=self.row_for(other),
            dst_ref=self.landing.at[other],
            send_sem=self.send_sems.at[other],
            recv_sem=self.recv_sems.at[other],
            device_id=device_of(other, self.columns),
            device_id_type=MESH_IDS,
        )

    def wait_arrivals(self):
        @pl.loop(1, self.count)
        def _(step):
            self.pair(lax.rem(self.me + step, self.count)).wait_recv()

    def wait_sends(self):
        @pl.loop(1, self.count)
        def _(step):
            self.pair(lax.rem(self.me + step, self.count)).wait_send()


def positions(rows, depth):
    dp = lax.axis_index("dp")
    column = lax.axis_index("fsdp")
    z, core = column // 2, column % 2
    others = [(dp ^ 1), (dp ^ 2)] if rows == 4 else [(dp + step) % rows for step in range(1, rows)]
    return dp, z, core, others


def block_of(array, line, row, shape, turned):
    if len(array.shape) == 4:
        return array.at[line, row]
    high, wide = (line, row) if turned else (row, line)
    height, width = shape
    return array.at[
        pl.ds(pl.multiple_of(high * height, height), height),
        pl.ds(pl.multiple_of(wide * width, width), width),
    ]


def whole_shape(shape, turned, rows, columns):
    height, width = shape
    if width % 128 == 0 and height % 32 == 0:
        return (columns * height, rows * width) if turned else (rows * height, columns * width)
    return (columns, rows, height, width)


def gather_kernel(rows, depth, *refs):
    shards = refs[:3]
    cond_rows, ada_ref, ada_bias, bias_row = refs[3:7]
    outs, mod_out, bias_out, cond_in = refs[7:10], refs[10], refs[11], refs[12]
    (
        own_sems, send_sems, recv_sems, bias_in, part_out, part_in,
        cond_send, cond_recv, part_send, part_recv, bias_send, bias_recv,
    ) = refs[13:]
    dp, z, core, others = positions(rows, depth)
    columns = 2 * depth
    column = lax.axis_index("fsdp")
    me = dp * columns + column
    sibling = place(dp, z, 1 - core)
    enter_barrier(me, rows, columns)
    sends = []

    cond_swap = Exchange(
        me, rows, columns, lambda target: cond_rows.at[target // columns], cond_in,
        cond_send, cond_recv)
    part_swap = Exchange(
        me, rows, columns, lambda target: part_out.at[target], part_in, part_send, part_recv)
    cond_swap.start()

    def bias_copy(target, slot):
        return pltpu.make_async_remote_copy(
            src_ref=bias_row, dst_ref=bias_in.at[slot], send_sem=bias_send.at[target],
            recv_sem=bias_recv.at[slot], device_id=(dp, target), device_id_type=MESH_IDS)

    @pl.loop(1, columns)
    def _(step):
        bias_copy(lax.rem(column + step, columns), column).start()

    bias_in[column] = bias_row[...]

    def slot_of(part, line, row):
        return block_of(outs[part], line, row, shards[part].shape, part == 2)

    def half_of(ref, part, which):
        half = shards[part].shape[0] // 2
        return ref.at[pl.ds(which * half, half)]

    def send(line, row, target, which=None, own=False):
        for part in range(3):
            destination = slot_of(part, line, row)
            source = shards[part] if own else destination
            if which is not None:
                source, destination = half_of(source, part, which), half_of(destination, part, which)
            copy = pltpu.make_async_remote_copy(
                src_ref=source,
                dst_ref=destination,
                send_sem=send_sems.at[len(sends)],
                recv_sem=recv_sems.at[which or 0, part, line, row],
                device_id=target,
                device_id_type=MESH_IDS,
            )
            copy.start()
            sends.append(copy)

    def arrive(line, row, which=None):
        for part in range(3):
            destination = slot_of(part, line, row)
            if which is not None:
                destination = half_of(destination, part, which)
            pltpu.make_async_remote_copy(
                src_ref=destination,
                dst_ref=destination,
                send_sem=send_sems.at[0],
                recv_sem=recv_sems.at[which or 0, part, line, row],
                device_id=sibling,
                device_id_type=MESH_IDS,
            ).wait_recv()

    own = z * 2 + core
    steps = z_order(depth)
    lines = [((z - step) % depth) * 2 + core for step in steps]
    for other in others:
        send(own, dp, place(other, z, core), own=True)
    for step in steps[1:]:
        send(own, dp, place(dp, (z + step) % depth, core), own=True)
    send(own, dp, sibling, own=True)
    keeps = [
        pltpu.make_async_copy(shards[part], slot_of(part, own, dp), own_sems.at[part])
        for part in range(3)
    ]
    for keep in keeps:
        keep.start()
    cond_swap.wait_arrivals()
    high, wide = ada_ref.shape
    part = jnp.dot(
        cond_in[:, 0, :high].astype(bfloat), ada_ref[...], preferred_element_type=jnp.float32)
    part_out[:, 0, :wide] = part + jnp.where(dp == 0, ada_bias[...], 0.0)
    part_swap.start()
    for turn in range(depth + 2):
        if 0 < turn < depth:
            line = lines[turn]
            arrive(line, dp)
            for other in others:
                send(line, dp, place(other, z, core))
            send(line, dp, sibling)
        if 1 <= turn <= depth:
            line = lines[turn - 1]
            for position, other in enumerate(others):
                arrive(line, other)
                if rows == 4:
                    send(line, other, place(others[1 - position], z, core), which=position)
                send(line, other, sibling)
        if turn >= 2 and rows == 4:
            line = lines[turn - 2]
            arrive(line, dp ^ 3, 0)
            arrive(line, dp ^ 3, 1)
            send(line, dp ^ 3, sibling)
    for line in lines:
        for row in range(rows):
            arrive(line + 1 - 2 * core, (dp + row) % rows)
    part_swap.wait_arrivals()
    for block in range(columns):
        total = part_in[block]
        for row in range(1, rows):
            total = total + part_in[row * columns + block]
        mod_out[block] = total

    @pl.loop(1, columns)
    def _(step):
        other = lax.rem(column + step, columns)
        bias_copy(other, other).wait_recv()
        bias_copy(other, other).wait_send()

    bias_out[...] = bias_in[...]
    for keep in keeps:
        keep.wait()
    for copy in sends:
        copy.wait_send()
    cond_swap.wait_sends()
    part_swap.wait_sends()


def round_up(width):
    return -(-width // 128) * 128


def gather_shards(shards, cond_rows, ada_weight, ada_bias, bias_row, rows, columns):
    depth = columns // 2
    total = rows * columns
    mod_pad = round_up(ada_weight.shape[1])
    vmem = pl.BlockSpec(memory_space=pltpu.VMEM)
    dma = pltpu.SemaphoreType.DMA
    row_shape = lambda count, width: jax.ShapeDtypeStruct((count, 1, width), jnp.float32)
    row_buffer = lambda count, width: pltpu.VMEM((count, 1, width), jnp.float32)
    count = (depth - 1) + depth * rows + depth * (rows - 1) + (2 * depth if rows == 4 else 0)
    shapes = [
        whole_shape(shard.shape, part == 2, rows, columns) for part, shard in enumerate(shards)
    ]
    return pl.pallas_call(
        functools.partial(gather_kernel, rows, depth),
        out_shape=[jax.ShapeDtypeStruct(shape, bfloat) for shape in shapes]
        + [row_shape(columns, mod_pad), row_shape(columns, bias_row.shape[-1]),
           row_shape(total, cond_rows.shape[-1])],
        in_specs=[pl.BlockSpec(memory_space=pl.ANY)] * 3 + [vmem] * 4,
        out_specs=[pl.BlockSpec(memory_space=pl.ANY)] * 3 + [vmem] * 3,
        scratch_shapes=[
            dma((3,)),
            dma((3 * count,)),
            dma((2, 3, columns, rows)),
            row_buffer(columns, bias_row.shape[-1]),
            row_buffer(total, mod_pad),
            row_buffer(total, mod_pad),
            dma((total,)), dma((total,)), dma((total,)), dma((total,)),
            dma((columns,)), dma((columns,)),
        ],
        compiler_params=pltpu.CompilerParams(
            collective_id=0, has_side_effects=True, vmem_limit_bytes=32 * 2**20),
        name="gather_shards",
    )(*shards, cond_rows, ada_weight, ada_bias, bias_row)


def scatter_kernel(rows, depth, *refs):
    grads = refs[:3]
    leaving, cond_in, ada_ref, slope = refs[3:7]
    outs, ada_grad, sums_out, cond_grad = refs[7:10], refs[10], refs[11], refs[12]
    refs = refs[13:]
    helds, pairs_in, planes_in, crosses_in, alongs_in = (
        refs[3 * kind : 3 + 3 * kind] for kind in range(5)
    )
    (
        load_sems, pair_send, pair_recv, plane_send, plane_recv,
        cross_send, cross_recv, along_send, along_recv,
        all_rows, back_out, back_in, row_send, row_recv, back_send, back_recv,
    ) = refs[15:]
    dp, z, core, others = positions(rows, depth)
    columns = 2 * depth
    me = dp * columns + lax.axis_index("fsdp")
    row_swap = Exchange(
        me, rows, columns, lambda target: leaving.at[lax.rem(target, columns)], all_rows,
        row_send, row_recv)
    back_swap = Exchange(
        me, rows, columns, lambda target: back_out.at[target], back_in, back_send, back_recv)
    sibling = place(dp, z, 1 - core)
    targets = [dp ^ 3, dp ^ 1, dp ^ 2, dp] if rows == 4 else others + [dp]
    steps = z_order(depth)[::-1]
    enter_barrier(me, rows, columns)
    row_swap.start()
    waits = []

    def remote(source, destination, send_sem, recv_sem, target):
        copy = pltpu.make_async_remote_copy(
            src_ref=source, dst_ref=destination, send_sem=send_sem, recv_sem=recv_sem,
            device_id=target, device_id_type=MESH_IDS,
        )
        copy.start()
        waits.append(copy)
        return copy

    def add(first, others_in, length, target):
        chunk = 48 if length % 48 == 0 else 16

        @pl.loop(0, length // chunk)
        def _(index):
            piece = pl.ds(pl.multiple_of(index * chunk, chunk), chunk)
            total = first[piece, :].astype(jnp.float32)
            for other in others_in:
                total = total + other[piece, :].astype(jnp.float32)
            target[piece, :] = total.astype(target.dtype)

    lines = [(z + step) % depth for step in steps]
    pairs, loads, planes, crosses, alongs = {}, {}, {}, {}, {}
    for turn, line in enumerate(lines):
        for slot, target in enumerate(targets):
            for part in range(3):
                key = (part, turn, slot)
                shape = outs[part].shape
                pairs[key] = remote(
                    block_of(grads[part], line * 2 + 1 - core, target, shape, part == 2),
                    pairs_in[part].at[turn, slot], pair_send.at[key], pair_recv.at[key], sibling)
                loads[key] = pltpu.make_async_copy(
                    block_of(grads[part], line * 2 + core, target, shape, part == 2),
                    helds[part].at[turn, slot], load_sems.at[key])
                loads[key].start()
    last = len(targets) - 1
    for turn in range(depth + 2):
        if turn == depth - 1:
            row_swap.wait_arrivals()
            high, wide = ada_ref.shape
            arrived = all_rows[:, 0, :]
            sums_out[...] = jnp.sum(arrived, axis=0, keepdims=True)
            ada_grad[...] = contract_exact(cond_in[:, 0, :high], arrived[:, :wide])
            back_out[:, 0, :high] = lax.dot_general(
                arrived[:, :wide], ada_ref[...].astype(jnp.float32), (((1,), (1,)), ((), ())),
                precision=highest)
            back_swap.start()
        if turn < depth:
            for slot in range(len(targets)):
                for part in range(3):
                    key = (part, turn, slot)
                    height = outs[part].shape[0]
                    half = height // 2
                    loads[key].wait()
                    pairs[key].wait_recv()
                    here = helds[part].at[turn, slot]
                    add(here, [pairs_in[part].at[turn, slot]], height, here)
                    if rows == 4 and slot == 0:
                        for position in range(2):
                            key = (part, turn, position)
                            crosses[key] = remote(
                                helds[part].at[turn, 0, pl.ds((1 - position) * half, half)],
                                crosses_in[part].at[turn, position],
                                cross_send.at[key], cross_recv.at[key],
                                place(others[position], z, core))
                    if rows != 4 and slot < last:
                        planes[key] = remote(
                            here, planes_in[part].at[turn, slot], plane_send.at[key],
                            plane_recv.at[key], place(targets[slot], z, core))
        if rows == 4 and 1 <= turn <= depth:
            now = turn - 1
            for position in range(2):
                for part in range(3):
                    half = outs[part].shape[0] // 2
                    crosses[part, now, 1 - position].wait_recv()
                    piece = helds[part].at[now, 1 + position, pl.ds(position * half, half)]
                    add(piece, [crosses_in[part].at[now, 1 - position]], half, piece)
                    key = (part, now, position)
                    planes[key] = remote(
                        helds[part].at[now, 1 + position], planes_in[part].at[now, position],
                        plane_send.at[key], plane_recv.at[key],
                        place(others[position], z, core))
        if turn >= 2:
            now = turn - 2
            for part in range(3):
                for slot in range(len(others)):
                    planes[part, now, slot].wait_recv()
                here = helds[part].at[now, last]
                arrived = [planes_in[part].at[now, slot] for slot in range(len(others))]
                add(here, arrived, outs[part].shape[0], here)
                if now < depth - 1:
                    key = (part, now)
                    alongs[key] = remote(
                        here, alongs_in[part].at[now], along_send.at[key], along_recv.at[key],
                        place(dp, lines[now], core))
    for part in range(3):
        for now in range(depth - 1):
            alongs[part, now].wait_recv()
        arrived = [alongs_in[part].at[now] for now in range(depth - 1)]
        add(helds[part].at[depth - 1, last], arrived, outs[part].shape[0], outs[part])
    back_swap.wait_arrivals()
    for row in range(rows):
        total = back_in[row * columns]
        for block in range(1, columns):
            total = total + back_in[row * columns + block]
        cond_grad[row] = total * slope[row]
    for copy in waits:
        copy.wait_send()
    row_swap.wait_sends()
    back_swap.wait_sends()


def scatter_shards(grads, leaving, cond_in, ada_weight, slope, shapes, rows, columns):
    depth = columns // 2
    total = rows * columns
    vmem = pl.BlockSpec(memory_space=pltpu.VMEM)
    row_buffer = lambda count, width: pltpu.VMEM((count, 1, width), jnp.float32)
    peers = 2 if rows == 4 else rows - 1
    dma = pltpu.SemaphoreType.DMA
    buffers = []
    for lead in ((depth, rows), (depth, rows), (depth, peers), (depth, 2), (depth - 1,)):
        for height, width in shapes:
            if lead == (depth, 2) and len(buffers) >= 9:
                height = height // 2 if rows == 4 else 16
            buffers.append(pltpu.VMEM(lead + (height, width), bfloat))
    return pl.pallas_call(
        functools.partial(scatter_kernel, rows, depth),
        out_shape=[jax.ShapeDtypeStruct(shape, jnp.float32) for shape in shapes]
        + [jax.ShapeDtypeStruct(ada_weight.shape, jnp.float32),
           jax.ShapeDtypeStruct((1, leaving.shape[-1]), jnp.float32),
           jax.ShapeDtypeStruct(slope.shape, jnp.float32)],
        in_specs=[pl.BlockSpec(memory_space=pl.ANY)] * 3 + [vmem] * 4,
        out_specs=[vmem] * 6,
        scratch_shapes=buffers + [
            dma((3, depth, rows)), dma((3, depth, rows)), dma((3, depth, rows)),
            dma((3, depth, peers)), dma((3, depth, peers)),
            dma((3, depth, 2)), dma((3, depth, 2)),
            dma((3, depth - 1)), dma((3, depth - 1)),
            row_buffer(total, leaving.shape[-1]),
            row_buffer(total, slope.shape[-1]), row_buffer(total, slope.shape[-1]),
            dma((total,)), dma((total,)), dma((total,)), dma((total,)),
        ],
        compiler_params=pltpu.CompilerParams(
            collective_id=1, has_side_effects=True, vmem_limit_bytes=50 * 2**20),
        name="scatter_shards",
    )(*grads, leaving, cond_in, ada_weight, slope)


def normalize_rows(values):
    center = jnp.mean(values, axis=-1, keepdims=True)
    spread = jnp.mean(jnp.square(values - center), axis=-1, keepdims=True)
    inverse = lax.rsqrt(spread + 1e-06)
    return ((values - center) * inverse, inverse)


def norm_backward(grad_normed, normed, inverse):
    centered = grad_normed - jnp.mean(grad_normed, axis=-1, keepdims=True)
    return inverse * (centered - normed * jnp.mean(grad_normed * normed, axis=-1, keepdims=True))


def contract_rows(left_rows, right_rows):
    return lax.dot_general(
        left_rows, right_rows, (((0,), (0,)), ((), ())), preferred_element_type=jnp.float32
    )


def contract_exact(left_rows, right_rows):
    return lax.dot_general(left_rows, right_rows, (((0,), (0,)), ((), ())), precision=highest)


def against_weight(grad_rows, weight):
    return lax.dot_general(
        grad_rows, weight, (((1,), (1,)), ((), ())), preferred_element_type=jnp.float32
    )


def dot_plain(left, right):
    return jnp.dot(left, right, preferred_element_type=jnp.float32)


def columns_sum(values):
    return jnp.sum(values, axis=0, keepdims=True)


class Swap:
    def __init__(self, me, size, device, row_for, landing, send_sems, recv_sems):
        self.me, self.size, self.device = me, size, device
        self.row_for, self.landing = row_for, landing
        self.send_sems, self.recv_sems = send_sems, recv_sems
        self.copies = []

    def start(self):
        for step in range(1, self.size):
            other = lax.rem(self.me + step, self.size)
            copy = pltpu.make_async_remote_copy(
                src_ref=self.row_for(other),
                dst_ref=self.landing.at[self.me],
                send_sem=self.send_sems.at[step],
                recv_sem=self.recv_sems.at[step],
                device_id=self.device(other),
                device_id_type=MESH_IDS,
            )
            copy.start()
            self.copies.append(copy)
        self.landing[self.me] = self.row_for(self.me)[...]

    def wait_arrivals(self):
        for copy in self.copies:
            copy.wait_recv()

    def wait_sends(self):
        for copy in self.copies:
            copy.wait_send()


class Gather:
    def __init__(self, rows, depth, where, shards, outs, own_sems, send_sems, recv_sems):
        self.rows, self.depth = rows, depth
        self.dp, self.z, self.core, self.others = where
        self.shards, self.outs = shards, outs
        self.own_sems, self.send_sems, self.recv_sems = own_sems, send_sems, recv_sems
        self.sibling = place(self.dp, self.z, 1 - self.core)
        self.sends = []
        self.keeps = []
        self.own = self.z * 2 + self.core
        self.steps = [0] + list(range(2, depth)) + [1]
        self.lines = [(self.z ^ step) * 2 + self.core for step in self.steps]
        self.units = [(part, turn) for part in range(3) for turn in range(depth)]
        self.helped = depth - 1

    def slot_of(self, part, line, row):
        return block_of(self.outs[part], line, row, self.shards[part].shape, part == 2)

    def half_of(self, ref, part, which):
        half = self.shards[part].shape[0] // 2
        return ref.at[pl.ds(which * half, half)]

    def send(self, part, line, row, target, which=None, own=False):
        destination = self.slot_of(part, line, row)
        source = self.shards[part] if own else destination
        if which is not None:
            source, destination = (
                self.half_of(source, part, which), self.half_of(destination, part, which))
        copy = pltpu.make_async_remote_copy(
            src_ref=source,
            dst_ref=destination,
            send_sem=self.send_sems.at[len(self.sends)],
            recv_sem=self.recv_sems.at[which or 0, part, line, row],
            device_id=target,
            device_id_type=MESH_IDS,
        )
        copy.start()
        self.sends.append(copy)

    def arrive(self, part, line, row, which=None):
        destination = self.slot_of(part, line, row)
        if which is not None:
            destination = self.half_of(destination, part, which)
        pltpu.make_async_remote_copy(
            src_ref=destination,
            dst_ref=destination,
            send_sem=self.send_sems.at[0],
            recv_sem=self.recv_sems.at[which or 0, part, line, row],
            device_id=self.sibling,
            device_id_type=MESH_IDS,
        ).wait_recv()

    def send_own(self, part):
        for other in self.others:
            self.send(part, self.own, self.dp, place(other, self.z, self.core), own=True)
        self.send(part, self.own, self.dp, self.sibling, own=True)
        keep = pltpu.make_async_copy(
            self.shards[part], self.slot_of(part, self.own, self.dp), self.own_sems.at[part])
        keep.start()
        self.keeps.append(keep)

    def send_deep(self, index):
        if index < len(self.units):
            part, turn = self.units[index]
            if turn:
                target = place(self.dp, self.z ^ self.steps[turn], self.core)
                self.send(part, self.own, self.dp, target, own=True)

    def turn(self, index):
        dp, z, core = self.dp, self.z, self.core
        count = len(self.units)
        self.send_deep(index + AHEAD)
        if index in (1, 2):
            self.send_own(index)
        if index < count:
            part, turn = self.units[index]
            line = self.lines[turn]
            if turn:
                self.arrive(part, line, dp)
                which = 0 if turn == self.helped else None
                for other in self.others:
                    self.send(part, line, dp, place(other, z, core), which=which)
                self.send(part, line, dp, self.sibling)
        if LAG <= index < count + LAG:
            part, turn = self.units[index - LAG]
            line = self.lines[turn]
            for position, other in enumerate(self.others):
                if turn == self.helped:
                    self.arrive(part, line, other, 0)
                    self.arrive(part, line, other, 1)
                else:
                    self.arrive(part, line, other)
                    self.send(
                        part, line, other, place(self.others[1 - position], z, core),
                        which=position)
                if turn == 0:
                    self.send(part, line, other, place(dp, z ^ 1, core), which=1)
                self.send(part, line, other, self.sibling)
        if 2 * LAG <= index:
            part, turn = self.units[index - 2 * LAG]
            line = self.lines[turn]
            if turn == self.helped:
                self.arrive(part, line, dp ^ 3)
            else:
                self.arrive(part, line, dp ^ 3, 0)
                self.arrive(part, line, dp ^ 3, 1)
            if turn == 0:
                self.send(part, line, dp ^ 3, place(dp, z ^ 1, core))
            self.send(part, line, dp ^ 3, self.sibling)

    def finish_part(self, part):
        for line in self.lines:
            for row in range(self.rows):
                self.arrive(part, line + 1 - 2 * self.core, (self.dp + row) % self.rows)
        self.keeps[part].wait()

    def wait_sends(self):
        for copy in self.sends:
            copy.wait_send()


class Scatter:
    def __init__(self, rows, depth, where, shapes, grads, buffers, sems):
        self.rows, self.depth, self.shapes, self.grads = rows, depth, shapes, grads
        self.dp, self.z, self.core, self.others = where
        (
            self.held, self.planes_in, self.crosses_in, self.alongs_in, self.help_in, self.half_in,
        ) = (buffers[3 * kind : 3 * kind + 3] for kind in range(6))
        (
            self.pair_send, self.pair_recv, self.plane_send, self.plane_recv,
            self.cross_send, self.cross_recv, self.along_send, self.along_recv,
            self.help_send, self.help_recv,
        ) = sems
        self.sibling = place(self.dp, self.z, 1 - self.core)
        self.targets = [self.dp ^ 3, self.dp ^ 1, self.dp ^ 2, self.dp]
        self.lines = [self.z ^ step for step in [1] + list(range(2, depth))[::-1] + [0]]
        self.units = [(part, turn) for part in (2, 1, 0) for turn in range(depth)]
        self.pairs, self.planes, self.crosses, self.alongs, self.helps = {}, {}, {}, {}, {}

    def remote(self, source, destination, send_sem, recv_sem, target):
        copy = pltpu.make_async_remote_copy(
            src_ref=source, dst_ref=destination, send_sem=send_sem, recv_sem=recv_sem,
            device_id=target, device_id_type=MESH_IDS)
        copy.start()
        return copy

    def block(self, part, line, target):
        return block_of(self.grads[part], line, target, self.shapes[part], part == 2)

    def add(self, first, others_in, length, target):
        chunk = 48

        @pl.loop(0, length // chunk)
        def _(index):
            piece = pl.ds(pl.multiple_of(index * chunk, chunk), chunk)
            total = first[piece, :].astype(jnp.float32)
            for other in others_in:
                total = total + other[piece, :].astype(jnp.float32)
            target[piece, :] = total.astype(target.dtype)

    def help(self, part, slot, source, destination):
        self.helps[part, slot] = self.remote(
            source, destination, self.help_send.at[part, slot], self.help_recv.at[part, slot],
            place(self.dp, self.z ^ 1, self.core))

    def start_pairs(self, part):
        for turn, line in enumerate(self.lines):
            for slot, target in enumerate(self.targets):
                key = (part, turn, slot)
                self.pairs[key] = self.remote(
                    self.block(part, line * 2 + 1 - self.core, target),
                    self.held[part].at[turn, slot], self.pair_send.at[key],
                    self.pair_recv.at[key], self.sibling)

    def wait_pairs_sent(self, part):
        for turn in range(self.depth):
            for slot in range(self.rows):
                self.pairs[part, turn, slot].wait_send()

    def turn(self, index):
        last = self.rows - 1
        count = len(self.units)
        if index < count:
            part, turn = self.units[index]
            height = self.shapes[part][0]
            half = height // 2
            for slot, target in enumerate(self.targets):
                self.pairs[part, turn, slot].wait_recv()
                here = self.held[part].at[turn, slot]
                own = self.block(part, self.lines[turn] * 2 + self.core, target)
                arrived = [here]
                if turn == self.depth - 1 and slot == 0:
                    self.helps[part, 0].wait_recv()
                    arrived.append(self.help_in[part])
                self.add(own, arrived, height, here)
                if turn == self.depth - 1 and slot in (1, 2):
                    self.helps[part, slot].wait_recv()
                    piece = self.held[part].at[turn, slot, pl.ds(half, half)]
                    self.add(piece, [self.half_in[part].at[slot - 1]], half, piece)
                if turn == 0 and slot == 0:
                    self.help(part, 0, here, self.help_in[part])
                elif turn == 0 and slot < 3:
                    self.help(
                        part, slot, self.held[part].at[turn, slot, pl.ds(half, half)],
                        self.half_in[part].at[slot - 1])
                    key = (part, turn, slot - 1)
                    self.planes[key] = self.remote(
                        self.held[part].at[turn, slot, pl.ds(0, half)],
                        self.planes_in[part].at[turn, slot - 1, pl.ds(0, half)],
                        self.plane_send.at[key], self.plane_recv.at[key],
                        place(self.others[slot - 1], self.z, self.core))
                elif slot == 0:
                    for position in range(2):
                        key = (part, turn, position)
                        self.crosses[key] = self.remote(
                            self.held[part].at[turn, 0, pl.ds((1 - position) * half, half)],
                            self.crosses_in[part].at[turn, position],
                            self.cross_send.at[key], self.cross_recv.at[key],
                            place(self.others[position], self.z, self.core))
        if LAG <= index < count + LAG:
            part, turn = self.units[index - LAG]
            half = self.shapes[part][0] // 2
            for position in range(2 if turn else 0):
                self.crosses[part, turn, 1 - position].wait_recv()
                piece = self.held[part].at[turn, 1 + position, pl.ds(position * half, half)]
                self.add(piece, [self.crosses_in[part].at[turn, 1 - position]], half, piece)
                key = (part, turn, position)
                self.planes[key] = self.remote(
                    self.held[part].at[turn, 1 + position], self.planes_in[part].at[turn, position],
                    self.plane_send.at[key], self.plane_recv.at[key],
                    place(self.others[position], self.z, self.core))
        if 2 * LAG <= index:
            part, turn = self.units[index - 2 * LAG]
            for position in range(2):
                self.planes[part, turn, position].wait_recv()
            height = self.shapes[part][0] if turn else self.shapes[part][0] // 2
            here = self.held[part].at[turn, last]
            piece = self.held[part].at[turn, last, pl.ds(0, height)]
            arrived = [
                self.planes_in[part].at[turn, position, pl.ds(0, height)] for position in range(2)]
            self.add(piece, arrived, height, piece)
            if turn < self.depth - 1:
                key = (part, turn)
                self.alongs[key] = self.remote(
                    here, self.alongs_in[part].at[turn], self.along_send.at[key],
                    self.along_recv.at[key], place(self.dp, self.lines[turn], self.core))

    def finish_part(self, part):
        total = self.held[part][self.depth - 1, self.rows - 1].astype(jnp.float32)
        for turn in range(self.depth - 1):
            self.alongs[part, turn].wait_recv()
            total = total + self.alongs_in[part][turn].astype(jnp.float32)
        return total

    def wait_sends(self):
        for copies in (self.planes, self.crosses, self.alongs, self.helps):
            for copy in copies.values():
                copy.wait_send()


def layer_kernel(rows, depth, *refs):
    sources, live_ref, outs = refs[2:13], refs[13], refs[14:22]
    landed = refs[22:33]
    results = landed[:2] + refs[33:39]
    (
        latents, cotangent, conditioning, ada_ref, ada_bias, qkv_shard, qv_shard, proj_shard,
        proj_bias_shard, fc1_bias_shard, fc2_bias_shard,
    ) = landed
    block_out, latent_grad, ada_grad, qkv_grad, proj_grad, fc1_grad, fc2_grad, small = results
    mixed_shard, cond_rows, slope, load_sems, store_sems = refs[39:44]
    shards = (mixed_shard, refs[0], refs[1])
    refs = refs[44:]
    weights, grads = refs[:3], (refs[3], refs[4], refs[3])
    scatter_buffers, scatter_sems = refs[5:23], refs[23:33]
    (
        own_sems, send_sems, recv_sems, swap_send, swap_recv,
        cond_across, cond_own, cond_along, cond_in, part_out, part_across, part_row, part_along,
        leaving, rows_along, rows_across, back_out, back_across, back_row, back_along,
        mod, qkv_bias, proj_bias, fc1_bias, fc2_bias, mod_grad, qkv_sums, proj_sums, fc1_sums,
        fc2_sums, inverse_one, inverse_two, normed_one, normed_two, middle, branch, wide,
        hidden_one, hidden_one_t, hidden_two, hidden_two_t, attended, attended_t,
        grad_mlp, grad_mlp_t, projected,
        grad_proj_mixed, activated, grad_pre, grad_natural, grad_state, probability,
    ) = refs[33:]
    grad_mixed, grad_attended = grad_pre, hidden_one
    mixed, fc1, fc2_turned = weights
    where = positions(rows, depth)
    dp = where[0]
    columns = 2 * depth
    column = lax.axis_index("fsdp")
    length = latents.shape[0]
    qkv_part, proj_part = 3 * D // columns, D // columns
    block = qkv_part + proj_part
    edge = qkv_part // 128 * 128
    rest = block - edge
    lead = qkv_part - edge
    scale_factor = HEAD ** (-0.5)
    ada_rows, mod_width = ada_ref.shape
    mod_pad = round_up(mod_width)
    loads = [
        pltpu.make_async_copy(source, target, load_sems.at[at])
        for at, (source, target) in enumerate(zip(sources, landed))]
    for at in (2, 5, 7, 6, 8, 9, 10, 0, 3, 4, 1):
        loads[at].start()
    stores = []

    def store(at):
        copy = pltpu.make_async_copy(results[at], outs[at], store_sems.at[at])
        copy.start()
        stores.append(copy)

    barrier = pltpu.get_barrier_semaphore()
    partners = [(lax.rem(dp + step, rows), column) for step in range(1, rows)]
    partners += [(dp, lax.rem(column + step, columns)) for step in range(1, columns)]
    for partner in partners:
        pl.semaphore_signal(barrier, inc=1, device_id=partner, device_id_type=MESH_IDS)
    live = live_ref[0].astype(jnp.float32)
    loads[2].wait()
    cond_value = conditioning[...].astype(jnp.float32)
    logistic = 1.0 / (1.0 + jnp.exp(-cond_value))
    slope[...] = logistic * (1.0 + cond_value * (1.0 - logistic))
    cond_act = (cond_value * logistic).astype(bfloat).astype(jnp.float32)
    for row in range(rows):
        cond_rows[row, :, :ada_rows] = cond_act[:, row * ada_rows : (row + 1) * ada_rows]
    pl.semaphore_wait(barrier, len(partners))
    gather = Gather(rows, depth, where, shards, weights, own_sems, send_sems, recv_sems)
    scatter = Scatter(
        rows, depth, where, [shard.shape for shard in shards], grads, scatter_buffers, scatter_sems)
    swaps = []

    def swap_across(row_for, landing):
        at = len(swaps)
        swaps.append(Swap(
            dp, rows, lambda other: (other, column), row_for, landing,
            swap_send.at[at], swap_recv.at[at]))
        return swaps[-1]

    def swap_along(row_for, landing):
        at = len(swaps)
        swaps.append(Swap(
            column, columns, lambda other: (dp, other), row_for, landing,
            swap_send.at[at], swap_recv.at[at]))
        return swaps[-1]

    cond_first = swap_across(
        lambda other: cond_rows.at[other], cond_across)
    cond_second = swap_along(lambda other: cond_own, cond_along)
    part_first = swap_across(lambda other: part_out.at[other], part_across)
    part_second = swap_along(lambda other: part_row.at[other], part_along)
    rows_first = swap_along(lambda other: leaving.at[other], rows_along)
    rows_second = swap_across(lambda other: rows_along, rows_across)
    back_first = swap_across(lambda other: back_out.at[other], back_across)
    back_second = swap_along(lambda other: back_row.at[other], back_along)
    cond_first.start()
    loads[5].wait()
    loads[7].wait()
    mixed_shard[:, :qkv_part] = qkv_shard[...]
    mixed_shard[:, qkv_part:] = proj_shard[...]
    for index in range(AHEAD):
        gather.send_deep(index)
    gather.send_own(0)

    def piece(kind):
        return mod[:, kind * D : (kind + 1) * D]

    def share_condition():
        cond_first.wait_arrivals()
        cond_own[:rows] = cond_across[...]
        bias_row = []
        for at in (6, 8, 9, 10):
            loads[at].wait()
            bias_row.append(landed[at][...].astype(jnp.float32).reshape(1, -1))
        bias_row = jnp.concatenate(bias_row, axis=1)
        pad = cond_own.shape[-1]
        for at in range(bias_row.shape[1] // pad):
            cond_own[rows + at] = bias_row[:, at * pad : (at + 1) * pad]
        cond_second.start()

    def start_modulation():
        cond_second.wait_arrivals()
        cond_in[...] = jnp.concatenate(
            [cond_along[source, row] for row in range(rows) for source in range(columns)], axis=0)
        loads[3].wait()
        loads[4].wait()
        part = dot_plain(cond_in[:, :ada_rows].astype(bfloat), ada_ref[...])
        own_bias = ada_bias[...].astype(jnp.float32).reshape(1, -1)
        part = part + jnp.where(dp == 0, own_bias, 0.0)
        for row in range(rows):
            part_out[row, :, :mod_width] = part[row * columns : (row + 1) * columns]
        part_first.start()

    def sum_modulation():
        part_first.wait_arrivals()
        total = part_across[0]
        for row in range(1, rows):
            total = total + part_across[row]
        part_row[:, 0, :] = total
        part_second.start()

    def normalize_first():
        loads[0].wait()
        normed, inverse = normalize_rows(latents[...].astype(jnp.float32))
        normed_one[...] = normed
        inverse_one[...] = inverse

    def finish_modulation():
        part_second.wait_arrivals()
        mod[...] = jnp.concatenate(
            [part_along[source][:, :mod_width] for source in range(columns)], axis=1)
        bias_parts = [
            jnp.concatenate(
                [cond_along[source, row] for row in range(rows, cond_along.shape[1])], axis=1)
            for source in range(columns)]
        low = 0
        naturals = []
        for width in (2 * D // columns, D // columns, FF // columns, D // columns):
            naturals.append(jnp.concatenate(
                [part[:, low : low + width] for part in bias_parts], axis=1))
            low += width
        qkv_bias[:, :D] = naturals[0][:, :D]
        qkv_bias[:, D : 2 * D] = jnp.zeros((1, D), jnp.float32)
        qkv_bias[:, 2 * D :] = naturals[0][:, D:]
        proj_bias[...] = naturals[1]
        fc1_bias[...] = naturals[2]
        fc2_bias[...] = naturals[3]
        hidden = (normed_one[...] * (1.0 + piece(1)) + piece(0)).astype(bfloat)
        hidden_one[...] = hidden
        hidden_one_t[...] = hidden.T

    def start_gradient():
        loads[1].wait()
        grad = (piece(5) * (live * cotangent[...].astype(jnp.float32))).astype(bfloat)
        grad_mlp[...] = grad
        grad_mlp_t[...] = grad.T
        fc2_sums[...] = columns_sum(grad.astype(jnp.float32))

    def span(index, width):
        return pl.ds(pl.multiple_of(index * width, width), width)

    def project():
        @pl.loop(0, columns)
        def _(index):
            wide[:, span(index, block)] = dot_plain(hidden_one[...], mixed[:, span(index, block)])

        for index in range(columns):
            natural = slice(index * qkv_part, (index + 1) * qkv_part)
            projected[:, natural] = (
                wide[:, index * block : index * block + qkv_part] + qkv_bias[:, natural]
            ).astype(bfloat)

    def head_slabs(source, pair):
        return [
            source[:, pl.ds(pl.multiple_of(kind * D + pair * 128, 128), 128)] for kind in range(3)]

    def own_lanes(which):
        lane = lax.broadcasted_iota(jnp.int32, (length, 128), 1)
        return lane < HEAD if which == 0 else lane >= HEAD

    def attend(low, high):
        @pl.loop(low, high)
        def _(pair):
            queries, keys, values = head_slabs(projected, pair)
            zero = jnp.zeros_like(queries)
            results = []
            for which in range(2):
                scores = against_weight(
                    jnp.where(own_lanes(which), queries, zero), keys) * scale_factor
                shifted = jnp.exp(scores - jnp.max(scores, axis=-1, keepdims=True))
                exact = shifted / jnp.sum(shifted, axis=-1, keepdims=True)
                probability[2 * pair + which] = exact
                results.append(dot_plain(exact.astype(bfloat), values))
            attended[:, span(pair, 128)] = jnp.where(
                own_lanes(0), results[0], results[1]).astype(bfloat)

    def finish_attention():
        attended_t[...] = attended[...].T

        @pl.loop(0, columns)
        def _(index):
            tail = pl.ds(pl.multiple_of(index * block + edge, 128), rest)
            wide[:, span(index, rest)] = dot_plain(attended[...], mixed[:, tail])

        for index in range(columns):
            natural = slice(index * proj_part, (index + 1) * proj_part)
            branch[:, natural] = (
                wide[:, index * rest + lead : (index + 1) * rest] + proj_bias[:, natural])
        total = latents[...].astype(jnp.float32) + piece(2) * branch[...]
        middle[...] = total
        normed, inverse = normalize_rows(total)
        normed_two[...] = normed
        inverse_two[...] = inverse
        hidden = (normed * (1.0 + piece(4)) + piece(3)).astype(bfloat)
        hidden_two[...] = hidden
        hidden_two_t[...] = hidden.T

    chunk = 1536
    chunks = FF // chunk

    def expand(low, high):
        @pl.loop(low, high)
        def _(index):
            part = span(index, chunk)
            value = dot_plain(hidden_two[...], fc1[:, part]) + fc1_bias[:, part]
            root = 0.7978845608028654
            square = value * value
            bend = jnp.tanh(root * (value + 0.044715 * (square * value)))
            activated[:, part] = (0.5 * value * (1.0 + bend)).astype(bfloat)
            wide[:, part] = 0.5 * (1.0 + bend) + 0.5 * value * (1.0 - bend * bend) * (
                root * (1.0 + 3 * 0.044715 * square))

    def fc2_weight_grad(low, high):
        @pl.loop(low, high)
        def _(index):
            part = span(index, chunk)
            grads[2][:, part] = dot_plain(grad_mlp_t[...], activated[:, part]).astype(bfloat)

    def after_part_zero():
        gather.finish_part(0)
        project()

    def after_part_one():
        gather.finish_part(1)
        expand(0, 1)

    def send_fc2_grad():
        fc2_weight_grad(1, 2)
        scatter.start_pairs(2)

    hooks = [
        share_condition, normalize_first, start_modulation, None, sum_modulation, None,
        finish_modulation, start_gradient, after_part_zero, lambda: attend(0, 3),
        lambda: attend(3, 6), finish_attention, after_part_one, lambda: expand(1, 2),
        lambda: fc2_weight_grad(0, 1), send_fc2_grad,
    ]
    for index, hook in enumerate(hooks):
        gather.turn(index)
        if hook is not None:
            hook()
    scatter.turn(0)
    gather.finish_part(2)
    third = 256

    def finish_forward():
        @pl.loop(0, D // third)
        def _(index):
            part = span(index, third)
            branch_part = against_weight(activated[...], fc2_turned[part, :]) + fc2_bias[:, part]
            live_grad = live * cotangent[:, part].astype(jnp.float32)
            last = pl.ds(pl.multiple_of(5 * D + index * third, third), third)
            block_out[:, part] = (
                live * (middle[:, part] + mod[:, last] * branch_part)).astype(bfloat)
            mod_grad[:, last] = columns_sum(live_grad * branch_part)

        store(0)

    def fc1_weight_grad(low, high):
        @pl.loop(low, high)
        def _(index):
            part = span(index, chunk)
            grad = (dot_plain(grad_mlp[...], fc2_turned[:, part]) * wide[:, part]).astype(bfloat)
            grad_pre[:, part] = grad
            fc1_sums[:, part] = columns_sum(grad.astype(jnp.float32))
            grads[1][:, part] = dot_plain(hidden_two_t[...], grad).astype(bfloat)

    def hidden_two_back():
        @pl.loop(0, D // third)
        def _(index):
            part = span(index, third)
            grad_state[:, part] = against_weight(grad_pre[...], fc1[part, :])

    def middle_back():
        grad_hidden = grad_state[...]
        mod_grad[:, 3 * D : 4 * D] = columns_sum(grad_hidden)
        mod_grad[:, 4 * D : 5 * D] = columns_sum(grad_hidden * normed_two[...])
        grad_middle = live * cotangent[...].astype(jnp.float32) + norm_backward(
            grad_hidden * (1.0 + piece(4)), normed_two[...], inverse_two[...])
        mod_grad[:, 2 * D : 3 * D] = columns_sum(grad_middle * branch[...])
        grad_state[...] = grad_middle
        grad_branch = (piece(2) * grad_middle).astype(bfloat)
        proj_sums[...] = columns_sum(grad_branch.astype(jnp.float32))
        for index in range(columns):
            grad_proj_mixed[:, index * rest : index * rest + lead] = jnp.zeros(
                (length, lead), bfloat)
            grad_proj_mixed[:, index * rest + lead : (index + 1) * rest] = (
                grad_branch[:, index * proj_part : (index + 1) * proj_part])
        total = None
        for index in range(columns):
            term = against_weight(
                grad_proj_mixed[:, index * rest : (index + 1) * rest],
                mixed[:, index * block + edge : (index + 1) * block])
            total = term if total is None else total + term
        grad_attended[...] = total.astype(bfloat)

    def attend_back(low, high):
        @pl.loop(low, high)
        def _(pair):
            queries, keys, values = head_slabs(projected, pair)
            grad_out = grad_attended[:, span(pair, 128)]
            zero = jnp.zeros_like(grad_out)
            results = []
            for which in range(2):
                exact = probability[2 * pair + which]
                grad_prob = against_weight(jnp.where(own_lanes(which), grad_out, zero), values)
                inner = jnp.sum(exact * grad_prob, axis=-1, keepdims=True)
                grad_scores = (exact * (grad_prob - inner)).astype(bfloat)
                results.append((
                    dot_plain(grad_scores, keys) * scale_factor,
                    contract_rows(grad_scores, queries) * scale_factor,
                    contract_rows(exact.astype(bfloat), grad_out)))
            for kind in range(3):
                grad_natural[:, pl.ds(pl.multiple_of(kind * D + pair * 128, 128), 128)] = jnp.where(
                    own_lanes(0), results[0][kind], results[1][kind]).astype(bfloat)

    def mixed_weight_grad():
        qkv_sums[...] = columns_sum(grad_natural[...].astype(jnp.float32))
        for index in range(columns):
            grad_mixed[:, index * block : index * block + qkv_part] = (
                grad_natural[:, index * qkv_part : (index + 1) * qkv_part])
            grad_mixed[:, index * block + qkv_part : (index + 1) * block] = jnp.zeros(
                (length, proj_part), bfloat)
        scatter.wait_pairs_sent(2)

        @pl.loop(0, columns)
        def _(index):
            low = pl.multiple_of(index * block, 128)
            grads[0][:, pl.ds(low, edge)] = dot_plain(
                hidden_one_t[...], grad_mixed[:, pl.ds(low, edge)]).astype(bfloat)
            tail = pl.ds(pl.multiple_of(index * block + edge, 128), rest)
            grads[0][:, tail] = (
                dot_plain(hidden_one_t[...], grad_mixed[:, tail])
                + dot_plain(attended_t[...], grad_proj_mixed[:, span(index, rest)])).astype(bfloat)

    def finish_backward():
        @pl.loop(0, D // third)
        def _(index):
            part = span(index, third)
            branch[:, part] = against_weight(grad_mixed[...], mixed[part, :])

        grad_hidden = branch[...]
        mod_grad[:, :D] = columns_sum(grad_hidden)
        mod_grad[:, D : 2 * D] = columns_sum(grad_hidden * normed_one[...])
        latent_grad[...] = (grad_state[...] + norm_backward(
            grad_hidden * (1.0 + piece(1)), normed_one[...], inverse_one[...])).astype(bfloat)
        store(1)
        pad = jnp.zeros((1, mod_pad - mod_width), jnp.float32)
        qv_sums = jnp.concatenate([qkv_sums[:, :D], qkv_sums[:, 2 * D :]], axis=1)
        rows_of = (qv_sums, proj_sums[...], fc1_sums[...], fc2_sums[...])
        every = mod_grad[...]
        for index in range(columns):
            pieces = [every[:, index * mod_width : (index + 1) * mod_width], pad]
            for row in rows_of:
                share = row.shape[1] // columns
                pieces.append(row[:, index * share : (index + 1) * share])
            leaving[index] = jnp.concatenate(pieces, axis=1)
        rows_first.start()

    def share_rows():
        rows_first.wait_arrivals()
        rows_second.start()

    def own_sums():
        rows_second.wait_arrivals()
        arrived = jnp.concatenate([rows_across[row, :, 0, :] for row in range(rows)], axis=0)
        small[:, D:] = columns_sum(arrived)
        ada_grad[...] = contract_exact(cond_in[:, :ada_rows], arrived[:, :mod_width])
        store(2)
        back = lax.dot_general(
            arrived[:, :mod_width], ada_ref[...].astype(jnp.float32), (((1,), (1,)), ((), ())),
            precision=highest)
        for row in range(rows):
            back_out[row, :, :ada_rows] = back[row * columns : (row + 1) * columns]
        back_first.start()

    def share_back():
        back_first.wait_arrivals()
        for row in range(rows):
            back_row[:, row, 0, :] = back_across[row]
        back_second.start()

    def finish_condition():
        back_second.wait_arrivals()
        total = back_along[0]
        for source in range(1, columns):
            total = total + back_along[source]
        small[:, :D] = jnp.concatenate(
            [total[row][:, :ada_rows] for row in range(rows)], axis=1) * slope[...]
        store(7)

    def finish_fc2():
        fc2_grad[...] = scatter.finish_part(2)
        store(6)

    def finish_fc1():
        fc1_grad[...] = scatter.finish_part(1)
        store(5)

    def send_fc1_grad():
        fc1_weight_grad(1, 2)
        scatter.start_pairs(1)

    def send_mixed_grad():
        mixed_weight_grad()
        scatter.start_pairs(0)

    hooks = [
        lambda: fc1_weight_grad(0, 1), send_fc1_grad, hidden_two_back, middle_back,
        lambda: attend_back(0, 3), lambda: attend_back(3, 6), send_mixed_grad,
        finish_forward, finish_backward, finish_fc2, share_rows, own_sums, finish_fc1,
        share_back, finish_condition,
    ]
    for index, hook in enumerate(hooks):
        hook()
        scatter.turn(index + 1)
    total = scatter.finish_part(0)
    qkv_grad[...] = total[:, :qkv_part]
    proj_grad[...] = total[:, qkv_part:]
    store(3)
    store(4)
    scatter.wait_pairs_sent(1)
    scatter.wait_pairs_sent(0)
    scatter.wait_sends()
    gather.wait_sends()
    for swap in swaps:
        swap.wait_sends()
    for copy in stores:
        copy.wait()


def emit_kernel(*refs):
    sources, outs, held, sems = refs[:8], refs[8:21], refs[21:35], refs[35]
    loads = [
        pltpu.make_async_copy(source, hold, sems.at[0, at])
        for at, (source, hold) in enumerate(zip(sources, held[:1] + held[7:]))]
    stores = [
        pltpu.make_async_copy(hold, out, sems.at[1, at])
        for at, (hold, out) in enumerate(zip(held[1:], outs))]
    for load in loads:
        load.start()
    loads[0].wait()
    small, cond_grad, rows_out = held[0], held[1], held[2:7]
    cond_grad[...] = small[:, :D]
    low = D
    for out in rows_out:
        width = out.shape[0]
        out[...] = small[0, low : low + width]
        low += round_up(width) if low == D else width
    for store in stores[:6]:
        store.start()
    for load, store in zip(loads[1:], stores[6:]):
        load.wait()
        store.start()
    for store in stores:
        store.wait()


def emit(small, wholes, widths):
    anywhere = pl.BlockSpec(memory_space=pl.ANY)
    outs = [jax.ShapeDtypeStruct((1, D), jnp.float32)]
    outs += [jax.ShapeDtypeStruct((width,), jnp.float32) for width in widths]
    outs += [jax.ShapeDtypeStruct(whole.shape, whole.dtype) for whole in wholes]
    return pl.pallas_call(
        emit_kernel,
        out_shape=outs,
        in_specs=[anywhere] * (1 + len(wholes)),
        out_specs=[anywhere] * len(outs),
        scratch_shapes=[pltpu.VMEM(small.shape, small.dtype)]
        + [pltpu.VMEM(out.shape, out.dtype) for out in outs]
        + [pltpu.SemaphoreType.DMA((2, len(outs)))],
        name="emit",
    )(small, *wholes)


def run_layer(fc1_shard, fc2_turned_shard, sources, latent_count, rows, columns):
    latents, _, conditioning, ada_weight, _, qkv_shard, _, proj_shard = sources[:8]
    depth = columns // 2
    qkv_part, proj_part = qkv_shard.shape[1], proj_shard.shape[1]
    shards = (
        jax.ShapeDtypeStruct((qkv_shard.shape[0], qkv_part + proj_part), bfloat),
        fc1_shard, fc2_turned_shard)
    ada_rows, mod_width = ada_weight.shape
    cond_pad = round_up(ada_rows)
    bias_width = sum(sources[at].shape[0] for at in (6, 8, 9, 10))
    group = rows + bias_width // cond_pad
    count = (depth - 1) + depth * rows + depth * (rows - 1) + 2 * depth
    total = rows * columns
    mod_pad = round_up(mod_width)
    length = latents.shape[0]
    anywhere = pl.BlockSpec(memory_space=pl.ANY)
    dma = pltpu.SemaphoreType.DMA
    shapes = [
        whole_shape(shard.shape, part == 2, rows, columns) for part, shard in enumerate(shards)]
    row_buffer = lambda count, width: pltpu.VMEM((count, 1, width), jnp.float32)
    wide_row = lambda width: pltpu.VMEM((1, width), jnp.float32)
    single = lambda width: pltpu.VMEM((length, width), jnp.float32)
    half = lambda width: pltpu.VMEM((length, width), bfloat)
    turned = pltpu.VMEM((D, length), bfloat)
    rest = 128 * columns
    buffers = []
    for lead in ((depth, rows), (depth, 2), (depth, 2), (depth - 1,), (), (2,)):
        for shard in shards:
            height, width = shard.shape
            height = height // 2 if len(buffers) // 3 in (2, 5) else height
            buffers.append(pltpu.VMEM(lead + (height, width), bfloat))
    float_out = lambda *shape: jax.ShapeDtypeStruct(shape, jnp.float32)
    outs = [
        jax.ShapeDtypeStruct((length, D), bfloat),
        jax.ShapeDtypeStruct((length, D), bfloat),
        float_out(ada_rows, mod_width),
        float_out(qkv_shard.shape[0], qkv_part),
        float_out(qkv_shard.shape[0], proj_part),
        float_out(*fc1_shard.shape),
        float_out(*fc2_turned_shard.shape),
        float_out(1, D + mod_pad + bias_width),
    ]
    return pl.pallas_call(
        functools.partial(layer_kernel, rows, depth),
        out_shape=outs,
        in_specs=[anywhere] * 13 + [pl.BlockSpec(memory_space=pltpu.SMEM)],
        out_specs=[anywhere] * 8,
        scratch_shapes=[pltpu.VMEM(source.shape, source.dtype) for source in sources]
        + [pltpu.VMEM(out.shape, out.dtype) for out in outs[2:]]
        + [
            pltpu.VMEM(shards[0].shape, bfloat), row_buffer(rows, cond_pad), wide_row(D),
            dma((len(sources),)), dma((len(outs),)),
        ]
        + [pltpu.VMEM(shape, bfloat) for shape in shapes + shapes[:2]]
        + buffers + [
            dma((3, depth, rows)), dma((3, depth, rows)),
            dma((3, depth, 2)), dma((3, depth, 2)), dma((3, depth, 2)), dma((3, depth, 2)),
            dma((3, depth - 1)), dma((3, depth - 1)), dma((3, 3)), dma((3, 3)),
            dma((3,)), dma((3 * count,)), dma((2, 3, columns, rows)),
            dma((8, columns)), dma((8, columns)),
            row_buffer(rows, cond_pad), row_buffer(group, cond_pad),
            pltpu.VMEM((columns, group, 1, cond_pad), jnp.float32),
            pltpu.VMEM((total, cond_pad), jnp.float32),
            pltpu.VMEM((rows, columns, mod_pad), jnp.float32),
            pltpu.VMEM((rows, columns, mod_pad), jnp.float32),
            row_buffer(columns, mod_pad), row_buffer(columns, mod_pad),
            row_buffer(columns, mod_pad + bias_width), row_buffer(columns, mod_pad + bias_width),
            pltpu.VMEM((rows, columns, 1, mod_pad + bias_width), jnp.float32),
            pltpu.VMEM((rows, columns, cond_pad), jnp.float32),
            pltpu.VMEM((rows, columns, cond_pad), jnp.float32),
            pltpu.VMEM((columns, rows, 1, cond_pad), jnp.float32),
            pltpu.VMEM((columns, rows, 1, cond_pad), jnp.float32),
            wide_row(6 * D), wide_row(3 * D), wide_row(D), wide_row(FF), wide_row(D),
            wide_row(6 * D), wide_row(3 * D), wide_row(D), wide_row(FF), wide_row(D),
            single(1), single(1), single(D), single(D), single(D), single(D), single(FF),
            half(D), turned, half(D), turned, half(D), turned,
            half(D), turned, half(3 * D),
            half(rest), half(FF), half(FF), half(3 * D), single(D), pltpu.VMEM((HEADS, length, length), jnp.float32),
        ],
        compiler_params=pltpu.CompilerParams(
            collective_id=2, has_side_effects=True, vmem_limit_bytes=62 * 2**20),
        name="run_layer",
    )(fc1_shard, fc2_turned_shard, *sources, latent_count)


def pick(mixed, columns, kind):
    width = mixed.shape[1] // columns
    edge = 3 * width // 4
    low, high = (0, edge) if kind == 0 else (edge, width)
    return jnp.concatenate(
        [mixed[:, block * width + low : block * width + high] for block in range(columns)], axis=1
    )


def spread(rows_in, columns, kind):
    width = rows_in.shape[1] // columns
    rest = width // 3 if kind == 0 else 3 * width
    zeros = jnp.zeros((rows_in.shape[0], rest), rows_in.dtype)
    pieces = []
    for block in range(columns):
        piece = rows_in[:, block * width : (block + 1) * width]
        pieces += [piece, zeros] if kind == 0 else [zeros, piece]
    return jnp.concatenate(pieces, axis=1)


def layer(latent_rows, live, cot_rows, modulation, weights, biases, columns):
    mixed_weight, fc1_weight, fc2_turned = weights
    qv_bias, proj_bias, fc1_bias, fc2_bias = biases
    length = latent_rows.shape[0]
    rows_wide = latent_rows.astype(jnp.float32)
    shift_one, scale_one, gate_one, shift_two, scale_two, gate_two = jnp.split(
        modulation, 6, axis=-1
    )
    normed_one, inverse_one = normalize_rows(rows_wide)
    hidden_one = (normed_one * (1.0 + scale_one) + shift_one).astype(bfloat)
    qkv_bias = jnp.concatenate([qv_bias[:D], jnp.zeros((D,), jnp.float32), qv_bias[D:]])
    projected = (
        pick(jnp.dot(hidden_one, mixed_weight, preferred_element_type=jnp.float32), columns, 0)
        + qkv_bias
    ).astype(bfloat)
    queries = projected[:, :D].reshape(length, HEADS, HEAD)
    key_rows = projected[:, D : 2 * D].reshape(length, HEADS, HEAD)
    values = projected[:, 2 * D :].reshape(length, HEADS, HEAD)
    scale_factor = HEAD ** (-0.5)
    scores = (
        jnp.einsum("qhe,khe->hqk", queries, key_rows, preferred_element_type=jnp.float32)
        * scale_factor
    )
    row_max = jnp.max(scores, axis=-1, keepdims=True)
    shifted = jnp.exp(scores - row_max)
    row_total = jnp.sum(shifted, axis=-1, keepdims=True)
    exact_probability = shifted / row_total
    probability = exact_probability.astype(bfloat)
    attended = jnp.einsum("hqk,khe->qhe", probability, values, preferred_element_type=jnp.float32)
    attended = attended.reshape(length, D).astype(bfloat)
    branch = pick(jnp.dot(attended, mixed_weight, preferred_element_type=jnp.float32), columns, 1)
    branch = branch + proj_bias
    middle = rows_wide + gate_one * branch
    normed_two, inverse_two = normalize_rows(middle)
    hidden_two = (normed_two * (1.0 + scale_two) + shift_two).astype(bfloat)
    pre_gelu = jnp.dot(hidden_two, fc1_weight, preferred_element_type=jnp.float32) + fc1_bias
    activated, gelu_pull = jax.vjp(
        lambda argument: jax.nn.gelu(argument, approximate=True), pre_gelu
    )
    activated = activated.astype(bfloat)
    mlp_out = against_weight(activated, fc2_turned) + fc2_bias
    block_out = (live * (middle + gate_two * mlp_out)).astype(bfloat)

    grad_out = live * cot_rows.astype(jnp.float32)
    gate_two_grad = jnp.sum(grad_out * mlp_out, axis=0, keepdims=True)
    grad_mlp = (gate_two * grad_out).astype(bfloat)
    fc2_bias_grad = jnp.sum(grad_mlp.astype(jnp.float32), axis=0)
    grad_act = jnp.dot(grad_mlp, fc2_turned, preferred_element_type=jnp.float32)
    grad_pre = gelu_pull(grad_act)[0].astype(bfloat)
    fc1_bias_grad = jnp.sum(grad_pre.astype(jnp.float32), axis=0)
    grad_hidden_two = against_weight(grad_pre, fc1_weight)
    shift_two_grad = jnp.sum(grad_hidden_two, axis=0, keepdims=True)
    scale_two_grad = jnp.sum(grad_hidden_two * normed_two, axis=0, keepdims=True)
    grad_middle = grad_out + norm_backward(
        grad_hidden_two * (1.0 + scale_two), normed_two, inverse_two
    )
    gate_one_grad = jnp.sum(grad_middle * branch, axis=0, keepdims=True)
    grad_branch = (gate_one * grad_middle).astype(bfloat)
    proj_bias_grad = jnp.sum(grad_branch.astype(jnp.float32), axis=0)
    spread_branch = spread(grad_branch, columns, 1)
    grad_attended = (
        against_weight(spread_branch, mixed_weight).astype(bfloat).reshape(length, HEADS, HEAD)
    )
    grad_prob = jnp.einsum(
        "qhe,khe->hqk", grad_attended, values, preferred_element_type=jnp.float32
    )
    inner_sum = jnp.sum(exact_probability * grad_prob, axis=-1, keepdims=True)
    grad_scores = (exact_probability * (grad_prob - inner_sum)).astype(bfloat)
    grad_queries = (
        jnp.einsum("hqk,khe->qhe", grad_scores, key_rows, preferred_element_type=jnp.float32)
        * scale_factor
    )
    grad_keys = (
        jnp.einsum("hqk,qhe->khe", grad_scores, queries, preferred_element_type=jnp.float32)
        * scale_factor
    )
    grad_values = jnp.einsum(
        "hqk,qhe->khe", probability, grad_attended, preferred_element_type=jnp.float32
    )
    grad_projected = jnp.concatenate(
        [
            grad_queries.reshape(length, D),
            grad_keys.reshape(length, D),
            grad_values.reshape(length, D),
        ],
        axis=1,
    ).astype(bfloat)
    summed = jnp.sum(grad_projected.astype(jnp.float32), axis=0)
    qv_bias_grad = jnp.concatenate([summed[:D], summed[2 * D :]])
    spread_projected = spread(grad_projected, columns, 0)
    grad_hidden_one = against_weight(spread_projected, mixed_weight)
    shift_one_grad = jnp.sum(grad_hidden_one, axis=0, keepdims=True)
    scale_one_grad = jnp.sum(grad_hidden_one * normed_one, axis=0, keepdims=True)
    latent_grad = (
        grad_middle + norm_backward(grad_hidden_one * (1.0 + scale_one), normed_one, inverse_one)
    ).astype(bfloat)
    mod_grad = jnp.concatenate(
        [
            shift_one_grad,
            scale_one_grad,
            gate_one_grad,
            shift_two_grad,
            scale_two_grad,
            gate_two_grad,
        ],
        axis=-1,
    )
    weight_grads = (
        contract_rows(
            jnp.concatenate([hidden_one, attended]),
            jnp.concatenate([spread_projected, spread_branch]),
        ).astype(bfloat),
        contract_rows(hidden_two, grad_pre).astype(bfloat),
        contract_rows(grad_mlp, activated).astype(bfloat),
    )
    bias_grads = (qv_bias_grad, proj_bias_grad, fc1_bias_grad, fc2_bias_grad)
    return block_out, latent_grad, mod_grad, weight_grads, bias_grads


def flatten_blocks(blocks, turned):
    if blocks.ndim == 2:
        return blocks
    columns, rows, height, width = blocks.shape
    if turned:
        return blocks.transpose(0, 2, 1, 3).reshape(columns * height, rows * width)
    return blocks.transpose(1, 2, 0, 3).reshape(rows * height, columns * width)


def cut_blocks(whole, shape, turned, rows, columns):
    if len(whole_shape(shape, turned, rows, columns)) == 2:
        return whole
    height, width = shape
    if turned:
        return whole.reshape(columns, height, rows, width).transpose(0, 2, 1, 3)
    return whole.reshape(rows, height, columns, width).transpose(2, 0, 1, 3)


def per_device(
    latents,
    conditioning,
    cotangent,
    latent_count,
    ada_weight,
    ada_bias,
    qkv_weight,
    qv_bias,
    proj_weight,
    proj_bias,
    fc1_weight,
    fc1_bias,
    fc2_weight,
    fc2_bias,
):
    rows, columns = lax.axis_size("dp"), lax.axis_size("fsdp")
    if rows == 4 and columns == 8:
        sources = (
            latents[0], cotangent[0], conditioning, ada_weight, ada_bias, qkv_weight, qv_bias,
            proj_weight, proj_bias, fc1_bias, fc2_bias)
        *wholes, small = run_layer(
            fc1_weight, fc2_weight.T, sources, latent_count, rows, columns)
        widths = [bias.shape[0] for bias in (ada_bias, qv_bias, proj_bias, fc1_bias, fc2_bias)]
        (
            cond_grad, ada_bias_grad, qv_bias_grad, proj_bias_grad, fc1_bias_grad, fc2_bias_grad,
            block_out, latent_grad, ada_grad, qkv_grad, proj_grad, fc1_grad, fc2_turned_grad,
        ) = emit(small, wholes, widths)
        return (
            block_out[None], latent_grad[None], cond_grad, ada_grad, ada_bias_grad, qkv_grad,
            qv_bias_grad, proj_grad, proj_bias_grad, fc1_grad, fc1_bias_grad, fc2_turned_grad.T,
            fc2_bias_grad,
        )
    live = latent_count[0].astype(jnp.float32)
    depth = ada_weight.shape[0]
    mod_width = ada_weight.shape[1]
    mod_pad = round_up(mod_width)
    own_biases = (qv_bias, proj_bias, fc1_bias, fc2_bias)
    widths = [bias.shape[0] for bias in own_biases]
    cuts = [sum(widths[:place]) for place in range(len(widths))]

    def split_cond(row):
        pad = round_up(depth) - depth
        return jnp.pad(row.reshape(rows, 1, depth), ((0, 0), (0, 0), (0, pad)))

    cond_row = conditioning.astype(jnp.float32)
    cond_act, silu_pull = jax.vjp(jax.nn.silu, cond_row)
    slope = silu_pull(jnp.ones_like(cond_row))[0]
    cond_rows = split_cond(cond_act.astype(bfloat).astype(jnp.float32))
    bias_row = jnp.concatenate(own_biases).astype(jnp.float32).reshape(1, -1)

    qkv_width = qkv_weight.shape[1]
    shards = (
        jnp.concatenate([qkv_weight, proj_weight], axis=1),
        fc1_weight,
        fc2_weight.T,
    )
    shapes = [shard.shape for shard in shards]
    ada_row = ada_bias.astype(jnp.float32).reshape(1, -1)
    *blocks, mod_blocks, bias_blocks, cond_in = gather_shards(
        shards, cond_rows, ada_weight, ada_row, bias_row,
        rows, columns)
    modulation = mod_blocks[:, :, :mod_width].reshape(1, -1)
    biases = tuple(
        bias_blocks[:, :, cut : cut + width].reshape(-1) for cut, width in zip(cuts, widths)
    )
    weights = [flatten_blocks(block, part == 2) for part, block in enumerate(blocks)]
    block_out, latent_grad, mod_grad, weight_grads, bias_grads = layer(
        latents[0], live, cotangent[0], modulation, weights, biases, columns
    )
    grads = [
        cut_blocks(grad, shapes[part], part == 2, rows, columns)
        for part, grad in enumerate(weight_grads)
    ]
    leaving = jnp.concatenate(
        [jnp.pad(mod_grad.reshape(columns, -1), ((0, 0), (0, mod_pad - mod_width)))]
        + [grad.reshape(columns, -1) for grad in bias_grads], axis=1
    ).reshape(columns, 1, -1)
    mixed_grad, fc1_grad, fc2_turned_grad, ada_grad, sums, cond_grad = scatter_shards(
        grads, leaving, cond_in, ada_weight, split_cond(slope), shapes, rows, columns)
    qkv_grad, proj_grad = mixed_grad[:, :qkv_width], mixed_grad[:, qkv_width:]
    fc2_grad = fc2_turned_grad.T
    ada_bias_grad = sums[0, :mod_width]
    bias_sums = [
        sums[0, mod_pad + cut : mod_pad + cut + width] for cut, width in zip(cuts, widths)]
    cond_grad = cond_grad[:, :, :depth].reshape(1, -1)
    return (
        block_out[None],
        latent_grad[None],
        cond_grad,
        ada_grad,
        ada_bias_grad,
        qkv_grad,
        bias_sums[0],
        proj_grad,
        bias_sums[1],
        fc1_grad,
        bias_sums[2],
        fc2_grad,
        bias_sums[3],
    )


def solution(mesh):
    in_specs = (
        P(("dp", "fsdp"), None, None),
        P(("dp", "fsdp"), None),
        P(("dp", "fsdp"), None, None),
        P(("dp", "fsdp")),
        P("dp", "fsdp"),
        P("fsdp"),
        P("dp", "fsdp"),
        P("fsdp"),
        P("dp", "fsdp"),
        P("fsdp"),
        P("dp", "fsdp"),
        P("fsdp"),
        P("dp", "fsdp"),
        P("fsdp"),
    )
    out_specs = (
        P(("dp", "fsdp"), None, None),
        P(("dp", "fsdp"), None, None),
        P(("dp", "fsdp"), None),
        P("dp", "fsdp"),
        P("fsdp"),
        P("dp", "fsdp"),
        P("fsdp"),
        P("dp", "fsdp"),
        P("fsdp"),
        P("dp", "fsdp"),
        P("fsdp"),
        P("dp", "fsdp"),
        P("fsdp"),
    )
    return jax.shard_map(
        per_device, mesh=mesh, in_specs=in_specs, out_specs=out_specs, check_vma=False
    )
```
